32 devices in a mesh: dp: 8 (over y, x, core), tensor: 4 (over z).
Axes of the slice: x: 2, y: 2, z: 4, core: 2. Of those that a mesh axis runs over, the one named last changes fastest.
Arguments:
- layer_input: bfloat16 [8, 640, 768], P('dp'), may hold values from -6 to 6
- segment_ids: int32 [8, 640], P('dp'), may hold values from 0 to 3, never falling along the last dimension, each value on 1 to 256 neighbouring positions
- token_types: int32 [8, 640], P('dp'), may hold values 0 or 1
- query_weight: float32 [4, 768, 768], P(None, 'dp', 'tensor'), may hold values from -0.21875 to 0.21875
- key_weight: float32 [768, 768], P('dp', 'tensor'), may hold values from -0.21875 to 0.21875
- value_weight: float32 [768, 768], P('dp', 'tensor'), may hold values from -0.21875 to 0.21875
- out_weight: float32 [768, 768], P('tensor', 'dp'), may hold values from -0.875 to 0.875
- up_weight: float32 [768, 3072], P('dp', 'tensor'), may hold values from -0.21875 to 0.21875
- down_weight: float32 [3072, 768], P('tensor', 'dp'), may hold values from -0.109375 to 0.109375
- query_bias: float32 [4, 768], P(None, 'tensor'), may hold values from -3 to 3
- value_bias: float32 [768], P('tensor'), may hold values from -3 to 3
- out_bias: float32 [768], replicated, may hold values from -2 to 2
- up_bias: float32 [3072], P('tensor'), may hold values from -3 to 3
- down_bias: float32 [768], replicated, may hold values from -2 to 2
- attn_gain: float32 [768], replicated, may hold values from 0.1 to 1.9
- attn_shift: float32 [768], replicated, may hold values from -2 to 2
- ffn_gain: float32 [768], replicated, may hold values from 0.1 to 1.9
- ffn_shift: float32 [768], replicated, may hold values from -2 to 2
- cotangent: bfloat16 [8, 640, 768], P('dp'), may hold values from -6 to 6
Outputs:
- output: bfloat16 [8, 640, 768], P('dp')
- input_grad: bfloat16 [8, 640, 768], P('dp')
- query_grad: float32 [4, 768, 768], P(None, 'dp', 'tensor')
- key_grad: float32 [768, 768], P('dp', 'tensor')
- value_grad: float32 [768, 768], P('dp', 'tensor')
- outproj_grad: float32 [768, 768], P('tensor', 'dp')
- upproj_grad: float32 [768, 3072], P('dp', 'tensor')
- downproj_grad: float32 [3072, 768], P('tensor', 'dp')
- querybias_grad: float32 [4, 768], P(None, 'tensor')
- valuebias_grad: float32 [768], P('tensor')
- outbias_grad: float32 [768], replicated
- upbias_grad: float32 [3072], P('tensor')
- downbias_grad: float32 [768], replicated
- attngain_grad: float32 [768], replicated
- attnshift_grad: float32 [768], replicated
- ffngain_grad: float32 [768], replicated
- ffnshift_grad: float32 [768], replicated
The draws below stay inside these ranges and needn't reach their ends.
Inputs may be any that keep to these rules, and one draw needn't show every extreme that they name: `segment_ids`: along a row segment numbers never fall, and one segment spans at most 256 positions.
All inputs are finite; a program needn't handle non-finite values. No bound on the sum of `token_types` on one device may be relied on, other than what follows from the above.
Results may differ from the reference program's by a relative error of at most 0.013.
The reference program's roundings to bfloat16 on the way count: a program that leaves them out, or rounds other values in their place, can miss the bound.
Values may be sent and summed in bfloat16 or wider, within the bound.
A program may use at most 128 MiB of HBM per device.

```python
import math
import jax
import jax.numpy as jnp
import numpy as np
from jax import lax

D = 768
HEADS = 12
HD = 64
FF = 3072
LEN = 640
SEGS = 4
MOST = 256
SEQS = 8


def with_ends(entries, rng, smallest, largest):
    index_at = [jax.random.randint(jax.random.fold_in(rng, axis), (), 0, length) for axis, length in enumerate(entries.shape)]
    main_axis = entries.shape.index(max(entries.shape))
    neighbour = index_at[:main_axis] + [(index_at[main_axis] + 1) % entries.shape[main_axis]] + index_at[main_axis + 1:]
    return entries.at[tuple(index_at)].set(smallest).at[tuple(neighbour)].set(largest)


def block_scale(own_key, shape, shards, least, largest):
    def one(axis_at, parts):
        heights = jax.random.uniform(jax.random.fold_in(jax.random.fold_in(own_key, 6), axis_at), (parts,), jnp.float32, least / len(shards), largest / len(shards))
        return jnp.repeat(jnp.exp(heights), shape[axis_at] // parts).reshape((-1,) + (1,) * (len(shape) - axis_at - 1))

    level = one(*shards[0])
    for cut in shards[1:]:
        level = level * one(*cut)
    return level


def length_profile(number_of, total, reach, slope):
    loads = [(1 << 20) // math.isqrt(rank ** slope) + 1 for rank in range(2, number_of + 1)]
    rest, counts = total - reach - (number_of - 1), [1] * (number_of - 1)
    while rest > 0:
        movable = [i for i in range(number_of - 1) if counts[i] < reach]
        mass, remaining = sum([loads[i] for i in movable]), rest
        for i in movable:
            more = min(reach - counts[i], max(1, remaining * loads[i] // mass), rest)
            counts[i] = counts[i] + more
            rest = rest - more
    return np.array([reach] + counts)


def uneven(stream_key, number_of, total, bound, slope):
    if number_of == 2:
        one = jax.random.randint(stream_key, (), max(1, total - bound), min(bound, total - 1) + 1)
        return jnp.stack([one, total - one])
    tallies = jnp.asarray(length_profile(number_of, total, bound, slope), jnp.int32)
    pairs = (number_of - 1) // 2
    donor, sink = tallies[1:1 + 2 * pairs:2], tallies[2:2 + 2 * pairs:2]
    slack = jnp.minimum(donor - 1, bound - sink)
    moved = jax.random.randint(jax.random.fold_in(stream_key, 1), (pairs,), 0, 1 << 20) % (slack + 1)
    tallies = tallies.at[1:1 + 2 * pairs:2].set(donor - moved).at[2:2 + 2 * pairs:2].set(sink + moved)
    return tallies[jax.random.permutation(jax.random.fold_in(stream_key, 2), number_of)]


def normal_values(rng, dims, width, most, cuts=(), dtype=jnp.bfloat16):
    loudness = block_scale(rng, dims, cuts, -0.22, 0.18) if cuts else 1.0
    entries = jax.random.normal(rng, dims, jnp.float32) * width * loudness
    return jnp.minimum(jnp.maximum(entries, -most), most).astype(dtype)


def setup_inputs(seed: int = 0) -> dict:
    streams_of = jax.random.split(jax.random.key(seed), 20)
    layer_input = normal_values(streams_of[0], (SEQS, LEN, D), 1.0, 6.0, ((0, 8),))
    segment_ids = jax.vmap(lambda own: jnp.searchsorted(jnp.cumsum(uneven(own, SEGS, LEN, MOST, 0)), jnp.arange(LEN), side="right"))(jax.random.split(streams_of[1], SEQS)).reshape((SEQS, LEN)).astype(jnp.int32)
    token_types = with_ends((jax.random.randint(streams_of[2], (SEQS, LEN), 0, 5) < 1).astype(jnp.int32), jax.random.fold_in(streams_of[2], 1), 0, 1)
    query_weight = normal_values(streams_of[3], (4, D, D), D ** -0.5, 0.21875, ((1, 8), (2, 4)), jnp.float32)
    key_weight = normal_values(streams_of[4], (D, D), D ** -0.5, 0.21875, ((0, 8), (1, 4)), jnp.float32)
    value_weight = normal_values(streams_of[5], (D, D), D ** -0.5, 0.21875, ((0, 8), (1, 4)), jnp.float32)
    out_weight = normal_values(streams_of[6], (D, D), (D // 16) ** -0.5, 0.875, ((0, 4), (1, 8)), jnp.float32)
    up_weight = normal_values(streams_of[7], (D, FF), D ** -0.5, 0.21875, ((0, 8), (1, 4)), jnp.float32)
    down_weight = normal_values(streams_of[8], (FF, D), FF ** -0.5, 0.109375, ((0, 4), (1, 8)), jnp.float32)
    query_bias = normal_values(streams_of[9], (4, D), 0.5, 3.0, ((1, 4),), jnp.float32)
    value_bias = normal_values(streams_of[10], (D,), 0.5, 3.0, ((0, 4),), jnp.float32)
    out_bias = normal_values(streams_of[11], (D,), 0.3, 2.0, (), jnp.float32)
    up_bias = normal_values(streams_of[12], (FF,), 0.5, 3.0, ((0, 4),), jnp.float32)
    down_bias = normal_values(streams_of[13], (D,), 0.3, 2.0, (), jnp.float32)
    attn_gain = jnp.clip(1.0 + 0.18 * jax.random.normal(streams_of[14], (D,), jnp.float32), 0.1, 1.9)
    attn_shift = normal_values(streams_of[15], (D,), 0.3, 2.0, (), jnp.float32)
    ffn_gain = jnp.clip(1.0 + 0.18 * jax.random.normal(streams_of[16], (D,), jnp.float32), 0.1, 1.9)
    ffn_shift = normal_values(streams_of[17], (D,), 0.3, 2.0, (), jnp.float32)
    cotangent = normal_values(streams_of[18], (SEQS, LEN, D), 1.0, 6.0, ((0, 8),))
    return {"layer_input": layer_input, "segment_ids": segment_ids, "token_types": token_types, "query_weight": query_weight, "key_weight": key_weight, "value_weight": value_weight, "out_weight": out_weight, "up_weight": up_weight, "down_weight": down_weight, "query_bias": query_bias, "value_bias": value_bias, "out_bias": out_bias, "up_bias": up_bias, "down_bias": down_bias, "attn_gain": attn_gain, "attn_shift": attn_shift, "ffn_gain": ffn_gain, "ffn_shift": ffn_shift, "cotangent": cotangent}


EPSILON = 1e-05
SCALING = 0.125
NEGATIVE = -1000000000.0
HIGHEST = lax.Precision.HIGHEST

@jax.custom_vjp
def low(v):
    return lax.optimization_barrier(v.astype(jnp.bfloat16)).astype(jnp.float32)

@jax.custom_vjp
def low_back(v):
    return v

def low_keep(v):
    return (low(v), None)

def low_pass(kept, grad):
    return (grad,)

def back_keep(v):
    return (v, None)

def back_low(kept, grad):
    return (low(grad),)
low.defvjp(low_keep, low_pass)
low_back.defvjp(back_keep, back_low)

def layer_norm(values, norm_gain, norm_shift):
    centre = values - lax.optimization_barrier(jnp.mean(values, axis=-1, keepdims=True))
    spread = lax.optimization_barrier(jnp.mean(centre * centre, axis=-1, keepdims=True))
    return centre * lax.rsqrt(spread + EPSILON) * norm_gain + norm_shift

def attend(packed):
    query_rows, keys_seq, values_seq, segment_row, type_row = packed
    word_tok = (type_row == 0)[:, None]
    word_query = jnp.where(word_tok, query_rows[0], query_rows[2]).reshape(LEN, HEADS, HD)
    entity_query = jnp.where(word_tok, query_rows[1], query_rows[3]).reshape(LEN, HEADS, HD)
    key_heads = keys_seq.reshape(LEN, HEADS, HD)
    value_heads = values_seq.reshape(LEN, HEADS, HD)
    to_words = jnp.einsum('qhd,khd->hqk', word_query, key_heads, precision=HIGHEST)
    to_entities = jnp.einsum('qhd,khd->hqk', entity_query, key_heads, precision=HIGHEST)
    scores = low_back(jnp.where((type_row == 0)[None, None, :], to_words, to_entities) * SCALING)
    allowed = (segment_row[:, None] == segment_row[None, :])[None]
    scores = jnp.where(allowed, scores, NEGATIVE)
    row_top = lax.optimization_barrier(jnp.max(scores, axis=-1, keepdims=True))
    weights = jnp.exp(scores - row_top)
    attn_probs = weights / lax.optimization_barrier(jnp.sum(weights, axis=-1, keepdims=True))
    context = jnp.einsum('hqk,khd->qhd', low(attn_probs), value_heads, precision=HIGHEST)
    return context.reshape(LEN, D)

def forward(hidden, query_weight, key_weight, value_weight, out_weight, up_weight, down_weight, query_bias, value_bias, out_bias, up_bias, down_bias, attn_gain, attn_shift, ffn_gain, ffn_shift, segment_ids, token_types):
    tokens = hidden.reshape(-1, D)
    seq_count = tokens.shape[0] // LEN
    query_rows = jnp.einsum('td,cde->cte', tokens, low(query_weight), precision=HIGHEST)
    query_rows = low(low_back(query_rows) + query_bias[:, None, :])
    keys_all = low(low_back(jnp.dot(tokens, low(key_weight), precision=HIGHEST)))
    values_all = low(low_back(jnp.dot(tokens, low(value_weight), precision=HIGHEST)) + value_bias)
    queries_seq = jnp.transpose(query_rows.reshape(4, seq_count, LEN, D), (1, 0, 2, 3))
    context = lax.map(jax.checkpoint(attend), (queries_seq, keys_all.reshape(seq_count, LEN, D), values_all.reshape(seq_count, LEN, D), segment_ids, token_types))
    context = low(low_back(context.reshape(-1, D)))
    attended = low_back(jnp.dot(context, low(out_weight), precision=HIGHEST)) + out_bias
    normed = layer_norm(tokens + attended, attn_gain, attn_shift)
    pre_act = low_back(jnp.dot(low(normed), low(up_weight), precision=HIGHEST)) + up_bias
    activated = jax.nn.gelu(pre_act, approximate=False)
    ffn_out = low_back(jnp.dot(low(activated), low(down_weight), precision=HIGHEST)) + down_bias
    return layer_norm(normed + ffn_out, ffn_gain, ffn_shift).reshape(hidden.shape)

def reference(layer_input, segment_ids, token_types, query_weight, key_weight, value_weight, out_weight, up_weight, down_weight, query_bias, value_bias, out_bias, up_bias, down_bias, attn_gain, attn_shift, ffn_gain, ffn_shift, cotangent):
    params = (layer_input.astype(jnp.float32), query_weight.astype(jnp.float32), key_weight.astype(jnp.float32), value_weight.astype(jnp.float32), out_weight.astype(jnp.float32), up_weight.astype(jnp.float32), down_weight.astype(jnp.float32), query_bias.astype(jnp.float32), value_bias.astype(jnp.float32), out_bias.astype(jnp.float32), up_bias.astype(jnp.float32), down_bias.astype(jnp.float32), attn_gain.astype(jnp.float32), attn_shift.astype(jnp.float32), ffn_gain.astype(jnp.float32), ffn_shift.astype(jnp.float32))

    def closed(*values):
        return forward(*values, segment_ids, token_types)
    result, pullback = jax.vjp(closed, *params)
    gradients = pullback(cotangent.astype(jnp.float32))
    return (result.astype(jnp.bfloat16), gradients[0].astype(jnp.bfloat16), gradients[1], gradients[2], gradients[3], gradients[4], gradients[5], gradients[6], gradients[7], gradients[8], gradients[9], gradients[10], gradients[11], gradients[12], gradients[13], gradients[14], gradients[15])
```

```python
from functools import partial

import jax
import jax.numpy as jnp
from jax import lax
from jax.experimental import pallas as pl
from jax.experimental.pallas import tpu as pltpu
from jax.sharding import PartitionSpec as P

HD = 64


EPSILON = 1e-05
SCALING = 0.125
NEGATIVE = -1000000000.0


def layer_norm_keep(values, norm_gain, norm_shift):
    centre = values - jnp.mean(values, axis=-1, keepdims=True)
    inverse = lax.rsqrt(jnp.mean(centre * centre, axis=-1, keepdims=True) + EPSILON)
    normal = centre * inverse
    return (normal * norm_gain + norm_shift, normal, inverse)


def layer_norm_back(upstream, normal, inverse, norm_gain):
    scaled = upstream * norm_gain
    gain_grad = jnp.sum(upstream * normal, axis=0)
    shift_grad = jnp.sum(upstream, axis=0)
    inner_term = (
        scaled
        - jnp.mean(scaled, axis=-1, keepdims=True)
        - normal * jnp.mean(scaled * normal, axis=-1, keepdims=True)
    )
    return (inverse * inner_term, gain_grad, shift_grad)


def heads_of(matrix):
    return matrix.reshape(matrix.shape[0], -1, HD)


def pick_queries(query_rows, type_row):
    word_tok = (type_row == 0)[:, None]
    return (
        jnp.where(word_tok, query_rows[0], query_rows[2]),
        jnp.where(word_tok, query_rows[1], query_rows[3]),
    )


def score_block(word_heads, entity_heads, key_heads, segment_row, type_row):
    to_words = jnp.einsum("qhd,khd->hqk", word_heads, key_heads, preferred_element_type=jnp.float32)
    to_entities = jnp.einsum(
        "qhd,khd->hqk", entity_heads, key_heads, preferred_element_type=jnp.float32
    )
    scores = jnp.where((type_row == 0)[None, None, :], to_words, to_entities) * SCALING
    allowed = (segment_row[:, None] == segment_row[None, :])[None]
    return jnp.where(allowed, scores, NEGATIVE)


def attend_forward(packed):
    query_rows, key_seq, value_seq, segment_row, type_row = packed
    word_query, entity_query = pick_queries(query_rows, type_row)
    scores = score_block(
        heads_of(word_query), heads_of(entity_query), heads_of(key_seq), segment_row, type_row
    )
    row_top = jnp.max(scores, axis=-1, keepdims=True)
    weights = jnp.exp(scores - row_top)
    totals = jnp.sum(weights, axis=-1, keepdims=True)
    attn_probs = (weights / totals).astype(jnp.bfloat16)
    context = jnp.einsum(
        "hqk,khd->qhd", attn_probs, heads_of(value_seq), preferred_element_type=jnp.float32
    )
    log_total = (row_top + jnp.log(totals))[..., 0]
    return (context.reshape(context.shape[0], -1).astype(jnp.bfloat16), log_total)


def attend_backward(packed):
    query_rows, key_seq, value_seq, segment_row, type_row, log_total, context_grad = packed
    word_query, entity_query = pick_queries(query_rows, type_row)
    word_heads = heads_of(word_query)
    entity_heads = heads_of(entity_query)
    key_heads = heads_of(key_seq)
    value_heads = heads_of(value_seq)
    grad_heads = heads_of(context_grad)
    scores = score_block(word_heads, entity_heads, key_heads, segment_row, type_row)
    attn_probs = jnp.exp(scores - log_total[..., None])
    prob_grad = jnp.einsum(
        "qhd,khd->hqk", grad_heads, value_heads, preferred_element_type=jnp.float32
    )
    score_grad = attn_probs * (prob_grad - jnp.sum(attn_probs * prob_grad, axis=-1, keepdims=True))
    score_low = score_grad.astype(jnp.bfloat16)
    word_key = (type_row == 0)[None, None, :]
    zeroes = jnp.zeros_like(score_low)
    word_part = jnp.where(word_key, score_low, zeroes)
    entity_part = jnp.where(word_key, zeroes, score_low)
    word_qgrad = (
        jnp.einsum("hqk,khd->qhd", word_part, key_heads, preferred_element_type=jnp.float32)
        * SCALING
    )
    entity_qgrad = (
        jnp.einsum("hqk,khd->qhd", entity_part, key_heads, preferred_element_type=jnp.float32)
        * SCALING
    )
    key_delta = (
        jnp.einsum("hqk,qhd->khd", word_part, word_heads, preferred_element_type=jnp.float32)
        + jnp.einsum("hqk,qhd->khd", entity_part, entity_heads, preferred_element_type=jnp.float32)
    ) * SCALING
    value_delta = jnp.einsum(
        "hqk,qhd->khd",
        attn_probs.astype(jnp.bfloat16),
        grad_heads,
        preferred_element_type=jnp.float32,
    )
    row_count = word_qgrad.shape[0]
    return (
        word_qgrad.reshape(row_count, -1),
        entity_qgrad.reshape(row_count, -1),
        key_delta.reshape(row_count, -1),
        value_delta.reshape(row_count, -1),
    )


def row_share(partial_rows):
    return lax.psum_scatter(partial_rows, "tensor", scatter_dimension=0, tiled=True)


def row_whole(rounded_rows):
    return lax.all_gather(rounded_rows, "tensor", axis=0, tiled=True)


def shards(
    layer_input,
    segment_ids,
    token_types,
    query_weight,
    key_weight,
    value_weight,
    out_weight,
    up_weight,
    down_weight,
    query_bias,
    value_bias,
    out_bias,
    up_bias,
    down_bias,
    attn_gain,
    attn_shift,
    ffn_gain,
    ffn_shift,
    cotangent,
):
    seq_count, seq_length, model_width = layer_input.shape
    tokens = layer_input.reshape(-1, model_width)
    row_count = tokens.shape[0]
    share = row_count // lax.axis_size("tensor")
    first_row = lax.axis_index("tensor") * share

    def own_rows(matrix):
        return lax.dynamic_slice_in_dim(matrix, first_row, share, 0)

    def combine_rows(partial_rows):
        return row_share(partial_rows)

    def whole_rows(rounded_rows):
        return row_whole(rounded_rows)

    query_complete, key_full, value_full, out_full = (
        lax.all_gather(query_weight.astype(jnp.bfloat16), "dp", axis=1, tiled=True),
        lax.all_gather(key_weight.astype(jnp.bfloat16), "dp", axis=0, tiled=True),
        lax.all_gather(value_weight.astype(jnp.bfloat16), "dp", axis=0, tiled=True),
        lax.all_gather(out_weight.astype(jnp.bfloat16), "dp", axis=1, tiled=True),
    )
    local_width = key_full.shape[1]
    query_rows = jnp.einsum(
        "gow,qwk->gqok", layer_input, query_complete, preferred_element_type=jnp.float32
    )
    query_rows = (query_rows + query_bias[None, :, None, :]).astype(jnp.bfloat16)
    keys_all = jnp.dot(layer_input, key_full, preferred_element_type=jnp.float32).astype(
        jnp.bfloat16
    )
    values_all = (
        jnp.dot(layer_input, value_full, preferred_element_type=jnp.float32) + value_bias
    ).astype(jnp.bfloat16)
    context, log_total = lax.map(
        attend_forward, (query_rows, keys_all, values_all, segment_ids, token_types)
    )
    context_rows = context.reshape(-1, local_width)
    attended = combine_rows(jnp.dot(context_rows, out_full, preferred_element_type=jnp.float32))
    residual = own_rows(tokens).astype(jnp.float32) + attended + out_bias
    normed, normal_one, inverse_one = layer_norm_keep(residual, attn_gain, attn_shift)
    normed_low = whole_rows(normed.astype(jnp.bfloat16))
    up_full, down_full = (
        lax.all_gather(up_weight.astype(jnp.bfloat16), "dp", axis=0, tiled=True),
        lax.all_gather(down_weight.astype(jnp.bfloat16), "dp", axis=1, tiled=True),
    )
    pre_act = jnp.dot(normed_low, up_full, preferred_element_type=jnp.float32) + up_bias
    activated, gelu_pull = jax.vjp(partial(jax.nn.gelu, approximate=False), pre_act)
    act_low = activated.astype(jnp.bfloat16)
    ffn_out = (
        combine_rows(jnp.dot(act_low, down_full, preferred_element_type=jnp.float32)) + down_bias
    )
    normed_out, normal_two, inverse_two = layer_norm_keep(normed + ffn_out, ffn_gain, ffn_shift)
    output = whole_rows(normed_out.astype(jnp.bfloat16)).reshape(layer_input.shape)
    upstream = own_rows(cotangent.reshape(-1, model_width)).astype(jnp.float32)
    sum_grad, ffngain_grad, ffnshift_grad = layer_norm_back(
        upstream, normal_two, inverse_two, ffn_gain
    )
    downbias_grad = jnp.sum(sum_grad, axis=0)
    sum_low = whole_rows(sum_grad.astype(jnp.bfloat16))
    up_back, down_back = (
        lax.all_gather(up_weight.astype(jnp.bfloat16), "dp", axis=0, tiled=True),
        lax.all_gather(down_weight.astype(jnp.bfloat16), "dp", axis=1, tiled=True),
    )
    down_local = jnp.dot(act_low.T, sum_low, preferred_element_type=jnp.float32)
    act_grad = jnp.dot(sum_low, down_back.T, preferred_element_type=jnp.float32)
    (pre_grad,) = gelu_pull(act_grad)
    upbias_grad = jnp.sum(pre_grad, axis=0)
    pre_low = pre_grad.astype(jnp.bfloat16)
    up_local = jnp.dot(normed_low.T, pre_low, preferred_element_type=jnp.float32)
    upproj_grad, downproj_grad = (
        lax.psum_scatter(up_local, "dp", scatter_dimension=0, tiled=True),
        lax.psum_scatter(down_local, "dp", scatter_dimension=1, tiled=True),
    )
    normed_grad = (
        combine_rows(jnp.dot(pre_low, up_back.T, preferred_element_type=jnp.float32)) + sum_grad
    )
    resid_grad, attngain_grad, attnshift_grad = layer_norm_back(
        normed_grad, normal_one, inverse_one, attn_gain
    )
    outbias_grad = jnp.sum(resid_grad, axis=0)
    resid_low = whole_rows(resid_grad.astype(jnp.bfloat16))
    query_pullback, key_pullback, value_pullback, out_back = (
        lax.all_gather(query_weight.astype(jnp.bfloat16), "dp", axis=1, tiled=True),
        lax.all_gather(key_weight.astype(jnp.bfloat16), "dp", axis=0, tiled=True),
        lax.all_gather(value_weight.astype(jnp.bfloat16), "dp", axis=0, tiled=True),
        lax.all_gather(out_weight.astype(jnp.bfloat16), "dp", axis=1, tiled=True),
    )
    outproj_local = jnp.dot(context_rows.T, resid_low, preferred_element_type=jnp.float32)
    context_grad = jnp.dot(resid_low, out_back.T, preferred_element_type=jnp.float32).astype(
        jnp.bfloat16
    )
    context_grad = context_grad.reshape(seq_count, seq_length, local_width)
    word_qgrad, entity_qgrad, key_delta, value_delta = lax.map(
        attend_backward,
        (query_rows, keys_all, values_all, segment_ids, token_types, log_total, context_grad),
    )
    is_word = (token_types == 0)[..., None]
    zero_rows = jnp.zeros_like(word_qgrad)
    query_delta = jnp.stack(
        [
            jnp.where(is_word, word_qgrad, zero_rows),
            jnp.where(is_word, entity_qgrad, zero_rows),
            jnp.where(is_word, zero_rows, word_qgrad),
            jnp.where(is_word, zero_rows, entity_qgrad),
        ],
        axis=1,
    )
    querybias_grad = jnp.sum(query_delta, axis=(0, 2))
    valuebias_grad = jnp.sum(value_delta, axis=(0, 1))
    query_reduced = query_delta.astype(jnp.bfloat16)
    key_reduced = key_delta.astype(jnp.bfloat16)
    value_reduced = value_delta.astype(jnp.bfloat16)
    query_local = jnp.einsum(
        "nvh,nkvw->khw", layer_input, query_reduced, preferred_element_type=jnp.float32
    )
    key_shard = jnp.einsum(
        "pui,pun->in", layer_input, key_reduced, preferred_element_type=jnp.float32
    )
    value_local = jnp.einsum(
        "pui,pun->in", layer_input, value_reduced, preferred_element_type=jnp.float32
    )
    input_part = (
        jnp.einsum(
            "kayo,azo->kyz", query_reduced, query_pullback, preferred_element_type=jnp.float32
        )
        + jnp.einsum("ohz,wz->ohw", key_reduced, key_pullback, preferred_element_type=jnp.float32)
        + jnp.einsum(
            "ohz,wz->ohw", value_reduced, value_pullback, preferred_element_type=jnp.float32
        )
    )
    input_total = combine_rows(input_part.reshape(-1, model_width))
    input_grad = whole_rows((input_total + resid_grad).astype(jnp.bfloat16)).reshape(
        layer_input.shape
    )
    query_grad, key_grad, value_grad, outproj_grad = (
        lax.psum_scatter(query_local, "dp", scatter_dimension=1, tiled=True),
        lax.psum_scatter(key_shard, "dp", scatter_dimension=0, tiled=True),
        lax.psum_scatter(value_local, "dp", scatter_dimension=0, tiled=True),
        lax.psum_scatter(outproj_local, "dp", scatter_dimension=1, tiled=True),
    )
    querybias_grad, valuebias_grad, upbias_grad = lax.psum(
        (querybias_grad, valuebias_grad, upbias_grad), "dp"
    )
    outbias_grad, downbias_grad, attngain_grad, attnshift_grad, ffngain_grad, ffnshift_grad = (
        lax.psum(
            (
                outbias_grad,
                downbias_grad,
                attngain_grad,
                attnshift_grad,
                ffngain_grad,
                ffnshift_grad,
            ),
            ("dp", "tensor"),
        )
    )
    return (
        output,
        input_grad,
        query_grad,
        key_grad,
        value_grad,
        outproj_grad,
        upproj_grad,
        downproj_grad,
        querybias_grad,
        valuebias_grad,
        outbias_grad,
        upbias_grad,
        downbias_grad,
        attngain_grad,
        attnshift_grad,
        ffngain_grad,
        ffnshift_grad,
    )


MESH = pl.DeviceIdType.MESH
BF = jnp.bfloat16
F32 = jnp.float32
BLOCK = 128


def fits(mesh):
    return mesh.shape["dp"] == 8 and mesh.shape["tensor"] == 4


def nn(a, b):
    return lax.dot_general(a, b, (((1,), (0,)), ((), ())), preferred_element_type=F32)


def nt(a, b):
    return lax.dot_general(a, b, (((1,), (1,)), ((), ())), preferred_element_type=F32)


def tn(a, b):
    return lax.dot_general(a, b, (((0,), (0,)), ((), ())), preferred_element_type=F32)


def norm_rows(values):
    centre = values - jnp.mean(values, axis=-1, keepdims=True)
    inverse = lax.rsqrt(jnp.mean(centre * centre, axis=-1, keepdims=True) + EPSILON)
    return centre * inverse, inverse


def norm_rows_back(upstream, normal, inverse, gain):
    scaled = upstream * gain
    return inverse * (
        scaled
        - jnp.mean(scaled, axis=-1, keepdims=True)
        - normal * jnp.mean(scaled * normal, axis=-1, keepdims=True)
    )


class Net:
    def __init__(self, send, recv, peer):
        self.send, self.recv, self.peer = send, recv, peer
        self.sends = 0
        self.banks = 0
        self.pending = []

    def bank(self, count):
        base = self.banks
        self.banks += count
        return base

    def start(self, src, dst, sem, device, when=None):
        slot = self.sends
        self.sends += 1

        def make():
            return pltpu.make_async_remote_copy(
                src_ref=src,
                dst_ref=dst,
                send_sem=self.send.at[slot],
                recv_sem=self.recv.at[sem],
                device_id=device,
                device_id_type=MESH,
            )

        if when is None:
            make().start()
        else:
            pl.when(when)(lambda: make().start())
        self.pending.append((make, when))

    def wait(self, dst, sem, when=None):
        def make():
            return pltpu.make_async_remote_copy(
                src_ref=dst,
                dst_ref=dst,
                send_sem=self.send.at[0],
                recv_sem=self.recv.at[sem],
                device_id=self.peer,
                device_id_type=MESH,
            )

        if when is None:
            make().wait_recv()
        else:
            pl.when(when)(lambda: make().wait_recv())

    def drain(self):
        for make, when in self.pending:
            if when is None:
                make().wait_send()
            else:
                pl.when(when)(lambda make=make: make().wait_send())
        self.pending = []


SENDS = 120
RECVS = 160


def layer_kernel(
    x_ref, seg_ref, typ_ref, qw_ref, kw_ref, vw_ref, ow_ref, uw_ref, dw_ref, qb_ref, vb_ref,
    ob_ref, ub_ref, db_ref, ag_ref, as_ref, fg_ref, fs_ref, cot_ref,
    out_ref, ig_ref, qg_ref, kg_ref, vg_ref, og_ref, ug_ref, dg_ref, small_ref,
    wq, wo, own, wf, ubs, segc, wordc, xt, bias, qq, kv, kk, kvt, kkt, probs, ctx, ct,
    a_s, n1_s, r1_s, act, gelu_d, gl, parts, rs_send, rs_recv, du_s, dub, dzb,
    grad, ry, fs_b, rx, fr, dh_s, dct, dc, dco, go, go_r, so, rp, sp, rz,
    dqkv, dxp, dxr, gq, gq_r, sq, gp, sv, vb8, sw, vz,
    send_sems, recv_sems,
):
    d = lax.axis_index("dp")
    t = lax.axis_index("tensor")
    c = d % 2
    x = (d // 2) % 2
    y = d // 4
    j = d % 4
    chip = d // 2
    sib = d + 1 - 2 * c
    xn = d + 2 - 4 * x
    yn = d + 4 - 8 * y
    rows = x_ref.shape[1]
    quarter = rows // 4
    width = x_ref.shape[2]
    strip = qw_ref.shape[1]
    local = kw_ref.shape[1]
    heads = local // HD
    blocks = rows // BLOCK
    own_rows = pl.ds(pl.multiple_of(t * quarter, 16), quarter)
    net = Net(send_sems, recv_sems, (sib, t))

    def flip_x(device):
        return device + 2 - 4 * ((device // 2) % 2)

    def flip_y(device):
        return device + 4 - 8 * (device // 4)

    dg = flip_y(xn)
    part_m, part_o = parts.at[0:2], parts.at[2:4]
    sums_a, sums_b = parts.reshape(rows, width), gelu_d.reshape(rows, width)
    dqq = [sums_a.at[:, BLOCK * h : BLOCK * (h + 1)] for h in range(heads)]
    dkk = [sums_a.at[:, BLOCK * (heads + h) : BLOCK * (heads + h + 1)] for h in range(heads)]
    dvv = [sums_b.at[:, BLOCK * h : BLOCK * (h + 1)] for h in range(heads)]

    barrier = pltpu.get_barrier_semaphore()
    for m in range(1, 8):
        pl.semaphore_signal(barrier, 1, device_id=((d + m) % 8, t), device_id_type=MESH)
    for k in range(1, 4):
        for m in range(4):
            pl.semaphore_signal(
                barrier, 1, device_id=(4 * y + (j + m) % 4, (t + k) % 4), device_id_type=MESH
            )
    pl.semaphore_wait(barrier, 19)

    for h in range(heads):
        at = slice(HD * h, HD * (h + 1))
        piece = jnp.concatenate(
            [qw_ref[i, :, at] for i in range(4)] + [kw_ref[:, at], vw_ref[:, at]], axis=1
        )
        wq[d, :, 6 * HD * h : 6 * HD * (h + 1)] = piece.astype(BF)

    class PlaneGather:
        def __init__(self, ref_of):
            self.ref_of, self.bank = ref_of, net.bank(8)

        def copy(self, block, device):
            net.start(self.ref_of(block), self.ref_of(block), self.bank + block, (device, t))

        def begin(self):
            for device in (xn, yn, dg, sib):
                self.copy(d, device)

        def middle(self):
            for block in (xn, yn, dg):
                net.wait(self.ref_of(block), self.bank + block)
                self.copy(block, sib)

        def end(self):
            for block in (sib, flip_x(sib), flip_y(sib), flip_x(flip_y(sib))):
                net.wait(self.ref_of(block), self.bank + block)

    gather_q = PlaneGather(lambda b: wq.at[b])
    gather_q.begin()

    def wide_t(value, high, wide):
        r, w = value.shape
        if w < wide:
            value = jnp.concatenate([value, jnp.zeros((r, wide - w), value.dtype)], axis=1)
        if r < high:
            value = jnp.concatenate([value, jnp.zeros((high - r, wide), value.dtype)], axis=0)
        return value.T

    wo[t, d] = wide_t(ow_ref[...], 256, 128)[:strip, :local].astype(BF)
    own[0] = uw_ref[...].astype(BF)
    own[1] = dw_ref[...].astype(BF)
    ubs[t] = jnp.broadcast_to(ub_ref[...][None], ubs.shape[1:])

    wo_z = net.bank(4)
    ub_z = net.bank(4)
    wf_z = net.bank(8)
    wf_y = net.bank(8)
    for k in range(1, 4):
        s = (t + k) % 4
        net.start(wo.at[t, d], wo.at[t, d], wo_z + t, (d, s))
        net.start(ubs.at[t], ubs.at[t], ub_z + t, (d, s))
    mine = j == t
    for i in range(2):
        for k in range(1, 4):
            net.start(own.at[i], wf.at[i, d], wf_z + 4 * i + j, (4 * y + t, (t + k) % 4))
        net.start(own.at[i], wf.at[i, d], wf_z + 4 * i + j, (4 * y + t, t), when=jnp.logical_not(mine))

    @pl.when(mine)
    def _():
        for i in range(2):
            wf[i, d] = own[i]

    for b in range(blocks):
        at = slice(BLOCK * b, BLOCK * (b + 1))
        segc[at, :] = jnp.broadcast_to(seg_ref[:, at].astype(F32), (BLOCK, BLOCK)).T
        wordc[at, :] = jnp.broadcast_to((typ_ref[:, at] == 0).astype(F32), (BLOCK, BLOCK)).T
    xt[...] = x_ref[0].T
    for h in range(heads):
        at = slice(HD * h, HD * (h + 1))
        bias[:, 6 * HD * h : 6 * HD * (h + 1)] = jnp.concatenate(
            [qb_ref[i : i + 1, at] for i in range(4)] + [jnp.zeros((1, HD), F32), vb_ref[at][None]],
            axis=1,
        )

    gather_q.middle()
    gather_q.end()

    low_half = lax.broadcasted_iota(jnp.int32, (rows, BLOCK), 1) < HD
    is_word = wordc[...] > 0.5
    for h in range(heads):
        base = 6 * HD * h
        at = slice(BLOCK * h, BLOCK * (h + 1))
        made = nn(x_ref[0], wq[:, :, base : base + 6 * HD].reshape(width, 6 * HD))
        made = made + bias[:, base : base + 6 * HD]
        qq[:, at] = jnp.where(is_word, made[:, :BLOCK], made[:, BLOCK : 2 * BLOCK]).astype(BF)
        both = made[:, 2 * BLOCK :]
        keys = jnp.where(low_half, both, pltpu.roll(both, HD, 1))
        keys = jnp.where(jnp.logical_xor(is_word, low_half), 0.0, keys)
        kv[:, at] = both.astype(BF)
        kk[:, at] = keys.astype(BF)
        kvt[h] = both.T.astype(BF)
        kkt[h] = keys.T.astype(BF)

    gather_o = PlaneGather(lambda b: wo.at[:, b])
    for k in range(1, 4):
        s = (t + k) % 4
        net.wait(wo.at[s, d], wo_z + s)
    gather_o.begin()

    ct_z = net.bank(4)

    def span(b):
        return BLOCK * max(0, b - 2), BLOCK * min(blocks, b + 3)

    kept = [0]
    for b in range(blocks):
        kept.append(kept[-1] + span(b)[1] - span(b)[0])
    for b in range(blocks):
        lo, hi = span(b)
        at_q = slice(BLOCK * b, BLOCK * (b + 1))
        same = segc[lo:hi, :] == seg_ref[:, at_q].astype(F32)
        found = []
        for h in range(heads):
            at = slice(BLOCK * h, BLOCK * (h + 1))
            scores = nt(kk[lo:hi, at], qq[at_q, at]) * SCALING
            scores = jnp.where(same, scores, NEGATIVE)
            weights = jnp.exp(scores - jnp.max(scores, axis=0, keepdims=True))
            weights = weights * (1.0 / jnp.sum(weights, axis=0, keepdims=True))
            probs[h, kept[b] : kept[b + 1]] = weights
            found.append(nn(kvt[h, HD:, lo:hi], weights.astype(BF)))
        found.append(jnp.zeros((HD, BLOCK), F32))
        ctx[at_q, :] = jnp.concatenate(found, axis=0).T[:, :local].astype(BF)
        if b > 0:
            s = b - 1
            src = ctx.at[quarter * s : quarter * (s + 1)]
            net.start(src, ct.at[t], ct_z + t, (d, s), when=t != s)
    ct[t] = ctx[own_rows, :]

    gather_o.middle()

    for i in range(1):
        for m in range(4):
            r = (j + m) % 4
            net.wait(wf.at[i, 4 * y + r], wf_z + 4 * i + r, when=jnp.logical_or(r != j, j != t))
            net.start(wf.at[i, 4 * y + r], wf.at[i, 4 * y + r], wf_y + 4 * i + r, (yn, t))
    gather_o.end()

    for k in range(1, 4):
        s = (t + k) % 4
        net.wait(ct.at[s], ct_z + s)
    attended = nt(ct[0], wo[0].reshape(width, local))
    for s in range(1, 4):
        attended = attended + nt(ct[s], wo[s].reshape(width, local))
    normal, inverse = norm_rows(x_ref[0, own_rows, :].astype(F32) + attended + ob_ref[...][None])
    n1_s[...] = normal
    r1_s[...] = jnp.broadcast_to(inverse, r1_s.shape)
    normed = normal * ag_ref[...][None] + as_ref[...][None]
    a_s[...] = normed
    act[j] = normed.astype(BF)

    class RowGather:
        def __init__(self, ref):
            self.ref, self.bank = ref, net.bank(4)

        def copy(self, rank, device):
            net.start(self.ref.at[rank], self.ref.at[rank], self.bank + rank, (device, t))

        def begin(self):
            self.copy(j, xn)
            self.copy(j, sib)

        def near(self):
            net.wait(self.ref.at[sib % 4], self.bank + sib % 4)

        def middle(self):
            net.wait(self.ref.at[xn % 4], self.bank + xn % 4)
            self.copy(xn % 4, sib)

        def far(self):
            net.wait(self.ref.at[flip_x(sib) % 4], self.bank + flip_x(sib) % 4)

    class RowSum:
        def __init__(self, index):
            self.index, self.bank = index, net.bank(3)

        def hand(self, slot, partial_rows):
            where = 3 * self.index + slot
            rs_send[where] = partial_rows.astype(BF)
            net.start(
                rs_send.at[where], rs_recv.at[where], self.bank + slot, (xn if slot == 2 else sib, t)
            )

        def take(self, slot):
            where = 3 * self.index + slot
            net.wait(rs_recv.at[where], self.bank + slot)
            return rs_recv[where].astype(F32)

        def own_half(self):
            self.hand(0, part_m[1 - c])

        def other_half(self):
            self.hand(1, part_o[1 - c])
            self.hand(2, part_o[c] + self.take(1))

        def total(self):
            return part_m[c] + self.take(0) + self.take(2)

    rows_a = RowGather(act)
    rows_a.begin()
    for i in range(1, 2):
        for m in range(4):
            r = (j + m) % 4
            net.wait(wf.at[i, 4 * y + r], wf_z + 4 * i + r, when=jnp.logical_or(r != j, j != t))
            net.start(wf.at[i, 4 * y + r], wf.at[i, 4 * y + r], wf_y + 4 * i + r, (yn, t))
    rows_a.middle()
    rows_a.near()
    for k in range(1, 4):
        s = (t + k) % 4
        net.wait(ubs.at[s], ub_z + s)
    for m in range(4):
        r = 4 * (1 - y) + (j + m) % 4
        net.wait(wf.at[0, r], wf_y + (j + m) % 4)

    near = pl.ds(2 * x, 2)
    away = pl.ds(2 - 2 * x, 2)

    def feed(half):
        hidden = nn(act[half].reshape(2 * quarter, width), wf[0].reshape(width, width))
        hidden = hidden + ubs[j][:1]
        bell = 0.5 * (1.0 + lax.erf(hidden * 0.7071067811865476))
        slope = bell + hidden * (0.3989422804014327 * jnp.exp(-0.5 * hidden * hidden))
        gelu_d[half] = slope.reshape(2, quarter, width)
        gl[half] = (hidden * bell).astype(BF).reshape(2, quarter, width)

    def feed_out(half, part):
        made = nt(gl[half].reshape(2 * quarter, width), wf[1].reshape(width, width))
        part[...] = made.reshape(2, quarter, width)

    feed(near)
    rows_a.far()
    feed(away)
    for m in range(4):
        r = 4 * (1 - y) + (j + m) % 4
        net.wait(wf.at[1, r], wf_y + 4 + (j + m) % 4)
    sum_f = RowSum(0)
    feed_out(away, part_o)
    sum_f.hand(1, part_o[1 - c])
    feed_out(near, part_m)
    sum_f.own_half()
    sum_f.hand(2, part_o[c] + sum_f.take(1))
    ffn_out = sum_f.total() + db_ref[...][None]

    normal, inverse = norm_rows(a_s[...] + ffn_out)
    out_ref[0, own_rows, :] = (normal * fg_ref[...][None] + fs_ref[...][None]).astype(BF)
    out_z = net.bank(4)
    for k in range(1, 4):
        net.start(out_ref.at[0, own_rows], out_ref.at[0, own_rows], out_z + t, (d, (t + k) % 4))
    upstream = cot_ref[0, own_rows, :].astype(F32)
    du = norm_rows_back(upstream, normal, inverse, fg_ref[...][None])
    dub[j] = du.astype(BF)
    rows_u = RowGather(dub)
    rows_u.begin()
    du_s[...] = du
    sv[...] = jnp.zeros_like(sv)
    sv[0:1] = jnp.sum(upstream * normal, axis=0, keepdims=True)
    sv[1:2] = jnp.sum(upstream, axis=0, keepdims=True)
    sv[2:3] = jnp.sum(du, axis=0, keepdims=True)

    def feed_back(half, part):
        made = nn(dub[half].reshape(2 * quarter, width), wf[1].reshape(width, width))
        made = made * gelu_d[half].reshape(2 * quarter, width)
        dzb[half] = made.astype(BF).reshape(2, quarter, width)
        back = nt(made.astype(BF), wf[0].reshape(width, width))
        part[...] = back.reshape(2, quarter, width)
        return jnp.sum(made, axis=0, keepdims=True)

    rows_u.near()
    up_sum = feed_back(near, part_m)
    sum_b = RowSum(1)
    sum_b.own_half()
    rows_u.middle()
    rows_u.far()
    up_sum = up_sum + feed_back(away, part_o)
    sum_b.hand(1, part_o[1 - c])
    sum_b.hand(2, part_o[c] + sum_b.take(1))
    rank_rows = lax.broadcasted_iota(jnp.int32, (4, width), 0)
    sv[6:10] = jnp.where(rank_rows == j, up_sum, 0.0)

    ry_b = net.bank(2)
    theirs = pl.ds(4 * (1 - y), 4)
    ours = pl.ds(4 * y, 4)
    for i, (left, right) in ((1, (dub, gl)), (0, (act, dzb))):
        made = tn(left[...].reshape(4 * quarter, width), right[...].reshape(4 * quarter, width))
        grad[i] = made.astype(BF).reshape(8, strip, width)
        net.start(grad.at[i, theirs], ry.at[i], ry_b + i, (yn, t))

    da = du_s[...] + sum_b.total()
    normal = n1_s[...]
    dh = norm_rows_back(da, normal, r1_s[:, :1], ag_ref[...][None])
    dh_s[...] = dh
    dhb = dh.astype(BF)
    dc_z = net.bank(4)
    for k in range(1, 4):
        s = (t + k) % 4
        dct[s] = nn(dhb, wo[s].reshape(width, local)).astype(BF)
        net.start(dct.at[s], dc.at[t], dc_z + t, (d, s))
    dc[t] = nn(dhb, wo[t].reshape(width, local)).astype(BF)
    sv[3:4] = jnp.sum(da * normal, axis=0, keepdims=True)
    sv[4:5] = jnp.sum(da, axis=0, keepdims=True)
    sv[5:6] = jnp.sum(dh, axis=0, keepdims=True)
    for s in range(4):
        made = tn(dhb, ct[s]).astype(BF).reshape(4, 2, strip, local)
        for i in range(2):
            go[i, :, s] = made[:, i]
    go_b = net.bank(1)
    net.start(go.at[1 - c], go_r, go_b, (sib, t))

    rx_b = net.bank(4)
    for i in (1, 0):
        net.wait(ry.at[i], ry_b + i)
        fs_b[:, i] = (grad[i, ours].astype(F32) + ry[i].astype(F32)).astype(BF)
    for r in (sib, xn, flip_x(sib)):
        net.start(fs_b.at[r % 4], rx.at[j], rx_b + j, (r, t))
    rx[j] = fs_b[j]

    net.wait(go_r, go_b)
    so[...] = (go[c].astype(F32) + go_r[...].astype(F32)).astype(BF)
    rp_b = net.bank(4)
    for r in (xn, yn, dg):
        net.start(so.at[r // 2], rp.at[chip], rp_b + chip, (r, t))
    rp[chip] = so[chip]

    for k in range(1, 4):
        s = (t + k) % 4
        net.wait(dc.at[s], dc_z + s)
    dctx = dc[...].reshape(rows, local)
    for h in range(heads):
        dco[:, BLOCK * h : BLOCK * (h + 1)] = jnp.concatenate(
            [jnp.zeros((rows, HD), BF), dctx[:, HD * h : HD * (h + 1)]], axis=1
        )
    for h in range(heads):
        dkk[h][...] = jnp.zeros((rows, BLOCK), F32)
        dvv[h][...] = jnp.zeros((rows, BLOCK), F32)
    for b in range(blocks):
        lo, hi = span(b)
        at_q = slice(BLOCK * b, BLOCK * (b + 1))
        for h in range(heads):
            at = slice(BLOCK * h, BLOCK * (h + 1))
            weights = probs[h, kept[b] : kept[b + 1]]
            dp = nt(kv[lo:hi, at], dco[at_q, at])
            ds = weights * (dp - jnp.sum(weights * dp, axis=0, keepdims=True))
            dsb = ds.astype(BF)
            dkk[h][lo:hi] += nn(dsb, qq[at_q, at])
            dvv[h][lo:hi] += nn(weights.astype(BF), dco[at_q, at])
            dqq[h][at_q] = nn(kkt[h, :, lo:hi], dsb).T * SCALING

    fr_b = net.bank(4)
    for m in range(4):
        r = (j + m) % 4
        if m:
            net.wait(rx.at[r], rx_b + r)
        net.start(rx.at[r], fr.at[t], fr_b + t, (d, r), when=r != t)
    fr[t] = rx[t]

    for h in range(heads):
        base = 6 * HD * h
        first = jnp.where(is_word, dqq[h][...], 0.0)
        second = jnp.where(is_word, 0.0, dqq[h][...])
        keys = dkk[h][...]
        keys = jnp.where(is_word, keys, pltpu.roll(keys, HD, 1)) * SCALING
        third = jnp.where(low_half, keys, dvv[h][...])
        for i, part in enumerate((first, second, third)):
            at = slice(base + BLOCK * i, base + BLOCK * (i + 1))
            dqkv[:, at] = part.astype(BF)
            row, col = divmod(base + BLOCK * i, width)
            sv[10 + row : 11 + row, col : col + BLOCK] = jnp.sum(part, axis=0, keepdims=True)

    made = nt(dqkv[...], wq[...].reshape(width, 6 * local))
    dxp[...] = made.astype(BF).reshape(4, quarter, width)
    dx_z = net.bank(4)
    for k in range(1, 4):
        s = (t + k) % 4
        net.start(dxp.at[s], dxr.at[t], dx_z + t, (d, s))
    vb8[d] = sv[...]
    sv_b = net.bank(8)
    for m in range(1, 8):
        net.start(sv, vb8.at[d], sv_b + d, ((d + m) % 8, t))

    made = nn(xt[...], dqkv[...]).astype(BF).reshape(4, 2, strip, 6 * local)
    for i in range(2):
        gq[i] = made[:, i]
    gq_b = net.bank(1)
    net.start(gq.at[1 - c], gq_r, gq_b, (sib, t))

    for r in (xn, yn, dg):
        net.wait(rp.at[r // 2], rp_b + r // 2)
    total = rp[0].astype(F32)
    for k in range(1, 4):
        total = total + rp[k].astype(F32)
    sp[...] = total.astype(BF)
    rz_b = net.bank(4)
    for k in range(1, 4):
        s = (t + k) % 4
        net.start(sp.at[s], rz.at[t], rz_b + t, (d, s))
    rz[t] = sp[t]

    net.wait(gq_r, gq_b)
    sq[...] = (gq[c].astype(F32) + gq_r[...].astype(F32)).astype(BF)
    gp_b = net.bank(4)
    for r in (xn, yn, dg):
        net.start(sq.at[r // 2], gp.at[chip], gp_b + chip, (r, t))
    gp[chip] = sq[chip]

    for m in range(1, 8):
        s = (d + m) % 8
        net.wait(vb8.at[s], sv_b + s)
    total = vb8[0]
    for m in range(1, 8):
        total = total + vb8[m]
    sw[...] = total
    vz_b = net.bank(4)
    for k in range(1, 4):
        net.start(sw, vz.at[t], vz_b + t, (d, (t + k) % 4))
    vz[t] = sw[...]

    for k in range(1, 4):
        s = (t + k) % 4
        net.wait(dxr.at[s], dx_z + s)
    total = dxp[t].astype(F32) + dh_s[...]
    for k in range(1, 4):
        total = total + dxr[(t + k) % 4].astype(F32)
    ig_ref[0, own_rows, :] = total.astype(BF)
    ig_z = net.bank(4)
    for k in range(1, 4):
        net.start(ig_ref.at[0, own_rows], ig_ref.at[0, own_rows], ig_z + t, (d, (t + k) % 4))

    for k in range(1, 4):
        s = (t + k) % 4
        net.wait(vz.at[s], vz_b + s)
    total = vz[0]
    for s in range(1, 4):
        total = total + vz[s]
    up_total = jnp.sum(jnp.where(rank_rows == t, total[6:10], 0.0), axis=0, keepdims=True)
    small_ref[0:6] = total[0:6]
    small_ref[6:7] = up_total
    small_ref[8:10] = sw[10:12]

    for k in range(1, 4):
        s = (t + k) % 4
        net.wait(fr.at[s], fr_b + s)
    total = fr[0].astype(F32)
    for s in range(1, 4):
        total = total + fr[s].astype(F32)
    ug_ref[...] = total[0]
    dg_ref[...] = total[1]

    for k in range(1, 4):
        s = (t + k) % 4
        net.wait(rz.at[s], rz_b + s)
    total = rz[0].astype(F32)
    for s in range(1, 4):
        total = total + rz[s].astype(F32)
    og_ref[...] = wide_t(total, BLOCK, 256)[:local, :strip]

    for r in (xn, yn, dg):
        net.wait(gp.at[r // 2], gp_b + r // 2)
    total = gp[0].astype(F32)
    for k in range(1, 4):
        total = total + gp[k].astype(F32)
    for h in range(heads):
        base = 6 * HD * h
        at = slice(HD * h, HD * (h + 1))
        for i in range(4):
            qg_ref[i, :, at] = total[:, base + HD * i : base + HD * (i + 1)]
        kg_ref[:, at] = total[:, base + 4 * HD : base + 5 * HD]
        vg_ref[:, at] = total[:, base + 5 * HD : base + 6 * HD]

    for k in range(1, 4):
        s = (t + k) % 4
        rows_s = pl.ds(pl.multiple_of(s * quarter, 16), quarter)
        net.wait(out_ref.at[0, rows_s], out_z + s)
        net.wait(ig_ref.at[0, rows_s], ig_z + s)
    net.drain()


def end_kernel(*refs):
    sources, small = refs[:8], refs[8]
    targets, (qbg, vbg), vectors = refs[9:17], refs[17:19], refs[19:26]
    for source, target in zip(sources, targets):
        target[...] = source[...]
    fgg, fsg, dbg, agg, asg, obg, ubg = (small[i] for i in range(7))
    for ref, value in zip(vectors, (obg, ubg, dbg, agg, asg, fgg, fsg)):
        ref[...] = value
    width = small.shape[1]
    values = []
    for h in range(vbg.shape[0] // HD):
        row, col = divmod(6 * HD * h, width)
        piece = small[8 + row : 9 + row, col : col + 6 * HD]
        for i in range(4):
            qbg[i : i + 1, HD * h : HD * (h + 1)] = piece[:, HD * i : HD * (i + 1)]
        values.append(piece[:, 5 * HD :])
    vbg[...] = jnp.concatenate(values, axis=1)[0]


def fused(
    layer_input, segment_ids, token_types, query_weight, key_weight, value_weight, out_weight,
    up_weight, down_weight, query_bias, value_bias, out_bias, up_bias, down_bias, attn_gain,
    attn_shift, ffn_gain, ffn_shift, cotangent,
):
    rows, width = layer_input.shape[1:]
    strip, local = key_weight.shape
    quarter, heads, blocks = rows // 4, local // HD, rows // BLOCK
    kept = sum(BLOCK * (min(blocks, b + 3) - max(0, b - 2)) for b in range(blocks))
    args = [
        layer_input, segment_ids, token_types, query_weight, key_weight, value_weight, out_weight,
        up_weight, down_weight.T, query_bias, value_bias, out_bias, up_bias, down_bias, attn_gain,
        attn_shift, ffn_gain, ffn_shift, cotangent,
    ]

    def like(v, dtype=F32):
        return jax.ShapeDtypeStruct(v.shape, dtype)

    outs = [
        like(layer_input, BF), like(layer_input, BF), like(query_weight), like(key_weight),
        like(value_weight), like(out_weight), like(up_weight), jax.ShapeDtypeStruct((strip, width), F32),
        jax.ShapeDtypeStruct((16, width), F32),
    ]
    v = pltpu.VMEM
    scratch = [
        v((8, strip, 6 * local), BF), v((4, 8, strip, local), BF), v((2, strip, width), BF),
        v((2, 8, strip, width), BF), v((4, 8, width), F32), v((rows, BLOCK), F32),
        v((rows, BLOCK), F32), v((width, rows), BF), v((1, 6 * local), F32),
        v((rows, heads * BLOCK), BF), v((rows, heads * BLOCK), BF), v((rows, heads * BLOCK), BF),
        v((heads, BLOCK, rows), BF), v((heads, BLOCK, rows), BF),
        v((heads, kept, BLOCK), F32), v((rows, local), BF), v((4, quarter, local), BF),
        v((quarter, width), F32), v((quarter, width), F32), v((quarter, BLOCK), F32),
        v((4, quarter, width), BF), v((4, quarter, width), F32), v((4, quarter, width), BF),
        v((4, quarter, width), F32),
        v((6, quarter, width), BF), v((6, quarter, width), BF),
        v((quarter, width), F32), v((4, quarter, width), BF), v((4, quarter, width), BF),
        v((2, 8, strip, width), BF), v((2, 4, strip, width), BF), v((4, 2, strip, width), BF),
        v((4, 2, strip, width), BF), v((4, 2, strip, width), BF),
        v((quarter, width), F32), v((4, quarter, local), BF), v((4, quarter, local), BF),
        v((rows, heads * BLOCK), BF),
        v((2, 4, 4, strip, local), BF), v((4, 4, strip, local), BF), v((4, 4, strip, local), BF),
        v((4, 4, strip, local), BF), v((4, strip, local), BF), v((4, strip, local), BF),
        v((rows, 6 * local), BF), v((4, quarter, width), BF), v((4, quarter, width), BF),
        v((2, 4, strip, 6 * local), BF), v((4, strip, 6 * local), BF),
        v((4, strip, 6 * local), BF), v((4, strip, 6 * local), BF),
        v((16, width), F32), v((8, 16, width), F32), v((16, width), F32), v((4, 16, width), F32),
        pltpu.SemaphoreType.DMA((SENDS,)), pltpu.SemaphoreType.DMA((RECVS,)),
    ]
    spec = pl.BlockSpec(memory_space=pltpu.VMEM)
    made = pl.pallas_call(
        layer_kernel,
        out_shape=outs,
        in_specs=[spec] * len(args),
        out_specs=[spec] * len(outs),
        scratch_shapes=scratch,
        compiler_params=pltpu.CompilerParams(
            collective_id=0, has_side_effects=True, vmem_limit_bytes=58 << 20
        ),
        name="layer",
    )(*args)
    *large, small = made
    vector = jax.ShapeDtypeStruct((width,), F32)
    ended = pl.pallas_call(
        end_kernel,
        out_shape=[like(v, v.dtype) for v in large]
        + [like(query_bias), jax.ShapeDtypeStruct((local,), F32)]
        + [vector] * 7,
        in_specs=[spec] * len(made),
        out_specs=[spec] * 17,
        name="finish",
    )(*large, small)
    return (*ended[:7], ended[7].T, *ended[8:])


def solution(mesh):
    in_specs = (
        P("dp", None, None),
        P("dp", None),
        P("dp", None),
        P(None, "dp", "tensor"),
        P("dp", "tensor"),
        P("dp", "tensor"),
        P("tensor", "dp"),
        P("dp", "tensor"),
        P("tensor", "dp"),
        P(None, "tensor"),
        P("tensor"),
        P(),
        P("tensor"),
        P(),
        P(),
        P(),
        P(),
        P(),
        P("dp", None, None),
    )
    out_specs = (
        P("dp", None, None),
        P("dp", None, None),
        P(None, "dp", "tensor"),
        P("dp", "tensor"),
        P("dp", "tensor"),
        P("tensor", "dp"),
        P("dp", "tensor"),
        P("tensor", "dp"),
        P(None, "tensor"),
        P("tensor"),
        P(),
        P("tensor"),
        P(),
        P(),
        P(),
        P(),
        P(),
    )
    step = fused if fits(mesh) else shards
    return jax.shard_map(step, mesh=mesh, in_specs=in_specs, out_specs=out_specs, check_vma=False)
```

```python
from functools import partial

import jax
import jax.numpy as jnp
from jax import lax
from jax.experimental import pallas as pl
from jax.experimental.pallas import tpu as pltpu
from jax.sharding import PartitionSpec as P

HD = 64


EPSILON = 1e-05
SCALING = 0.125
NEGATIVE = -1000000000.0


def layer_norm_keep(values, norm_gain, norm_shift):
    centre = values - jnp.mean(values, axis=-1, keepdims=True)
    inverse = lax.rsqrt(jnp.mean(centre * centre, axis=-1, keepdims=True) + EPSILON)
    normal = centre * inverse
    return (normal * norm_gain + norm_shift, normal, inverse)


def layer_norm_back(upstream, normal, inverse, norm_gain):
    scaled = upstream * norm_gain
    gain_grad = jnp.sum(upstream * normal, axis=0)
    shift_grad = jnp.sum(upstream, axis=0)
    inner_term = (
        scaled
        - jnp.mean(scaled, axis=-1, keepdims=True)
        - normal * jnp.mean(scaled * normal, axis=-1, keepdims=True)
    )
    return (inverse * inner_term, gain_grad, shift_grad)


def heads_of(matrix):
    return matrix.reshape(matrix.shape[0], -1, HD)


def pick_queries(query_rows, type_row):
    word_tok = (type_row == 0)[:, None]
    return (
        jnp.where(word_tok, query_rows[0], query_rows[2]),
        jnp.where(word_tok, query_rows[1], query_rows[3]),
    )


def score_block(word_heads, entity_heads, key_heads, segment_row, type_row):
    to_words = jnp.einsum("qhd,khd->hqk", word_heads, key_heads, preferred_element_type=jnp.float32)
    to_entities = jnp.einsum(
        "qhd,khd->hqk", entity_heads, key_heads, preferred_element_type=jnp.float32
    )
    scores = jnp.where((type_row == 0)[None, None, :], to_words, to_entities) * SCALING
    allowed = (segment_row[:, None] == segment_row[None, :])[None]
    return jnp.where(allowed, scores, NEGATIVE)


def attend_forward(packed):
    query_rows, key_seq, value_seq, segment_row, type_row = packed
    word_query, entity_query = pick_queries(query_rows, type_row)
    scores = score_block(
        heads_of(word_query), heads_of(entity_query), heads_of(key_seq), segment_row, type_row
    )
    row_top = jnp.max(scores, axis=-1, keepdims=True)
    weights = jnp.exp(scores - row_top)
    totals = jnp.sum(weights, axis=-1, keepdims=True)
    attn_probs = (weights / totals).astype(jnp.bfloat16)
    context = jnp.einsum(
        "hqk,khd->qhd", attn_probs, heads_of(value_seq), preferred_element_type=jnp.float32
    )
    log_total = (row_top + jnp.log(totals))[..., 0]
    return (context.reshape(context.shape[0], -1).astype(jnp.bfloat16), log_total)


def attend_backward(packed):
    query_rows, key_seq, value_seq, segment_row, type_row, log_total, context_grad = packed
    word_query, entity_query = pick_queries(query_rows, type_row)
    word_heads = heads_of(word_query)
    entity_heads = heads_of(entity_query)
    key_heads = heads_of(key_seq)
    value_heads = heads_of(value_seq)
    grad_heads = heads_of(context_grad)
    scores = score_block(word_heads, entity_heads, key_heads, segment_row, type_row)
    attn_probs = jnp.exp(scores - log_total[..., None])
    prob_grad = jnp.einsum(
        "qhd,khd->hqk", grad_heads, value_heads, preferred_element_type=jnp.float32
    )
    score_grad = attn_probs * (prob_grad - jnp.sum(attn_probs * prob_grad, axis=-1, keepdims=True))
    score_low = score_grad.astype(jnp.bfloat16)
    word_key = (type_row == 0)[None, None, :]
    zeroes = jnp.zeros_like(score_low)
    word_part = jnp.where(word_key, score_low, zeroes)
    entity_part = jnp.where(word_key, zeroes, score_low)
    word_qgrad = (
        jnp.einsum("hqk,khd->qhd", word_part, key_heads, preferred_element_type=jnp.float32)
        * SCALING
    )
    entity_qgrad = (
        jnp.einsum("hqk,khd->qhd", entity_part, key_heads, preferred_element_type=jnp.float32)
        * SCALING
    )
    key_delta = (
        jnp.einsum("hqk,qhd->khd", word_part, word_heads, preferred_element_type=jnp.float32)
        + jnp.einsum("hqk,qhd->khd", entity_part, entity_heads, preferred_element_type=jnp.float32)
    ) * SCALING
    value_delta = jnp.einsum(
        "hqk,qhd->khd",
        attn_probs.astype(jnp.bfloat16),
        grad_heads,
        preferred_element_type=jnp.float32,
    )
    row_count = word_qgrad.shape[0]
    return (
        word_qgrad.reshape(row_count, -1),
        entity_qgrad.reshape(row_count, -1),
        key_delta.reshape(row_count, -1),
        value_delta.reshape(row_count, -1),
    )


def row_share(partial_rows):
    return lax.psum_scatter(partial_rows, "tensor", scatter_dimension=0, tiled=True)


def row_whole(rounded_rows):
    return lax.all_gather(rounded_rows, "tensor", axis=0, tiled=True)


def shards(
    layer_input,
    segment_ids,
    token_types,
    query_weight,
    key_weight,
    value_weight,
    out_weight,
    up_weight,
    down_weight,
    query_bias,
    value_bias,
    out_bias,
    up_bias,
    down_bias,
    attn_gain,
    attn_shift,
    ffn_gain,
    ffn_shift,
    cotangent,
):
    seq_count, seq_length, model_width = layer_input.shape
    tokens = layer_input.reshape(-1, model_width)
    row_count = tokens.shape[0]
    share = row_count // lax.axis_size("tensor")
    first_row = lax.axis_index("tensor") * share

    def own_rows(matrix):
        return lax.dynamic_slice_in_dim(matrix, first_row, share, 0)

    def combine_rows(partial_rows):
        return row_share(partial_rows)

    def whole_rows(rounded_rows):
        return row_whole(rounded_rows)

    query_complete, key_full, value_full, out_full = (
        lax.all_gather(query_weight.astype(jnp.bfloat16), "dp", axis=1, tiled=True),
        lax.all_gather(key_weight.astype(jnp.bfloat16), "dp", axis=0, tiled=True),
        lax.all_gather(value_weight.astype(jnp.bfloat16), "dp", axis=0, tiled=True),
        lax.all_gather(out_weight.astype(jnp.bfloat16), "dp", axis=1, tiled=True),
    )
    local_width = key_full.shape[1]
    query_rows = jnp.einsum(
        "gow,qwk->gqok", layer_input, query_complete, preferred_element_type=jnp.float32
    )
    query_rows = (query_rows + query_bias[None, :, None, :]).astype(jnp.bfloat16)
    keys_all = jnp.dot(layer_input, key_full, preferred_element_type=jnp.float32).astype(
        jnp.bfloat16
    )
    values_all = (
        jnp.dot(layer_input, value_full, preferred_element_type=jnp.float32) + value_bias
    ).astype(jnp.bfloat16)
    context, log_total = lax.map(
        attend_forward, (query_rows, keys_all, values_all, segment_ids, token_types)
    )
    context_rows = context.reshape(-1, local_width)
    attended = combine_rows(jnp.dot(context_rows, out_full, preferred_element_type=jnp.float32))
    residual = own_rows(tokens).astype(jnp.float32) + attended + out_bias
    normed, normal_one, inverse_one = layer_norm_keep(residual, attn_gain, attn_shift)
    normed_low = whole_rows(normed.astype(jnp.bfloat16))
    up_full, down_full = (
        lax.all_gather(up_weight.astype(jnp.bfloat16), "dp", axis=0, tiled=True),
        lax.all_gather(down_weight.astype(jnp.bfloat16), "dp", axis=1, tiled=True),
    )
    pre_act = jnp.dot(normed_low, up_full, preferred_element_type=jnp.float32) + up_bias
    activated, gelu_pull = jax.vjp(partial(jax.nn.gelu, approximate=False), pre_act)
    act_low = activated.astype(jnp.bfloat16)
    ffn_out = (
        combine_rows(jnp.dot(act_low, down_full, preferred_element_type=jnp.float32)) + down_bias
    )
    normed_out, normal_two, inverse_two = layer_norm_keep(normed + ffn_out, ffn_gain, ffn_shift)
    output = whole_rows(normed_out.astype(jnp.bfloat16)).reshape(layer_input.shape)
    upstream = own_rows(cotangent.reshape(-1, model_width)).astype(jnp.float32)
    sum_grad, ffngain_grad, ffnshift_grad = layer_norm_back(
        upstream, normal_two, inverse_two, ffn_gain
    )
    downbias_grad = jnp.sum(sum_grad, axis=0)
    sum_low = whole_rows(sum_grad.astype(jnp.bfloat16))
    up_back, down_back = (
        lax.all_gather(up_weight.astype(jnp.bfloat16), "dp", axis=0, tiled=True),
        lax.all_gather(down_weight.astype(jnp.bfloat16), "dp", axis=1, tiled=True),
    )
    down_local = jnp.dot(act_low.T, sum_low, preferred_element_type=jnp.float32)
    act_grad = jnp.dot(sum_low, down_back.T, preferred_element_type=jnp.float32)
    (pre_grad,) = gelu_pull(act_grad)
    upbias_grad = jnp.sum(pre_grad, axis=0)
    pre_low = pre_grad.astype(jnp.bfloat16)
    up_local = jnp.dot(normed_low.T, pre_low, preferred_element_type=jnp.float32)
    upproj_grad, downproj_grad = (
        lax.psum_scatter(up_local, "dp", scatter_dimension=0, tiled=True),
        lax.psum_scatter(down_local, "dp", scatter_dimension=1, tiled=True),
    )
    normed_grad = (
        combine_rows(jnp.dot(pre_low, up_back.T, preferred_element_type=jnp.float32)) + sum_grad
    )
    resid_grad, attngain_grad, attnshift_grad = layer_norm_back(
        normed_grad, normal_one, inverse_one, attn_gain
    )
    outbias_grad = jnp.sum(resid_grad, axis=0)
    resid_low = whole_rows(resid_grad.astype(jnp.bfloat16))
    query_pullback, key_pullback, value_pullback, out_back = (
        lax.all_gather(query_weight.astype(jnp.bfloat16), "dp", axis=1, tiled=True),
        lax.all_gather(key_weight.astype(jnp.bfloat16), "dp", axis=0, tiled=True),
        lax.all_gather(value_weight.astype(jnp.bfloat16), "dp", axis=0, tiled=True),
        lax.all_gather(out_weight.astype(jnp.bfloat16), "dp", axis=1, tiled=True),
    )
    outproj_local = jnp.dot(context_rows.T, resid_low, preferred_element_type=jnp.float32)
    context_grad = jnp.dot(resid_low, out_back.T, preferred_element_type=jnp.float32).astype(
        jnp.bfloat16
    )
    context_grad = context_grad.reshape(seq_count, seq_length, local_width)
    word_qgrad, entity_qgrad, key_delta, value_delta = lax.map(
        attend_backward,
        (query_rows, keys_all, values_all, segment_ids, token_types, log_total, context_grad),
    )
    is_word = (token_types == 0)[..., None]
    zero_rows = jnp.zeros_like(word_qgrad)
    query_delta = jnp.stack(
        [
            jnp.where(is_word, word_qgrad, zero_rows),
            jnp.where(is_word, entity_qgrad, zero_rows),
            jnp.where(is_word, zero_rows, word_qgrad),
            jnp.where(is_word, zero_rows, entity_qgrad),
        ],
        axis=1,
    )
    querybias_grad = jnp.sum(query_delta, axis=(0, 2))
    valuebias_grad = jnp.sum(value_delta, axis=(0, 1))
    query_reduced = query_delta.astype(jnp.bfloat16)
    key_reduced = key_delta.astype(jnp.bfloat16)
    value_reduced = value_delta.astype(jnp.bfloat16)
    query_local = jnp.einsum(
        "nvh,nkvw->khw", layer_input, query_reduced, preferred_element_type=jnp.float32
    )
    key_shard = jnp.einsum(
        "pui,pun->in", layer_input, key_reduced, preferred_element_type=jnp.float32
    )
    value_local = jnp.einsum(
        "pui,pun->in", layer_input, value_reduced, preferred_element_type=jnp.float32
    )
    input_part = (
        jnp.einsum(
            "kayo,azo->kyz", query_reduced, query_pullback, preferred_element_type=jnp.float32
        )
        + jnp.einsum("ohz,wz->ohw", key_reduced, key_pullback, preferred_element_type=jnp.float32)
        + jnp.einsum(
            "ohz,wz->ohw", value_reduced, value_pullback, preferred_element_type=jnp.float32
        )
    )
    input_total = combine_rows(input_part.reshape(-1, model_width))
    input_grad = whole_rows((input_total + resid_grad).astype(jnp.bfloat16)).reshape(
        layer_input.shape
    )
    query_grad, key_grad, value_grad, outproj_grad = (
        lax.psum_scatter(query_local, "dp", scatter_dimension=1, tiled=True),
        lax.psum_scatter(key_shard, "dp", scatter_dimension=0, tiled=True),
        lax.psum_scatter(value_local, "dp", scatter_dimension=0, tiled=True),
        lax.psum_scatter(outproj_local, "dp", scatter_dimension=1, tiled=True),
    )
    querybias_grad, valuebias_grad, upbias_grad = lax.psum(
        (querybias_grad, valuebias_grad, upbias_grad), "dp"
    )
    outbias_grad, downbias_grad, attngain_grad, attnshift_grad, ffngain_grad, ffnshift_grad = (
        lax.psum(
            (
                outbias_grad,
                downbias_grad,
                attngain_grad,
                attnshift_grad,
                ffngain_grad,
                ffnshift_grad,
            ),
            ("dp", "tensor"),
        )
    )
    return (
        output,
        input_grad,
        query_grad,
        key_grad,
        value_grad,
        outproj_grad,
        upproj_grad,
        downproj_grad,
        querybias_grad,
        valuebias_grad,
        outbias_grad,
        upbias_grad,
        downbias_grad,
        attngain_grad,
        attnshift_grad,
        ffngain_grad,
        ffnshift_grad,
    )


MESH = pl.DeviceIdType.MESH
BF = jnp.bfloat16
F32 = jnp.float32
BLOCK = 128


def fits(mesh):
    return mesh.shape["dp"] == 8 and mesh.shape["tensor"] == 4


def nn(a, b):
    return lax.dot_general(a, b, (((1,), (0,)), ((), ())), preferred_element_type=F32)


def nt(a, b):
    return lax.dot_general(a, b, (((1,), (1,)), ((), ())), preferred_element_type=F32)


def tn(a, b):
    return lax.dot_general(a, b, (((0,), (0,)), ((), ())), preferred_element_type=F32)


def norm_rows(values):
    centre = values - jnp.mean(values, axis=-1, keepdims=True)
    inverse = lax.rsqrt(jnp.mean(centre * centre, axis=-1, keepdims=True) + EPSILON)
    return centre * inverse, inverse


def norm_rows_back(upstream, normal, inverse, gain):
    scaled = upstream * gain
    return inverse * (
        scaled
        - jnp.mean(scaled, axis=-1, keepdims=True)
        - normal * jnp.mean(scaled * normal, axis=-1, keepdims=True)
    )


class Net:
    def __init__(self, send, recv, peer):
        self.send, self.recv, self.peer = send, recv, peer
        self.sends = 0
        self.banks = 0
        self.pending = []

    def bank(self, count):
        base = self.banks
        self.banks += count
        return base

    def start(self, src, dst, sem, device, when=None, group=None):
        slot = self.sends
        self.sends += 1

        def make():
            return pltpu.make_async_remote_copy(
                src_ref=src,
                dst_ref=dst,
                send_sem=self.send.at[slot],
                recv_sem=self.recv.at[sem],
                device_id=device,
                device_id_type=MESH,
            )

        if when is None:
            make().start()
        else:
            pl.when(when)(lambda: make().start())
        self.pending.append((make, when, group))

    def wait(self, dst, sem, when=None):
        def make():
            return pltpu.make_async_remote_copy(
                src_ref=dst,
                dst_ref=dst,
                send_sem=self.send.at[0],
                recv_sem=self.recv.at[sem],
                device_id=self.peer,
                device_id_type=MESH,
            )

        if when is None:
            make().wait_recv()
        else:
            pl.when(when)(lambda: make().wait_recv())

    def settle(self, *groups):
        for make, when, group in self.pending:
            if groups and group not in groups:
                continue
            if when is None:
                make().wait_send()
            else:
                pl.when(when)(lambda make=make: make().wait_send())
        self.pending = [p for p in self.pending if groups and p[2] not in groups]


SENDS = 192
RECVS = 224


def layer_kernel(
    x_ref, seg_ref, typ_ref, qw_ref, kw_ref, vw_ref, ow_ref, uw_ref, dw_ref, qb_ref, vb_ref,
    ob_ref, ub_ref, db_ref, ag_ref, as_ref, fg_ref, fs_ref, cot_ref,
    out_ref, ig_ref, qg_ref, kg_ref, vg_ref, og_ref, ug_ref, dg_ref, small_ref,
    wq, wo, own, own_y, wf, ubs, segc, wordc, xt, bias, qq, kv, kk, kvt, kkt, probs, ctx, ct,
    a_s, n1_s, r1_s, act, gelu_d, gl, parts, rs_send, rs_recv, dub, dzb,
    ry, rx, fr_in, fr_cross, fr_back, dct, dc, dco, go_r, rp, sp, rz,
    dqkv, dx_in, dx_cross, dx_back, gq_r, gp, sv, vb8, sw, vz,
    send_sems, recv_sems,
):
    d = lax.axis_index("dp")
    t = lax.axis_index("tensor")
    c = d % 2
    x = (d // 2) % 2
    y = d // 4
    j = d % 4
    chip = d // 2
    sib = d + 1 - 2 * c
    xn = d + 2 - 4 * x
    yn = d + 4 - 8 * y
    rows = x_ref.shape[1]
    quarter = rows // 4
    width = x_ref.shape[2]
    strip = qw_ref.shape[1]
    local = kw_ref.shape[1]
    heads = local // HD
    blocks = rows // BLOCK
    own_rows = pl.ds(pl.multiple_of(t * quarter, 16), quarter)
    net = Net(send_sems, recv_sems, (sib, t))

    def flip_x(device):
        return device + 2 - 4 * ((device // 2) % 2)

    def flip_y(device):
        return device + 4 - 8 * (device // 4)

    dg = flip_y(xn)
    part_m, part_o = parts.at[0:2], parts.at[2:4]
    sums_a, sums_b = parts.reshape(rows, width), gelu_d.reshape(rows, width)
    dqq = [sums_a.at[:, BLOCK * h : BLOCK * (h + 1)] for h in range(heads)]
    dkk = [sums_a.at[:, BLOCK * (heads + h) : BLOCK * (heads + h + 1)] for h in range(heads)]
    dvv = [sums_b.at[:, BLOCK * h : BLOCK * (h + 1)] for h in range(heads)]

    low_z = t < 2
    is_end = jnp.logical_or(t == 0, t == 3)
    is_mid = jnp.logical_not(is_end)
    z_out = jnp.where(low_z, t + 1, t - 1)
    z_back = jnp.where(low_z, 0, 3)

    def place(e):
        return jnp.where(low_z, e, 3 - e)

    def joint(one, other):
        return other if one is None else jnp.logical_and(one, other)

    class LineGather:
        def __init__(self, view, group=None):
            self.view, self.bank, self.group = view, net.bank(4), group

        def copy(self, owner, to, when):
            ref = self.view(owner)
            net.start(ref, ref, self.bank + owner, (d, to), when=when, group=self.group)

        def wait(self, owner, when=None):
            net.wait(self.view(owner), self.bank + owner, when=when)

        def begin(self):
            self.copy(t, z_out, None)
            self.copy(t, z_back, is_mid)

        def step(self, n):
            if n == 1:
                self.wait(place(0), is_mid)
                self.copy(place(0), z_out, is_mid)
                self.wait(place(2), is_mid)
                self.copy(place(2), z_back, is_mid)
            if n == 2:
                self.wait(place(3), is_mid)
                self.copy(place(3), z_back, is_mid)
            self.wait(place(n), is_end)

    def new_owners(n):
        if n == 0:
            return ((t, None),)
        if n == 1:
            return ((jnp.where(is_mid, place(0), place(1)), None), (place(2), is_mid))
        return ((jnp.where(is_mid, place(3), place(2)), None),) if n == 2 else ((place(3), is_end),)

    class LineReduce:
        def __init__(self, own, came, cross, back):
            self.own, self.came, self.cross, self.back = own, came, cross, back
            self.in_b, self.cross_b, self.back_b = net.bank(4), net.bank(4), net.bank(1)

        def begin(self):
            for e in (3, 2, 1):
                net.start(self.own(e), self.came.at[e - 1], self.in_b + e, (d, z_out), when=is_end)

        def add(self, e, ref):
            @pl.when(is_mid)
            def _():
                ref[...] = (self.own(e)[...].astype(F32) + ref[...].astype(F32)).astype(BF)

        def through(self, e):
            ref = self.came.at[e - 1]
            net.wait(ref, self.in_b + e, when=is_mid)
            self.add(e, ref)
            net.start(ref, self.cross.at[3 - e], self.cross_b + 3 - e, (d, z_out), when=is_mid)

        def pass_back(self):
            net.wait(self.cross.at[0], self.cross_b, when=is_mid)
            self.add(0, self.cross.at[0])
            net.start(self.cross.at[0], self.back, self.back_b, (d, z_back), when=is_mid)

        def total(self):
            net.wait(self.came.at[0], self.in_b + 1, when=is_mid)
            net.wait(self.cross.at[1], self.cross_b + 1, when=is_mid)
            net.wait(self.back, self.back_b, when=is_end)
            others = self.came[0].astype(F32) + self.cross[1].astype(F32)
            mine = self.own(jnp.where(is_mid, 1, 0))[...].astype(F32)
            return mine + jnp.where(is_mid, others, self.back[...].astype(F32))

    barrier = pltpu.get_barrier_semaphore()
    for m in range(1, 8):
        pl.semaphore_signal(barrier, 1, device_id=((d + m) % 8, t), device_id_type=MESH)
    for k in range(1, 4):
        pl.semaphore_signal(barrier, 1, device_id=(d, (t + k) % 4), device_id_type=MESH)
    pl.semaphore_wait(barrier, 10)

    for h in range(heads):
        at = slice(HD * h, HD * (h + 1))
        piece = jnp.concatenate(
            [qw_ref[i, :, at] for i in range(4)] + [kw_ref[:, at], vw_ref[:, at]], axis=1
        )
        wq[d, :, 6 * HD * h : 6 * HD * (h + 1)] = piece.astype(BF)

    class PlaneGather:
        def __init__(self, group, *views):
            self.views, self.bank, self.group = views, net.bank(8 * len(views)), group

        def copy(self, view, block, device):
            ref = self.views[view](block)
            net.start(ref, ref, self.bank + 8 * view + block, (device, t), group=self.group)

        def wait(self, view, block):
            net.wait(self.views[view](block), self.bank + 8 * view + block)

        def begin(self):
            for view, device in ((0, yn), (1, xn), (1, yn), (0, xn), (0, sib), (1, sib)):
                self.copy(view, d, device)

        def middle(self):
            self.wait(0, yn)
            self.copy(0, yn, xn)
            self.wait(1, xn)
            self.copy(1, xn, yn)
            self.copy(0, yn, sib)
            self.copy(1, xn, sib)
            for view, block in ((1, yn), (0, xn)):
                self.wait(view, block)
                self.copy(view, block, sib)

        def late(self):
            for view in range(2):
                self.wait(view, dg)
                self.copy(view, dg, sib)

        def end(self):
            for block in (sib, flip_x(sib), flip_y(sib), flip_x(flip_y(sib))):
                for view in range(len(self.views)):
                    self.wait(view, block)

    gather_q = PlaneGather("q", lambda b: wq.at[b, : strip // 2], lambda b: wq.at[b, strip // 2 :])
    gather_q.begin()

    def wide_t(value, high, wide):
        r, w = value.shape
        if w < wide:
            value = jnp.concatenate([value, jnp.zeros((r, wide - w), value.dtype)], axis=1)
        if r < high:
            value = jnp.concatenate([value, jnp.zeros((high - r, wide), value.dtype)], axis=0)
        return value.T

    wo[t, d] = wide_t(ow_ref[...], 256, 128)[:strip, :local].astype(BF)
    own[0, t] = uw_ref[...].astype(BF)
    own[1, t] = dw_ref[...].astype(BF)
    ubs[t] = jnp.broadcast_to(ub_ref[...][None], ubs.shape[1:])

    ub_z = net.bank(4)
    wf_x = net.bank(16)
    wf_y = net.bank(8)

    line_o = LineGather(lambda s: wo.at[s, d], "o")
    line_f = [LineGather(lambda s, i=i: own.at[i, s]) for i in range(2)]

    def hop_x(i, source, row, s, when=None):
        target = wf.at[i, row]
        sem = wf_x + 8 * i + row
        net.start(source, target, sem, (4 * y + s, t), when=joint(when, s != j))

        @pl.when(joint(when, s == j))
        def _():
            target[...] = source[...]

    def hop_y(n):
        for s, when in new_owners(n):
            net.start(own.at[0, s], own_y.at[s], wf_y + s, (yn, t), when=when)

    line_o.begin()
    line_f[0].begin()
    hop_y(0)
    for k in range(1, 4):
        net.start(ubs.at[t], ubs.at[t], ub_z + t, (d, (t + k) % 4))
    for b in range(blocks):
        at = slice(BLOCK * b, BLOCK * (b + 1))
        segc[at, :] = jnp.broadcast_to(seg_ref[:, at].astype(F32), (BLOCK, BLOCK)).T
        wordc[at, :] = jnp.broadcast_to((typ_ref[:, at] == 0).astype(F32), (BLOCK, BLOCK)).T
    xt[...] = x_ref[0].T
    for h in range(heads):
        at = slice(HD * h, HD * (h + 1))
        bias[:, 6 * HD * h : 6 * HD * (h + 1)] = jnp.concatenate(
            [qb_ref[i : i + 1, at] for i in range(4)] + [jnp.zeros((1, HD), F32), vb_ref[at][None]],
            axis=1,
        )

    gather_q.middle()
    line_o.step(1)
    line_f[0].step(1)
    hop_y(1)
    line_f[1].begin()
    gather_q.late()
    line_o.step(2)
    line_f[0].step(2)
    hop_y(2)
    gather_q.end()
    low_half = lax.broadcasted_iota(jnp.int32, (rows, BLOCK), 1) < HD
    is_word = wordc[...] > 0.5
    for h in range(heads):
        base = 6 * HD * h
        at = slice(BLOCK * h, BLOCK * (h + 1))
        made = nn(x_ref[0], wq[:, :, base : base + 6 * HD].reshape(width, 6 * HD))
        made = made + bias[:, base : base + 6 * HD]
        qq[:, at] = jnp.where(is_word, made[:, :BLOCK], made[:, BLOCK : 2 * BLOCK]).astype(BF)
        both = made[:, 2 * BLOCK :]
        keys = jnp.where(low_half, both, pltpu.roll(both, HD, 1))
        keys = jnp.where(jnp.logical_xor(is_word, low_half), 0.0, keys)
        kv[:, at] = both.astype(BF)
        kk[:, at] = keys.astype(BF)
        kvt[h] = both.T[HD:].astype(BF)
        kkt[h] = keys.T.astype(BF)

    line_o.step(3)
    line_f[0].step(3)
    hop_y(3)
    gather_o = PlaneGather("o", lambda b: wo.at[0:2, b], lambda b: wo.at[2:4, b])
    gather_o.begin()
    for n in range(4):
        for s, when in new_owners(n):
            hop_x(0, own.at[0, s], d, s, when)
    line_f[1].step(1)
    ct_z = net.bank(4)

    def span(b):
        return BLOCK * max(0, b - 2), BLOCK * min(blocks, b + 3)

    kept = [0]
    for b in range(blocks):
        kept.append(kept[-1] + span(b)[1] - span(b)[0])
    for b in range(blocks):
        lo, hi = span(b)
        at_q = slice(BLOCK * b, BLOCK * (b + 1))
        same = segc[lo:hi, :] == seg_ref[:, at_q].astype(F32)
        found = []
        for h in range(heads):
            at = slice(BLOCK * h, BLOCK * (h + 1))
            scores = nt(kk[lo:hi, at], qq[at_q, at]) * SCALING
            scores = jnp.where(same, scores, NEGATIVE)
            weights = jnp.exp(scores - jnp.max(scores, axis=0, keepdims=True))
            weights = weights * (1.0 / jnp.sum(weights, axis=0, keepdims=True))
            probs[h, kept[b] : kept[b + 1]] = weights
            found.append(nn(kvt[h, :, lo:hi], weights.astype(BF)))
        found.append(jnp.zeros((HD, BLOCK), F32))
        ctx[at_q, :] = jnp.concatenate(found, axis=0).T[:, :local].astype(BF)
        if b == 2:
            line_f[1].step(2)
        if b > 0:
            s = b - 1
            src = ctx.at[quarter * s : quarter * (s + 1)]
            net.start(src, ct.at[t], ct_z + t, (d, s), when=t != s)
    ct[t] = ctx[own_rows, :]

    line_f[1].step(3)
    for n in range(4):
        for s, when in new_owners(n):
            hop_x(1, own.at[1, s], d, s, when)
    gather_o.middle()
    for s in range(4):
        net.wait(own_y.at[s], wf_y + s)
        hop_x(0, own_y.at[s], yn, s)
    gather_o.late()
    gather_o.end()
    for k in range(1, 4):
        s = (t + k) % 4
        net.wait(ct.at[s], ct_z + s)
    attended = nt(ct[0], wo[0].reshape(width, local))
    for s in range(1, 4):
        attended = attended + nt(ct[s], wo[s].reshape(width, local))
    normal, inverse = norm_rows(x_ref[0, own_rows, :].astype(F32) + attended + ob_ref[...][None])
    n1_s[...] = normal
    r1_s[...] = jnp.broadcast_to(inverse, r1_s.shape)
    normed = normal * ag_ref[...][None] + as_ref[...][None]
    a_s[...] = normed
    act[j] = normed.astype(BF)

    def rows_of(ref, first, count):
        return lambda owner: ref.at[
            0, pl.ds(pl.multiple_of(owner * quarter + first, 16), count)
        ]

    class RowGather:
        def __init__(self, ref):
            self.ref, self.bank = ref, net.bank(4)

        def copy(self, rank, device):
            net.start(self.ref.at[rank], self.ref.at[rank], self.bank + rank, (device, t))

        def begin(self):
            self.copy(j, xn)
            self.copy(j, sib)

        def near(self):
            net.wait(self.ref.at[sib % 4], self.bank + sib % 4)

        def middle(self):
            net.wait(self.ref.at[xn % 4], self.bank + xn % 4)
            self.copy(xn % 4, sib)

        def far(self):
            net.wait(self.ref.at[flip_x(sib) % 4], self.bank + flip_x(sib) % 4)

    class RowSum:
        def __init__(self, index):
            self.index, self.bank = index, net.bank(3)

        def hand(self, slot, partial_rows):
            where = 3 * self.index + slot
            rs_send[where] = partial_rows.astype(BF)
            net.start(
                rs_send.at[where], rs_recv.at[where], self.bank + slot, (xn if slot == 2 else sib, t)
            )

        def take(self, slot):
            where = 3 * self.index + slot
            net.wait(rs_recv.at[where], self.bank + slot)
            return rs_recv[where].astype(F32)

        def own_half(self):
            self.hand(0, part_m[1 - c])

        def other_half(self):
            self.hand(1, part_o[1 - c])
            self.hand(2, part_o[c] + self.take(1))

        def total(self):
            return part_m[c] + self.take(0) + self.take(2)

    rows_a = RowGather(act)
    rows_a.begin()
    for m in range(4):
        r = 4 * y + (j + m) % 4
        if m:
            net.wait(wf.at[1, r], wf_x + 8 + r)
        net.start(wf.at[1, r], wf.at[1, r], wf_y + 4 + (j + m) % 4, (yn, t), group="f")
    rows_a.middle()
    rows_a.near()
    for k in range(1, 4):
        s = (t + k) % 4
        net.wait(ubs.at[s], ub_z + s)
    for m in range(1, 4):
        for r in (4 * y + (j + m) % 4, 4 * (1 - y) + (j + m) % 4):
            net.wait(wf.at[0, r], wf_x + r)
    near = pl.ds(2 * x, 2)
    away = pl.ds(2 - 2 * x, 2)

    def feed(half):
        hidden = nn(act[half].reshape(2 * quarter, width), wf[0].reshape(width, width))
        hidden = hidden + ubs[j][:1]
        bell = 0.5 * (1.0 + lax.erf(hidden * 0.7071067811865476))
        slope = bell + hidden * (0.3989422804014327 * jnp.exp(-0.5 * hidden * hidden))
        gelu_d[half] = slope.reshape(2, quarter, width)
        gl[half] = (hidden * bell).astype(BF).reshape(2, quarter, width)

    def feed_out(half, part):
        made = nt(gl[half].reshape(2 * quarter, width), wf[1].reshape(width, width))
        part[...] = made.reshape(2, quarter, width)

    feed(near)
    rows_a.far()
    feed(away)
    for m in range(4):
        r = 4 * (1 - y) + (j + m) % 4
        net.wait(wf.at[1, r], wf_y + 4 + (j + m) % 4)
    sum_f = RowSum(0)
    feed_out(away, part_o)
    sum_f.hand(1, part_o[1 - c])
    feed_out(near, part_m)
    sum_f.own_half()
    sum_f.hand(2, part_o[c] + sum_f.take(1))
    ffn_out = sum_f.total() + db_ref[...][None]

    normal, inverse = norm_rows(a_s[...] + ffn_out)
    out_ref[0, own_rows, :] = (normal * fg_ref[...][None] + fs_ref[...][None]).astype(BF)
    line_out = LineGather(rows_of(out_ref, 0, quarter))
    line_out.begin()
    upstream = cot_ref[0, own_rows, :].astype(F32)
    du = norm_rows_back(upstream, normal, inverse, fg_ref[...][None])
    dub[j] = du.astype(BF)
    rows_u = RowGather(dub)
    rows_u.begin()
    a_s[...] = du
    sv[...] = jnp.zeros_like(sv)
    sv[0:1] = jnp.sum(upstream * normal, axis=0, keepdims=True)
    sv[1:2] = jnp.sum(upstream, axis=0, keepdims=True)
    sv[2:3] = jnp.sum(du, axis=0, keepdims=True)

    def feed_back(half, part):
        made = nn(dub[half].reshape(2 * quarter, width), wf[1].reshape(width, width))
        made = made * gelu_d[half].reshape(2 * quarter, width)
        dzb[half] = made.astype(BF).reshape(2, quarter, width)
        back = nt(made.astype(BF), wf[0].reshape(width, width))
        part[...] = back.reshape(2, quarter, width)
        return jnp.sum(made, axis=0, keepdims=True)

    rows_u.near()
    up_sum = feed_back(near, part_m)
    sum_b = RowSum(1)
    sum_b.own_half()
    line_out.step(1)
    rows_u.middle()
    rows_u.far()
    up_sum = up_sum + feed_back(away, part_o)
    sum_b.hand(1, part_o[1 - c])
    sum_b.hand(2, part_o[c] + sum_b.take(1))
    rank_rows = lax.broadcasted_iota(jnp.int32, (4, width), 0)
    sv[6:10] = jnp.where(rank_rows == j, up_sum, 0.0)

    ry_b = net.bank(2)
    theirs = pl.ds(4 * (1 - y), 4)
    ours = pl.ds(4 * y, 4)
    def feed_grad(i, left, right):
        made = tn(left[...].reshape(4 * quarter, width), right[...].reshape(4 * quarter, width))
        wf[i] = made.astype(BF).reshape(8, strip, width)

    net.settle("f")
    feed_grad(1, dub, gl)
    net.start(wf.at[1, theirs], ry.at[1], ry_b + 1, (yn, t))
    feed_grad(0, act, dzb)
    da = a_s[...] + sum_b.total()
    line_out.step(2)
    normal = n1_s[...]
    dh = norm_rows_back(da, normal, r1_s[:, :1], ag_ref[...][None])
    a_s[...] = dh
    dhb = dh.astype(BF)
    dc_z = net.bank(4)
    for k in range(1, 4):
        s = (t + k) % 4
        dct[s] = nn(dhb, wo[s].reshape(width, local)).astype(BF)
        net.start(dct.at[s], dc.at[t], dc_z + t, (d, s))
    dc[t] = nn(dhb, wo[t].reshape(width, local)).astype(BF)
    net.start(wf.at[0, theirs], ry.at[0], ry_b, (yn, t))
    sv[3:4] = jnp.sum(da * normal, axis=0, keepdims=True)
    sv[4:5] = jnp.sum(da, axis=0, keepdims=True)
    sv[5:6] = jnp.sum(dh, axis=0, keepdims=True)
    net.settle("o")
    for s in range(4):
        wo[s] = tn(dhb, ct[s]).astype(BF).reshape(8, strip, local)
    by_core = wo.reshape(4, 4, 2, strip, local)
    go_b = net.bank(1)
    net.start(by_core.at[:, :, 1 - c], go_r, go_b, (sib, t))

    rx_b = net.bank(8)

    def over_y(i):
        net.wait(ry.at[i], ry_b + i)
        ry[i] = (wf[i, ours].astype(F32) + ry[i].astype(F32)).astype(BF)
        for r in (xn, flip_x(sib), sib):
            net.start(ry.at[i, r % 4], rx.at[i, j], rx_b + 4 * i + j, (r, t))
        rx[i, j] = ry[i, j]

    for k in range(1, 4):
        s = (t + k) % 4
        net.wait(dc.at[s], dc_z + s)
    dctx = dc[...].reshape(rows, local)
    for h in range(heads):
        dco[:, BLOCK * h : BLOCK * (h + 1)] = jnp.concatenate(
            [jnp.zeros((rows, HD), BF), dctx[:, HD * h : HD * (h + 1)]], axis=1
        )
    for h in range(heads):
        dkk[h][...] = jnp.zeros((rows, BLOCK), F32)
        dvv[h][...] = jnp.zeros((rows, BLOCK), F32)
    for b in range(blocks):
        lo, hi = span(b)
        at_q = slice(BLOCK * b, BLOCK * (b + 1))
        for h in range(heads):
            at = slice(BLOCK * h, BLOCK * (h + 1))
            weights = probs[h, kept[b] : kept[b + 1]]
            dp = nt(kv[lo:hi, at], dco[at_q, at])
            ds = weights * (dp - jnp.sum(weights * dp, axis=0, keepdims=True))
            dsb = ds.astype(BF)
            dkk[h][lo:hi] += nn(dsb, qq[at_q, at])
            dvv[h][lo:hi] += nn(weights.astype(BF), dco[at_q, at])
            dqq[h][at_q] = nn(kkt[h, :, lo:hi], dsb).T * SCALING

    over_y(1)
    for h in range(heads):
        base = 6 * HD * h
        first = jnp.where(is_word, dqq[h][...], 0.0)
        second = jnp.where(is_word, 0.0, dqq[h][...])
        keys = dkk[h][...]
        keys = jnp.where(is_word, keys, pltpu.roll(keys, HD, 1)) * SCALING
        third = jnp.where(low_half, keys, dvv[h][...])
        for i, part in enumerate((first, second, third)):
            at = slice(base + BLOCK * i, base + BLOCK * (i + 1))
            dqkv[:, at] = part.astype(BF)
            row, col = divmod(base + BLOCK * i, width)
            sv[10 + row : 11 + row, col : col + BLOCK] = jnp.sum(part, axis=0, keepdims=True)

    made = nt(dqkv[...], wq[...].reshape(width, 6 * local))
    dzb[...] = made.astype(BF).reshape(4, quarter, width)
    part = quarter // 2
    line_dx, line_in = [], []
    for q in range(2):
        cut = pl.ds(part * q, part)
        line_dx.append(
            LineReduce(
                lambda e, cut=cut: dzb.at[place(e), cut],
                dx_in.at[q], dx_cross.at[q], dx_back.at[q],
            )
        )
        line_in.append(LineGather(rows_of(ig_ref, part * q, part)))

    def arrive(q):
        total = line_dx[q].total() + a_s[part * q : part * (q + 1)]
        ig_ref[0, pl.ds(pl.multiple_of(t * quarter + part * q, 16), part)] = total.astype(BF)
        line_in[q].begin()

    line_w = [
        LineReduce(
            lambda e, i=i: rx.at[i, place(e)], fr_in.at[i], fr_cross.at[i], fr_back.at[i]
        )
        for i in range(2)
    ]

    def strips_on(i):
        for m in range(1, 4):
            r = (j + m) % 4
            net.wait(rx.at[i, r], rx_b + 4 * i + r)
        line_w[i].begin()

    line_dx[0].begin()
    line_dx[1].begin()
    vb8[d] = sv[...]
    sv_b = net.bank(8)
    for m in range(1, 8):
        net.start(sv, vb8.at[d], sv_b + d, ((d + m) % 8, t))

    net.settle("q")
    wq[...] = nn(xt[...], dqkv[...]).astype(BF).reshape(8, strip, 6 * local)
    q_by_core = wq.reshape(4, 2, strip, 6 * local)
    gq_b = net.bank(1)
    net.start(q_by_core.at[:, 1 - c], gq_r, gq_b, (sib, t))
    line_dx[0].through(3)
    line_dx[0].through(2)
    net.wait(go_r, go_b)
    go_r[...] = (by_core[:, :, c].astype(F32) + go_r[...].astype(F32)).astype(BF)
    rp_b = net.bank(4)
    for r in (xn, yn, dg):
        net.start(go_r.at[:, r // 2], rp.at[chip], rp_b + chip, (r, t))
    rp[chip] = go_r[:, chip]

    strips_on(1)
    line_dx[1].through(3)
    line_dx[1].through(2)
    line_dx[0].pass_back()
    over_y(0)
    net.wait(gq_r, gq_b)
    gq_r[...] = (q_by_core[:, c].astype(F32) + gq_r[...].astype(F32)).astype(BF)
    gp_b = net.bank(4)
    for r in (xn, yn, dg):
        net.start(gq_r.at[r // 2], gp.at[chip], gp_b + chip, (r, t))
    gp[chip] = gq_r[chip]

    line_dx[1].pass_back()
    arrive(0)
    line_w[1].through(3)
    line_w[1].through(2)
    arrive(1)
    for m in range(1, 8):
        s = (d + m) % 8
        net.wait(vb8.at[s], sv_b + s)
    total = vb8[0]
    for m in range(1, 8):
        total = total + vb8[m]
    sw[...] = total
    vz_b = net.bank(4)
    for k in range(1, 4):
        net.start(sw, vz.at[t], vz_b + t, (d, (t + k) % 4))
    vz[t] = sw[...]

    line_in[0].step(1)
    strips_on(0)
    line_in[1].step(1)
    line_w[1].pass_back()
    line_in[0].step(2)
    line_in[1].step(2)
    line_w[0].through(3)
    line_w[0].through(2)
    for r in (xn, yn, dg):
        net.wait(rp.at[r // 2], rp_b + r // 2)
    total = rp[0].astype(F32)
    for k in range(1, 4):
        total = total + rp[k].astype(F32)
    sp[...] = total.astype(BF)
    rz_b = net.bank(4)
    for k in range(1, 4):
        s = (t + k) % 4
        net.start(sp.at[s], rz.at[t], rz_b + t, (d, s))
    rz[t] = sp[t]

    for k in range(1, 4):
        s = (t + k) % 4
        net.wait(vz.at[s], vz_b + s)
    total = vz[0]
    for s in range(1, 4):
        total = total + vz[s]
    up_total = jnp.sum(jnp.where(rank_rows == t, total[6:10], 0.0), axis=0, keepdims=True)
    small_ref[0:6] = total[0:6]
    small_ref[6:7] = up_total
    small_ref[8:10] = sw[10:12]

    line_w[0].pass_back()
    dg_ref[...] = line_w[1].total()
    ug_ref[...] = line_w[0].total()
    for k in range(1, 4):
        s = (t + k) % 4
        net.wait(rz.at[s], rz_b + s)
    total = rz[0].astype(F32)
    for s in range(1, 4):
        total = total + rz[s].astype(F32)
    og_ref[...] = wide_t(total, BLOCK, 256)[:local, :strip]

    for r in (xn, yn, dg):
        net.wait(gp.at[r // 2], gp_b + r // 2)
    total = gp[0].astype(F32)
    for k in range(1, 4):
        total = total + gp[k].astype(F32)
    for h in range(heads):
        base = 6 * HD * h
        at = slice(HD * h, HD * (h + 1))
        for i in range(4):
            qg_ref[i, :, at] = total[:, base + HD * i : base + HD * (i + 1)]
        kg_ref[:, at] = total[:, base + 4 * HD : base + 5 * HD]
        vg_ref[:, at] = total[:, base + 5 * HD : base + 6 * HD]

    line_out.step(3)
    for q in range(2):
        line_in[q].step(3)
    net.settle()
    assert net.sends <= SENDS and net.banks <= RECVS, (net.sends, net.banks)


def end_kernel(*refs):
    sources, small = refs[:8], refs[8]
    targets, (qbg, vbg), vectors = refs[9:17], refs[17:19], refs[19:26]
    for source, target in zip(sources, targets):
        target[...] = source[...]
    fgg, fsg, dbg, agg, asg, obg, ubg = (small[i] for i in range(7))
    for ref, value in zip(vectors, (obg, ubg, dbg, agg, asg, fgg, fsg)):
        ref[...] = value
    width = small.shape[1]
    values = []
    for h in range(vbg.shape[0] // HD):
        row, col = divmod(6 * HD * h, width)
        piece = small[8 + row : 9 + row, col : col + 6 * HD]
        for i in range(4):
            qbg[i : i + 1, HD * h : HD * (h + 1)] = piece[:, HD * i : HD * (i + 1)]
        values.append(piece[:, 5 * HD :])
    vbg[...] = jnp.concatenate(values, axis=1)[0]


def fused(
    layer_input, segment_ids, token_types, query_weight, key_weight, value_weight, out_weight,
    up_weight, down_weight, query_bias, value_bias, out_bias, up_bias, down_bias, attn_gain,
    attn_shift, ffn_gain, ffn_shift, cotangent,
):
    rows, width = layer_input.shape[1:]
    strip, local = key_weight.shape
    quarter, heads, blocks = rows // 4, local // HD, rows // BLOCK
    kept = sum(BLOCK * (min(blocks, b + 3) - max(0, b - 2)) for b in range(blocks))
    args = [
        layer_input, segment_ids, token_types, query_weight, key_weight, value_weight, out_weight,
        up_weight, down_weight.T, query_bias, value_bias, out_bias, up_bias, down_bias, attn_gain,
        attn_shift, ffn_gain, ffn_shift, cotangent,
    ]

    def like(v, dtype=F32):
        return jax.ShapeDtypeStruct(v.shape, dtype)

    outs = [
        like(layer_input, BF), like(layer_input, BF), like(query_weight), like(key_weight),
        like(value_weight), like(out_weight), like(up_weight), jax.ShapeDtypeStruct((strip, width), F32),
        jax.ShapeDtypeStruct((16, width), F32),
    ]
    v = pltpu.VMEM
    scratch = [
        v((8, strip, 6 * local), BF), v((4, 8, strip, local), BF), v((2, 4, strip, width), BF), v((4, strip, width), BF),
        v((2, 8, strip, width), BF), v((4, 8, width), F32), v((rows, BLOCK), F32),
        v((rows, BLOCK), F32), v((width, rows), BF), v((1, 6 * local), F32),
        v((rows, heads * BLOCK), BF), v((rows, heads * BLOCK), BF), v((rows, heads * BLOCK), BF),
        v((heads, HD, rows), BF), v((heads, BLOCK, rows), BF),
        v((heads, kept, BLOCK), F32), v((rows, local), BF), v((4, quarter, local), BF),
        v((quarter, width), F32), v((quarter, width), F32), v((quarter, BLOCK), F32),
        v((4, quarter, width), BF), v((4, quarter, width), F32), v((4, quarter, width), BF),
        v((4, quarter, width), F32),
        v((6, quarter, width), BF), v((6, quarter, width), BF),
        v((4, quarter, width), BF), v((4, quarter, width), BF),
        v((2, 4, strip, width), BF),
        v((2, 4, strip, width), BF), v((2, 3, strip, width), BF),
        v((2, 2, strip, width), BF), v((2, strip, width), BF),
        v((4, quarter, local), BF), v((4, quarter, local), BF),
        v((rows, heads * BLOCK), BF),
        v((4, 4, strip, local), BF), v((4, 4, strip, local), BF), v((4, strip, local), BF),
        v((4, strip, local), BF),
        v((rows, 6 * local), BF),
        v((2, 3, quarter // 2, width), BF), v((2, 2, quarter // 2, width), BF),
        v((2, quarter // 2, width), BF),
        v((4, strip, 6 * local), BF), v((4, strip, 6 * local), BF),
        v((16, width), F32), v((8, 16, width), F32), v((16, width), F32), v((4, 16, width), F32),
        pltpu.SemaphoreType.DMA((SENDS,)), pltpu.SemaphoreType.DMA((RECVS,)),
    ]
    spec = pl.BlockSpec(memory_space=pltpu.VMEM)
    made = pl.pallas_call(
        layer_kernel,
        out_shape=outs,
        in_specs=[spec] * len(args),
        out_specs=[spec] * len(outs),
        scratch_shapes=scratch,
        compiler_params=pltpu.CompilerParams(
            collective_id=0, has_side_effects=True, vmem_limit_bytes=58 << 20
        ),
        name="layer",
    )(*args)
    *large, small = made
    vector = jax.ShapeDtypeStruct((width,), F32)
    ended = pl.pallas_call(
        end_kernel,
        out_shape=[like(v, v.dtype) for v in large]
        + [like(query_bias), jax.ShapeDtypeStruct((local,), F32)]
        + [vector] * 7,
        in_specs=[spec] * len(made),
        out_specs=[spec] * 17,
        name="finish",
    )(*large, small)
    return (*ended[:7], ended[7].T, *ended[8:])


def solution(mesh):
    in_specs = (
        P("dp", None, None),
        P("dp", None),
        P("dp", None),
        P(None, "dp", "tensor"),
        P("dp", "tensor"),
        P("dp", "tensor"),
        P("tensor", "dp"),
        P("dp", "tensor"),
        P("tensor", "dp"),
        P(None, "tensor"),
        P("tensor"),
        P(),
        P("tensor"),
        P(),
        P(),
        P(),
        P(),
        P(),
        P("dp", None, None),
    )
    out_specs = (
        P("dp", None, None),
        P("dp", None, None),
        P(None, "dp", "tensor"),
        P("dp", "tensor"),
        P("dp", "tensor"),
        P("tensor", "dp"),
        P("dp", "tensor"),
        P("tensor", "dp"),
        P(None, "tensor"),
        P("tensor"),
        P(),
        P("tensor"),
        P(),
        P(),
        P(),
        P(),
        P(),
    )
    step = fused if fits(mesh) else shards
    return jax.shard_map(step, mesh=mesh, in_specs=in_specs, out_specs=out_specs, check_vma=False)
```

```python
from functools import partial

import jax
import jax.numpy as jnp
from jax import lax
from jax.experimental import pallas as pl
from jax.experimental.pallas import tpu as pltpu
from jax.sharding import PartitionSpec as P

HD = 64


EPSILON = 1e-05
SCALING = 0.125
NEGATIVE = -1000000000.0


def layer_norm_keep(values, norm_gain, norm_shift):
    centre = values - jnp.mean(values, axis=-1, keepdims=True)
    inverse = lax.rsqrt(jnp.mean(centre * centre, axis=-1, keepdims=True) + EPSILON)
    normal = centre * inverse
    return (normal * norm_gain + norm_shift, normal, inverse)


def layer_norm_back(upstream, normal, inverse, norm_gain):
    scaled = upstream * norm_gain
    gain_grad = jnp.sum(upstream * normal, axis=0)
    shift_grad = jnp.sum(upstream, axis=0)
    inner_term = (
        scaled
        - jnp.mean(scaled, axis=-1, keepdims=True)
        - normal * jnp.mean(scaled * normal, axis=-1, keepdims=True)
    )
    return (inverse * inner_term, gain_grad, shift_grad)


def heads_of(matrix):
    return matrix.reshape(matrix.shape[0], -1, HD)


def pick_queries(query_rows, type_row):
    word_tok = (type_row == 0)[:, None]
    return (
        jnp.where(word_tok, query_rows[0], query_rows[2]),
        jnp.where(word_tok, query_rows[1], query_rows[3]),
    )


def score_block(word_heads, entity_heads, key_heads, segment_row, type_row):
    to_words = jnp.einsum("qhd,khd->hqk", word_heads, key_heads, preferred_element_type=jnp.float32)
    to_entities = jnp.einsum(
        "qhd,khd->hqk", entity_heads, key_heads, preferred_element_type=jnp.float32
    )
    scores = jnp.where((type_row == 0)[None, None, :], to_words, to_entities) * SCALING
    allowed = (segment_row[:, None] == segment_row[None, :])[None]
    return jnp.where(allowed, scores, NEGATIVE)


def attend_forward(packed):
    query_rows, key_seq, value_seq, segment_row, type_row = packed
    word_query, entity_query = pick_queries(query_rows, type_row)
    scores = score_block(
        heads_of(word_query), heads_of(entity_query), heads_of(key_seq), segment_row, type_row
    )
    row_top = jnp.max(scores, axis=-1, keepdims=True)
    weights = jnp.exp(scores - row_top)
    totals = jnp.sum(weights, axis=-1, keepdims=True)
    attn_probs = (weights / totals).astype(jnp.bfloat16)
    context = jnp.einsum(
        "hqk,khd->qhd", attn_probs, heads_of(value_seq), preferred_element_type=jnp.float32
    )
    log_total = (row_top + jnp.log(totals))[..., 0]
    return (context.reshape(context.shape[0], -1).astype(jnp.bfloat16), log_total)


def attend_backward(packed):
    query_rows, key_seq, value_seq, segment_row, type_row, log_total, context_grad = packed
    word_query, entity_query = pick_queries(query_rows, type_row)
    word_heads = heads_of(word_query)
    entity_heads = heads_of(entity_query)
    key_heads = heads_of(key_seq)
    value_heads = heads_of(value_seq)
    grad_heads = heads_of(context_grad)
    scores = score_block(word_heads, entity_heads, key_heads, segment_row, type_row)
    attn_probs = jnp.exp(scores - log_total[..., None])
    prob_grad = jnp.einsum(
        "qhd,khd->hqk", grad_heads, value_heads, preferred_element_type=jnp.float32
    )
    score_grad = attn_probs * (prob_grad - jnp.sum(attn_probs * prob_grad, axis=-1, keepdims=True))
    score_low = score_grad.astype(jnp.bfloat16)
    word_key = (type_row == 0)[None, None, :]
    zeroes = jnp.zeros_like(score_low)
    word_part = jnp.where(word_key, score_low, zeroes)
    entity_part = jnp.where(word_key, zeroes, score_low)
    word_qgrad = (
        jnp.einsum("hqk,khd->qhd", word_part, key_heads, preferred_element_type=jnp.float32)
        * SCALING
    )
    entity_qgrad = (
        jnp.einsum("hqk,khd->qhd", entity_part, key_heads, preferred_element_type=jnp.float32)
        * SCALING
    )
    key_delta = (
        jnp.einsum("hqk,qhd->khd", word_part, word_heads, preferred_element_type=jnp.float32)
        + jnp.einsum("hqk,qhd->khd", entity_part, entity_heads, preferred_element_type=jnp.float32)
    ) * SCALING
    value_delta = jnp.einsum(
        "hqk,qhd->khd",
        attn_probs.astype(jnp.bfloat16),
        grad_heads,
        preferred_element_type=jnp.float32,
    )
    row_count = word_qgrad.shape[0]
    return (
        word_qgrad.reshape(row_count, -1),
        entity_qgrad.reshape(row_count, -1),
        key_delta.reshape(row_count, -1),
        value_delta.reshape(row_count, -1),
    )


def row_share(partial_rows):
    return lax.psum_scatter(partial_rows, "tensor", scatter_dimension=0, tiled=True)


def row_whole(rounded_rows):
    return lax.all_gather(rounded_rows, "tensor", axis=0, tiled=True)


def shards(
    layer_input,
    segment_ids,
    token_types,
    query_weight,
    key_weight,
    value_weight,
    out_weight,
    up_weight,
    down_weight,
    query_bias,
    value_bias,
    out_bias,
    up_bias,
    down_bias,
    attn_gain,
    attn_shift,
    ffn_gain,
    ffn_shift,
    cotangent,
):
    seq_count, seq_length, model_width = layer_input.shape
    tokens = layer_input.reshape(-1, model_width)
    row_count = tokens.shape[0]
    share = row_count // lax.axis_size("tensor")
    first_row = lax.axis_index("tensor") * share

    def own_rows(matrix):
        return lax.dynamic_slice_in_dim(matrix, first_row, share, 0)

    def combine_rows(partial_rows):
        return row_share(partial_rows)

    def whole_rows(rounded_rows):
        return row_whole(rounded_rows)

    query_complete, key_full, value_full, out_full = (
        lax.all_gather(query_weight.astype(jnp.bfloat16), "dp", axis=1, tiled=True),
        lax.all_gather(key_weight.astype(jnp.bfloat16), "dp", axis=0, tiled=True),
        lax.all_gather(value_weight.astype(jnp.bfloat16), "dp", axis=0, tiled=True),
        lax.all_gather(out_weight.astype(jnp.bfloat16), "dp", axis=1, tiled=True),
    )
    local_width = key_full.shape[1]
    query_rows = jnp.einsum(
        "gow,qwk->gqok", layer_input, query_complete, preferred_element_type=jnp.float32
    )
    query_rows = (query_rows + query_bias[None, :, None, :]).astype(jnp.bfloat16)
    keys_all = jnp.dot(layer_input, key_full, preferred_element_type=jnp.float32).astype(
        jnp.bfloat16
    )
    values_all = (
        jnp.dot(layer_input, value_full, preferred_element_type=jnp.float32) + value_bias
    ).astype(jnp.bfloat16)
    context, log_total = lax.map(
        attend_forward, (query_rows, keys_all, values_all, segment_ids, token_types)
    )
    context_rows = context.reshape(-1, local_width)
    attended = combine_rows(jnp.dot(context_rows, out_full, preferred_element_type=jnp.float32))
    residual = own_rows(tokens).astype(jnp.float32) + attended + out_bias
    normed, normal_one, inverse_one = layer_norm_keep(residual, attn_gain, attn_shift)
    normed_low = whole_rows(normed.astype(jnp.bfloat16))
    up_full, down_full = (
        lax.all_gather(up_weight.astype(jnp.bfloat16), "dp", axis=0, tiled=True),
        lax.all_gather(down_weight.astype(jnp.bfloat16), "dp", axis=1, tiled=True),
    )
    pre_act = jnp.dot(normed_low, up_full, preferred_element_type=jnp.float32) + up_bias
    activated, gelu_pull = jax.vjp(partial(jax.nn.gelu, approximate=False), pre_act)
    act_low = activated.astype(jnp.bfloat16)
    ffn_out = (
        combine_rows(jnp.dot(act_low, down_full, preferred_element_type=jnp.float32)) + down_bias
    )
    normed_out, normal_two, inverse_two = layer_norm_keep(normed + ffn_out, ffn_gain, ffn_shift)
    output = whole_rows(normed_out.astype(jnp.bfloat16)).reshape(layer_input.shape)
    upstream = own_rows(cotangent.reshape(-1, model_width)).astype(jnp.float32)
    sum_grad, ffngain_grad, ffnshift_grad = layer_norm_back(
        upstream, normal_two, inverse_two, ffn_gain
    )
    downbias_grad = jnp.sum(sum_grad, axis=0)
    sum_low = whole_rows(sum_grad.astype(jnp.bfloat16))
    up_back, down_back = (
        lax.all_gather(up_weight.astype(jnp.bfloat16), "dp", axis=0, tiled=True),
        lax.all_gather(down_weight.astype(jnp.bfloat16), "dp", axis=1, tiled=True),
    )
    down_local = jnp.dot(act_low.T, sum_low, preferred_element_type=jnp.float32)
    act_grad = jnp.dot(sum_low, down_back.T, preferred_element_type=jnp.float32)
    (pre_grad,) = gelu_pull(act_grad)
    upbias_grad = jnp.sum(pre_grad, axis=0)
    pre_low = pre_grad.astype(jnp.bfloat16)
    up_local = jnp.dot(normed_low.T, pre_low, preferred_element_type=jnp.float32)
    upproj_grad, downproj_grad = (
        lax.psum_scatter(up_local, "dp", scatter_dimension=0, tiled=True),
        lax.psum_scatter(down_local, "dp", scatter_dimension=1, tiled=True),
    )
    normed_grad = (
        combine_rows(jnp.dot(pre_low, up_back.T, preferred_element_type=jnp.float32)) + sum_grad
    )
    resid_grad, attngain_grad, attnshift_grad = layer_norm_back(
        normed_grad, normal_one, inverse_one, attn_gain
    )
    outbias_grad = jnp.sum(resid_grad, axis=0)
    resid_low = whole_rows(resid_grad.astype(jnp.bfloat16))
    query_pullback, key_pullback, value_pullback, out_back = (
        lax.all_gather(query_weight.astype(jnp.bfloat16), "dp", axis=1, tiled=True),
        lax.all_gather(key_weight.astype(jnp.bfloat16), "dp", axis=0, tiled=True),
        lax.all_gather(value_weight.astype(jnp.bfloat16), "dp", axis=0, tiled=True),
        lax.all_gather(out_weight.astype(jnp.bfloat16), "dp", axis=1, tiled=True),
    )
    outproj_local = jnp.dot(context_rows.T, resid_low, preferred_element_type=jnp.float32)
    context_grad = jnp.dot(resid_low, out_back.T, preferred_element_type=jnp.float32).astype(
        jnp.bfloat16
    )
    context_grad = context_grad.reshape(seq_count, seq_length, local_width)
    word_qgrad, entity_qgrad, key_delta, value_delta = lax.map(
        attend_backward,
        (query_rows, keys_all, values_all, segment_ids, token_types, log_total, context_grad),
    )
    is_word = (token_types == 0)[..., None]
    zero_rows = jnp.zeros_like(word_qgrad)
    query_delta = jnp.stack(
        [
            jnp.where(is_word, word_qgrad, zero_rows),
            jnp.where(is_word, entity_qgrad, zero_rows),
            jnp.where(is_word, zero_rows, word_qgrad),
            jnp.where(is_word, zero_rows, entity_qgrad),
        ],
        axis=1,
    )
    querybias_grad = jnp.sum(query_delta, axis=(0, 2))
    valuebias_grad = jnp.sum(value_delta, axis=(0, 1))
    query_reduced = query_delta.astype(jnp.bfloat16)
    key_reduced = key_delta.astype(jnp.bfloat16)
    value_reduced = value_delta.astype(jnp.bfloat16)
    query_local = jnp.einsum(
        "nvh,nkvw->khw", layer_input, query_reduced, preferred_element_type=jnp.float32
    )
    key_shard = jnp.einsum(
        "pui,pun->in", layer_input, key_reduced, preferred_element_type=jnp.float32
    )
    value_local = jnp.einsum(
        "pui,pun->in", layer_input, value_reduced, preferred_element_type=jnp.float32
    )
    input_part = (
        jnp.einsum(
            "kayo,azo->kyz", query_reduced, query_pullback, preferred_element_type=jnp.float32
        )
        + jnp.einsum("ohz,wz->ohw", key_reduced, key_pullback, preferred_element_type=jnp.float32)
        + jnp.einsum(
            "ohz,wz->ohw", value_reduced, value_pullback, preferred_element_type=jnp.float32
        )
    )
    input_total = combine_rows(input_part.reshape(-1, model_width))
    input_grad = whole_rows((input_total + resid_grad).astype(jnp.bfloat16)).reshape(
        layer_input.shape
    )
    query_grad, key_grad, value_grad, outproj_grad = (
        lax.psum_scatter(query_local, "dp", scatter_dimension=1, tiled=True),
        lax.psum_scatter(key_shard, "dp", scatter_dimension=0, tiled=True),
        lax.psum_scatter(value_local, "dp", scatter_dimension=0, tiled=True),
        lax.psum_scatter(outproj_local, "dp", scatter_dimension=1, tiled=True),
    )
    querybias_grad, valuebias_grad, upbias_grad = lax.psum(
        (querybias_grad, valuebias_grad, upbias_grad), "dp"
    )
    outbias_grad, downbias_grad, attngain_grad, attnshift_grad, ffngain_grad, ffnshift_grad = (
        lax.psum(
            (
                outbias_grad,
                downbias_grad,
                attngain_grad,
                attnshift_grad,
                ffngain_grad,
                ffnshift_grad,
            ),
            ("dp", "tensor"),
        )
    )
    return (
        output,
        input_grad,
        query_grad,
        key_grad,
        value_grad,
        outproj_grad,
        upproj_grad,
        downproj_grad,
        querybias_grad,
        valuebias_grad,
        outbias_grad,
        upbias_grad,
        downbias_grad,
        attngain_grad,
        attnshift_grad,
        ffngain_grad,
        ffnshift_grad,
    )


MESH = pl.DeviceIdType.MESH
BF = jnp.bfloat16
F32 = jnp.float32
BLOCK = 128


def fits(mesh):
    return mesh.shape["dp"] == 8 and mesh.shape["tensor"] == 4


def nn(a, b):
    return lax.dot_general(a, b, (((1,), (0,)), ((), ())), preferred_element_type=F32)


def nt(a, b):
    return lax.dot_general(a, b, (((1,), (1,)), ((), ())), preferred_element_type=F32)


def tn(a, b):
    return lax.dot_general(a, b, (((0,), (0,)), ((), ())), preferred_element_type=F32)


def norm_rows(values):
    centre = values - jnp.mean(values, axis=-1, keepdims=True)
    inverse = lax.rsqrt(jnp.mean(centre * centre, axis=-1, keepdims=True) + EPSILON)
    return centre * inverse, inverse


def norm_rows_back(upstream, normal, inverse, gain):
    scaled = upstream * gain
    return inverse * (
        scaled
        - jnp.mean(scaled, axis=-1, keepdims=True)
        - normal * jnp.mean(scaled * normal, axis=-1, keepdims=True)
    )


class Net:
    def __init__(self, send, recv, peer):
        self.send, self.recv, self.peer = send, recv, peer
        self.sends = 0
        self.banks = 0
        self.pending = []

    def bank(self, count):
        base = self.banks
        self.banks += count
        return base

    def start(self, src, dst, sem, device, when=None, group=None):
        slot = self.sends
        self.sends += 1

        def make():
            return pltpu.make_async_remote_copy(
                src_ref=src,
                dst_ref=dst,
                send_sem=self.send.at[slot],
                recv_sem=self.recv.at[sem],
                device_id=device,
                device_id_type=MESH,
            )

        if when is None:
            make().start()
        else:
            pl.when(when)(lambda: make().start())
        self.pending.append((make, when, group))

    def wait(self, dst, sem, when=None):
        def make():
            return pltpu.make_async_remote_copy(
                src_ref=dst,
                dst_ref=dst,
                send_sem=self.send.at[0],
                recv_sem=self.recv.at[sem],
                device_id=self.peer,
                device_id_type=MESH,
            )

        if when is None:
            make().wait_recv()
        else:
            pl.when(when)(lambda: make().wait_recv())

    def settle(self, *groups):
        for make, when, group in self.pending:
            if groups and group not in groups:
                continue
            if when is None:
                make().wait_send()
            else:
                pl.when(when)(lambda make=make: make().wait_send())
        self.pending = [p for p in self.pending if groups and p[2] not in groups]


SENDS = 192
RECVS = 224


def layer_kernel(
    x_ref, seg_ref, typ_ref, qw_ref, kw_ref, vw_ref, ow_ref, uw_ref, dw_ref, qb_ref, vb_ref,
    ob_ref, ub_ref, db_ref, ag_ref, as_ref, fg_ref, fs_ref, cot_ref,
    out_ref, ig_ref, qg_ref, kg_ref, vg_ref, og_ref, ug_ref, dg_ref, small_ref,
    wq, wo, own, wf, ubs, segc, wordc, xt, bias, qq, kv, kk, kvt, kkt, probs, ctx, ct,
    a_s, n1_s, r1_s, act, gelu_d, gl, parts, rs_send, rs_recv, dub, dzb,
    st_a, st_b, st_c, st_d, st_e, st_f, dct, dc, dco, go_r, rp, sp, rz,
    dqkv, dx_in, dx_cross, dx_back, gq_r, gp, sv, small_s, small_r, sw, vz,
    send_sems, recv_sems,
):
    d = lax.axis_index("dp")
    t = lax.axis_index("tensor")
    c = d % 2
    x = (d // 2) % 2
    y = d // 4
    pair = t % 2
    j = 2 * pair + c
    block = pair + 2 * c
    home = block == t
    zp = t + 1 - 2 * pair
    zq = (t + 2) % 4
    host = 2 * (d // 2) + t // 2
    chip = d // 2
    sib = d + 1 - 2 * c
    xn = d + 2 - 4 * x
    yn = d + 4 - 8 * y
    rows = x_ref.shape[1]
    quarter = rows // 4
    width = x_ref.shape[2]
    strip = qw_ref.shape[1]
    local = kw_ref.shape[1]
    heads = local // HD
    blocks = rows // BLOCK
    own_rows = pl.ds(pl.multiple_of(t * quarter, 16), quarter)
    net = Net(send_sems, recv_sems, (sib, t))

    def flip_x(device):
        return device + 2 - 4 * ((device // 2) % 2)

    def flip_y(device):
        return device + 4 - 8 * (device // 4)

    dg = flip_y(xn)
    part_m, part_o = parts.at[0:2], parts.at[2:4]
    sums_a, sums_b = parts.reshape(rows, width), gelu_d.reshape(rows, width)
    dqq = [sums_a.at[:, BLOCK * h : BLOCK * (h + 1)] for h in range(heads)]
    dkk = [sums_a.at[:, BLOCK * (heads + h) : BLOCK * (heads + h + 1)] for h in range(heads)]
    dvv = [sums_b.at[:, BLOCK * h : BLOCK * (h + 1)] for h in range(heads)]

    low_z = t < 2
    is_end = jnp.logical_or(t == 0, t == 3)
    is_mid = jnp.logical_not(is_end)
    z_out = jnp.where(low_z, t + 1, t - 1)
    z_back = jnp.where(low_z, 0, 3)

    def place(e):
        return jnp.where(low_z, e, 3 - e)

    def joint(one, other):
        return other if one is None else jnp.logical_and(one, other)

    class LineGather:
        def __init__(self, view, group=None):
            self.view, self.bank, self.group = view, net.bank(4), group

        def copy(self, owner, to, when):
            ref = self.view(owner)
            net.start(ref, ref, self.bank + owner, (d, to), when=when, group=self.group)

        def wait(self, owner, when=None):
            net.wait(self.view(owner), self.bank + owner, when=when)

        def begin(self):
            self.copy(t, z_out, None)
            self.copy(t, z_back, is_mid)

        def step(self, n):
            if n == 1:
                self.wait(place(0), is_mid)
                self.copy(place(0), z_out, is_mid)
                self.wait(place(2), is_mid)
                self.copy(place(2), z_back, is_mid)
            if n == 2:
                self.wait(place(3), is_mid)
                self.copy(place(3), z_back, is_mid)
            self.wait(place(n), is_end)

    class LineReduce:
        def __init__(self, own, came, cross, back):
            self.own, self.came, self.cross, self.back = own, came, cross, back
            self.in_b, self.cross_b, self.back_b = net.bank(4), net.bank(4), net.bank(1)

        def depart(self, e):
            net.start(self.own(e), self.came.at[e - 1], self.in_b + e, (d, z_out), when=is_end)

        def add(self, e, ref):
            @pl.when(is_mid)
            def _():
                ref[...] = (self.own(e)[...].astype(F32) + ref[...].astype(F32)).astype(BF)

        def through(self, e):
            ref = self.came.at[e - 1]
            net.wait(ref, self.in_b + e, when=is_mid)
            self.add(e, ref)
            net.start(ref, self.cross.at[3 - e], self.cross_b + 3 - e, (d, z_out), when=is_mid)

        def pass_back(self):
            net.wait(self.cross.at[0], self.cross_b, when=is_mid)
            self.add(0, self.cross.at[0])
            net.start(self.cross.at[0], self.back, self.back_b, (d, z_back), when=is_mid)

        def total(self):
            net.wait(self.came.at[0], self.in_b + 1, when=is_mid)
            net.wait(self.cross.at[1], self.cross_b + 1, when=is_mid)
            net.wait(self.back, self.back_b, when=is_end)
            others = self.came[0].astype(F32) + self.cross[1].astype(F32)
            mine = self.own(jnp.where(is_mid, 1, 0))[...].astype(F32)
            return mine + jnp.where(is_mid, others, self.back[...].astype(F32))

    barrier = pltpu.get_barrier_semaphore()
    for m in range(1, 8):
        pl.semaphore_signal(barrier, 1, device_id=((d + m) % 8, t), device_id_type=MESH)
    for k in range(1, 4):
        pl.semaphore_signal(barrier, 1, device_id=(d, (t + k) % 4), device_id_type=MESH)
    pl.semaphore_signal(barrier, 1, device_id=(sib, zq), device_id_type=MESH)
    pl.semaphore_wait(barrier, 11)

    for h in range(heads):
        at = slice(HD * h, HD * (h + 1))
        piece = jnp.concatenate(
            [qw_ref[i, :, at] for i in range(4)] + [kw_ref[:, at], vw_ref[:, at]], axis=1
        )
        wq[d, :, 6 * HD * h : 6 * HD * (h + 1)] = piece.astype(BF)

    class PlaneGather:
        def __init__(self, group, *views):
            self.views, self.bank, self.group = views, net.bank(8 * len(views)), group

        def copy(self, view, block, device):
            ref = self.views[view](block)
            net.start(ref, ref, self.bank + 8 * view + block, (device, t), group=self.group)

        def wait(self, view, block):
            net.wait(self.views[view](block), self.bank + 8 * view + block)

        def begin(self):
            for view, device in ((0, yn), (1, xn), (1, yn), (0, xn), (0, sib), (1, sib)):
                self.copy(view, d, device)

        def middle(self):
            self.wait(0, yn)
            self.copy(0, yn, xn)
            self.wait(1, xn)
            self.copy(1, xn, yn)
            self.copy(0, yn, sib)
            self.copy(1, xn, sib)
            for view, block in ((1, yn), (0, xn)):
                self.wait(view, block)
                self.copy(view, block, sib)

        def late(self):
            for view in range(2):
                self.wait(view, dg)
                self.copy(view, dg, sib)

        def end(self):
            for block in (sib, flip_x(sib), flip_y(sib), flip_x(flip_y(sib))):
                for view in range(len(self.views)):
                    self.wait(view, block)

    gather_q = PlaneGather("q", lambda b: wq.at[b, : strip // 2], lambda b: wq.at[b, strip // 2 :])
    gather_q.begin()

    def wide_t(value, high, wide):
        r, w = value.shape
        if w < wide:
            value = jnp.concatenate([value, jnp.zeros((r, wide - w), value.dtype)], axis=1)
        if r < high:
            value = jnp.concatenate([value, jnp.zeros((high - r, wide), value.dtype)], axis=0)
        return value.T

    wo[t, d] = wide_t(ow_ref[...], 256, 128)[:strip, :local].astype(BF)
    own[0] = uw_ref[...].astype(BF)
    own[1] = dw_ref[...].astype(BF)
    ubs[t] = jnp.broadcast_to(ub_ref[...][None], ubs.shape[1:])

    ub_z = net.bank(1)
    wf_a = net.bank(4)

    class ChipGather:
        def __init__(self, i):
            self.i, self.bank = i, net.bank(8)

        def send(self):
            i = self.i
            for plane, when in ((zq, None), (t, host != d)):
                net.start(own.at[i], wf.at[i, d], wf_a + 2 * i + c, (host, plane), when=when)

            @pl.when(host == d)
            def _():
                wf[i, d] = own[i]

        def copy(self, view, of, device):
            ref = wf.at[self.i, 2 * (of // 2) + view]
            net.start(ref, ref, self.bank + 2 * (of // 2) + view, (device, t), group="f")

        def wait(self, view, of):
            net.wait(wf.at[self.i, 2 * (of // 2) + view], self.bank + 2 * (of // 2) + view)

        def begin(self):
            i = self.i
            net.wait(wf.at[i, d], wf_a + 2 * i + c, when=jnp.logical_not(home))
            net.wait(wf.at[i, sib], wf_a + 2 * i + 1 - c)
            for view, device in ((0, yn), (1, xn), (1, yn), (0, xn)):
                self.copy(view, d, device)

        def middle(self):
            self.wait(0, yn)
            self.copy(0, yn, xn)
            self.wait(1, xn)
            self.copy(1, xn, yn)

        def end(self):
            for view, of in ((1, yn), (0, xn), (0, dg), (1, dg)):
                self.wait(view, of)

    up, down = ChipGather(0), ChipGather(1)
    wo_z = net.bank(4)
    for k in (2, 1, 3):
        net.start(wo.at[t, d], wo.at[t, d], wo_z + t, (d, (t + k) % 4), group="o")
    net.start(ubs.at[t], ubs.at[t], ub_z, (d, zq))
    up.send()
    for b in range(blocks):
        at = slice(BLOCK * b, BLOCK * (b + 1))
        segc[at, :] = jnp.broadcast_to(seg_ref[:, at].astype(F32), (BLOCK, BLOCK)).T
        wordc[at, :] = jnp.broadcast_to((typ_ref[:, at] == 0).astype(F32), (BLOCK, BLOCK)).T
    xt[...] = x_ref[0].T
    for h in range(heads):
        at = slice(HD * h, HD * (h + 1))
        bias[:, 6 * HD * h : 6 * HD * (h + 1)] = jnp.concatenate(
            [qb_ref[i : i + 1, at] for i in range(4)] + [jnp.zeros((1, HD), F32), vb_ref[at][None]],
            axis=1,
        )

    gather_q.middle()
    down.send()
    for k in range(1, 4):
        s = (t + k) % 4
        net.wait(wo.at[s, d], wo_z + s)
    gather_o = PlaneGather("o", lambda b: wo.at[0:2, b], lambda b: wo.at[2:4, b])
    gather_o.begin()
    gather_q.late()
    gather_q.end()
    low_half = lax.broadcasted_iota(jnp.int32, (rows, BLOCK), 1) < HD
    is_word = wordc[...] > 0.5
    for h in range(heads):
        base = 6 * HD * h
        at = slice(BLOCK * h, BLOCK * (h + 1))
        made = nn(x_ref[0], wq[:, :, base : base + 6 * HD].reshape(width, 6 * HD))
        made = made + bias[:, base : base + 6 * HD]
        qq[:, at] = jnp.where(is_word, made[:, :BLOCK], made[:, BLOCK : 2 * BLOCK]).astype(BF)
        both = made[:, 2 * BLOCK :]
        keys = jnp.where(low_half, both, pltpu.roll(both, HD, 1))
        keys = jnp.where(jnp.logical_xor(is_word, low_half), 0.0, keys)
        kv[:, at] = both.astype(BF)
        kk[:, at] = keys.astype(BF)
        kvt[h] = both.T[HD:].astype(BF)
        kkt[h] = keys.T.astype(BF)

    gather_o.middle()
    up.begin()
    ct_z = net.bank(4)

    def span(b):
        return BLOCK * max(0, b - 2), BLOCK * min(blocks, b + 3)

    kept = [0]
    for b in range(blocks):
        kept.append(kept[-1] + span(b)[1] - span(b)[0])
    for b in range(blocks):
        lo, hi = span(b)
        at_q = slice(BLOCK * b, BLOCK * (b + 1))
        same = segc[lo:hi, :] == seg_ref[:, at_q].astype(F32)
        found = []
        for h in range(heads):
            at = slice(BLOCK * h, BLOCK * (h + 1))
            scores = nt(kk[lo:hi, at], qq[at_q, at]) * SCALING
            scores = jnp.where(same, scores, NEGATIVE)
            weights = jnp.exp(scores - jnp.max(scores, axis=0, keepdims=True))
            weights = weights * (1.0 / jnp.sum(weights, axis=0, keepdims=True))
            probs[h, kept[b] : kept[b + 1]] = weights
            found.append(nn(kvt[h, :, lo:hi], weights.astype(BF)))
        found.append(jnp.zeros((HD, BLOCK), F32))
        ctx[at_q, :] = jnp.concatenate(found, axis=0).T[:, :local].astype(BF)
        if b == 3:
            down.begin()
        if b > 0:
            s = b - 1
            src = ctx.at[quarter * s : quarter * (s + 1)]
            net.start(src, ct.at[t], ct_z + t, (d, s), when=t != s)
    ct[t] = ctx[own_rows, :]

    up.middle()
    gather_o.late()
    gather_o.end()
    for k in range(1, 4):
        s = (t + k) % 4
        net.wait(ct.at[s], ct_z + s)
    attended = nt(ct[0], wo[0].reshape(width, local))
    for s in range(1, 4):
        attended = attended + nt(ct[s], wo[s].reshape(width, local))
    normal, inverse = norm_rows(x_ref[0, own_rows, :].astype(F32) + attended + ob_ref[...][None])
    n1_s[...] = normal
    r1_s[...] = jnp.broadcast_to(inverse, r1_s.shape)
    normed = normal * ag_ref[...][None] + as_ref[...][None]
    a_s[...] = normed
    act[j] = normed.astype(BF)

    def rows_of(ref, first, count):
        return lambda owner: ref.at[
            0, pl.ds(pl.multiple_of(owner * quarter + first, 16), count)
        ]

    part = quarter // 2
    chunk = [slice(part * q, part * (q + 1)) for q in range(2)]

    class RowGather:
        def __init__(self, ref):
            self.ref, self.bank = ref, net.bank(8)

        def copy(self, q, rank, device):
            ref = self.ref.at[rank, chunk[q]]
            net.start(ref, ref, self.bank + 4 * q + rank, device)

        def wait(self, q, rank):
            net.wait(self.ref.at[rank, chunk[q]], self.bank + 4 * q + rank)

        def begin(self, q):
            self.copy(q, j, (d, zp))
            self.copy(q, j, (sib, t))

        def near(self, q):
            self.wait(q, 2 * pair + 1 - c)

        def middle(self, q):
            self.wait(q, 2 - 2 * pair + c)
            self.copy(q, 2 - 2 * pair + c, (sib, t))

        def far(self, q):
            self.wait(q, 3 - 2 * pair - c)

    class RowSum:
        def __init__(self, index):
            self.index, self.bank = index, net.bank(6)

        def hand(self, q, slot, partial_rows):
            where = 3 * self.index + slot
            rs_send[where, chunk[q]] = partial_rows.astype(BF)
            net.start(
                rs_send.at[where, chunk[q]], rs_recv.at[where, chunk[q]], self.bank + 3 * q + slot,
                (d, zp) if slot == 2 else (sib, t),
            )

        def take(self, q, slot):
            where = 3 * self.index + slot
            net.wait(rs_recv.at[where, chunk[q]], self.bank + 3 * q + slot)
            return rs_recv[where, chunk[q]].astype(F32)

        def near(self, q):
            self.hand(q, 0, part_m[1 - c, chunk[q]])

        def away(self, q):
            self.hand(q, 1, part_o[1 - c, chunk[q]])

        def across(self, q):
            self.hand(q, 2, part_o[c, chunk[q]] + self.take(q, 1))

        def total(self, q):
            return part_m[c, chunk[q]] + self.take(q, 0) + self.take(q, 2)

    rows_a = RowGather(act)
    rows_a.begin(0)
    rows_a.begin(1)
    down.middle()
    rows_a.middle(0)
    rows_a.middle(1)
    rows_a.near(0)
    rows_a.near(1)
    net.wait(ubs.at[zq], ub_z)
    up.end()
    near = pl.ds(2 * pair, 2)
    away = pl.ds(2 - 2 * pair, 2)

    def feed(half, q):
        hidden = nn(act[half, chunk[q]].reshape(2 * part, width), wf[0].reshape(width, width))
        hidden = hidden + ubs[block][:1]
        bell = 0.5 * (1.0 + lax.erf(hidden * 0.7071067811865476))
        slope = bell + hidden * (0.3989422804014327 * jnp.exp(-0.5 * hidden * hidden))
        gelu_d[half, chunk[q]] = slope.reshape(2, part, width)
        gl[half, chunk[q]] = (hidden * bell).astype(BF).reshape(2, part, width)

    def feed_out(half, q, partial_ref):
        made = nt(gl[half, chunk[q]].reshape(2 * part, width), wf[1].reshape(width, width))
        partial_ref[:, chunk[q]] = made.reshape(2, part, width)

    feed(near, 0)
    feed(near, 1)
    for q in range(2):
        rows_a.far(q)
        feed(away, q)
    down.end()
    sum_f = RowSum(0)
    feed_out(away, 0, part_o)
    sum_f.away(0)
    feed_out(near, 0, part_m)
    sum_f.near(0)
    feed_out(away, 1, part_o)
    sum_f.away(1)
    sum_f.across(0)
    feed_out(near, 1, part_m)
    sum_f.near(1)
    sum_f.across(1)
    rows_u = RowGather(dub)
    gain_sum, shift_sum, bias_sum = 0.0, 0.0, 0.0
    for q in range(2):
        ffn_out = sum_f.total(q) + db_ref[...][None]
        normal, inverse = norm_rows(a_s[chunk[q]] + ffn_out)
        rows_q = pl.ds(pl.multiple_of(t * quarter + part * q, 16), part)
        out_ref[0, rows_q, :] = (normal * fg_ref[...][None] + fs_ref[...][None]).astype(BF)
        upstream = cot_ref[0, rows_q, :].astype(F32)
        du = norm_rows_back(upstream, normal, inverse, fg_ref[...][None])
        dub[j, chunk[q]] = du.astype(BF)
        rows_u.begin(q)
        a_s[chunk[q]] = du
        gain_sum = gain_sum + jnp.sum(upstream * normal, axis=0, keepdims=True)
        shift_sum = shift_sum + jnp.sum(upstream, axis=0, keepdims=True)
        bias_sum = bias_sum + jnp.sum(du, axis=0, keepdims=True)
    line_out = [LineGather(rows_of(out_ref, part * q, part)) for q in range(2)]
    line_out[0].begin()
    sv[...] = jnp.zeros_like(sv)
    sv[0:1] = gain_sum
    sv[1:2] = shift_sum
    sv[2:3] = bias_sum

    def feed_back(half, q, partial_ref):
        made = nn(dub[half, chunk[q]].reshape(2 * part, width), wf[1].reshape(width, width))
        made = made * gelu_d[half, chunk[q]].reshape(2 * part, width)
        low = made.astype(BF)
        dzb[half, chunk[q]] = low.reshape(2, part, width)
        partial_ref[:, chunk[q]] = nt(low, wf[0].reshape(width, width)).reshape(2, part, width)
        return jnp.sum(made, axis=0, keepdims=True)

    sum_b = RowSum(1)
    up_sum = 0.0
    for q in range(2):
        rows_u.near(q)
        up_sum = up_sum + feed_back(near, q, part_m)
        sum_b.near(q)
    rows_u.middle(0)
    rows_u.far(0)
    up_sum = up_sum + feed_back(away, 0, part_o)
    sum_b.away(0)
    rows_u.middle(1)
    sum_b.across(0)
    rows_u.far(1)
    up_sum = up_sum + feed_back(away, 1, part_o)
    sum_b.away(1)
    rank_rows = lax.broadcasted_iota(jnp.int32, (4, width), 0)
    sv[8:12] = jnp.where(rank_rows == block, up_sum, 0.0)
    half = width // 2

    class StripSum:
        def __init__(self, i):
            self.i, self.bank = i, net.bank(6)
            self.by_chip = wf.at[i].reshape(2, 2, 2, strip, width)

        def begin(self, left, right):
            made = tn(left[...].reshape(4 * quarter, width), right[...].reshape(4 * quarter, width))
            wf[self.i] = made.astype(BF).reshape(8, strip, width)
            net.start(
                self.by_chip.at[:, 1 - x, :, :, :half], st_a.at[self.i], self.bank, (xn, t)
            )
            net.start(
                self.by_chip.at[1 - y, :, :, :, half:], st_b.at[self.i], self.bank + 1, (yn, t)
            )

        def turn(self):
            i = self.i
            net.wait(st_a.at[i], self.bank)
            st_a[i] = (st_a[i].astype(F32) + self.by_chip[:, x, :, :, :half].astype(F32)).astype(BF)
            net.start(st_a.at[i, 1 - y], st_c.at[i], self.bank + 2, (yn, t))
            net.wait(st_b.at[i], self.bank + 1)
            st_b[i] = (st_b[i].astype(F32) + self.by_chip[y, :, :, :, half:].astype(F32)).astype(BF)
            net.start(st_b.at[i, 1 - x], st_d.at[i], self.bank + 3, (xn, t))

        def deliver(self):
            i = self.i
            net.wait(st_c.at[i], self.bank + 2)
            st_e[i, :, :, :half] = (st_c[i].astype(F32) + st_a[i, y].astype(F32)).astype(BF)
            net.wait(st_d.at[i], self.bank + 3)
            st_e[i, :, :, half:] = (st_d[i].astype(F32) + st_b[i, x].astype(F32)).astype(BF)
            slot = jnp.where(home, 0, 1)
            for core in range(2):
                net.start(
                    st_e.at[i, core], st_f.at[i, slot], self.bank + 4 + slot,
                    (2 * (d // 2) + core, block),
                    when=jnp.logical_or(c != core, jnp.logical_not(home)),
                )

            @pl.when(home)
            def _():
                st_f[i, 0] = st_e[i, c]

        def total(self):
            i = self.i
            net.wait(st_f.at[i, 0], self.bank + 4, when=host != d)
            net.wait(st_f.at[i, 1], self.bank + 5)
            return st_f[i, 0].astype(F32) + st_f[i, 1].astype(F32)

    class SmallSum:
        def __init__(self, index):
            self.index, self.bank = index, net.bank(3)

        def start(self, step):
            ref = small_s.at[self.index, step]
            net.start(ref, small_r.at[self.index, step], self.bank + step, ((sib, xn, yn)[step], t))

        def begin(self, values):
            small_s[self.index, 0] = values
            self.start(0)

        def step(self, n):
            net.wait(small_r.at[self.index, n - 1], self.bank + n - 1)
            small_s[self.index, n] = small_s[self.index, n - 1] + small_r[self.index, n - 1]
            if n < 3:
                self.start(n)

    net.settle("f")
    down_sum, up_sums = StripSum(1), StripSum(0)
    down_sum.begin(dub, gl)
    sum_b.across(1)
    line_out[1].begin()
    up_sums.begin(act, dzb)
    dc_z = net.bank(8)
    gain_sum, shift_sum, bias_sum, dhb = 0.0, 0.0, 0.0, []
    for q in range(2):
        da = a_s[chunk[q]] + sum_b.total(q)
        normal = n1_s[chunk[q]]
        dh = norm_rows_back(da, normal, r1_s[chunk[q], :1], ag_ref[...][None])
        a_s[chunk[q]] = dh
        dhb.append(dh.astype(BF))
        for k in (2, 1, 3):
            s = (t + k) % 4
            dct[s, chunk[q]] = nn(dhb[q], wo[s].reshape(width, local)).astype(BF)
            net.start(dct.at[s, chunk[q]], dc.at[t, chunk[q]], dc_z + 4 * q + t, (d, s))
        dc[t, chunk[q]] = nn(dhb[q], wo[t].reshape(width, local)).astype(BF)
        gain_sum = gain_sum + jnp.sum(da * normal, axis=0, keepdims=True)
        shift_sum = shift_sum + jnp.sum(da, axis=0, keepdims=True)
        bias_sum = bias_sum + jnp.sum(dh, axis=0, keepdims=True)
    dhb = jnp.concatenate(dhb, axis=0)
    line_out[0].step(1)
    line_out[1].step(1)
    sv[3:4] = gain_sum
    sv[4:5] = shift_sum
    sv[5:6] = bias_sum
    small_a = SmallSum(0)
    small_a.begin(sv[...])
    net.settle("o")
    for s in range(4):
        wo[s] = tn(dhb, ct[s]).astype(BF).reshape(8, strip, local)
    by_core = wo.reshape(4, 4, 2, strip, local)
    go_b = net.bank(1)
    net.start(by_core.at[:, :, 1 - c], go_r, go_b, (sib, t))

    down_sum.turn()
    net.wait(go_r, go_b)
    go_r[...] = (by_core[:, :, c].astype(F32) + go_r[...].astype(F32)).astype(BF)
    rp_b = net.bank(4)
    for r in (xn, yn, dg):
        net.start(go_r.at[:, r // 2], rp.at[chip], rp_b + chip, (r, t))
    rp[chip] = go_r[:, chip]
    for k in range(1, 4):
        s = (t + k) % 4
        for q in range(2):
            net.wait(dc.at[s, chunk[q]], dc_z + 4 * q + s)
    dctx = dc[...].reshape(rows, local)
    for h in range(heads):
        dco[:, BLOCK * h : BLOCK * (h + 1)] = jnp.concatenate(
            [jnp.zeros((rows, HD), BF), dctx[:, HD * h : HD * (h + 1)]], axis=1
        )
    for h in range(heads):
        dkk[h][...] = jnp.zeros((rows, BLOCK), F32)
        dvv[h][...] = jnp.zeros((rows, BLOCK), F32)
    for b in range(blocks):
        lo, hi = span(b)
        at_q = slice(BLOCK * b, BLOCK * (b + 1))
        for h in range(heads):
            at = slice(BLOCK * h, BLOCK * (h + 1))
            weights = probs[h, kept[b] : kept[b + 1]]
            dp = nt(kv[lo:hi, at], dco[at_q, at])
            ds = weights * (dp - jnp.sum(weights * dp, axis=0, keepdims=True))
            dsb = ds.astype(BF)
            dkk[h][lo:hi] += nn(dsb, qq[at_q, at])
            dvv[h][lo:hi] += nn(weights.astype(BF), dco[at_q, at])
            dqq[h][at_q] = nn(kkt[h, :, lo:hi], dsb).T * SCALING

    line_out[0].step(2)
    line_out[1].step(2)
    up_sums.turn()
    for h in range(heads):
        base = 6 * HD * h
        first = jnp.where(is_word, dqq[h][...], 0.0)
        second = jnp.where(is_word, 0.0, dqq[h][...])
        keys = dkk[h][...]
        keys = jnp.where(is_word, keys, pltpu.roll(keys, HD, 1)) * SCALING
        third = jnp.where(low_half, keys, dvv[h][...])
        for i, piece in enumerate((first, second, third)):
            at = slice(base + BLOCK * i, base + BLOCK * (i + 1))
            dqkv[:, at] = piece.astype(BF)
            row, col = divmod(base + BLOCK * i, width)
            sv[row : row + 1, col : col + BLOCK] = jnp.sum(piece, axis=0, keepdims=True)

    made = nt(dqkv[...], wq[...].reshape(width, 6 * local))
    dzb[...] = made.astype(BF).reshape(4, quarter, width)
    line_dx, line_in = [], []
    for q in range(2):
        cut = pl.ds(part * q, part)
        line_dx.append(
            LineReduce(
                lambda e, cut=cut: dzb.at[place(e), cut],
                dx_in.at[q], dx_cross.at[q], dx_back.at[q],
            )
        )
        line_in.append(LineGather(rows_of(ig_ref, part * q, part)))

    def arrive(q):
        total = line_dx[q].total() + a_s[part * q : part * (q + 1)]
        ig_ref[0, pl.ds(pl.multiple_of(t * quarter + part * q, 16), part)] = total.astype(BF)
        line_in[q].begin()

    for q, e in ((0, 3), (0, 2), (1, 3), (1, 2), (0, 1), (1, 1)):
        line_dx[q].depart(e)
    down_sum.deliver()
    small_a.step(1)
    small_b = SmallSum(1)
    small_b.begin(sv[...])

    net.settle("q")
    wq[...] = nn(xt[...], dqkv[...]).astype(BF).reshape(8, strip, 6 * local)
    q_by_core = wq.reshape(4, 2, strip, 6 * local)
    gq_b = net.bank(1)
    net.start(q_by_core.at[:, 1 - c], gq_r, gq_b, (sib, t))
    line_dx[0].through(3)
    line_dx[0].through(2)
    small_a.step(2)
    line_dx[1].through(3)
    line_dx[1].through(2)
    line_dx[0].pass_back()
    net.wait(gq_r, gq_b)
    gq_r[...] = (q_by_core[:, c].astype(F32) + gq_r[...].astype(F32)).astype(BF)
    gp_b = net.bank(4)
    for r in (xn, yn, dg):
        net.start(gq_r.at[r // 2], gp.at[chip], gp_b + chip, (r, t))
    gp[chip] = gq_r[chip]

    line_dx[1].pass_back()
    arrive(0)
    arrive(1)
    up_sums.deliver()
    small_a.step(3)
    vz_b = net.bank(5)
    mine8 = pl.ds(pl.multiple_of(8 * c, 8), 8)
    sent8 = small_s.at[0, 3, mine8]
    for k in range(1, 4):
        net.start(sent8, vz.at[t], vz_b + t, (d, (t + k) % 4))
    vz[t] = sent8[...]
    small_b.step(1)
    line_in[0].step(1)
    line_in[1].step(1)
    for r in (xn, yn, dg):
        net.wait(rp.at[r // 2], rp_b + r // 2)
    total = rp[0].astype(F32)
    for k in range(1, 4):
        total = total + rp[k].astype(F32)
    sp[...] = total.astype(BF)
    rz_b = net.bank(4)
    for k in range(1, 4):
        s = (t + k) % 4
        net.start(sp.at[s], rz.at[t], rz_b + t, (d, s))
    rz[t] = sp[t]

    small_b.step(2)
    for k in range(1, 4):
        net.wait(vz.at[(t + k) % 4], vz_b + (t + k) % 4)
    total = vz[0]
    for k in range(1, 4):
        total = total + vz[k]
    sw[mine8] = total
    net.start(sw.at[mine8], sw.at[mine8], vz_b + 4, (sib, t))
    line_in[0].step(2)
    line_in[1].step(2)
    small_b.step(3)
    net.wait(sw.at[pl.ds(pl.multiple_of(8 - 8 * c, 8), 8)], vz_b + 4)
    small_ref[0:6] = sw[0:6]
    small_ref[6:7] = jnp.sum(jnp.where(rank_rows == t, sw[8:12], 0.0), axis=0, keepdims=True)
    small_ref[8:10] = small_s[1, 3, 0:2]
    dg_ref[...] = down_sum.total()
    ug_ref[...] = up_sums.total()
    for k in range(1, 4):
        s = (t + k) % 4
        net.wait(rz.at[s], rz_b + s)
    total = rz[0].astype(F32)
    for s in range(1, 4):
        total = total + rz[s].astype(F32)
    og_ref[...] = wide_t(total, BLOCK, 256)[:local, :strip]

    for r in (xn, yn, dg):
        net.wait(gp.at[r // 2], gp_b + r // 2)
    total = gp[0].astype(F32)
    for k in range(1, 4):
        total = total + gp[k].astype(F32)
    for h in range(heads):
        base = 6 * HD * h
        at = slice(HD * h, HD * (h + 1))
        for i in range(4):
            qg_ref[i, :, at] = total[:, base + HD * i : base + HD * (i + 1)]
        kg_ref[:, at] = total[:, base + 4 * HD : base + 5 * HD]
        vg_ref[:, at] = total[:, base + 5 * HD : base + 6 * HD]

    line_out[0].step(3)
    line_out[1].step(3)
    for q in range(2):
        line_in[q].step(3)
    net.settle()
    assert net.sends <= SENDS and net.banks <= RECVS, (net.sends, net.banks)


def end_kernel(*refs):
    sources, small = refs[:8], refs[8]
    targets, (qbg, vbg), vectors = refs[9:17], refs[17:19], refs[19:26]
    for source, target in zip(sources, targets):
        target[...] = source[...]
    fgg, fsg, dbg, agg, asg, obg, ubg = (small[i] for i in range(7))
    for ref, value in zip(vectors, (obg, ubg, dbg, agg, asg, fgg, fsg)):
        ref[...] = value
    width = small.shape[1]
    values = []
    for h in range(vbg.shape[0] // HD):
        row, col = divmod(6 * HD * h, width)
        piece = small[8 + row : 9 + row, col : col + 6 * HD]
        for i in range(4):
            qbg[i : i + 1, HD * h : HD * (h + 1)] = piece[:, HD * i : HD * (i + 1)]
        values.append(piece[:, 5 * HD :])
    vbg[...] = jnp.concatenate(values, axis=1)[0]


def fused(
    layer_input, segment_ids, token_types, query_weight, key_weight, value_weight, out_weight,
    up_weight, down_weight, query_bias, value_bias, out_bias, up_bias, down_bias, attn_gain,
    attn_shift, ffn_gain, ffn_shift, cotangent,
):
    rows, width = layer_input.shape[1:]
    strip, local = key_weight.shape
    quarter, heads, blocks = rows // 4, local // HD, rows // BLOCK
    kept = sum(BLOCK * (min(blocks, b + 3) - max(0, b - 2)) for b in range(blocks))
    args = [
        layer_input, segment_ids, token_types, query_weight, key_weight, value_weight, out_weight,
        up_weight, down_weight.T, query_bias, value_bias, out_bias, up_bias, down_bias, attn_gain,
        attn_shift, ffn_gain, ffn_shift, cotangent,
    ]

    def like(v, dtype=F32):
        return jax.ShapeDtypeStruct(v.shape, dtype)

    outs = [
        like(layer_input, BF), like(layer_input, BF), like(query_weight), like(key_weight),
        like(value_weight), like(out_weight), like(up_weight), jax.ShapeDtypeStruct((strip, width), F32),
        jax.ShapeDtypeStruct((16, width), F32),
    ]
    v = pltpu.VMEM
    scratch = [
        v((8, strip, 6 * local), BF), v((4, 8, strip, local), BF), v((2, strip, width), BF),
        v((2, 8, strip, width), BF), v((4, 8, width), F32), v((rows, BLOCK), F32),
        v((rows, BLOCK), F32), v((width, rows), BF), v((1, 6 * local), F32),
        v((rows, heads * BLOCK), BF), v((rows, heads * BLOCK), BF), v((rows, heads * BLOCK), BF),
        v((heads, HD, rows), BF), v((heads, BLOCK, rows), BF),
        v((heads, kept, BLOCK), F32), v((rows, local), BF), v((4, quarter, local), BF),
        v((quarter, width), F32), v((quarter, width), F32), v((quarter, BLOCK), F32),
        v((4, quarter, width), BF), v((4, quarter, width), F32), v((4, quarter, width), BF),
        v((4, quarter, width), F32),
        v((6, quarter, width), BF), v((6, quarter, width), BF),
        v((4, quarter, width), BF), v((4, quarter, width), BF),
        v((2, 2, 2, strip, width // 2), BF), v((2, 2, 2, strip, width // 2), BF),
        v((2, 2, strip, width // 2), BF), v((2, 2, strip, width // 2), BF),
        v((2, 2, strip, width), BF), v((2, 2, strip, width), BF),
        v((4, quarter, local), BF), v((4, quarter, local), BF),
        v((rows, heads * BLOCK), BF),
        v((4, 4, strip, local), BF), v((4, 4, strip, local), BF), v((4, strip, local), BF),
        v((4, strip, local), BF),
        v((rows, 6 * local), BF),
        v((2, 3, quarter // 2, width), BF), v((2, 2, quarter // 2, width), BF),
        v((2, quarter // 2, width), BF),
        v((4, strip, 6 * local), BF), v((4, strip, 6 * local), BF),
        v((16, width), F32), v((2, 4, 16, width), F32), v((2, 3, 16, width), F32),
        v((16, width), F32), v((4, 8, width), F32),
        pltpu.SemaphoreType.DMA((SENDS,)), pltpu.SemaphoreType.DMA((RECVS,)),
    ]
    spec = pl.BlockSpec(memory_space=pltpu.VMEM)
    made = pl.pallas_call(
        layer_kernel,
        out_shape=outs,
        in_specs=[spec] * len(args),
        out_specs=[spec] * len(outs),
        scratch_shapes=scratch,
        compiler_params=pltpu.CompilerParams(
            collective_id=0, has_side_effects=True, vmem_limit_bytes=58 << 20
        ),
        name="layer",
    )(*args)
    *large, small = made
    vector = jax.ShapeDtypeStruct((width,), F32)
    ended = pl.pallas_call(
        end_kernel,
        out_shape=[like(v, v.dtype) for v in large]
        + [like(query_bias), jax.ShapeDtypeStruct((local,), F32)]
        + [vector] * 7,
        in_specs=[spec] * len(made),
        out_specs=[spec] * 17,
        name="finish",
    )(*large, small)
    return (*ended[:7], ended[7].T, *ended[8:])


def solution(mesh):
    in_specs = (
        P("dp", None, None),
        P("dp", None),
        P("dp", None),
        P(None, "dp", "tensor"),
        P("dp", "tensor"),
        P("dp", "tensor"),
        P("tensor", "dp"),
        P("dp", "tensor"),
        P("tensor", "dp"),
        P(None, "tensor"),
        P("tensor"),
        P(),
        P("tensor"),
        P(),
        P(),
        P(),
        P(),
        P(),
        P("dp", None, None),
    )
    out_specs = (
        P("dp", None, None),
        P("dp", None, None),
        P(None, "dp", "tensor"),
        P("dp", "tensor"),
        P("dp", "tensor"),
        P("tensor", "dp"),
        P("dp", "tensor"),
        P("tensor", "dp"),
        P(None, "tensor"),
        P("tensor"),
        P(),
        P("tensor"),
        P(),
        P(),
        P(),
        P(),
        P(),
    )
    step = fused if fits(mesh) else shards
    return jax.shard_map(step, mesh=mesh, in_specs=in_specs, out_specs=out_specs, check_vma=False)
```

```python
from functools import partial

import jax
import jax.numpy as jnp
from jax import lax
from jax.experimental import pallas as pl
from jax.experimental.pallas import tpu as pltpu
from jax.sharding import PartitionSpec as P

HD = 64


EPSILON = 1e-05
SCALING = 0.125
NEGATIVE = -1000000000.0


def layer_norm_keep(values, norm_gain, norm_shift):
    centre = values - jnp.mean(values, axis=-1, keepdims=True)
    inverse = lax.rsqrt(jnp.mean(centre * centre, axis=-1, keepdims=True) + EPSILON)
    normal = centre * inverse
    return (normal * norm_gain + norm_shift, normal, inverse)


def layer_norm_back(upstream, normal, inverse, norm_gain):
    scaled = upstream * norm_gain
    gain_grad = jnp.sum(upstream * normal, axis=0)
    shift_grad = jnp.sum(upstream, axis=0)
    inner_term = (
        scaled
        - jnp.mean(scaled, axis=-1, keepdims=True)
        - normal * jnp.mean(scaled * normal, axis=-1, keepdims=True)
    )
    return (inverse * inner_term, gain_grad, shift_grad)


def heads_of(matrix):
    return matrix.reshape(matrix.shape[0], -1, HD)


def pick_queries(query_rows, type_row):
    word_tok = (type_row == 0)[:, None]
    return (
        jnp.where(word_tok, query_rows[0], query_rows[2]),
        jnp.where(word_tok, query_rows[1], query_rows[3]),
    )


def score_block(word_heads, entity_heads, key_heads, segment_row, type_row):
    to_words = jnp.einsum("qhd,khd->hqk", word_heads, key_heads, preferred_element_type=jnp.float32)
    to_entities = jnp.einsum(
        "qhd,khd->hqk", entity_heads, key_heads, preferred_element_type=jnp.float32
    )
    scores = jnp.where((type_row == 0)[None, None, :], to_words, to_entities) * SCALING
    allowed = (segment_row[:, None] == segment_row[None, :])[None]
    return jnp.where(allowed, scores, NEGATIVE)


def attend_forward(packed):
    query_rows, key_seq, value_seq, segment_row, type_row = packed
    word_query, entity_query = pick_queries(query_rows, type_row)
    scores = score_block(
        heads_of(word_query), heads_of(entity_query), heads_of(key_seq), segment_row, type_row
    )
    row_top = jnp.max(scores, axis=-1, keepdims=True)
    weights = jnp.exp(scores - row_top)
    totals = jnp.sum(weights, axis=-1, keepdims=True)
    attn_probs = (weights / totals).astype(jnp.bfloat16)
    context = jnp.einsum(
        "hqk,khd->qhd", attn_probs, heads_of(value_seq), preferred_element_type=jnp.float32
    )
    log_total = (row_top + jnp.log(totals))[..., 0]
    return (context.reshape(context.shape[0], -1).astype(jnp.bfloat16), log_total)


def attend_backward(packed):
    query_rows, key_seq, value_seq, segment_row, type_row, log_total, context_grad = packed
    word_query, entity_query = pick_queries(query_rows, type_row)
    word_heads = heads_of(word_query)
    entity_heads = heads_of(entity_query)
    key_heads = heads_of(key_seq)
    value_heads = heads_of(value_seq)
    grad_heads = heads_of(context_grad)
    scores = score_block(word_heads, entity_heads, key_heads, segment_row, type_row)
    attn_probs = jnp.exp(scores - log_total[..., None])
    prob_grad = jnp.einsum(
        "qhd,khd->hqk", grad_heads, value_heads, preferred_element_type=jnp.float32
    )
    score_grad = attn_probs * (prob_grad - jnp.sum(attn_probs * prob_grad, axis=-1, keepdims=True))
    score_low = score_grad.astype(jnp.bfloat16)
    word_key = (type_row == 0)[None, None, :]
    zeroes = jnp.zeros_like(score_low)
    word_part = jnp.where(word_key, score_low, zeroes)
    entity_part = jnp.where(word_key, zeroes, score_low)
    word_qgrad = (
        jnp.einsum("hqk,khd->qhd", word_part, key_heads, preferred_element_type=jnp.float32)
        * SCALING
    )
    entity_qgrad = (
        jnp.einsum("hqk,khd->qhd", entity_part, key_heads, preferred_element_type=jnp.float32)
        * SCALING
    )
    key_delta = (
        jnp.einsum("hqk,qhd->khd", word_part, word_heads, preferred_element_type=jnp.float32)
        + jnp.einsum("hqk,qhd->khd", entity_part, entity_heads, preferred_element_type=jnp.float32)
    ) * SCALING
    value_delta = jnp.einsum(
        "hqk,qhd->khd",
        attn_probs.astype(jnp.bfloat16),
        grad_heads,
        preferred_element_type=jnp.float32,
    )
    row_count = word_qgrad.shape[0]
    return (
        word_qgrad.reshape(row_count, -1),
        entity_qgrad.reshape(row_count, -1),
        key_delta.reshape(row_count, -1),
        value_delta.reshape(row_count, -1),
    )


def row_share(partial_rows):
    return lax.psum_scatter(partial_rows, "tensor", scatter_dimension=0, tiled=True)


def row_whole(rounded_rows):
    return lax.all_gather(rounded_rows, "tensor", axis=0, tiled=True)


def shards(
    layer_input,
    segment_ids,
    token_types,
    query_weight,
    key_weight,
    value_weight,
    out_weight,
    up_weight,
    down_weight,
    query_bias,
    value_bias,
    out_bias,
    up_bias,
    down_bias,
    attn_gain,
    attn_shift,
    ffn_gain,
    ffn_shift,
    cotangent,
):
    seq_count, seq_length, model_width = layer_input.shape
    tokens = layer_input.reshape(-1, model_width)
    row_count = tokens.shape[0]
    share = row_count // lax.axis_size("tensor")
    first_row = lax.axis_index("tensor") * share

    def own_rows(matrix):
        return lax.dynamic_slice_in_dim(matrix, first_row, share, 0)

    def combine_rows(partial_rows):
        return row_share(partial_rows)

    def whole_rows(rounded_rows):
        return row_whole(rounded_rows)

    query_complete, key_full, value_full, out_full = (
        lax.all_gather(query_weight.astype(jnp.bfloat16), "dp", axis=1, tiled=True),
        lax.all_gather(key_weight.astype(jnp.bfloat16), "dp", axis=0, tiled=True),
        lax.all_gather(value_weight.astype(jnp.bfloat16), "dp", axis=0, tiled=True),
        lax.all_gather(out_weight.astype(jnp.bfloat16), "dp", axis=1, tiled=True),
    )
    local_width = key_full.shape[1]
    query_rows = jnp.einsum(
        "gow,qwk->gqok", layer_input, query_complete, preferred_element_type=jnp.float32
    )
    query_rows = (query_rows + query_bias[None, :, None, :]).astype(jnp.bfloat16)
    keys_all = jnp.dot(layer_input, key_full, preferred_element_type=jnp.float32).astype(
        jnp.bfloat16
    )
    values_all = (
        jnp.dot(layer_input, value_full, preferred_element_type=jnp.float32) + value_bias
    ).astype(jnp.bfloat16)
    context, log_total = lax.map(
        attend_forward, (query_rows, keys_all, values_all, segment_ids, token_types)
    )
    context_rows = context.reshape(-1, local_width)
    attended = combine_rows(jnp.dot(context_rows, out_full, preferred_element_type=jnp.float32))
    residual = own_rows(tokens).astype(jnp.float32) + attended + out_bias
    normed, normal_one, inverse_one = layer_norm_keep(residual, attn_gain, attn_shift)
    normed_low = whole_rows(normed.astype(jnp.bfloat16))
    up_full, down_full = (
        lax.all_gather(up_weight.astype(jnp.bfloat16), "dp", axis=0, tiled=True),
        lax.all_gather(down_weight.astype(jnp.bfloat16), "dp", axis=1, tiled=True),
    )
    pre_act = jnp.dot(normed_low, up_full, preferred_element_type=jnp.float32) + up_bias
    activated, gelu_pull = jax.vjp(partial(jax.nn.gelu, approximate=False), pre_act)
    act_low = activated.astype(jnp.bfloat16)
    ffn_out = (
        combine_rows(jnp.dot(act_low, down_full, preferred_element_type=jnp.float32)) + down_bias
    )
    normed_out, normal_two, inverse_two = layer_norm_keep(normed + ffn_out, ffn_gain, ffn_shift)
    output = whole_rows(normed_out.astype(jnp.bfloat16)).reshape(layer_input.shape)
    upstream = own_rows(cotangent.reshape(-1, model_width)).astype(jnp.float32)
    sum_grad, ffngain_grad, ffnshift_grad = layer_norm_back(
        upstream, normal_two, inverse_two, ffn_gain
    )
    downbias_grad = jnp.sum(sum_grad, axis=0)
    sum_low = whole_rows(sum_grad.astype(jnp.bfloat16))
    up_back, down_back = (
        lax.all_gather(up_weight.astype(jnp.bfloat16), "dp", axis=0, tiled=True),
        lax.all_gather(down_weight.astype(jnp.bfloat16), "dp", axis=1, tiled=True),
    )
    down_local = jnp.dot(act_low.T, sum_low, preferred_element_type=jnp.float32)
    act_grad = jnp.dot(sum_low, down_back.T, preferred_element_type=jnp.float32)
    (pre_grad,) = gelu_pull(act_grad)
    upbias_grad = jnp.sum(pre_grad, axis=0)
    pre_low = pre_grad.astype(jnp.bfloat16)
    up_local = jnp.dot(normed_low.T, pre_low, preferred_element_type=jnp.float32)
    upproj_grad, downproj_grad = (
        lax.psum_scatter(up_local, "dp", scatter_dimension=0, tiled=True),
        lax.psum_scatter(down_local, "dp", scatter_dimension=1, tiled=True),
    )
    normed_grad = (
        combine_rows(jnp.dot(pre_low, up_back.T, preferred_element_type=jnp.float32)) + sum_grad
    )
    resid_grad, attngain_grad, attnshift_grad = layer_norm_back(
        normed_grad, normal_one, inverse_one, attn_gain
    )
    outbias_grad = jnp.sum(resid_grad, axis=0)
    resid_low = whole_rows(resid_grad.astype(jnp.bfloat16))
    query_pullback, key_pullback, value_pullback, out_back = (
        lax.all_gather(query_weight.astype(jnp.bfloat16), "dp", axis=1, tiled=True),
        lax.all_gather(key_weight.astype(jnp.bfloat16), "dp", axis=0, tiled=True),
        lax.all_gather(value_weight.astype(jnp.bfloat16), "dp", axis=0, tiled=True),
        lax.all_gather(out_weight.astype(jnp.bfloat16), "dp", axis=1, tiled=True),
    )
    outproj_local = jnp.dot(context_rows.T, resid_low, preferred_element_type=jnp.float32)
    context_grad = jnp.dot(resid_low, out_back.T, preferred_element_type=jnp.float32).astype(
        jnp.bfloat16
    )
    context_grad = context_grad.reshape(seq_count, seq_length, local_width)
    word_qgrad, entity_qgrad, key_delta, value_delta = lax.map(
        attend_backward,
        (query_rows, keys_all, values_all, segment_ids, token_types, log_total, context_grad),
    )
    is_word = (token_types == 0)[..., None]
    zero_rows = jnp.zeros_like(word_qgrad)
    query_delta = jnp.stack(
        [
            jnp.where(is_word, word_qgrad, zero_rows),
            jnp.where(is_word, entity_qgrad, zero_rows),
            jnp.where(is_word, zero_rows, word_qgrad),
            jnp.where(is_word, zero_rows, entity_qgrad),
        ],
        axis=1,
    )
    querybias_grad = jnp.sum(query_delta, axis=(0, 2))
    valuebias_grad = jnp.sum(value_delta, axis=(0, 1))
    query_reduced = query_delta.astype(jnp.bfloat16)
    key_reduced = key_delta.astype(jnp.bfloat16)
    value_reduced = value_delta.astype(jnp.bfloat16)
    query_local = jnp.einsum(
        "nvh,nkvw->khw", layer_input, query_reduced, preferred_element_type=jnp.float32
    )
    key_shard = jnp.einsum(
        "pui,pun->in", layer_input, key_reduced, preferred_element_type=jnp.float32
    )
    value_local = jnp.einsum(
        "pui,pun->in", layer_input, value_reduced, preferred_element_type=jnp.float32
    )
    input_part = (
        jnp.einsum(
            "kayo,azo->kyz", query_reduced, query_pullback, preferred_element_type=jnp.float32
        )
        + jnp.einsum("ohz,wz->ohw", key_reduced, key_pullback, preferred_element_type=jnp.float32)
        + jnp.einsum(
            "ohz,wz->ohw", value_reduced, value_pullback, preferred_element_type=jnp.float32
        )
    )
    input_total = combine_rows(input_part.reshape(-1, model_width))
    input_grad = whole_rows((input_total + resid_grad).astype(jnp.bfloat16)).reshape(
        layer_input.shape
    )
    query_grad, key_grad, value_grad, outproj_grad = (
        lax.psum_scatter(query_local, "dp", scatter_dimension=1, tiled=True),
        lax.psum_scatter(key_shard, "dp", scatter_dimension=0, tiled=True),
        lax.psum_scatter(value_local, "dp", scatter_dimension=0, tiled=True),
        lax.psum_scatter(outproj_local, "dp", scatter_dimension=1, tiled=True),
    )
    querybias_grad, valuebias_grad, upbias_grad = lax.psum(
        (querybias_grad, valuebias_grad, upbias_grad), "dp"
    )
    outbias_grad, downbias_grad, attngain_grad, attnshift_grad, ffngain_grad, ffnshift_grad = (
        lax.psum(
            (
                outbias_grad,
                downbias_grad,
                attngain_grad,
                attnshift_grad,
                ffngain_grad,
                ffnshift_grad,
            ),
            ("dp", "tensor"),
        )
    )
    return (
        output,
        input_grad,
        query_grad,
        key_grad,
        value_grad,
        outproj_grad,
        upproj_grad,
        downproj_grad,
        querybias_grad,
        valuebias_grad,
        outbias_grad,
        upbias_grad,
        downbias_grad,
        attngain_grad,
        attnshift_grad,
        ffngain_grad,
        ffnshift_grad,
    )


MESH = pl.DeviceIdType.MESH
BF = jnp.bfloat16
F32 = jnp.float32
BLOCK = 128


def fits(mesh):
    return mesh.shape["dp"] == 8 and mesh.shape["tensor"] == 4


def nn(a, b):
    return lax.dot_general(a, b, (((1,), (0,)), ((), ())), preferred_element_type=F32)


def nt(a, b):
    return lax.dot_general(a, b, (((1,), (1,)), ((), ())), preferred_element_type=F32)


def tn(a, b):
    return lax.dot_general(a, b, (((0,), (0,)), ((), ())), preferred_element_type=F32)


def norm_rows(values):
    centre = values - jnp.mean(values, axis=-1, keepdims=True)
    inverse = lax.rsqrt(jnp.mean(centre * centre, axis=-1, keepdims=True) + EPSILON)
    return centre * inverse, inverse


def norm_rows_back(upstream, normal, inverse, gain):
    scaled = upstream * gain
    return inverse * (
        scaled
        - jnp.mean(scaled, axis=-1, keepdims=True)
        - normal * jnp.mean(scaled * normal, axis=-1, keepdims=True)
    )


class Net:
    def __init__(self, send, recv, peer):
        self.send, self.recv, self.peer = send, recv, peer
        self.sends = 0
        self.locals = 0
        self.banks = 0
        self.pending = []

    def bank(self, count):
        base = self.banks
        self.banks += count
        return base

    def start(self, src, dst, sem, device, when=None, group=None):
        slot = self.sends % SENDS
        self.sends += 1
        self.finish([p for p in self.pending if p[3] == slot])

        def make():
            return pltpu.make_async_remote_copy(
                src_ref=src,
                dst_ref=dst,
                send_sem=self.send.at[slot],
                recv_sem=self.recv.at[sem],
                device_id=device,
                device_id_type=MESH,
            )

        if when is None:
            make().start()
        else:
            pl.when(when)(lambda: make().start())
        self.pending.append((make, when, group, slot))

    def finish(self, entries):
        for make, when, _, _ in entries:
            if when is None:
                make().wait_send()
            else:
                pl.when(when)(lambda make=make: make().wait_send())
        self.pending = [p for p in self.pending if p not in entries]

    def wait(self, dst, sem, when=None):
        def make():
            return pltpu.make_async_remote_copy(
                src_ref=dst,
                dst_ref=dst,
                send_sem=self.send.at[0],
                recv_sem=self.recv.at[sem],
                device_id=self.peer,
                device_id_type=MESH,
            )

        if when is None:
            make().wait_recv()
        else:
            pl.when(when)(lambda: make().wait_recv())

    def settle(self, *groups):
        self.finish([p for p in self.pending if not groups or p[2] in groups])


SENDS = 48
RECVS = 141


def layer_kernel(
    x_in, seg_ref, typ_ref, qw_in, kw_in, vw_in, ow_in, uw_in, dw_in, qb_ref, vb_ref,
    ob_ref, ub_ref, db_ref, ag_ref, as_ref, fg_ref, fs_ref, cot_in,
    out_end, ig_end, qg_end, kg_end, vg_end, og_end, ug_end, dg_end, small_end,
    x_ref, qw_ref, kw_ref, vw_ref, ow_ref, uw_ref, dw_ref, cot_ref,
    out_ref, ig_ref, qg_ref, kg_ref, vg_ref, og_ref, ug_ref, dg_ref, small_ref,
    wq, wo, own, wf, ubs, segc, wordc, xt, bias, qq, kv, kk, kvt, kkt, probs, ctx, ct,
    a_s, n1_s, r1_s, act, gelu_d, gl, parts, rs_send, rs_recv, dub, dzb,
    st_a, st_b, st_c, st_d, st_e, st_f, st_g, dct, dc, dco, go_r, rp, sp, rz,
    dqkv, dx_in, dx_cross, dx_back, gq_r, gp, sv, small_s, small_r, sent8, sw, vz,
    send_sems, recv_sems, local_sems,
):
    d = lax.axis_index("dp")
    t = lax.axis_index("tensor")
    c = d % 2
    x = (d // 2) % 2
    y = d // 4
    pair = t % 2
    j = 2 * pair + c
    block = pair + 2 * c
    home = block == t
    zp = t + 1 - 2 * pair
    zq = (t + 2) % 4
    host = 2 * (d // 2) + t // 2
    chip = d // 2
    sib = d + 1 - 2 * c
    xn = d + 2 - 4 * x
    yn = d + 4 - 8 * y
    rows = x_ref.shape[1]
    quarter = rows // 4
    width = x_ref.shape[2]
    strip = qw_ref.shape[1]
    local = kw_ref.shape[1]
    heads = local // HD
    blocks = rows // BLOCK
    own_rows = pl.ds(pl.multiple_of(t * quarter, 16), quarter)
    net = Net(send_sems, recv_sems, (sib, t))

    def flip_x(device):
        return device + 2 - 4 * ((device // 2) % 2)

    def flip_y(device):
        return device + 4 - 8 * (device // 4)

    dg = flip_y(xn)
    part_m, part_o = parts.at[0:2], parts.at[2:4]
    sums_a, sums_b = parts.reshape(rows, width), gelu_d.reshape(rows, width)
    dqq = [sums_a.at[:, BLOCK * h : BLOCK * (h + 1)] for h in range(heads)]
    dkk = [sums_a.at[:, BLOCK * (heads + h) : BLOCK * (heads + h + 1)] for h in range(heads)]
    dvv = [sums_b.at[:, BLOCK * h : BLOCK * (h + 1)] for h in range(heads)]

    low_z = t < 2
    is_end = jnp.logical_or(t == 0, t == 3)
    is_mid = jnp.logical_not(is_end)
    z_out = jnp.where(low_z, t + 1, t - 1)
    z_back = jnp.where(low_z, 0, 3)

    def place(e):
        return jnp.where(low_z, e, 3 - e)

    def joint(one, other):
        return other if one is None else jnp.logical_and(one, other)

    class LineGather:
        def __init__(self, view, group=None):
            self.view, self.bank, self.group = view, net.bank(4), group

        def copy(self, owner, to, when):
            ref = self.view(owner)
            net.start(ref, ref, self.bank + owner, (d, to), when=when, group=self.group)

        def wait(self, owner, when=None):
            net.wait(self.view(owner), self.bank + owner, when=when)

        def begin(self):
            self.copy(t, z_out, None)
            self.copy(t, z_back, is_mid)

        def step(self, n):
            if n == 1:
                self.wait(place(0), is_mid)
                self.copy(place(0), z_out, is_mid)
                self.wait(place(2), is_mid)
                self.copy(place(2), z_back, is_mid)
            if n == 2:
                self.wait(place(3), is_mid)
                self.copy(place(3), z_back, is_mid)
            self.wait(place(n), is_end)

    class LineReduce:
        def __init__(self, own, came, cross, back):
            self.own, self.came, self.cross, self.back = own, came, cross, back
            self.in_b, self.cross_b, self.back_b = net.bank(3), net.bank(2), net.bank(1)

        def depart(self, e):
            net.start(self.own(e), self.came.at[e - 1], self.in_b + e - 1, (d, z_out), when=is_end)

        def add(self, e, ref):
            @pl.when(is_mid)
            def _():
                ref[...] = (self.own(e)[...].astype(F32) + ref[...].astype(F32)).astype(BF)

        def through(self, e):
            ref = self.came.at[e - 1]
            net.wait(ref, self.in_b + e - 1, when=is_mid)
            self.add(e, ref)
            net.start(ref, self.cross.at[3 - e], self.cross_b + 3 - e, (d, z_out), when=is_mid)

        def pass_back(self):
            net.wait(self.cross.at[0], self.cross_b, when=is_mid)
            self.add(0, self.cross.at[0])
            net.start(self.cross.at[0], self.back, self.back_b, (d, z_back), when=is_mid)

        def total(self):
            net.wait(self.came.at[0], self.in_b, when=is_mid)
            net.wait(self.cross.at[1], self.cross_b + 1, when=is_mid)
            net.wait(self.back, self.back_b, when=is_end)
            others = self.came[0].astype(F32) + self.cross[1].astype(F32)
            mine = self.own(jnp.where(is_mid, 1, 0))[...].astype(F32)
            return mine + jnp.where(is_mid, others, self.back[...].astype(F32))

    class Local:
        def __init__(self, source, target):
            self.copy = pltpu.make_async_copy(source, target, local_sems.at[net.locals])
            net.locals += 1
            self.copy.start()

        def wait(self):
            self.copy.wait()

    in_q, in_k, in_v = Local(qw_in, qw_ref), Local(kw_in, kw_ref), Local(vw_in, vw_ref)
    in_o, in_u, in_d = Local(ow_in, ow_ref), Local(uw_in, uw_ref), Local(dw_in, dw_ref)
    in_x, in_cot = Local(x_in, x_ref), Local(cot_in, cot_ref)

    barrier = pltpu.get_barrier_semaphore()
    for m in range(1, 8):
        pl.semaphore_signal(barrier, 1, device_id=((d + m) % 8, t), device_id_type=MESH)
    for k in range(1, 4):
        pl.semaphore_signal(barrier, 1, device_id=(d, (t + k) % 4), device_id_type=MESH)
    pl.semaphore_signal(barrier, 1, device_id=(sib, zq), device_id_type=MESH)

    for arrived in (in_q, in_k, in_v):
        arrived.wait()
    for h in range(heads):
        at = slice(HD * h, HD * (h + 1))
        piece = jnp.concatenate(
            [qw_ref[i, :, at] for i in range(4)] + [kw_ref[:, at], vw_ref[:, at]], axis=1
        )
        wq[d, :, 6 * HD * h : 6 * HD * (h + 1)] = piece.astype(BF)

    pl.semaphore_wait(barrier, 11)

    class PlaneGather:
        def __init__(self, group, *views):
            self.views, self.bank, self.group = views, net.bank(8 * len(views)), group

        def copy(self, view, block, device):
            ref = self.views[view](block)
            net.start(ref, ref, self.bank + 8 * view + block, (device, t), group=self.group)

        def wait(self, view, block):
            net.wait(self.views[view](block), self.bank + 8 * view + block)

        def begin(self):
            for view, device in ((0, yn), (1, xn), (1, yn), (0, xn), (0, sib), (1, sib)):
                self.copy(view, d, device)

        def middle(self):
            self.wait(0, yn)
            self.copy(0, yn, xn)
            self.wait(1, xn)
            self.copy(1, xn, yn)
            self.copy(0, yn, sib)
            self.copy(1, xn, sib)
            for view, block in ((1, yn), (0, xn)):
                self.wait(view, block)
                self.copy(view, block, sib)

        def late(self):
            for view in range(2):
                self.wait(view, dg)
                self.copy(view, dg, sib)

        def end(self):
            for block in (sib, flip_x(sib), flip_y(sib), flip_x(flip_y(sib))):
                for view in range(len(self.views)):
                    self.wait(view, block)

    gather_q = PlaneGather("q", lambda b: wq.at[b, : strip // 2], lambda b: wq.at[b, strip // 2 :])
    gather_q.begin()

    def wide_t(value, high, wide):
        r, w = value.shape
        if w < wide:
            value = jnp.concatenate([value, jnp.zeros((r, wide - w), value.dtype)], axis=1)
        if r < high:
            value = jnp.concatenate([value, jnp.zeros((high - r, wide), value.dtype)], axis=0)
        return value.T

    for arrived in (in_o, in_u, in_d):
        arrived.wait()
    wo[t, d] = wide_t(ow_ref[...], 256, 128)[:strip, :local].astype(BF)
    own[0] = uw_ref[...].astype(BF)
    own[1] = dw_ref[...].astype(BF)
    ubs[t] = jnp.broadcast_to(ub_ref[...][None], ubs.shape[1:])

    ub_z = net.bank(1)
    wf_a = net.bank(4)

    class ChipGather:
        def __init__(self, i):
            self.i, self.bank = i, net.bank(8)

        def send(self):
            i = self.i
            for plane, when in ((zq, None), (t, host != d)):
                net.start(own.at[i], wf.at[i, d], wf_a + 2 * i + c, (host, plane), when=when)

            @pl.when(host == d)
            def _():
                wf[i, d] = own[i]

        def copy(self, view, of, device):
            ref = wf.at[self.i, 2 * (of // 2) + view]
            net.start(ref, ref, self.bank + 2 * (of // 2) + view, (device, t), group="f")

        def wait(self, view, of):
            net.wait(wf.at[self.i, 2 * (of // 2) + view], self.bank + 2 * (of // 2) + view)

        def begin(self):
            i = self.i
            net.wait(wf.at[i, d], wf_a + 2 * i + c, when=jnp.logical_not(home))
            net.wait(wf.at[i, sib], wf_a + 2 * i + 1 - c)
            for view, device in ((0, yn), (1, xn), (1, yn), (0, xn)):
                self.copy(view, d, device)

        def middle(self):
            self.wait(0, yn)
            self.copy(0, yn, xn)
            self.wait(1, xn)
            self.copy(1, xn, yn)

        def end(self):
            for view, of in ((1, yn), (0, xn), (0, dg), (1, dg)):
                self.wait(view, of)

    up, down = ChipGather(0), ChipGather(1)
    wo_z = net.bank(1)
    for k in (2, 1, 3):
        net.start(wo.at[t, d], wo.at[t, d], wo_z, (d, (t + k) % 4), group="o")
    for b in range(blocks):
        at = slice(BLOCK * b, BLOCK * (b + 1))
        segc[at, :] = jnp.broadcast_to(seg_ref[:, at].astype(F32), (BLOCK, BLOCK)).T
        wordc[at, :] = jnp.broadcast_to((typ_ref[:, at] == 0).astype(F32), (BLOCK, BLOCK)).T
    in_x.wait()
    xt[...] = x_ref[0].T
    for h in range(heads):
        at = slice(HD * h, HD * (h + 1))
        bias[:, 6 * HD * h : 6 * HD * (h + 1)] = jnp.concatenate(
            [qb_ref[i : i + 1, at] for i in range(4)] + [jnp.zeros((1, HD), F32), vb_ref[at][None]],
            axis=1,
        )

    gather_q.middle()
    net.wait(wo.at[0:3, d], wo_z)
    gather_o = PlaneGather("o", lambda b: wo.at[0:2, b], lambda b: wo.at[2:4, b])
    gather_o.begin()
    up.send()
    net.start(ubs.at[t], ubs.at[t], ub_z, (d, zq))
    down.send()
    gather_q.late()
    gather_q.end()
    low_half = lax.broadcasted_iota(jnp.int32, (rows, BLOCK), 1) < HD
    is_word = wordc[...] > 0.5
    for h in range(heads):
        base = 6 * HD * h
        at = slice(BLOCK * h, BLOCK * (h + 1))
        made = nn(x_ref[0], wq[:, :, base : base + 6 * HD].reshape(width, 6 * HD))
        made = made + bias[:, base : base + 6 * HD]
        qq[:, at] = jnp.where(is_word, made[:, :BLOCK], made[:, BLOCK : 2 * BLOCK]).astype(BF)
        both = made[:, 2 * BLOCK :]
        keys = jnp.where(low_half, both, pltpu.roll(both, HD, 1))
        keys = jnp.where(jnp.logical_xor(is_word, low_half), 0.0, keys)
        kv[:, at] = both.astype(BF)
        kk[:, at] = keys.astype(BF)
        kvt[h] = both.T[HD:].astype(BF)
        kkt[h] = keys.T.astype(BF)

    gather_o.middle()
    up.begin()
    ct_z = net.bank(1)

    def span(b):
        return BLOCK * max(0, b - 2), BLOCK * min(blocks, b + 3)

    kept = [0]
    for b in range(blocks):
        kept.append(kept[-1] + span(b)[1] - span(b)[0])
    for b in range(blocks):
        lo, hi = span(b)
        at_q = slice(BLOCK * b, BLOCK * (b + 1))
        same = segc[lo:hi, :] == seg_ref[:, at_q].astype(F32)
        found = []
        for h in range(heads):
            at = slice(BLOCK * h, BLOCK * (h + 1))
            scores = nt(kk[lo:hi, at], qq[at_q, at]) * SCALING
            scores = jnp.where(same, scores, NEGATIVE)
            weights = jnp.exp(scores - jnp.max(scores, axis=0, keepdims=True))
            weights = weights * (1.0 / jnp.sum(weights, axis=0, keepdims=True))
            probs[h, kept[b] : kept[b + 1]] = weights
            found.append(nn(kvt[h, :, lo:hi], weights.astype(BF)))
        found.append(jnp.zeros((HD, BLOCK), F32))
        ctx[at_q, :] = jnp.concatenate(found, axis=0).T[:, :local].astype(BF)
        if b == 3:
            down.begin()
        if b > 0:
            s = b - 1
            src = ctx.at[quarter * s : quarter * (s + 1)]
            net.start(src, ct.at[t], ct_z, (d, s), when=t != s)
    ct[t] = ctx[own_rows, :]

    up.middle()
    gather_o.late()
    gather_o.end()
    net.wait(ct.at[0:3], ct_z)
    attended = nt(ct[0], wo[0].reshape(width, local))
    for s in range(1, 4):
        attended = attended + nt(ct[s], wo[s].reshape(width, local))
    normal, inverse = norm_rows(x_ref[0, own_rows, :].astype(F32) + attended + ob_ref[...][None])
    n1_s[...] = normal
    r1_s[...] = jnp.broadcast_to(inverse, r1_s.shape)
    normed = normal * ag_ref[...][None] + as_ref[...][None]
    a_s[...] = normed
    act[j] = normed.astype(BF)

    def rows_of(ref, first, count):
        return lambda owner: ref.at[
            0, pl.ds(pl.multiple_of(owner * quarter + first, 16), count)
        ]

    part = quarter // 2
    chunk = [slice(part * q, part * (q + 1)) for q in range(2)]

    class RowGather:
        def __init__(self, ref):
            self.ref, self.bank = ref, net.bank(8)

        def copy(self, q, rank, device):
            ref = self.ref.at[rank, chunk[q]]
            net.start(ref, ref, self.bank + 4 * q + rank, device)

        def wait(self, q, rank):
            net.wait(self.ref.at[rank, chunk[q]], self.bank + 4 * q + rank)

        def begin(self, q):
            self.copy(q, j, (d, zp))
            self.copy(q, j, (sib, t))

        def near(self, q):
            self.wait(q, 2 * pair + 1 - c)

        def middle(self, q):
            self.wait(q, 2 - 2 * pair + c)
            self.copy(q, 2 - 2 * pair + c, (sib, t))

        def far(self, q):
            self.wait(q, 3 - 2 * pair - c)

    class RowSum:
        def __init__(self, index):
            self.index, self.bank = index, net.bank(6)

        def hand(self, q, slot, partial_rows):
            where = 3 * self.index + slot
            rs_send[where, chunk[q]] = partial_rows.astype(BF)
            net.start(
                rs_send.at[where, chunk[q]], rs_recv.at[where, chunk[q]], self.bank + 3 * q + slot,
                (d, zp) if slot == 2 else (sib, t),
            )

        def take(self, q, slot):
            where = 3 * self.index + slot
            net.wait(rs_recv.at[where, chunk[q]], self.bank + 3 * q + slot)
            return rs_recv[where, chunk[q]].astype(F32)

        def near(self, q):
            self.hand(q, 0, part_m[1 - c, chunk[q]])

        def away(self, q):
            self.hand(q, 1, part_o[1 - c, chunk[q]])

        def across(self, q):
            self.hand(q, 2, part_o[c, chunk[q]] + self.take(q, 1))

        def total(self, q):
            return part_m[c, chunk[q]] + self.take(q, 0) + self.take(q, 2)

    rows_a = RowGather(act)
    rows_a.begin(0)
    rows_a.begin(1)
    down.middle()
    rows_a.middle(0)
    rows_a.middle(1)
    rows_a.near(0)
    rows_a.near(1)
    net.wait(ubs.at[zq], ub_z)
    up.end()
    near = pl.ds(2 * pair, 2)
    away = pl.ds(2 - 2 * pair, 2)

    def feed(half):
        hidden = nn(act[half].reshape(2 * quarter, width), wf[0].reshape(width, width))
        hidden = hidden + ubs[block][:1]
        bell = 0.5 * (1.0 + lax.erf(hidden * 0.7071067811865476))
        slope = bell + hidden * (0.3989422804014327 * jnp.exp(-0.5 * hidden * hidden))
        gelu_d[half] = slope.reshape(2, quarter, width)
        gl[half] = (hidden * bell).astype(BF).reshape(2, quarter, width)

    def feed_out(half, partial_ref):
        made = nt(gl[half].reshape(2 * quarter, width), wf[1].reshape(width, width))
        partial_ref[...] = made.reshape(2, quarter, width)

    feed(near)
    rows_a.far(0)
    rows_a.far(1)
    feed(away)
    down.end()
    sum_f = RowSum(0)
    feed_out(away, part_o)
    sum_f.away(0)
    sum_f.away(1)
    feed_out(near, part_m)
    sum_f.across(0)
    sum_f.across(1)
    sum_f.near(0)
    sum_f.near(1)
    in_cot.wait()
    rows_u = RowGather(dub)
    gain_sum, shift_sum, bias_sum = 0.0, 0.0, 0.0
    for q in range(2):
        ffn_out = sum_f.total(q) + db_ref[...][None]
        normal, inverse = norm_rows(a_s[chunk[q]] + ffn_out)
        rows_q = pl.ds(pl.multiple_of(t * quarter + part * q, 16), part)
        out_ref[0, rows_q, :] = (normal * fg_ref[...][None] + fs_ref[...][None]).astype(BF)
        upstream = cot_ref[0, rows_q, :].astype(F32)
        du = norm_rows_back(upstream, normal, inverse, fg_ref[...][None])
        dub[j, chunk[q]] = du.astype(BF)
        rows_u.begin(q)
        a_s[chunk[q]] = du
        gain_sum = gain_sum + jnp.sum(upstream * normal, axis=0, keepdims=True)
        shift_sum = shift_sum + jnp.sum(upstream, axis=0, keepdims=True)
        bias_sum = bias_sum + jnp.sum(du, axis=0, keepdims=True)
    line_out = [LineGather(rows_of(out_ref, part * q, part)) for q in range(2)]
    line_out[0].begin()
    sv[...] = jnp.zeros_like(sv)
    sv[0:1] = gain_sum
    sv[1:2] = shift_sum
    sv[2:3] = bias_sum

    def feed_back(half, rows_q, partial_ref):
        count = 2 * (rows_q.stop - rows_q.start)
        made = nn(dub[half, rows_q].reshape(count, width), wf[1].reshape(width, width))
        made = made * gelu_d[half, rows_q].reshape(count, width)
        low = made.astype(BF)
        dzb[half, rows_q] = low.reshape(2, count // 2, width)
        partial_ref[:, rows_q] = nt(low, wf[0].reshape(width, width)).reshape(2, count // 2, width)
        return jnp.sum(made, axis=0, keepdims=True)

    sum_b = RowSum(1)
    rows_u.near(0)
    rows_u.near(1)
    up_sum = feed_back(near, slice(0, quarter), part_m)
    sum_b.near(0)
    sum_b.near(1)
    rows_u.middle(0)
    rows_u.far(0)
    up_sum = up_sum + feed_back(away, chunk[0], part_o)
    sum_b.away(0)
    rows_u.middle(1)
    sum_b.across(0)
    rows_u.far(1)
    up_sum = up_sum + feed_back(away, chunk[1], part_o)
    sum_b.away(1)
    sv[6:7] = up_sum
    half = width // 2

    class StripSum:
        def __init__(self, i):
            self.i, self.bank = i, net.bank(9)
            self.by_chip = wf.at[i].reshape(2, 2, 2, strip, width)

        def make(self, left, right):
            made = tn(left[...].reshape(4 * quarter, width), right[...].reshape(4 * quarter, width))
            wf[self.i] = made.astype(BF).reshape(8, strip, width)

        def begin(self):
            net.start(
                self.by_chip.at[:, 1 - x, :, :, :half], st_a.at[self.i], self.bank, (xn, t)
            )
            net.start(
                self.by_chip.at[1 - y, :, :, :, half:], st_b.at[self.i], self.bank + 1, (yn, t)
            )

        def turn(self):
            i = self.i
            net.wait(st_a.at[i], self.bank)
            st_a[i] = (st_a[i].astype(F32) + self.by_chip[:, x, :, :, :half].astype(F32)).astype(BF)
            for core in range(2):
                net.start(
                    st_a.at[i, 1 - y, core], st_c.at[i, c], self.bank + 2 + c,
                    (2 * (yn // 2) + core, t),
                )
            net.start(st_a.at[i, y, 1 - c], st_g.at[i, 0], self.bank + 6, (sib, t))
            net.wait(st_b.at[i], self.bank + 1)
            st_b[i] = (st_b[i].astype(F32) + self.by_chip[y, :, :, :, half:].astype(F32)).astype(BF)
            for core in range(2):
                net.start(
                    st_b.at[i, 1 - x, core], st_d.at[i, c], self.bank + 4 + c,
                    (2 * (xn // 2) + core, t),
                )
            net.start(st_b.at[i, x, 1 - c], st_g.at[i, 1], self.bank + 7, (sib, t))

        def gather(self):
            i = self.i
            for core in range(2):
                net.wait(st_c.at[i, core], self.bank + 2 + core)
                net.wait(st_d.at[i, core], self.bank + 4 + core)
            net.wait(st_g.at[i, 0], self.bank + 6)
            net.wait(st_g.at[i, 1], self.bank + 7)
            for whose, first, second in (
                (c, st_a.at[i, y, c], st_b.at[i, x, c]), (1 - c, st_g.at[i, 0], st_g.at[i, 1])
            ):
                st_e[i, whose, :, :half] = (
                    first[...].astype(F32) + st_c[i, whose].astype(F32)
                ).astype(BF)
                st_e[i, whose, :, half:] = (
                    second[...].astype(F32) + st_d[i, whose].astype(F32)
                ).astype(BF)

        def deliver(self, when=None):
            i = self.i
            net.start(st_e.at[i, 1 - t // 2], st_f.at[i], self.bank + 8, (d, zq), when=when)

        def total(self):
            i = self.i
            net.wait(st_f.at[i], self.bank + 8)
            return st_e[i, t // 2].astype(F32) + st_f[i].astype(F32)

    class SmallSum:
        def __init__(self, index):
            self.index, self.bank = index, net.bank(2)

        def begin(self, values):
            i = self.index
            small_s[i, 0] = values
            for r in (xn, yn, dg):
                net.start(small_s.at[i, 0], small_r.at[i, chip], self.bank, (r, t))
            small_r[i, chip] = values

        def plane(self):
            i = self.index
            net.wait(small_r.at[i, 0:3], self.bank)
            total = small_r[i, 0]
            for k in range(1, 4):
                total = total + small_r[i, k]
            small_s[i, 1] = total
            net.start(small_s.at[i, 1], small_r.at[i, 4], self.bank + 1, (sib, t))

        def cores(self):
            net.wait(small_r.at[self.index, 4], self.bank + 1)
            return small_s[self.index, 1], small_r[self.index, 4]

    net.settle("f")
    down_sum, up_sums = StripSum(1), StripSum(0)
    down_sum.make(dub, gl)
    down_sum.begin()
    sum_b.across(1)
    line_out[1].begin()
    up_sums.make(act, dzb)
    up_sums.begin()
    dc_z = net.bank(1)
    gain_sum, shift_sum, bias_sum, dhb = 0.0, 0.0, 0.0, []
    for q in range(2):
        da = a_s[chunk[q]] + sum_b.total(q)
        normal = n1_s[chunk[q]]
        dh = norm_rows_back(da, normal, r1_s[chunk[q], :1], ag_ref[...][None])
        a_s[chunk[q]] = dh
        dhb.append(dh.astype(BF))
        for k in (2, 1, 3):
            s = (t + k) % 4
            dct[s, chunk[q]] = nn(dhb[q], wo[s].reshape(width, local)).astype(BF)
            net.start(dct.at[s, chunk[q]], dc.at[t, chunk[q]], dc_z, (d, s))
        dc[t, chunk[q]] = nn(dhb[q], wo[t].reshape(width, local)).astype(BF)
        gain_sum = gain_sum + jnp.sum(da * normal, axis=0, keepdims=True)
        shift_sum = shift_sum + jnp.sum(da, axis=0, keepdims=True)
        bias_sum = bias_sum + jnp.sum(dh, axis=0, keepdims=True)
    dhb = jnp.concatenate(dhb, axis=0)
    line_out[0].step(1)
    line_out[1].step(1)
    sv[3:4] = gain_sum
    sv[4:5] = shift_sum
    sv[5:6] = bias_sum
    small_a = SmallSum(0)
    small_a.begin(sv[...])
    down_sum.turn()
    net.settle("o")
    for s in range(4):
        wo[s] = tn(dhb, ct[s]).astype(BF).reshape(8, strip, local)
    by_core = wo.reshape(4, 4, 2, strip, local)
    go_b = net.bank(1)
    net.start(by_core.at[:, :, 1 - c], go_r, go_b, (sib, t))

    net.wait(dc.at[0:3], dc_z)
    up_sums.turn()
    net.wait(go_r, go_b)
    go_r[...] = (by_core[:, :, c].astype(F32) + go_r[...].astype(F32)).astype(BF)
    rp_b = net.bank(1)
    for r in (xn, yn, dg):
        net.start(go_r.at[:, r // 2], rp.at[chip], rp_b, (r, t))
    rp[chip] = go_r[:, chip]
    dctx = dc[...].reshape(rows, local)
    for h in range(heads):
        dco[:, BLOCK * h : BLOCK * (h + 1)] = jnp.concatenate(
            [jnp.zeros((rows, HD), BF), dctx[:, HD * h : HD * (h + 1)]], axis=1
        )
    for h in range(heads):
        dkk[h][...] = jnp.zeros((rows, BLOCK), F32)
        dvv[h][...] = jnp.zeros((rows, BLOCK), F32)
    for b in range(blocks):
        lo, hi = span(b)
        at_q = slice(BLOCK * b, BLOCK * (b + 1))
        for h in range(heads):
            at = slice(BLOCK * h, BLOCK * (h + 1))
            weights = probs[h, kept[b] : kept[b + 1]]
            dp = nt(kv[lo:hi, at], dco[at_q, at])
            ds = weights * (dp - jnp.sum(weights * dp, axis=0, keepdims=True))
            dsb = ds.astype(BF)
            dkk[h][lo:hi] += nn(dsb, qq[at_q, at])
            dvv[h][lo:hi] += nn(weights.astype(BF), dco[at_q, at])
            dqq[h][at_q] = nn(kkt[h, :, lo:hi], dsb).T * SCALING

    down_sum.gather()
    down_sum.deliver()
    small_a.plane()
    for h in range(heads):
        base = 6 * HD * h
        first = jnp.where(is_word, dqq[h][...], 0.0)
        second = jnp.where(is_word, 0.0, dqq[h][...])
        keys = dkk[h][...]
        keys = jnp.where(is_word, keys, pltpu.roll(keys, HD, 1)) * SCALING
        third = jnp.where(low_half, keys, dvv[h][...])
        for i, piece in enumerate((first, second, third)):
            at = slice(base + BLOCK * i, base + BLOCK * (i + 1))
            dqkv[:, at] = piece.astype(BF)
            row, col = divmod(base + BLOCK * i, width)
            sv[row : row + 1, col : col + BLOCK] = jnp.sum(piece, axis=0, keepdims=True)

    first_rows = pl.ds(pl.multiple_of(jnp.where(low_z, rows // 2, 0), 16), rows // 2)
    other_rows = pl.ds(pl.multiple_of(jnp.where(low_z, 0, rows // 2), 16), rows // 2)
    first_two = pl.ds(jnp.where(low_z, 2, 0), 2)
    other_two = pl.ds(jnp.where(low_z, 0, 2), 2)

    def back_to_input(rows_b, quarters):
        made = nt(dqkv[rows_b, :], wq[...].reshape(width, 6 * local))
        dzb[quarters] = made.astype(BF).reshape(2, quarter, width)

    line_dx, line_in = [], []
    for q in range(2):
        cut = pl.ds(part * q, part)
        line_dx.append(
            LineReduce(
                lambda e, cut=cut: dzb.at[place(e), cut],
                dx_in.at[q], dx_cross.at[q], dx_back.at[q],
            )
        )
        line_in.append(LineGather(rows_of(ig_ref, part * q, part)))

    def arrive(q):
        total = line_dx[q].total() + a_s[part * q : part * (q + 1)]
        ig_ref[0, pl.ds(pl.multiple_of(t * quarter + part * q, 16), part)] = total.astype(BF)
        line_in[q].begin()

    back_to_input(first_rows, first_two)
    for q, e in ((0, 3), (0, 2), (1, 3), (1, 2)):
        line_dx[q].depart(e)
    plane_sum, other_sum = small_a.cores()
    first_core = c == 0
    own_units, other_units = plane_sum[6:7], other_sum[6:7]
    sent8[0:6] = plane_sum[0:6] + other_sum[0:6]
    sent8[6:7] = jnp.where(first_core, own_units, other_units)
    sent8[7:8] = jnp.where(first_core, other_units, own_units)
    vz_b = net.bank(2)
    for k in (2, 1, 3):
        net.start(sent8, vz.at[t], vz_b, (d, (t + k) % 4), when=first_core)
    vz[t] = sent8[...]
    back_to_input(other_rows, other_two)
    line_dx[0].depart(1)
    line_dx[1].depart(1)
    up_sums.gather()
    up_sums.deliver(is_mid)
    small_b = SmallSum(1)
    small_b.begin(sv[...])

    net.settle("q")
    wq[...] = nn(xt[...], dqkv[...]).astype(BF).reshape(8, strip, 6 * local)
    q_by_core = wq.reshape(4, 2, strip, 6 * local)
    gq_b = net.bank(1)
    net.start(q_by_core.at[:, 1 - c], gq_r, gq_b, (sib, t))
    line_out[0].step(2)
    line_out[1].step(2)
    line_dx[0].through(3)
    line_dx[0].through(2)
    net.wait(gq_r, gq_b)
    gq_r[...] = (q_by_core[:, c].astype(F32) + gq_r[...].astype(F32)).astype(BF)
    gp_b = net.bank(1)
    for r in (xn, yn, dg):
        net.start(gq_r.at[r // 2], gp.at[chip], gp_b, (r, t))
    gp[chip] = gq_r[chip]

    line_dx[0].pass_back()
    net.wait(rp.at[0:3], rp_b)
    total = rp[0].astype(F32)
    for k in range(1, 4):
        total = total + rp[k].astype(F32)
    sp[...] = total.astype(BF)
    rz_b = net.bank(1)
    rz[t] = sp[t]

    def send_rz(when):
        for k in range(1, 4):
            s = (t + k) % 4
            net.start(sp.at[s], rz.at[t], rz_b, (d, s), when=when)

    send_rz(is_mid)
    line_dx[1].through(3)
    line_dx[1].through(2)
    line_dx[1].pass_back()
    line_out[0].step(3)
    line_out[1].step(3)
    ends = [Local(out_ref, out_end)]
    arrive(0)
    arrive(1)

    up_sums.deliver(is_end)
    send_rz(is_end)
    line_in[0].step(1)
    line_in[1].step(1)
    line_in[0].step(2)
    line_in[1].step(2)
    small_b.plane()
    net.wait(vz.at[0:3], vz_b, when=first_core)

    @pl.when(first_core)
    def _():
        total = vz[0]
        for k in range(1, 4):
            total = total + vz[k]
        sw[0:6] = total[0:6]
        units = vz[t] + vz[zq]
        sw[6:7] = jnp.where(t < 2, units[6:7], units[7:8])
        sw[7:8] = units[7:8]

    net.start(sw, sw, vz_b + 1, (sib, t), when=first_core)
    net.wait(sw, vz_b + 1, when=c == 1)
    small_ref[0:8] = sw[...]
    plane_sum, other_sum = small_b.cores()
    small_ref[8:16] = plane_sum + other_sum
    dg_ref[...] = down_sum.total()
    ug_ref[...] = up_sums.total()
    ends += [Local(dg_ref, dg_end), Local(ug_ref, ug_end), Local(small_ref, small_end)]
    net.wait(rz.at[0:3], rz_b)
    total = rz[0].astype(F32)
    for s in range(1, 4):
        total = total + rz[s].astype(F32)
    og_ref[...] = wide_t(total, BLOCK, 256)[:local, :strip]

    ends += [Local(og_ref, og_end)]
    net.wait(gp.at[0:3], gp_b)
    total = gp[0].astype(F32)
    for k in range(1, 4):
        total = total + gp[k].astype(F32)
    for h in range(heads):
        base = 6 * HD * h
        at = slice(HD * h, HD * (h + 1))
        for i in range(4):
            qg_ref[i, :, at] = total[:, base + HD * i : base + HD * (i + 1)]
        kg_ref[:, at] = total[:, base + 4 * HD : base + 5 * HD]
        vg_ref[:, at] = total[:, base + 5 * HD : base + 6 * HD]

    ends += [Local(qg_ref, qg_end), Local(kg_ref, kg_end), Local(vg_ref, vg_end)]
    for q in range(2):
        line_in[q].step(3)
    ends += [Local(ig_ref, ig_end)]
    net.settle()
    for copy in ends:
        copy.wait()
    assert net.banks == RECVS, net.banks


def end_kernel(*refs):
    sources, small = refs[:8], refs[8]
    targets, (qbg, vbg), vectors = refs[9:17], refs[17:19], refs[19:26]
    for source, target in zip(sources, targets):
        target[...] = source[...]
    fgg, fsg, dbg, agg, asg, obg, ubg = (small[i] for i in range(7))
    for ref, value in zip(vectors, (obg, ubg, dbg, agg, asg, fgg, fsg)):
        ref[...] = value
    width = small.shape[1]
    values = []
    for h in range(vbg.shape[0] // HD):
        row, col = divmod(6 * HD * h, width)
        piece = small[8 + row : 9 + row, col : col + 6 * HD]
        for i in range(4):
            qbg[i : i + 1, HD * h : HD * (h + 1)] = piece[:, HD * i : HD * (i + 1)]
        values.append(piece[:, 5 * HD :])
    vbg[...] = jnp.concatenate(values, axis=1)[0]


def fused(
    layer_input, segment_ids, token_types, query_weight, key_weight, value_weight, out_weight,
    up_weight, down_weight, query_bias, value_bias, out_bias, up_bias, down_bias, attn_gain,
    attn_shift, ffn_gain, ffn_shift, cotangent,
):
    rows, width = layer_input.shape[1:]
    strip, local = key_weight.shape
    quarter, heads, blocks = rows // 4, local // HD, rows // BLOCK
    kept = sum(BLOCK * (min(blocks, b + 3) - max(0, b - 2)) for b in range(blocks))
    args = [
        layer_input, segment_ids, token_types, query_weight, key_weight, value_weight, out_weight,
        up_weight, down_weight.T, query_bias, value_bias, out_bias, up_bias, down_bias, attn_gain,
        attn_shift, ffn_gain, ffn_shift, cotangent,
    ]

    def like(v, dtype=F32):
        return jax.ShapeDtypeStruct(v.shape, dtype)

    outs = [
        like(layer_input, BF), like(layer_input, BF), like(query_weight), like(key_weight),
        like(value_weight), like(out_weight), like(up_weight), jax.ShapeDtypeStruct((strip, width), F32),
        jax.ShapeDtypeStruct((16, width), F32),
    ]
    v = pltpu.VMEM
    scratch = [
        v(layer_input.shape, BF), v(query_weight.shape, F32), v(key_weight.shape, F32),
        v(value_weight.shape, F32), v(out_weight.shape, F32), v(up_weight.shape, F32),
        v((strip, width), F32), v(cotangent.shape, BF),
    ] + [v(o.shape, o.dtype) for o in outs] + [
        v((8, strip, 6 * local), BF), v((4, 8, strip, local), BF), v((2, strip, width), BF),
        v((2, 8, strip, width), BF), v((4, 8, width), F32), v((rows, BLOCK), F32),
        v((rows, BLOCK), F32), v((width, rows), BF), v((1, 6 * local), F32),
        v((rows, heads * BLOCK), BF), v((rows, heads * BLOCK), BF), v((rows, heads * BLOCK), BF),
        v((heads, HD, rows), BF), v((heads, BLOCK, rows), BF),
        v((heads, kept, BLOCK), F32), v((rows, local), BF), v((4, quarter, local), BF),
        v((quarter, width), F32), v((quarter, width), F32), v((quarter, BLOCK), F32),
        v((4, quarter, width), BF), v((4, quarter, width), F32), v((4, quarter, width), BF),
        v((4, quarter, width), F32),
        v((6, quarter, width), BF), v((6, quarter, width), BF),
        v((4, quarter, width), BF), v((4, quarter, width), BF),
        v((2, 2, 2, strip, width // 2), BF), v((2, 2, 2, strip, width // 2), BF),
        v((2, 2, strip, width // 2), BF), v((2, 2, strip, width // 2), BF),
        v((2, 2, strip, width), BF), v((2, strip, width), BF),
        v((2, 2, strip, width // 2), BF),
        v((4, quarter, local), BF), v((4, quarter, local), BF),
        v((rows, heads * BLOCK), BF),
        v((4, 4, strip, local), BF), v((4, 4, strip, local), BF), v((4, strip, local), BF),
        v((4, strip, local), BF),
        v((rows, 6 * local), BF),
        v((2, 3, quarter // 2, width), BF), v((2, 2, quarter // 2, width), BF),
        v((2, quarter // 2, width), BF),
        v((4, strip, 6 * local), BF), v((4, strip, 6 * local), BF),
        v((8, width), F32), v((2, 2, 8, width), F32), v((2, 5, 8, width), F32),
        v((8, width), F32), v((8, width), F32), v((4, 8, width), F32),
        pltpu.SemaphoreType.DMA((SENDS,)), pltpu.SemaphoreType.DMA((RECVS,)),
        pltpu.SemaphoreType.DMA((17,)),
    ]
    spec = pl.BlockSpec(memory_space=pltpu.VMEM)
    anywhere = pl.BlockSpec(memory_space=pl.ANY)
    large_args = (0, 3, 4, 5, 6, 7, 8, 18)
    made = pl.pallas_call(
        layer_kernel,
        out_shape=outs,
        in_specs=[anywhere if n in large_args else spec for n in range(len(args))],
        out_specs=[anywhere] * len(outs),
        scratch_shapes=scratch,
        compiler_params=pltpu.CompilerParams(
            collective_id=0, has_side_effects=True, vmem_limit_bytes=58 << 20
        ),
        name="layer",
    )(*args)
    *large, small = made
    vector = jax.ShapeDtypeStruct((width,), F32)
    ended = pl.pallas_call(
        end_kernel,
        out_shape=[like(v, v.dtype) for v in large]
        + [like(query_bias), jax.ShapeDtypeStruct((local,), F32)]
        + [vector] * 7,
        in_specs=[spec] * len(made),
        out_specs=[spec] * 17,
        name="finish",
    )(*large, small)
    return (*ended[:7], ended[7].T, *ended[8:])


def solution(mesh):
    in_specs = (
        P("dp", None, None),
        P("dp", None),
        P("dp", None),
        P(None, "dp", "tensor"),
        P("dp", "tensor"),
        P("dp", "tensor"),
        P("tensor", "dp"),
        P("dp", "tensor"),
        P("tensor", "dp"),
        P(None, "tensor"),
        P("tensor"),
        P(),
        P("tensor"),
        P(),
        P(),
        P(),
        P(),
        P(),
        P("dp", None, None),
    )
    out_specs = (
        P("dp", None, None),
        P("dp", None, None),
        P(None, "dp", "tensor"),
        P("dp", "tensor"),
        P("dp", "tensor"),
        P("tensor", "dp"),
        P("dp", "tensor"),
        P("tensor", "dp"),
        P(None, "tensor"),
        P("tensor"),
        P(),
        P("tensor"),
        P(),
        P(),
        P(),
        P(),
        P(),
    )
    step = fused if fits(mesh) else shards
    return jax.shard_map(step, mesh=mesh, in_specs=in_specs, out_specs=out_specs, check_vma=False)
```

```python
from functools import partial

import jax
import jax.numpy as jnp
from jax import lax
from jax.experimental import pallas as pl
from jax.experimental.pallas import tpu as pltpu
from jax.sharding import PartitionSpec as P

HD = 64


EPSILON = 1e-05
SCALING = 0.125
NEGATIVE = -1000000000.0


def layer_norm_keep(values, norm_gain, norm_shift):
    centre = values - jnp.mean(values, axis=-1, keepdims=True)
    inverse = lax.rsqrt(jnp.mean(centre * centre, axis=-1, keepdims=True) + EPSILON)
    normal = centre * inverse
    return (normal * norm_gain + norm_shift, normal, inverse)


def layer_norm_back(upstream, normal, inverse, norm_gain):
    scaled = upstream * norm_gain
    gain_grad = jnp.sum(upstream * normal, axis=0)
    shift_grad = jnp.sum(upstream, axis=0)
    inner_term = (
        scaled
        - jnp.mean(scaled, axis=-1, keepdims=True)
        - normal * jnp.mean(scaled * normal, axis=-1, keepdims=True)
    )
    return (inverse * inner_term, gain_grad, shift_grad)


def heads_of(matrix):
    return matrix.reshape(matrix.shape[0], -1, HD)


def pick_queries(query_rows, type_row):
    word_tok = (type_row == 0)[:, None]
    return (
        jnp.where(word_tok, query_rows[0], query_rows[2]),
        jnp.where(word_tok, query_rows[1], query_rows[3]),
    )


def score_block(word_heads, entity_heads, key_heads, segment_row, type_row):
    to_words = jnp.einsum("qhd,khd->hqk", word_heads, key_heads, preferred_element_type=jnp.float32)
    to_entities = jnp.einsum(
        "qhd,khd->hqk", entity_heads, key_heads, preferred_element_type=jnp.float32
    )
    scores = jnp.where((type_row == 0)[None, None, :], to_words, to_entities) * SCALING
    allowed = (segment_row[:, None] == segment_row[None, :])[None]
    return jnp.where(allowed, scores, NEGATIVE)


def attend_forward(packed):
    query_rows, key_seq, value_seq, segment_row, type_row = packed
    word_query, entity_query = pick_queries(query_rows, type_row)
    scores = score_block(
        heads_of(word_query), heads_of(entity_query), heads_of(key_seq), segment_row, type_row
    )
    row_top = jnp.max(scores, axis=-1, keepdims=True)
    weights = jnp.exp(scores - row_top)
    totals = jnp.sum(weights, axis=-1, keepdims=True)
    attn_probs = (weights / totals).astype(jnp.bfloat16)
    context = jnp.einsum(
        "hqk,khd->qhd", attn_probs, heads_of(value_seq), preferred_element_type=jnp.float32
    )
    log_total = (row_top + jnp.log(totals))[..., 0]
    return (context.reshape(context.shape[0], -1).astype(jnp.bfloat16), log_total)


def attend_backward(packed):
    query_rows, key_seq, value_seq, segment_row, type_row, log_total, context_grad = packed
    word_query, entity_query = pick_queries(query_rows, type_row)
    word_heads = heads_of(word_query)
    entity_heads = heads_of(entity_query)
    key_heads = heads_of(key_seq)
    value_heads = heads_of(value_seq)
    grad_heads = heads_of(context_grad)
    scores = score_block(word_heads, entity_heads, key_heads, segment_row, type_row)
    attn_probs = jnp.exp(scores - log_total[..., None])
    prob_grad = jnp.einsum(
        "qhd,khd->hqk", grad_heads, value_heads, preferred_element_type=jnp.float32
    )
    score_grad = attn_probs * (prob_grad - jnp.sum(attn_probs * prob_grad, axis=-1, keepdims=True))
    score_low = score_grad.astype(jnp.bfloat16)
    word_key = (type_row == 0)[None, None, :]
    zeroes = jnp.zeros_like(score_low)
    word_part = jnp.where(word_key, score_low, zeroes)
    entity_part = jnp.where(word_key, zeroes, score_low)
    word_qgrad = (
        jnp.einsum("hqk,khd->qhd", word_part, key_heads, preferred_element_type=jnp.float32)
        * SCALING
    )
    entity_qgrad = (
        jnp.einsum("hqk,khd->qhd", entity_part, key_heads, preferred_element_type=jnp.float32)
        * SCALING
    )
    key_delta = (
        jnp.einsum("hqk,qhd->khd", word_part, word_heads, preferred_element_type=jnp.float32)
        + jnp.einsum("hqk,qhd->khd", entity_part, entity_heads, preferred_element_type=jnp.float32)
    ) * SCALING
    value_delta = jnp.einsum(
        "hqk,qhd->khd",
        attn_probs.astype(jnp.bfloat16),
        grad_heads,
        preferred_element_type=jnp.float32,
    )
    row_count = word_qgrad.shape[0]
    return (
        word_qgrad.reshape(row_count, -1),
        entity_qgrad.reshape(row_count, -1),
        key_delta.reshape(row_count, -1),
        value_delta.reshape(row_count, -1),
    )


def row_share(partial_rows):
    return lax.psum_scatter(partial_rows, "tensor", scatter_dimension=0, tiled=True)


def row_whole(rounded_rows):
    return lax.all_gather(rounded_rows, "tensor", axis=0, tiled=True)


def shards(
    layer_input,
    segment_ids,
    token_types,
    query_weight,
    key_weight,
    value_weight,
    out_weight,
    up_weight,
    down_weight,
    query_bias,
    value_bias,
    out_bias,
    up_bias,
    down_bias,
    attn_gain,
    attn_shift,
    ffn_gain,
    ffn_shift,
    cotangent,
):
    seq_count, seq_length, model_width = layer_input.shape
    tokens = layer_input.reshape(-1, model_width)
    row_count = tokens.shape[0]
    share = row_count // lax.axis_size("tensor")
    first_row = lax.axis_index("tensor") * share

    def own_rows(matrix):
        return lax.dynamic_slice_in_dim(matrix, first_row, share, 0)

    def combine_rows(partial_rows):
        return row_share(partial_rows)

    def whole_rows(rounded_rows):
        return row_whole(rounded_rows)

    query_complete, key_full, value_full, out_full = (
        lax.all_gather(query_weight.astype(jnp.bfloat16), "dp", axis=1, tiled=True),
        lax.all_gather(key_weight.astype(jnp.bfloat16), "dp", axis=0, tiled=True),
        lax.all_gather(value_weight.astype(jnp.bfloat16), "dp", axis=0, tiled=True),
        lax.all_gather(out_weight.astype(jnp.bfloat16), "dp", axis=1, tiled=True),
    )
    local_width = key_full.shape[1]
    query_rows = jnp.einsum(
        "gow,qwk->gqok", layer_input, query_complete, preferred_element_type=jnp.float32
    )
    query_rows = (query_rows + query_bias[None, :, None, :]).astype(jnp.bfloat16)
    keys_all = jnp.dot(layer_input, key_full, preferred_element_type=jnp.float32).astype(
        jnp.bfloat16
    )
    values_all = (
        jnp.dot(layer_input, value_full, preferred_element_type=jnp.float32) + value_bias
    ).astype(jnp.bfloat16)
    context, log_total = lax.map(
        attend_forward, (query_rows, keys_all, values_all, segment_ids, token_types)
    )
    context_rows = context.reshape(-1, local_width)
    attended = combine_rows(jnp.dot(context_rows, out_full, preferred_element_type=jnp.float32))
    residual = own_rows(tokens).astype(jnp.float32) + attended + out_bias
    normed, normal_one, inverse_one = layer_norm_keep(residual, attn_gain, attn_shift)
    normed_low = whole_rows(normed.astype(jnp.bfloat16))
    up_full, down_full = (
        lax.all_gather(up_weight.astype(jnp.bfloat16), "dp", axis=0, tiled=True),
        lax.all_gather(down_weight.astype(jnp.bfloat16), "dp", axis=1, tiled=True),
    )
    pre_act = jnp.dot(normed_low, up_full, preferred_element_type=jnp.float32) + up_bias
    activated, gelu_pull = jax.vjp(partial(jax.nn.gelu, approximate=False), pre_act)
    act_low = activated.astype(jnp.bfloat16)
    ffn_out = (
        combine_rows(jnp.dot(act_low, down_full, preferred_element_type=jnp.float32)) + down_bias
    )
    normed_out, normal_two, inverse_two = layer_norm_keep(normed + ffn_out, ffn_gain, ffn_shift)
    output = whole_rows(normed_out.astype(jnp.bfloat16)).reshape(layer_input.shape)
    upstream = own_rows(cotangent.reshape(-1, model_width)).astype(jnp.float32)
    sum_grad, ffngain_grad, ffnshift_grad = layer_norm_back(
        upstream, normal_two, inverse_two, ffn_gain
    )
    downbias_grad = jnp.sum(sum_grad, axis=0)
    sum_low = whole_rows(sum_grad.astype(jnp.bfloat16))
    up_back, down_back = (
        lax.all_gather(up_weight.astype(jnp.bfloat16), "dp", axis=0, tiled=True),
        lax.all_gather(down_weight.astype(jnp.bfloat16), "dp", axis=1, tiled=True),
    )
    down_local = jnp.dot(act_low.T, sum_low, preferred_element_type=jnp.float32)
    act_grad = jnp.dot(sum_low, down_back.T, preferred_element_type=jnp.float32)
    (pre_grad,) = gelu_pull(act_grad)
    upbias_grad = jnp.sum(pre_grad, axis=0)
    pre_low = pre_grad.astype(jnp.bfloat16)
    up_local = jnp.dot(normed_low.T, pre_low, preferred_element_type=jnp.float32)
    upproj_grad, downproj_grad = (
        lax.psum_scatter(up_local, "dp", scatter_dimension=0, tiled=True),
        lax.psum_scatter(down_local, "dp", scatter_dimension=1, tiled=True),
    )
    normed_grad = (
        combine_rows(jnp.dot(pre_low, up_back.T, preferred_element_type=jnp.float32)) + sum_grad
    )
    resid_grad, attngain_grad, attnshift_grad = layer_norm_back(
        normed_grad, normal_one, inverse_one, attn_gain
    )
    outbias_grad = jnp.sum(resid_grad, axis=0)
    resid_low = whole_rows(resid_grad.astype(jnp.bfloat16))
    query_pullback, key_pullback, value_pullback, out_back = (
        lax.all_gather(query_weight.astype(jnp.bfloat16), "dp", axis=1, tiled=True),
        lax.all_gather(key_weight.astype(jnp.bfloat16), "dp", axis=0, tiled=True),
        lax.all_gather(value_weight.astype(jnp.bfloat16), "dp", axis=0, tiled=True),
        lax.all_gather(out_weight.astype(jnp.bfloat16), "dp", axis=1, tiled=True),
    )
    outproj_local = jnp.dot(context_rows.T, resid_low, preferred_element_type=jnp.float32)
    context_grad = jnp.dot(resid_low, out_back.T, preferred_element_type=jnp.float32).astype(
        jnp.bfloat16
    )
    context_grad = context_grad.reshape(seq_count, seq_length, local_width)
    word_qgrad, entity_qgrad, key_delta, value_delta = lax.map(
        attend_backward,
        (query_rows, keys_all, values_all, segment_ids, token_types, log_total, context_grad),
    )
    is_word = (token_types == 0)[..., None]
    zero_rows = jnp.zeros_like(word_qgrad)
    query_delta = jnp.stack(
        [
            jnp.where(is_word, word_qgrad, zero_rows),
            jnp.where(is_word, entity_qgrad, zero_rows),
            jnp.where(is_word, zero_rows, word_qgrad),
            jnp.where(is_word, zero_rows, entity_qgrad),
        ],
        axis=1,
    )
    querybias_grad = jnp.sum(query_delta, axis=(0, 2))
    valuebias_grad = jnp.sum(value_delta, axis=(0, 1))
    query_reduced = query_delta.astype(jnp.bfloat16)
    key_reduced = key_delta.astype(jnp.bfloat16)
    value_reduced = value_delta.astype(jnp.bfloat16)
    query_local = jnp.einsum(
        "nvh,nkvw->khw", layer_input, query_reduced, preferred_element_type=jnp.float32
    )
    key_shard = jnp.einsum(
        "pui,pun->in", layer_input, key_reduced, preferred_element_type=jnp.float32
    )
    value_local = jnp.einsum(
        "pui,pun->in", layer_input, value_reduced, preferred_element_type=jnp.float32
    )
    input_part = (
        jnp.einsum(
            "kayo,azo->kyz", query_reduced, query_pullback, preferred_element_type=jnp.float32
        )
        + jnp.einsum("ohz,wz->ohw", key_reduced, key_pullback, preferred_element_type=jnp.float32)
        + jnp.einsum(
            "ohz,wz->ohw", value_reduced, value_pullback, preferred_element_type=jnp.float32
        )
    )
    input_total = combine_rows(input_part.reshape(-1, model_width))
    input_grad = whole_rows((input_total + resid_grad).astype(jnp.bfloat16)).reshape(
        layer_input.shape
    )
    query_grad, key_grad, value_grad, outproj_grad = (
        lax.psum_scatter(query_local, "dp", scatter_dimension=1, tiled=True),
        lax.psum_scatter(key_shard, "dp", scatter_dimension=0, tiled=True),
        lax.psum_scatter(value_local, "dp", scatter_dimension=0, tiled=True),
        lax.psum_scatter(outproj_local, "dp", scatter_dimension=1, tiled=True),
    )
    querybias_grad, valuebias_grad, upbias_grad = lax.psum(
        (querybias_grad, valuebias_grad, upbias_grad), "dp"
    )
    outbias_grad, downbias_grad, attngain_grad, attnshift_grad, ffngain_grad, ffnshift_grad = (
        lax.psum(
            (
                outbias_grad,
                downbias_grad,
                attngain_grad,
                attnshift_grad,
                ffngain_grad,
                ffnshift_grad,
            ),
            ("dp", "tensor"),
        )
    )
    return (
        output,
        input_grad,
        query_grad,
        key_grad,
        value_grad,
        outproj_grad,
        upproj_grad,
        downproj_grad,
        querybias_grad,
        valuebias_grad,
        outbias_grad,
        upbias_grad,
        downbias_grad,
        attngain_grad,
        attnshift_grad,
        ffngain_grad,
        ffnshift_grad,
    )


MESH = pl.DeviceIdType.MESH
BF = jnp.bfloat16
F32 = jnp.float32
BLOCK = 128


def fits(mesh):
    return mesh.shape["dp"] == 8 and mesh.shape["tensor"] == 4


def nn(a, b):
    return lax.dot_general(a, b, (((1,), (0,)), ((), ())), preferred_element_type=F32)


def nt(a, b):
    return lax.dot_general(a, b, (((1,), (1,)), ((), ())), preferred_element_type=F32)


def tn(a, b):
    return lax.dot_general(a, b, (((0,), (0,)), ((), ())), preferred_element_type=F32)


def norm_rows(values):
    centre = values - jnp.mean(values, axis=-1, keepdims=True)
    inverse = lax.rsqrt(jnp.mean(centre * centre, axis=-1, keepdims=True) + EPSILON)
    return centre * inverse, inverse


def norm_rows_back(upstream, normal, inverse, gain):
    scaled = upstream * gain
    return inverse * (
        scaled
        - jnp.mean(scaled, axis=-1, keepdims=True)
        - normal * jnp.mean(scaled * normal, axis=-1, keepdims=True)
    )


class Net:
    def __init__(self, send, recv, peer):
        self.send, self.recv, self.peer = send, recv, peer
        self.sends = 0
        self.locals = 0
        self.banks = 0
        self.pending = []

    def bank(self, count):
        base = self.banks
        self.banks += count
        return base

    def start(self, src, dst, sem, device, when=None, group=None):
        slot = self.sends % SENDS
        self.sends += 1
        self.finish([p for p in self.pending if p[3] == slot])

        def make():
            return pltpu.make_async_remote_copy(
                src_ref=src,
                dst_ref=dst,
                send_sem=self.send.at[slot],
                recv_sem=self.recv.at[sem],
                device_id=device,
                device_id_type=MESH,
            )

        if when is None:
            make().start()
        else:
            pl.when(when)(lambda: make().start())
        self.pending.append((make, when, group, slot))

    def finish(self, entries):
        for make, when, _, _ in entries:
            if when is None:
                make().wait_send()
            else:
                pl.when(when)(lambda make=make: make().wait_send())
        self.pending = [p for p in self.pending if p not in entries]

    def wait(self, dst, sem, when=None):
        def make():
            return pltpu.make_async_remote_copy(
                src_ref=dst,
                dst_ref=dst,
                send_sem=self.send.at[0],
                recv_sem=self.recv.at[sem],
                device_id=self.peer,
                device_id_type=MESH,
            )

        if when is None:
            make().wait_recv()
        else:
            pl.when(when)(lambda: make().wait_recv())

    def settle(self, *groups):
        self.finish([p for p in self.pending if not groups or p[2] in groups])


SENDS = 48
RECVS = 141


def layer_kernel(
    x_in, seg_ref, typ_ref, qw_in, kw_in, vw_in, ow_in, uw_in, dw_in, qb_ref, vb_ref,
    ob_ref, ub_ref, db_ref, ag_ref, as_ref, fg_ref, fs_ref, cot_in,
    out_end, ig_end, qg_end, kg_end, vg_end, og_end, ug_end, dg_end, small_end,
    x_ref, qw_ref, kw_ref, vw_ref, ow_ref, uw_ref, dw_ref, cot_ref,
    out_ref, ig_ref, qg_ref, kg_ref, vg_ref, og_ref, ug_ref, dg_ref, small_ref,
    wq, wop, wo, own, wf, ubs, segc, wordc, xt, bias, qq, kv, kk, kvt, kkt, probs, ctx, ctp, ct, ctc,
    a_s, n1_s, r1_s, act, gelu_d, gl, parts, rs_send, rs_recv, dub, dzb,
    st_a, st_b, st_c, st_d, st_e, st_f, st_g, dct, dc, dco, go_r, rp, sp, rz,
    dqkv, dx_in, dx_cross, dx_back, gq_r, gp, sv, small_s, small_r, sent8, sw, vz,
    send_sems, recv_sems, local_sems,
):
    d = lax.axis_index("dp")
    t = lax.axis_index("tensor")
    c = d % 2
    x = (d // 2) % 2
    y = d // 4
    pair = t % 2
    j = 2 * pair + c
    block = pair + 2 * c
    home = block == t
    zp = t + 1 - 2 * pair
    zq = (t + 2) % 4
    host = 2 * (d // 2) + t // 2
    chip = d // 2
    sib = d + 1 - 2 * c
    xn = d + 2 - 4 * x
    yn = d + 4 - 8 * y
    rows = x_ref.shape[1]
    quarter = rows // 4
    width = x_ref.shape[2]
    strip = qw_ref.shape[1]
    local = kw_ref.shape[1]
    heads = local // HD
    blocks = rows // BLOCK
    own_rows = pl.ds(pl.multiple_of(t * quarter, 16), quarter)
    net = Net(send_sems, recv_sems, (sib, t))

    def flip_x(device):
        return device + 2 - 4 * ((device // 2) % 2)

    def flip_y(device):
        return device + 4 - 8 * (device // 4)

    dg = flip_y(xn)
    part_m, part_o = parts.at[0:2], parts.at[2:4]
    sums_a, sums_b = parts.reshape(rows, width), gelu_d.reshape(rows, width)
    dqq = [sums_a.at[:, BLOCK * h : BLOCK * (h + 1)] for h in range(heads)]
    dkk = [sums_a.at[:, BLOCK * (heads + h) : BLOCK * (heads + h + 1)] for h in range(heads)]
    dvv = [sums_b.at[:, BLOCK * h : BLOCK * (h + 1)] for h in range(heads)]

    low_z = t < 2
    is_end = jnp.logical_or(t == 0, t == 3)
    is_mid = jnp.logical_not(is_end)
    z_out = jnp.where(low_z, t + 1, t - 1)
    z_back = jnp.where(low_z, 0, 3)

    def place(e):
        return jnp.where(low_z, e, 3 - e)

    def joint(one, other):
        return other if one is None else jnp.logical_and(one, other)

    class LineGather:
        def __init__(self, view, group=None):
            self.view, self.bank, self.group = view, net.bank(4), group

        def copy(self, owner, to, when):
            ref = self.view(owner)
            net.start(ref, ref, self.bank + owner, (d, to), when=when, group=self.group)

        def wait(self, owner, when=None):
            net.wait(self.view(owner), self.bank + owner, when=when)

        def begin(self):
            self.copy(t, z_out, None)
            self.copy(t, z_back, is_mid)

        def step(self, n):
            if n == 1:
                self.wait(place(0), is_mid)
                self.copy(place(0), z_out, is_mid)
                self.wait(place(2), is_mid)
                self.copy(place(2), z_back, is_mid)
            if n == 2:
                self.wait(place(3), is_mid)
                self.copy(place(3), z_back, is_mid)
            self.wait(place(n), is_end)

    class LineReduce:
        def __init__(self, own, came, cross, back):
            self.own, self.came, self.cross, self.back = own, came, cross, back
            self.in_b, self.cross_b, self.back_b = net.bank(3), net.bank(2), net.bank(1)

        def depart(self, e):
            net.start(self.own(e), self.came.at[e - 1], self.in_b + e - 1, (d, z_out), when=is_end)

        def add(self, e, ref):
            @pl.when(is_mid)
            def _():
                ref[...] = (self.own(e)[...].astype(F32) + ref[...].astype(F32)).astype(BF)

        def through(self, e):
            ref = self.came.at[e - 1]
            net.wait(ref, self.in_b + e - 1, when=is_mid)
            self.add(e, ref)
            net.start(ref, self.cross.at[3 - e], self.cross_b + 3 - e, (d, z_out), when=is_mid)

        def pass_back(self):
            net.wait(self.cross.at[0], self.cross_b, when=is_mid)
            self.add(0, self.cross.at[0])
            net.start(self.cross.at[0], self.back, self.back_b, (d, z_back), when=is_mid)

        def total(self):
            net.wait(self.came.at[0], self.in_b, when=is_mid)
            net.wait(self.cross.at[1], self.cross_b + 1, when=is_mid)
            net.wait(self.back, self.back_b, when=is_end)
            others = self.came[0].astype(F32) + self.cross[1].astype(F32)
            mine = self.own(jnp.where(is_mid, 1, 0))[...].astype(F32)
            return mine + jnp.where(is_mid, others, self.back[...].astype(F32))

    class Local:
        def __init__(self, source, target):
            self.copy = pltpu.make_async_copy(source, target, local_sems.at[net.locals])
            net.locals += 1
            self.copy.start()

        def wait(self):
            self.copy.wait()

    in_q, in_k, in_v = Local(qw_in, qw_ref), Local(kw_in, kw_ref), Local(vw_in, vw_ref)
    in_o, in_u, in_d = Local(ow_in, ow_ref), Local(uw_in, uw_ref), Local(dw_in, dw_ref)
    in_x, in_cot = Local(x_in, x_ref), Local(cot_in, cot_ref)

    barrier = pltpu.get_barrier_semaphore()
    for m in range(1, 8):
        pl.semaphore_signal(barrier, 1, device_id=((d + m) % 8, t), device_id_type=MESH)
    for k in range(1, 4):
        pl.semaphore_signal(barrier, 1, device_id=(d, (t + k) % 4), device_id_type=MESH)
    pl.semaphore_signal(barrier, 1, device_id=(sib, zq), device_id_type=MESH)

    for arrived in (in_q, in_k, in_v):
        arrived.wait()
    for h in range(heads):
        at = slice(HD * h, HD * (h + 1))
        piece = jnp.concatenate(
            [qw_ref[i, :, at] for i in range(4)] + [kw_ref[:, at], vw_ref[:, at]], axis=1
        )
        wq[d, :, 6 * HD * h : 6 * HD * (h + 1)] = piece.astype(BF)

    pl.semaphore_wait(barrier, 11)

    class PlaneGather:
        def __init__(self, group, *views):
            self.views, self.bank, self.group = views, net.bank(8 * len(views)), group

        def copy(self, view, block, device):
            ref = self.views[view](block)
            net.start(ref, ref, self.bank + 8 * view + block, (device, t), group=self.group)

        def wait(self, view, block):
            net.wait(self.views[view](block), self.bank + 8 * view + block)

        def begin(self):
            for view, device in ((0, yn), (1, xn), (1, yn), (0, xn), (0, sib), (1, sib)):
                self.copy(view, d, device)

        def middle(self):
            self.wait(0, yn)
            self.copy(0, yn, xn)
            self.wait(1, xn)
            self.copy(1, xn, yn)
            self.copy(0, yn, sib)
            self.copy(1, xn, sib)
            for view, block in ((1, yn), (0, xn)):
                self.wait(view, block)
                self.copy(view, block, sib)

        def late(self):
            for view in range(2):
                self.wait(view, dg)
                self.copy(view, dg, sib)

        def end(self):
            for block in (sib, flip_x(sib), flip_y(sib), flip_x(flip_y(sib))):
                for view in range(len(self.views)):
                    self.wait(view, block)

    gather_q = PlaneGather("q", lambda b: wq.at[b, : strip // 2], lambda b: wq.at[b, strip // 2 :])
    gather_q.begin()

    def wide_t(value, high, wide):
        r, w = value.shape
        if w < wide:
            value = jnp.concatenate([value, jnp.zeros((r, wide - w), value.dtype)], axis=1)
        if r < high:
            value = jnp.concatenate([value, jnp.zeros((high - r, wide), value.dtype)], axis=0)
        return value.T

    for arrived in (in_o, in_u, in_d):
        arrived.wait()
    def pack(block):
        most = block.shape[0] // 2
        rest = block[:, BLOCK:]
        return jnp.concatenate(
            [block[:, :BLOCK], jnp.concatenate([rest[:most], rest[most:]], axis=1)], axis=0
        )

    def rest_of(packed, count):
        below = packed[count:]
        return jnp.concatenate([below[:, :HD], below[: count - below.shape[0], HD:]], axis=0)

    wop[t, d] = pack(wide_t(ow_ref[...], 256, 128)[:strip, :local]).astype(BF)
    own[0] = uw_ref[...].astype(BF)
    own[1] = dw_ref[...].astype(BF)
    ubs[t] = jnp.broadcast_to(ub_ref[...][None], ubs.shape[1:])

    ub_z = net.bank(1)
    wf_a = net.bank(4)

    class ChipGather:
        def __init__(self, i):
            self.i, self.bank = i, net.bank(8)

        def send(self):
            i = self.i
            for plane, when in ((zq, None), (t, host != d)):
                net.start(own.at[i], wf.at[i, d], wf_a + 2 * i + c, (host, plane), when=when)

            @pl.when(host == d)
            def _():
                wf[i, d] = own[i]

        def copy(self, view, of, device):
            ref = wf.at[self.i, 2 * (of // 2) + view]
            net.start(ref, ref, self.bank + 2 * (of // 2) + view, (device, t), group="f")

        def wait(self, view, of):
            net.wait(wf.at[self.i, 2 * (of // 2) + view], self.bank + 2 * (of // 2) + view)

        def begin(self):
            i = self.i
            net.wait(wf.at[i, d], wf_a + 2 * i + c, when=jnp.logical_not(home))
            net.wait(wf.at[i, sib], wf_a + 2 * i + 1 - c)
            for view, device in ((0, yn), (1, xn), (1, yn), (0, xn)):
                self.copy(view, d, device)

        def middle(self):
            self.wait(0, yn)
            self.copy(0, yn, xn)
            self.wait(1, xn)
            self.copy(1, xn, yn)

        def end(self):
            for view, of in ((1, yn), (0, xn), (0, dg), (1, dg)):
                self.wait(view, of)

    up, down = ChipGather(0), ChipGather(1)
    wo_z = net.bank(1)
    for k in (2, 1, 3):
        net.start(wop.at[t, d], wop.at[t, d], wo_z, (d, (t + k) % 4))
    for b in range(blocks):
        at = slice(BLOCK * b, BLOCK * (b + 1))
        segc[at, :] = jnp.broadcast_to(seg_ref[:, at].astype(F32), (BLOCK, BLOCK)).T
        wordc[at, :] = jnp.broadcast_to((typ_ref[:, at] == 0).astype(F32), (BLOCK, BLOCK)).T
    in_x.wait()
    xt[...] = x_ref[0].T
    for h in range(heads):
        at = slice(HD * h, HD * (h + 1))
        bias[:, 6 * HD * h : 6 * HD * (h + 1)] = jnp.concatenate(
            [qb_ref[i : i + 1, at] for i in range(4)] + [jnp.zeros((1, HD), F32), vb_ref[at][None]],
            axis=1,
        )

    gather_q.middle()
    net.wait(wop.at[0:3, d], wo_z)
    gather_o = PlaneGather("o", lambda b: wop.at[0:2, b], lambda b: wop.at[2:4, b])
    gather_o.begin()
    up.send()
    net.start(ubs.at[t], ubs.at[t], ub_z, (d, zq))
    down.send()
    gather_q.late()
    gather_q.end()
    low_half = lax.broadcasted_iota(jnp.int32, (rows, BLOCK), 1) < HD
    is_word = wordc[...] > 0.5
    for h in range(heads):
        base = 6 * HD * h
        at = slice(BLOCK * h, BLOCK * (h + 1))
        made = nn(x_ref[0], wq[:, :, base : base + 6 * HD].reshape(width, 6 * HD))
        made = made + bias[:, base : base + 6 * HD]
        qq[:, at] = jnp.where(is_word, made[:, :BLOCK], made[:, BLOCK : 2 * BLOCK]).astype(BF)
        both = made[:, 2 * BLOCK :]
        keys = jnp.where(low_half, both, pltpu.roll(both, HD, 1))
        keys = jnp.where(jnp.logical_xor(is_word, low_half), 0.0, keys)
        kv[:, at] = both.astype(BF)
        kk[:, at] = keys.astype(BF)
        kvt[h] = both.T[HD:].astype(BF)
        kkt[h] = keys.T.astype(BF)

    gather_o.middle()
    up.begin()
    ct_z = net.bank(1)

    def span(b):
        return BLOCK * max(0, b - 2), BLOCK * min(blocks, b + 3)

    kept = [0]
    for b in range(blocks):
        kept.append(kept[-1] + span(b)[1] - span(b)[0])
    for b in range(blocks):
        lo, hi = span(b)
        at_q = slice(BLOCK * b, BLOCK * (b + 1))
        same = segc[lo:hi, :] == seg_ref[:, at_q].astype(F32)
        found = []
        for h in range(heads):
            at = slice(BLOCK * h, BLOCK * (h + 1))
            scores = nt(kk[lo:hi, at], qq[at_q, at]) * SCALING
            scores = jnp.where(same, scores, NEGATIVE)
            weights = jnp.exp(scores - jnp.max(scores, axis=0, keepdims=True))
            weights = weights * (1.0 / jnp.sum(weights, axis=0, keepdims=True))
            probs[h, kept[b] : kept[b + 1]] = weights
            found.append(nn(kvt[h, :, lo:hi], weights.astype(BF)))
        found.append(jnp.zeros((HD, BLOCK), F32))
        ctx[at_q, :] = jnp.concatenate(found, axis=0).T[:, :local].astype(BF)
        if b == 3:
            down.begin()
        if b > 0:
            s = b - 1
            ctp[s] = pack(ctx[quarter * s : quarter * (s + 1), :])
            net.start(ctp.at[s], ct.at[t], ct_z, (d, s), when=t != s)
    ct[t] = ctp[t]

    up.middle()
    gather_o.late()
    gather_o.end()
    for s in range(4):
        wo[:, :, BLOCK * s : BLOCK * (s + 1)] = wop[s, :, :strip]
    most = strip // 2
    for s in (0, 2):
        at = slice(4 * BLOCK + HD * s, 4 * BLOCK + HD * (s + 2))
        one, other = wop[s, :, strip:], wop[s + 1, :, strip:]
        wo[:, :most, at] = jnp.concatenate([one[:, :, :HD], other[:, :, :HD]], axis=2)
        wo[:, most:, at] = jnp.concatenate([one[:, :, HD:], other[:, :, HD:]], axis=2)
    net.wait(ct.at[0:3], ct_z)
    for s in range(4):
        ctc[:, BLOCK * s : BLOCK * (s + 1)] = ct[s, :quarter]
    for s in (0, 2):
        ctc[:, 4 * BLOCK + HD * s : 4 * BLOCK + HD * (s + 2)] = jnp.concatenate(
            [rest_of(ct[s], quarter), rest_of(ct[s + 1], quarter)], axis=1
        )
    whole_wo = wo.reshape(width, width)
    attended = nt(ctc[...], whole_wo[...])
    normal, inverse = norm_rows(x_ref[0, own_rows, :].astype(F32) + attended + ob_ref[...][None])
    n1_s[...] = normal
    r1_s[...] = jnp.broadcast_to(inverse, r1_s.shape)
    normed = normal * ag_ref[...][None] + as_ref[...][None]
    a_s[...] = normed
    act[j] = normed.astype(BF)

    def rows_of(ref, first, count):
        return lambda owner: ref.at[
            0, pl.ds(pl.multiple_of(owner * quarter + first, 16), count)
        ]

    part = quarter // 2
    chunk = [slice(part * q, part * (q + 1)) for q in range(2)]

    class RowGather:
        def __init__(self, ref):
            self.ref, self.bank = ref, net.bank(8)

        def copy(self, q, rank, device):
            ref = self.ref.at[rank, chunk[q]]
            net.start(ref, ref, self.bank + 4 * q + rank, device)

        def wait(self, q, rank):
            net.wait(self.ref.at[rank, chunk[q]], self.bank + 4 * q + rank)

        def begin(self, q):
            self.copy(q, j, (d, zp))
            self.copy(q, j, (sib, t))

        def near(self, q):
            self.wait(q, 2 * pair + 1 - c)

        def middle(self, q):
            self.wait(q, 2 - 2 * pair + c)
            self.copy(q, 2 - 2 * pair + c, (sib, t))

        def far(self, q):
            self.wait(q, 3 - 2 * pair - c)

    class RowSum:
        def __init__(self, index):
            self.index, self.bank = index, net.bank(6)

        def hand(self, q, slot, partial_rows):
            where = 3 * self.index + slot
            rs_send[where, chunk[q]] = partial_rows.astype(BF)
            net.start(
                rs_send.at[where, chunk[q]], rs_recv.at[where, chunk[q]], self.bank + 3 * q + slot,
                (d, zp) if slot == 2 else (sib, t),
            )

        def take(self, q, slot):
            where = 3 * self.index + slot
            net.wait(rs_recv.at[where, chunk[q]], self.bank + 3 * q + slot)
            return rs_recv[where, chunk[q]].astype(F32)

        def near(self, q):
            self.hand(q, 0, part_m[1 - c, chunk[q]])

        def away(self, q):
            self.hand(q, 1, part_o[1 - c, chunk[q]])

        def across(self, q):
            self.hand(q, 2, part_o[c, chunk[q]] + self.take(q, 1))

        def total(self, q):
            return part_m[c, chunk[q]] + self.take(q, 0) + self.take(q, 2)

    rows_a = RowGather(act)
    rows_a.begin(0)
    rows_a.begin(1)
    down.middle()
    rows_a.middle(0)
    rows_a.middle(1)
    rows_a.near(0)
    rows_a.near(1)
    net.wait(ubs.at[zq], ub_z)
    up.end()
    near = pl.ds(2 * pair, 2)
    away = pl.ds(2 - 2 * pair, 2)

    def feed(half):
        hidden = nn(act[half].reshape(2 * quarter, width), wf[0].reshape(width, width))
        hidden = hidden + ubs[block][:1]
        bell = 0.5 * (1.0 + lax.erf(hidden * 0.7071067811865476))
        slope = bell + hidden * (0.3989422804014327 * jnp.exp(-0.5 * hidden * hidden))
        gelu_d[half] = slope.reshape(2, quarter, width)
        gl[half] = (hidden * bell).astype(BF).reshape(2, quarter, width)

    def feed_out(half, partial_ref):
        made = nt(gl[half].reshape(2 * quarter, width), wf[1].reshape(width, width))
        partial_ref[...] = made.reshape(2, quarter, width)

    feed(near)
    rows_a.far(0)
    rows_a.far(1)
    feed(away)
    down.end()
    sum_f = RowSum(0)
    feed_out(away, part_o)
    sum_f.away(0)
    sum_f.away(1)
    feed_out(near, part_m)
    sum_f.across(0)
    sum_f.across(1)
    sum_f.near(0)
    sum_f.near(1)
    in_cot.wait()
    rows_u = RowGather(dub)
    gain_sum, shift_sum, bias_sum = 0.0, 0.0, 0.0
    for q in range(2):
        ffn_out = sum_f.total(q) + db_ref[...][None]
        normal, inverse = norm_rows(a_s[chunk[q]] + ffn_out)
        rows_q = pl.ds(pl.multiple_of(t * quarter + part * q, 16), part)
        out_ref[0, rows_q, :] = (normal * fg_ref[...][None] + fs_ref[...][None]).astype(BF)
        upstream = cot_ref[0, rows_q, :].astype(F32)
        du = norm_rows_back(upstream, normal, inverse, fg_ref[...][None])
        dub[j, chunk[q]] = du.astype(BF)
        rows_u.begin(q)
        a_s[chunk[q]] = du
        gain_sum = gain_sum + jnp.sum(upstream * normal, axis=0, keepdims=True)
        shift_sum = shift_sum + jnp.sum(upstream, axis=0, keepdims=True)
        bias_sum = bias_sum + jnp.sum(du, axis=0, keepdims=True)
    line_out = [LineGather(rows_of(out_ref, part * q, part)) for q in range(2)]
    line_out[0].begin()
    sv[...] = jnp.zeros_like(sv)
    sv[0:1] = gain_sum
    sv[1:2] = shift_sum
    sv[2:3] = bias_sum

    def feed_back(half, rows_q, partial_ref):
        count = 2 * (rows_q.stop - rows_q.start)
        made = nn(dub[half, rows_q].reshape(count, width), wf[1].reshape(width, width))
        made = made * gelu_d[half, rows_q].reshape(count, width)
        low = made.astype(BF)
        dzb[half, rows_q] = low.reshape(2, count // 2, width)
        partial_ref[:, rows_q] = nt(low, wf[0].reshape(width, width)).reshape(2, count // 2, width)
        return jnp.sum(made, axis=0, keepdims=True)

    sum_b = RowSum(1)
    rows_u.near(0)
    rows_u.near(1)
    up_sum = feed_back(near, slice(0, quarter), part_m)
    sum_b.near(0)
    sum_b.near(1)
    rows_u.middle(0)
    rows_u.far(0)
    up_sum = up_sum + feed_back(away, chunk[0], part_o)
    sum_b.away(0)
    rows_u.middle(1)
    sum_b.across(0)
    rows_u.far(1)
    up_sum = up_sum + feed_back(away, chunk[1], part_o)
    sum_b.away(1)
    sv[6:7] = up_sum
    half = width // 2

    class StripSum:
        def __init__(self, i):
            self.i, self.bank = i, net.bank(9)
            self.by_chip = wf.at[i].reshape(2, 2, 2, strip, width)

        def make(self, left, right):
            made = tn(left[...].reshape(4 * quarter, width), right[...].reshape(4 * quarter, width))
            wf[self.i] = made.astype(BF).reshape(8, strip, width)

        def begin(self):
            net.start(
                self.by_chip.at[:, 1 - x, :, :, :half], st_a.at[self.i], self.bank, (xn, t)
            )
            net.start(
                self.by_chip.at[1 - y, :, :, :, half:], st_b.at[self.i], self.bank + 1, (yn, t)
            )

        def turn(self):
            i = self.i
            net.wait(st_a.at[i], self.bank)
            st_a[i] = (st_a[i].astype(F32) + self.by_chip[:, x, :, :, :half].astype(F32)).astype(BF)
            for core in range(2):
                net.start(
                    st_a.at[i, 1 - y, core], st_c.at[i, c], self.bank + 2 + c,
                    (2 * (yn // 2) + core, t),
                )
            net.start(st_a.at[i, y, 1 - c], st_g.at[i, 0], self.bank + 6, (sib, t))
            net.wait(st_b.at[i], self.bank + 1)
            st_b[i] = (st_b[i].astype(F32) + self.by_chip[y, :, :, :, half:].astype(F32)).astype(BF)
            for core in range(2):
                net.start(
                    st_b.at[i, 1 - x, core], st_d.at[i, c], self.bank + 4 + c,
                    (2 * (xn // 2) + core, t),
                )
            net.start(st_b.at[i, x, 1 - c], st_g.at[i, 1], self.bank + 7, (sib, t))

        def gather(self):
            i = self.i
            for core in range(2):
                net.wait(st_c.at[i, core], self.bank + 2 + core)
                net.wait(st_d.at[i, core], self.bank + 4 + core)
            net.wait(st_g.at[i, 0], self.bank + 6)
            net.wait(st_g.at[i, 1], self.bank + 7)
            for whose, first, second in (
                (c, st_a.at[i, y, c], st_b.at[i, x, c]), (1 - c, st_g.at[i, 0], st_g.at[i, 1])
            ):
                st_e[i, whose, :, :half] = (
                    first[...].astype(F32) + st_c[i, whose].astype(F32)
                ).astype(BF)
                st_e[i, whose, :, half:] = (
                    second[...].astype(F32) + st_d[i, whose].astype(F32)
                ).astype(BF)

        def deliver(self, when=None):
            i = self.i
            net.start(st_e.at[i, 1 - t // 2], st_f.at[i], self.bank + 8, (d, zq), when=when)

        def total(self):
            i = self.i
            net.wait(st_f.at[i], self.bank + 8)
            return st_e[i, t // 2].astype(F32) + st_f[i].astype(F32)

    class SmallSum:
        def __init__(self, index):
            self.index, self.bank = index, net.bank(2)

        def begin(self, values):
            i = self.index
            small_s[i, 0] = values
            for r in (xn, yn, dg):
                net.start(small_s.at[i, 0], small_r.at[i, chip], self.bank, (r, t))
            small_r[i, chip] = values

        def plane(self):
            i = self.index
            net.wait(small_r.at[i, 0:3], self.bank)
            total = small_r[i, 0]
            for k in range(1, 4):
                total = total + small_r[i, k]
            small_s[i, 1] = total
            net.start(small_s.at[i, 1], small_r.at[i, 4], self.bank + 1, (sib, t))

        def cores(self):
            net.wait(small_r.at[self.index, 4], self.bank + 1)
            return small_s[self.index, 1], small_r[self.index, 4]

    net.settle("f")
    down_sum, up_sums = StripSum(1), StripSum(0)
    down_sum.make(dub, gl)
    down_sum.begin()
    sum_b.across(1)
    line_out[1].begin()
    up_sums.make(act, dzb)
    up_sums.begin()
    dc_z = net.bank(1)
    gain_sum, shift_sum, bias_sum, dhb = 0.0, 0.0, 0.0, []
    for q in range(2):
        da = a_s[chunk[q]] + sum_b.total(q)
        normal = n1_s[chunk[q]]
        dh = norm_rows_back(da, normal, r1_s[chunk[q], :1], ag_ref[...][None])
        a_s[chunk[q]] = dh
        dhb.append(dh.astype(BF))
        made = nn(dhb[q], whole_wo[...])
        for s in range(4):
            rest = made[:, 4 * BLOCK + HD * s : 4 * BLOCK + HD * (s + 1)]
            rest = jnp.concatenate([rest, jnp.zeros((16, HD), F32)], axis=0)
            most = (part + 16) // 2
            dct[s, q] = jnp.concatenate(
                [
                    made[:, BLOCK * s : BLOCK * (s + 1)],
                    jnp.concatenate([rest[:most], rest[most:]], axis=1),
                ],
                axis=0,
            ).astype(BF)
        for k in (2, 1, 3):
            s = (t + k) % 4
            net.start(dct.at[s, q], dc.at[t, q], dc_z, (d, s))
        dc[t, q] = dct[t, q]
        gain_sum = gain_sum + jnp.sum(da * normal, axis=0, keepdims=True)
        shift_sum = shift_sum + jnp.sum(da, axis=0, keepdims=True)
        bias_sum = bias_sum + jnp.sum(dh, axis=0, keepdims=True)
    dhb = jnp.concatenate(dhb, axis=0)
    line_out[0].step(1)
    line_out[1].step(1)
    sv[3:4] = gain_sum
    sv[4:5] = shift_sum
    sv[5:6] = bias_sum
    small_a = SmallSum(0)
    small_a.begin(sv[...])
    down_sum.turn()
    wo[...] = tn(dhb, ctc[...]).astype(BF).reshape(8, strip, width)
    by_core = wo.reshape(4, 2, strip, width)
    go_b = net.bank(1)
    net.start(by_core.at[:, 1 - c], go_r, go_b, (sib, t))

    net.wait(dc.at[0:3], dc_z)
    up_sums.turn()
    net.wait(go_r, go_b)
    go_r[...] = (by_core[:, c].astype(F32) + go_r[...].astype(F32)).astype(BF)
    rp_b = net.bank(1)
    for r in (xn, yn, dg):
        net.start(go_r.at[r // 2], rp.at[chip], rp_b, (r, t))
    rp[chip] = go_r[chip]
    upper = lax.broadcasted_iota(jnp.int32, (part, BLOCK), 1) >= HD
    for s in range(4):
        for q in range(2):
            got = dc[s, q]
            at_q = slice(quarter * s + part * q, quarter * s + part * (q + 1))
            first = got[:part].astype(F32)
            blank = jnp.zeros((part, HD), BF)
            dco[at_q, :BLOCK] = jnp.concatenate([blank, got[:part, :HD]], axis=1)
            dco[at_q, BLOCK : 2 * BLOCK] = jnp.where(upper, first, 0.0).astype(BF)
            dco[at_q, 2 * BLOCK :] = jnp.concatenate([blank, rest_of(got, part)], axis=1)
    for h in range(heads):
        dkk[h][...] = jnp.zeros((rows, BLOCK), F32)
        dvv[h][...] = jnp.zeros((rows, BLOCK), F32)
    for b in range(blocks):
        lo, hi = span(b)
        at_q = slice(BLOCK * b, BLOCK * (b + 1))
        for h in range(heads):
            at = slice(BLOCK * h, BLOCK * (h + 1))
            weights = probs[h, kept[b] : kept[b + 1]]
            dp = nt(kv[lo:hi, at], dco[at_q, at])
            ds = weights * (dp - jnp.sum(weights * dp, axis=0, keepdims=True))
            dsb = ds.astype(BF)
            dkk[h][lo:hi] += nn(dsb, qq[at_q, at])
            dvv[h][lo:hi] += nn(weights.astype(BF), dco[at_q, at])
            dqq[h][at_q] = nn(kkt[h, :, lo:hi], dsb).T * SCALING

    down_sum.gather()
    down_sum.deliver()
    small_a.plane()
    for h in range(heads):
        base = 6 * HD * h
        first = jnp.where(is_word, dqq[h][...], 0.0)
        second = jnp.where(is_word, 0.0, dqq[h][...])
        keys = dkk[h][...]
        keys = jnp.where(is_word, keys, pltpu.roll(keys, HD, 1)) * SCALING
        third = jnp.where(low_half, keys, dvv[h][...])
        for i, piece in enumerate((first, second, third)):
            at = slice(base + BLOCK * i, base + BLOCK * (i + 1))
            dqkv[:, at] = piece.astype(BF)
            row, col = divmod(base + BLOCK * i, width)
            sv[row : row + 1, col : col + BLOCK] = jnp.sum(piece, axis=0, keepdims=True)

    first_rows = pl.ds(pl.multiple_of(jnp.where(low_z, rows // 2, 0), 16), rows // 2)
    other_rows = pl.ds(pl.multiple_of(jnp.where(low_z, 0, rows // 2), 16), rows // 2)
    first_two = pl.ds(jnp.where(low_z, 2, 0), 2)
    other_two = pl.ds(jnp.where(low_z, 0, 2), 2)

    def back_to_input(rows_b, quarters):
        made = nt(dqkv[rows_b, :], wq[...].reshape(width, 6 * local))
        dzb[quarters] = made.astype(BF).reshape(2, quarter, width)

    line_dx, line_in = [], []
    for q in range(2):
        cut = pl.ds(part * q, part)
        line_dx.append(
            LineReduce(
                lambda e, cut=cut: dzb.at[place(e), cut],
                dx_in.at[q], dx_cross.at[q], dx_back.at[q],
            )
        )
        line_in.append(LineGather(rows_of(ig_ref, part * q, part)))

    def arrive(q):
        total = line_dx[q].total() + a_s[part * q : part * (q + 1)]
        ig_ref[0, pl.ds(pl.multiple_of(t * quarter + part * q, 16), part)] = total.astype(BF)
        line_in[q].begin()

    back_to_input(first_rows, first_two)
    for q, e in ((0, 3), (0, 2), (1, 3), (1, 2)):
        line_dx[q].depart(e)
    plane_sum, other_sum = small_a.cores()
    first_core = c == 0
    own_units, other_units = plane_sum[6:7], other_sum[6:7]
    sent8[0:6] = plane_sum[0:6] + other_sum[0:6]
    sent8[6:7] = jnp.where(first_core, own_units, other_units)
    sent8[7:8] = jnp.where(first_core, other_units, own_units)
    vz_b = net.bank(2)
    for k in (2, 1, 3):
        net.start(sent8, vz.at[t], vz_b, (d, (t + k) % 4), when=first_core)
    vz[t] = sent8[...]
    back_to_input(other_rows, other_two)
    line_dx[0].depart(1)
    line_dx[1].depart(1)
    up_sums.gather()
    up_sums.deliver(is_mid)
    small_b = SmallSum(1)
    small_b.begin(sv[...])

    net.settle("q")
    wq[...] = nn(xt[...], dqkv[...]).astype(BF).reshape(8, strip, 6 * local)
    q_by_core = wq.reshape(4, 2, strip, 6 * local)
    gq_b = net.bank(1)
    net.start(q_by_core.at[:, 1 - c], gq_r, gq_b, (sib, t))
    line_out[0].step(2)
    line_out[1].step(2)
    line_dx[0].through(3)
    line_dx[0].through(2)
    net.wait(gq_r, gq_b)
    gq_r[...] = (q_by_core[:, c].astype(F32) + gq_r[...].astype(F32)).astype(BF)
    gp_b = net.bank(1)
    for r in (xn, yn, dg):
        net.start(gq_r.at[r // 2], gp.at[chip], gp_b, (r, t))
    gp[chip] = gq_r[chip]

    line_dx[0].pass_back()
    net.wait(rp.at[0:3], rp_b)
    total = rp[0].astype(F32)
    for k in range(1, 4):
        total = total + rp[k].astype(F32)
    for s in range(4):
        rest = total[:, 4 * BLOCK + HD * s : 4 * BLOCK + HD * (s + 1)]
        sp[s] = pack(
            jnp.concatenate([total[:, BLOCK * s : BLOCK * (s + 1)], rest], axis=1)
        ).astype(BF)
    rz_b = net.bank(1)
    rz[t] = sp[t]

    def send_rz(when):
        for k in range(1, 4):
            s = (t + k) % 4
            net.start(sp.at[s], rz.at[t], rz_b, (d, s), when=when)

    line_dx[1].through(3)
    line_dx[1].through(2)
    line_dx[1].pass_back()
    send_rz(is_mid)
    arrive(0)
    arrive(1)

    up_sums.deliver(is_end)
    send_rz(is_end)
    line_in[0].step(1)
    line_in[1].step(1)
    line_out[0].step(3)
    line_out[1].step(3)
    ends = [Local(out_ref, out_end)]
    line_in[0].step(2)
    line_in[1].step(2)
    small_b.plane()
    net.wait(vz.at[0:3], vz_b, when=first_core)

    @pl.when(first_core)
    def _():
        total = vz[0]
        for k in range(1, 4):
            total = total + vz[k]
        sw[0:6] = total[0:6]
        units = vz[t] + vz[zq]
        sw[6:7] = jnp.where(t < 2, units[6:7], units[7:8])
        sw[7:8] = units[7:8]

    net.start(sw, sw, vz_b + 1, (sib, t), when=first_core)
    net.wait(sw, vz_b + 1, when=c == 1)
    small_ref[0:8] = sw[...]
    plane_sum, other_sum = small_b.cores()
    small_ref[8:16] = plane_sum + other_sum
    dg_ref[...] = down_sum.total()
    ug_ref[...] = up_sums.total()
    ends += [Local(dg_ref, dg_end), Local(ug_ref, ug_end), Local(small_ref, small_end)]
    net.wait(rz.at[0:3], rz_b)
    total = rz[0].astype(F32)
    for s in range(1, 4):
        total = total + rz[s].astype(F32)
    total = jnp.concatenate([total[:strip], rest_of(total, strip)], axis=1)
    og_ref[...] = wide_t(total, BLOCK, 256)[:local, :strip]

    ends += [Local(og_ref, og_end)]
    net.wait(gp.at[0:3], gp_b)
    total = gp[0].astype(F32)
    for k in range(1, 4):
        total = total + gp[k].astype(F32)
    for h in range(heads):
        base = 6 * HD * h
        at = slice(HD * h, HD * (h + 1))
        for i in range(4):
            qg_ref[i, :, at] = total[:, base + HD * i : base + HD * (i + 1)]
        kg_ref[:, at] = total[:, base + 4 * HD : base + 5 * HD]
        vg_ref[:, at] = total[:, base + 5 * HD : base + 6 * HD]

    ends += [Local(qg_ref, qg_end), Local(kg_ref, kg_end), Local(vg_ref, vg_end)]
    for q in range(2):
        line_in[q].step(3)
    ends += [Local(ig_ref, ig_end)]
    net.settle()
    for copy in ends:
        copy.wait()
    assert net.banks == RECVS, net.banks


def end_kernel(*refs):
    sources, small = refs[:8], refs[8]
    targets, (qbg, vbg), vectors = refs[9:17], refs[17:19], refs[19:26]
    for source, target in zip(sources, targets):
        target[...] = source[...]
    fgg, fsg, dbg, agg, asg, obg, ubg = (small[i] for i in range(7))
    for ref, value in zip(vectors, (obg, ubg, dbg, agg, asg, fgg, fsg)):
        ref[...] = value
    width = small.shape[1]
    values = []
    for h in range(vbg.shape[0] // HD):
        row, col = divmod(6 * HD * h, width)
        piece = small[8 + row : 9 + row, col : col + 6 * HD]
        for i in range(4):
            qbg[i : i + 1, HD * h : HD * (h + 1)] = piece[:, HD * i : HD * (i + 1)]
        values.append(piece[:, 5 * HD :])
    vbg[...] = jnp.concatenate(values, axis=1)[0]


def fused(
    layer_input, segment_ids, token_types, query_weight, key_weight, value_weight, out_weight,
    up_weight, down_weight, query_bias, value_bias, out_bias, up_bias, down_bias, attn_gain,
    attn_shift, ffn_gain, ffn_shift, cotangent,
):
    rows, width = layer_input.shape[1:]
    strip, local = key_weight.shape
    quarter, heads, blocks = rows // 4, local // HD, rows // BLOCK
    kept = sum(BLOCK * (min(blocks, b + 3) - max(0, b - 2)) for b in range(blocks))
    args = [
        layer_input, segment_ids, token_types, query_weight, key_weight, value_weight, out_weight,
        up_weight, down_weight.T, query_bias, value_bias, out_bias, up_bias, down_bias, attn_gain,
        attn_shift, ffn_gain, ffn_shift, cotangent,
    ]

    def like(v, dtype=F32):
        return jax.ShapeDtypeStruct(v.shape, dtype)

    outs = [
        like(layer_input, BF), like(layer_input, BF), like(query_weight), like(key_weight),
        like(value_weight), like(out_weight), like(up_weight), jax.ShapeDtypeStruct((strip, width), F32),
        jax.ShapeDtypeStruct((16, width), F32),
    ]
    v = pltpu.VMEM
    scratch = [
        v(layer_input.shape, BF), v(query_weight.shape, F32), v(key_weight.shape, F32),
        v(value_weight.shape, F32), v(out_weight.shape, F32), v(up_weight.shape, F32),
        v((strip, width), F32), v(cotangent.shape, BF),
    ] + [v(o.shape, o.dtype) for o in outs] + [
        v((8, strip, 6 * local), BF), v((4, 8, 3 * strip // 2, BLOCK), BF), v((8, strip, width), BF),
        v((2, strip, width), BF),
        v((2, 8, strip, width), BF), v((4, 8, width), F32), v((rows, BLOCK), F32),
        v((rows, BLOCK), F32), v((width, rows), BF), v((1, 6 * local), F32),
        v((rows, heads * BLOCK), BF), v((rows, heads * BLOCK), BF), v((rows, heads * BLOCK), BF),
        v((heads, HD, rows), BF), v((heads, BLOCK, rows), BF),
        v((heads, kept, BLOCK), F32), v((rows, local), BF), v((4, 3 * quarter // 2, BLOCK), BF),
        v((4, 3 * quarter // 2, BLOCK), BF), v((quarter, width), BF),
        v((quarter, width), F32), v((quarter, width), F32), v((quarter, BLOCK), F32),
        v((4, quarter, width), BF), v((4, quarter, width), F32), v((4, quarter, width), BF),
        v((4, quarter, width), F32),
        v((6, quarter, width), BF), v((6, quarter, width), BF),
        v((4, quarter, width), BF), v((4, quarter, width), BF),
        v((2, 2, 2, strip, width // 2), BF), v((2, 2, 2, strip, width // 2), BF),
        v((2, 2, strip, width // 2), BF), v((2, 2, strip, width // 2), BF),
        v((2, 2, strip, width), BF), v((2, strip, width), BF),
        v((2, 2, strip, width // 2), BF),
        v((4, 2, BLOCK, BLOCK), BF), v((4, 2, BLOCK, BLOCK), BF),
        v((rows, heads * BLOCK), BF),
        v((4, strip, width), BF), v((4, strip, width), BF), v((4, 3 * strip // 2, BLOCK), BF),
        v((4, 3 * strip // 2, BLOCK), BF),
        v((rows, 6 * local), BF),
        v((2, 3, quarter // 2, width), BF), v((2, 2, quarter // 2, width), BF),
        v((2, quarter // 2, width), BF),
        v((4, strip, 6 * local), BF), v((4, strip, 6 * local), BF),
        v((8, width), F32), v((2, 2, 8, width), F32), v((2, 5, 8, width), F32),
        v((8, width), F32), v((8, width), F32), v((4, 8, width), F32),
        pltpu.SemaphoreType.DMA((SENDS,)), pltpu.SemaphoreType.DMA((RECVS,)),
        pltpu.SemaphoreType.DMA((17,)),
    ]
    spec = pl.BlockSpec(memory_space=pltpu.VMEM)
    anywhere = pl.BlockSpec(memory_space=pl.ANY)
    large_args = (0, 3, 4, 5, 6, 7, 8, 18)
    made = pl.pallas_call(
        layer_kernel,
        out_shape=outs,
        in_specs=[anywhere if n in large_args else spec for n in range(len(args))],
        out_specs=[anywhere] * len(outs),
        scratch_shapes=scratch,
        compiler_params=pltpu.CompilerParams(
            collective_id=0, has_side_effects=True, vmem_limit_bytes=58 << 20
        ),
        name="layer",
    )(*args)
    *large, small = made
    vector = jax.ShapeDtypeStruct((width,), F32)
    ended = pl.pallas_call(
        end_kernel,
        out_shape=[like(v, v.dtype) for v in large]
        + [like(query_bias), jax.ShapeDtypeStruct((local,), F32)]
        + [vector] * 7,
        in_specs=[spec] * len(made),
        out_specs=[spec] * 17,
        name="finish",
    )(*large, small)
    return (*ended[:7], ended[7].T, *ended[8:])


def solution(mesh):
    in_specs = (
        P("dp", None, None),
        P("dp", None),
        P("dp", None),
        P(None, "dp", "tensor"),
        P("dp", "tensor"),
        P("dp", "tensor"),
        P("tensor", "dp"),
        P("dp", "tensor"),
        P("tensor", "dp"),
        P(None, "tensor"),
        P("tensor"),
        P(),
        P("tensor"),
        P(),
        P(),
        P(),
        P(),
        P(),
        P("dp", None, None),
    )
    out_specs = (
        P("dp", None, None),
        P("dp", None, None),
        P(None, "dp", "tensor"),
        P("dp", "tensor"),
        P("dp", "tensor"),
        P("tensor", "dp"),
        P("dp", "tensor"),
        P("tensor", "dp"),
        P(None, "tensor"),
        P("tensor"),
        P(),
        P("tensor"),
        P(),
        P(),
        P(),
        P(),
        P(),
    )
    step = fused if fits(mesh) else shards
    return jax.shard_map(step, mesh=mesh, in_specs=in_specs, out_specs=out_specs, check_vma=False)
```

```python
from functools import partial

import jax
import jax.numpy as jnp
from jax import lax
from jax.experimental import pallas as pl
from jax.experimental.pallas import tpu as pltpu
from jax.sharding import PartitionSpec as P

HD = 64


EPSILON = 1e-05
SCALING = 0.125
NEGATIVE = -1000000000.0


def layer_norm_keep(values, norm_gain, norm_shift):
    centre = values - jnp.mean(values, axis=-1, keepdims=True)
    inverse = lax.rsqrt(jnp.mean(centre * centre, axis=-1, keepdims=True) + EPSILON)
    normal = centre * inverse
    return (normal * norm_gain + norm_shift, normal, inverse)


def layer_norm_back(upstream, normal, inverse, norm_gain):
    scaled = upstream * norm_gain
    gain_grad = jnp.sum(upstream * normal, axis=0)
    shift_grad = jnp.sum(upstream, axis=0)
    inner_term = (
        scaled
        - jnp.mean(scaled, axis=-1, keepdims=True)
        - normal * jnp.mean(scaled * normal, axis=-1, keepdims=True)
    )
    return (inverse * inner_term, gain_grad, shift_grad)


def heads_of(matrix):
    return matrix.reshape(matrix.shape[0], -1, HD)


def pick_queries(query_rows, type_row):
    word_tok = (type_row == 0)[:, None]
    return (
        jnp.where(word_tok, query_rows[0], query_rows[2]),
        jnp.where(word_tok, query_rows[1], query_rows[3]),
    )


def score_block(word_heads, entity_heads, key_heads, segment_row, type_row):
    to_words = jnp.einsum("qhd,khd->hqk", word_heads, key_heads, preferred_element_type=jnp.float32)
    to_entities = jnp.einsum(
        "qhd,khd->hqk", entity_heads, key_heads, preferred_element_type=jnp.float32
    )
    scores = jnp.where((type_row == 0)[None, None, :], to_words, to_entities) * SCALING
    allowed = (segment_row[:, None] == segment_row[None, :])[None]
    return jnp.where(allowed, scores, NEGATIVE)


def attend_forward(packed):
    query_rows, key_seq, value_seq, segment_row, type_row = packed
    word_query, entity_query = pick_queries(query_rows, type_row)
    scores = score_block(
        heads_of(word_query), heads_of(entity_query), heads_of(key_seq), segment_row, type_row
    )
    row_top = jnp.max(scores, axis=-1, keepdims=True)
    weights = jnp.exp(scores - row_top)
    totals = jnp.sum(weights, axis=-1, keepdims=True)
    attn_probs = (weights / totals).astype(jnp.bfloat16)
    context = jnp.einsum(
        "hqk,khd->qhd", attn_probs, heads_of(value_seq), preferred_element_type=jnp.float32
    )
    log_total = (row_top + jnp.log(totals))[..., 0]
    return (context.reshape(context.shape[0], -1).astype(jnp.bfloat16), log_total)


def attend_backward(packed):
    query_rows, key_seq, value_seq, segment_row, type_row, log_total, context_grad = packed
    word_query, entity_query = pick_queries(query_rows, type_row)
    word_heads = heads_of(word_query)
    entity_heads = heads_of(entity_query)
    key_heads = heads_of(key_seq)
    value_heads = heads_of(value_seq)
    grad_heads = heads_of(context_grad)
    scores = score_block(word_heads, entity_heads, key_heads, segment_row, type_row)
    attn_probs = jnp.exp(scores - log_total[..., None])
    prob_grad = jnp.einsum(
        "qhd,khd->hqk", grad_heads, value_heads, preferred_element_type=jnp.float32
    )
    score_grad = attn_probs * (prob_grad - jnp.sum(attn_probs * prob_grad, axis=-1, keepdims=True))
    score_low = score_grad.astype(jnp.bfloat16)
    word_key = (type_row == 0)[None, None, :]
    zeroes = jnp.zeros_like(score_low)
    word_part = jnp.where(word_key, score_low, zeroes)
    entity_part = jnp.where(word_key, zeroes, score_low)
    word_qgrad = (
        jnp.einsum("hqk,khd->qhd", word_part, key_heads, preferred_element_type=jnp.float32)
        * SCALING
    )
    entity_qgrad = (
        jnp.einsum("hqk,khd->qhd", entity_part, key_heads, preferred_element_type=jnp.float32)
        * SCALING
    )
    key_delta = (
        jnp.einsum("hqk,qhd->khd", word_part, word_heads, preferred_element_type=jnp.float32)
        + jnp.einsum("hqk,qhd->khd", entity_part, entity_heads, preferred_element_type=jnp.float32)
    ) * SCALING
    value_delta = jnp.einsum(
        "hqk,qhd->khd",
        attn_probs.astype(jnp.bfloat16),
        grad_heads,
        preferred_element_type=jnp.float32,
    )
    row_count = word_qgrad.shape[0]
    return (
        word_qgrad.reshape(row_count, -1),
        entity_qgrad.reshape(row_count, -1),
        key_delta.reshape(row_count, -1),
        value_delta.reshape(row_count, -1),
    )


def row_share(partial_rows):
    return lax.psum_scatter(partial_rows, "tensor", scatter_dimension=0, tiled=True)


def row_whole(rounded_rows):
    return lax.all_gather(rounded_rows, "tensor", axis=0, tiled=True)


def shards(
    layer_input,
    segment_ids,
    token_types,
    query_weight,
    key_weight,
    value_weight,
    out_weight,
    up_weight,
    down_weight,
    query_bias,
    value_bias,
    out_bias,
    up_bias,
    down_bias,
    attn_gain,
    attn_shift,
    ffn_gain,
    ffn_shift,
    cotangent,
):
    seq_count, seq_length, model_width = layer_input.shape
    tokens = layer_input.reshape(-1, model_width)
    row_count = tokens.shape[0]
    share = row_count // lax.axis_size("tensor")
    first_row = lax.axis_index("tensor") * share

    def own_rows(matrix):
        return lax.dynamic_slice_in_dim(matrix, first_row, share, 0)

    def combine_rows(partial_rows):
        return row_share(partial_rows)

    def whole_rows(rounded_rows):
        return row_whole(rounded_rows)

    query_complete, key_full, value_full, out_full = (
        lax.all_gather(query_weight.astype(jnp.bfloat16), "dp", axis=1, tiled=True),
        lax.all_gather(key_weight.astype(jnp.bfloat16), "dp", axis=0, tiled=True),
        lax.all_gather(value_weight.astype(jnp.bfloat16), "dp", axis=0, tiled=True),
        lax.all_gather(out_weight.astype(jnp.bfloat16), "dp", axis=1, tiled=True),
    )
    local_width = key_full.shape[1]
    query_rows = jnp.einsum(
        "gow,qwk->gqok", layer_input, query_complete, preferred_element_type=jnp.float32
    )
    query_rows = (query_rows + query_bias[None, :, None, :]).astype(jnp.bfloat16)
    keys_all = jnp.dot(layer_input, key_full, preferred_element_type=jnp.float32).astype(
        jnp.bfloat16
    )
    values_all = (
        jnp.dot(layer_input, value_full, preferred_element_type=jnp.float32) + value_bias
    ).astype(jnp.bfloat16)
    context, log_total = lax.map(
        attend_forward, (query_rows, keys_all, values_all, segment_ids, token_types)
    )
    context_rows = context.reshape(-1, local_width)
    attended = combine_rows(jnp.dot(context_rows, out_full, preferred_element_type=jnp.float32))
    residual = own_rows(tokens).astype(jnp.float32) + attended + out_bias
    normed, normal_one, inverse_one = layer_norm_keep(residual, attn_gain, attn_shift)
    normed_low = whole_rows(normed.astype(jnp.bfloat16))
    up_full, down_full = (
        lax.all_gather(up_weight.astype(jnp.bfloat16), "dp", axis=0, tiled=True),
        lax.all_gather(down_weight.astype(jnp.bfloat16), "dp", axis=1, tiled=True),
    )
    pre_act = jnp.dot(normed_low, up_full, preferred_element_type=jnp.float32) + up_bias
    activated, gelu_pull = jax.vjp(partial(jax.nn.gelu, approximate=False), pre_act)
    act_low = activated.astype(jnp.bfloat16)
    ffn_out = (
        combine_rows(jnp.dot(act_low, down_full, preferred_element_type=jnp.float32)) + down_bias
    )
    normed_out, normal_two, inverse_two = layer_norm_keep(normed + ffn_out, ffn_gain, ffn_shift)
    output = whole_rows(normed_out.astype(jnp.bfloat16)).reshape(layer_input.shape)
    upstream = own_rows(cotangent.reshape(-1, model_width)).astype(jnp.float32)
    sum_grad, ffngain_grad, ffnshift_grad = layer_norm_back(
        upstream, normal_two, inverse_two, ffn_gain
    )
    downbias_grad = jnp.sum(sum_grad, axis=0)
    sum_low = whole_rows(sum_grad.astype(jnp.bfloat16))
    up_back, down_back = (
        lax.all_gather(up_weight.astype(jnp.bfloat16), "dp", axis=0, tiled=True),
        lax.all_gather(down_weight.astype(jnp.bfloat16), "dp", axis=1, tiled=True),
    )
    down_local = jnp.dot(act_low.T, sum_low, preferred_element_type=jnp.float32)
    act_grad = jnp.dot(sum_low, down_back.T, preferred_element_type=jnp.float32)
    (pre_grad,) = gelu_pull(act_grad)
    upbias_grad = jnp.sum(pre_grad, axis=0)
    pre_low = pre_grad.astype(jnp.bfloat16)
    up_local = jnp.dot(normed_low.T, pre_low, preferred_element_type=jnp.float32)
    upproj_grad, downproj_grad = (
        lax.psum_scatter(up_local, "dp", scatter_dimension=0, tiled=True),
        lax.psum_scatter(down_local, "dp", scatter_dimension=1, tiled=True),
    )
    normed_grad = (
        combine_rows(jnp.dot(pre_low, up_back.T, preferred_element_type=jnp.float32)) + sum_grad
    )
    resid_grad, attngain_grad, attnshift_grad = layer_norm_back(
        normed_grad, normal_one, inverse_one, attn_gain
    )
    outbias_grad = jnp.sum(resid_grad, axis=0)
    resid_low = whole_rows(resid_grad.astype(jnp.bfloat16))
    query_pullback, key_pullback, value_pullback, out_back = (
        lax.all_gather(query_weight.astype(jnp.bfloat16), "dp", axis=1, tiled=True),
        lax.all_gather(key_weight.astype(jnp.bfloat16), "dp", axis=0, tiled=True),
        lax.all_gather(value_weight.astype(jnp.bfloat16), "dp", axis=0, tiled=True),
        lax.all_gather(out_weight.astype(jnp.bfloat16), "dp", axis=1, tiled=True),
    )
    outproj_local = jnp.dot(context_rows.T, resid_low, preferred_element_type=jnp.float32)
    context_grad = jnp.dot(resid_low, out_back.T, preferred_element_type=jnp.float32).astype(
        jnp.bfloat16
    )
    context_grad = context_grad.reshape(seq_count, seq_length, local_width)
    word_qgrad, entity_qgrad, key_delta, value_delta = lax.map(
        attend_backward,
        (query_rows, keys_all, values_all, segment_ids, token_types, log_total, context_grad),
    )
    is_word = (token_types == 0)[..., None]
    zero_rows = jnp.zeros_like(word_qgrad)
    query_delta = jnp.stack(
        [
            jnp.where(is_word, word_qgrad, zero_rows),
            jnp.where(is_word, entity_qgrad, zero_rows),
            jnp.where(is_word, zero_rows, word_qgrad),
            jnp.where(is_word, zero_rows, entity_qgrad),
        ],
        axis=1,
    )
    querybias_grad = jnp.sum(query_delta, axis=(0, 2))
    valuebias_grad = jnp.sum(value_delta, axis=(0, 1))
    query_reduced = query_delta.astype(jnp.bfloat16)
    key_reduced = key_delta.astype(jnp.bfloat16)
    value_reduced = value_delta.astype(jnp.bfloat16)
    query_local = jnp.einsum(
        "nvh,nkvw->khw", layer_input, query_reduced, preferred_element_type=jnp.float32
    )
    key_shard = jnp.einsum(
        "pui,pun->in", layer_input, key_reduced, preferred_element_type=jnp.float32
    )
    value_local = jnp.einsum(
        "pui,pun->in", layer_input, value_reduced, preferred_element_type=jnp.float32
    )
    input_part = (
        jnp.einsum(
            "kayo,azo->kyz", query_reduced, query_pullback, preferred_element_type=jnp.float32
        )
        + jnp.einsum("ohz,wz->ohw", key_reduced, key_pullback, preferred_element_type=jnp.float32)
        + jnp.einsum(
            "ohz,wz->ohw", value_reduced, value_pullback, preferred_element_type=jnp.float32
        )
    )
    input_total = combine_rows(input_part.reshape(-1, model_width))
    input_grad = whole_rows((input_total + resid_grad).astype(jnp.bfloat16)).reshape(
        layer_input.shape
    )
    query_grad, key_grad, value_grad, outproj_grad = (
        lax.psum_scatter(query_local, "dp", scatter_dimension=1, tiled=True),
        lax.psum_scatter(key_shard, "dp", scatter_dimension=0, tiled=True),
        lax.psum_scatter(value_local, "dp", scatter_dimension=0, tiled=True),
        lax.psum_scatter(outproj_local, "dp", scatter_dimension=1, tiled=True),
    )
    querybias_grad, valuebias_grad, upbias_grad = lax.psum(
        (querybias_grad, valuebias_grad, upbias_grad), "dp"
    )
    outbias_grad, downbias_grad, attngain_grad, attnshift_grad, ffngain_grad, ffnshift_grad = (
        lax.psum(
            (
                outbias_grad,
                downbias_grad,
                attngain_grad,
                attnshift_grad,
                ffngain_grad,
                ffnshift_grad,
            ),
            ("dp", "tensor"),
        )
    )
    return (
        output,
        input_grad,
        query_grad,
        key_grad,
        value_grad,
        outproj_grad,
        upproj_grad,
        downproj_grad,
        querybias_grad,
        valuebias_grad,
        outbias_grad,
        upbias_grad,
        downbias_grad,
        attngain_grad,
        attnshift_grad,
        ffngain_grad,
        ffnshift_grad,
    )


MESH = pl.DeviceIdType.MESH
BF = jnp.bfloat16
F32 = jnp.float32
BLOCK = 128


def fits(mesh):
    return mesh.shape["dp"] == 8 and mesh.shape["tensor"] == 4


def nn(a, b):
    return lax.dot_general(a, b, (((1,), (0,)), ((), ())), preferred_element_type=F32)


def nt(a, b):
    return lax.dot_general(a, b, (((1,), (1,)), ((), ())), preferred_element_type=F32)


def tn(a, b):
    return lax.dot_general(a, b, (((0,), (0,)), ((), ())), preferred_element_type=F32)


def norm_rows(values):
    centre = values - jnp.mean(values, axis=-1, keepdims=True)
    inverse = lax.rsqrt(jnp.mean(centre * centre, axis=-1, keepdims=True) + EPSILON)
    return centre * inverse, inverse


def norm_rows_back(upstream, normal, inverse, gain):
    scaled = upstream * gain
    return inverse * (
        scaled
        - jnp.mean(scaled, axis=-1, keepdims=True)
        - normal * jnp.mean(scaled * normal, axis=-1, keepdims=True)
    )


class Net:
    def __init__(self, send, recv, peer):
        self.send, self.recv, self.peer = send, recv, peer
        self.sends = 0
        self.locals = 0
        self.banks = 0
        self.pending = []

    def bank(self, count):
        base = self.banks
        self.banks += count
        return base

    def start(self, src, dst, sem, device, when=None, group=None):
        slot = self.sends % SENDS
        self.sends += 1
        self.finish([p for p in self.pending if p[3] == slot])

        def make():
            return pltpu.make_async_remote_copy(
                src_ref=src,
                dst_ref=dst,
                send_sem=self.send.at[slot],
                recv_sem=self.recv.at[sem],
                device_id=device,
                device_id_type=MESH,
            )

        if when is None:
            make().start()
        else:
            pl.when(when)(lambda: make().start())
        self.pending.append((make, when, group, slot))

    def finish(self, entries):
        for make, when, _, _ in entries:
            if when is None:
                make().wait_send()
            else:
                pl.when(when)(lambda make=make: make().wait_send())
        self.pending = [p for p in self.pending if p not in entries]

    def wait(self, dst, sem, when=None):
        def make():
            return pltpu.make_async_remote_copy(
                src_ref=dst,
                dst_ref=dst,
                send_sem=self.send.at[0],
                recv_sem=self.recv.at[sem],
                device_id=self.peer,
                device_id_type=MESH,
            )

        if when is None:
            make().wait_recv()
        else:
            pl.when(when)(lambda: make().wait_recv())

    def settle(self, *groups):
        self.finish([p for p in self.pending if not groups or p[2] in groups])


SENDS = 48
RECVS = 141


def layer_kernel(
    x_in, seg_ref, typ_ref, qw_in, kw_in, vw_in, ow_in, uw_in, dw_in, qb_ref, vb_ref,
    ob_ref, ub_ref, db_ref, ag_ref, as_ref, fg_ref, fs_ref, cot_in,
    out_end, ig_end, qg_end, kg_end, vg_end, og_end, ug_end, dg_end, small_end,
    x_ref, qw_ref, kw_ref, vw_ref, ow_ref, uw_ref, dw_ref, cot_ref,
    out_ref, ig_ref, qg_ref, kg_ref, vg_ref, og_ref, ug_ref, dg_ref, small_ref,
    wq, wop, wo, own, wf, ubs, segc, wordc, xt, bias, qq, kv, kk, kvt, kkt, probs, ctx, ctp, ct, ctc,
    a_s, n1_s, r1_s, act, gelu_d, gl, parts, rs_send, rs_recv, dub, dzb,
    st_a, st_b, st_c, st_d, st_e, st_f, st_g, dct, dc, dco, go_r, rp, sp, rz,
    dqkv, dx_in, dx_cross, dx_back, gq_r, gp, sv, small_s, small_r, sent8, sw, vz,
    send_sems, recv_sems, local_sems,
):
    d = lax.axis_index("dp")
    t = lax.axis_index("tensor")
    c = d % 2
    x = (d // 2) % 2
    y = d // 4
    pair = t % 2
    j = 2 * pair + c
    block = pair + 2 * c
    home = block == t
    zp = t + 1 - 2 * pair
    zq = (t + 2) % 4
    host = 2 * (d // 2) + t // 2
    chip = d // 2
    sib = d + 1 - 2 * c
    xn = d + 2 - 4 * x
    yn = d + 4 - 8 * y
    rows = x_ref.shape[1]
    quarter = rows // 4
    width = x_ref.shape[2]
    strip = qw_ref.shape[1]
    local = kw_ref.shape[1]
    heads = local // HD
    blocks = rows // BLOCK
    own_rows = pl.ds(pl.multiple_of(t * quarter, 16), quarter)
    net = Net(send_sems, recv_sems, (sib, t))

    def flip_x(device):
        return device + 2 - 4 * ((device // 2) % 2)

    def flip_y(device):
        return device + 4 - 8 * (device // 4)

    dg = flip_y(xn)
    part_m, part_o = parts.at[0:2], parts.at[2:4]
    sums_a, sums_b = parts.reshape(rows, width), gelu_d.reshape(rows, width)
    dqq = [sums_a.at[:, BLOCK * h : BLOCK * (h + 1)] for h in range(heads)]
    dkk = [sums_a.at[:, BLOCK * (heads + h) : BLOCK * (heads + h + 1)] for h in range(heads)]
    dvv = [sums_b.at[:, BLOCK * h : BLOCK * (h + 1)] for h in range(heads)]

    low_z = t < 2
    is_end = jnp.logical_or(t == 0, t == 3)
    is_mid = jnp.logical_not(is_end)
    z_out = jnp.where(low_z, t + 1, t - 1)
    z_back = jnp.where(low_z, 0, 3)

    def place(e):
        return jnp.where(low_z, e, 3 - e)

    def joint(one, other):
        return other if one is None else jnp.logical_and(one, other)

    class LineGather:
        def __init__(self, view, group=None):
            self.view, self.bank, self.group = view, net.bank(4), group

        def copy(self, owner, to, when):
            ref = self.view(owner)
            net.start(ref, ref, self.bank + owner, (d, to), when=when, group=self.group)

        def wait(self, owner, when=None):
            net.wait(self.view(owner), self.bank + owner, when=when)

        def begin(self):
            self.copy(t, z_out, None)
            self.copy(t, z_back, is_mid)

        def step(self, n):
            if n == 1:
                self.wait(place(0), is_mid)
                self.copy(place(0), z_out, is_mid)
                self.wait(place(2), is_mid)
                self.copy(place(2), z_back, is_mid)
            if n == 2:
                self.wait(place(3), is_mid)
                self.copy(place(3), z_back, is_mid)
            self.wait(place(n), is_end)

    class LineReduce:
        def __init__(self, own, came, cross, back):
            self.own, self.came, self.cross, self.back = own, came, cross, back
            self.in_b, self.cross_b, self.back_b = net.bank(3), net.bank(2), net.bank(1)

        def depart(self, e):
            net.start(self.own(e), self.came.at[e - 1], self.in_b + e - 1, (d, z_out), when=is_end)

        def add(self, e, ref):
            @pl.when(is_mid)
            def _():
                ref[...] = (self.own(e)[...].astype(F32) + ref[...].astype(F32)).astype(BF)

        def through(self, e):
            ref = self.came.at[e - 1]
            net.wait(ref, self.in_b + e - 1, when=is_mid)
            self.add(e, ref)
            net.start(ref, self.cross.at[3 - e], self.cross_b + 3 - e, (d, z_out), when=is_mid)

        def pass_back(self):
            net.wait(self.cross.at[0], self.cross_b, when=is_mid)
            self.add(0, self.cross.at[0])
            net.start(self.cross.at[0], self.back, self.back_b, (d, z_back), when=is_mid)

        def total(self):
            net.wait(self.came.at[0], self.in_b, when=is_mid)
            net.wait(self.cross.at[1], self.cross_b + 1, when=is_mid)
            net.wait(self.back, self.back_b, when=is_end)
            others = self.came[0].astype(F32) + self.cross[1].astype(F32)
            mine = self.own(jnp.where(is_mid, 1, 0))[...].astype(F32)
            return mine + jnp.where(is_mid, others, self.back[...].astype(F32))

    class Local:
        def __init__(self, source, target):
            self.copy = pltpu.make_async_copy(source, target, local_sems.at[net.locals])
            net.locals += 1
            self.copy.start()

        def wait(self):
            self.copy.wait()

    in_q, in_k, in_v = Local(qw_in, qw_ref), Local(kw_in, kw_ref), Local(vw_in, vw_ref)
    in_o, in_u, in_d = Local(ow_in, ow_ref), Local(uw_in, uw_ref), Local(dw_in, dw_ref)
    in_x, in_cot = Local(x_in, x_ref), Local(cot_in, cot_ref)

    barrier = pltpu.get_barrier_semaphore()
    for m in range(1, 8):
        pl.semaphore_signal(barrier, 1, device_id=((d + m) % 8, t), device_id_type=MESH)
    for k in range(1, 4):
        pl.semaphore_signal(barrier, 1, device_id=(d, (t + k) % 4), device_id_type=MESH)
    pl.semaphore_signal(barrier, 1, device_id=(sib, zq), device_id_type=MESH)

    for arrived in (in_q, in_k, in_v):
        arrived.wait()
    for h in range(heads):
        at = slice(HD * h, HD * (h + 1))
        piece = jnp.concatenate(
            [qw_ref[i, :, at] for i in range(4)] + [kw_ref[:, at], vw_ref[:, at]], axis=1
        )
        wq[d, :, 6 * HD * h : 6 * HD * (h + 1)] = piece.astype(BF)

    pl.semaphore_wait(barrier, 11)

    class PlaneGather:
        def __init__(self, group, *views):
            self.views, self.bank, self.group = views, net.bank(8 * len(views)), group

        def copy(self, view, block, device):
            ref = self.views[view](block)
            net.start(ref, ref, self.bank + 8 * view + block, (device, t), group=self.group)

        def wait(self, view, block):
            net.wait(self.views[view](block), self.bank + 8 * view + block)

        def begin(self):
            for view, device in ((0, yn), (1, xn), (1, yn), (0, xn), (0, sib), (1, sib)):
                self.copy(view, d, device)

        def middle(self):
            self.wait(0, yn)
            self.copy(0, yn, xn)
            self.wait(1, xn)
            self.copy(1, xn, yn)
            self.copy(0, yn, sib)
            self.copy(1, xn, sib)

        def middle2(self):
            for view, block in ((1, yn), (0, xn)):
                self.wait(view, block)
                self.copy(view, block, sib)

        def late(self):
            for view in range(2):
                self.wait(view, dg)
                self.copy(view, dg, sib)

        def end(self):
            for block in (sib, flip_x(sib), flip_y(sib), flip_x(flip_y(sib))):
                for view in range(len(self.views)):
                    self.wait(view, block)

    gather_q = PlaneGather("q", lambda b: wq.at[b, : strip // 2], lambda b: wq.at[b, strip // 2 :])
    gather_q.begin()

    def wide_t(value, high, wide):
        r, w = value.shape
        if w < wide:
            value = jnp.concatenate([value, jnp.zeros((r, wide - w), value.dtype)], axis=1)
        if r < high:
            value = jnp.concatenate([value, jnp.zeros((high - r, wide), value.dtype)], axis=0)
        return value.T

    for arrived in (in_o, in_u, in_d):
        arrived.wait()
    def pack(block):
        most = block.shape[0] // 2
        rest = block[:, BLOCK:]
        return jnp.concatenate(
            [block[:, :BLOCK], jnp.concatenate([rest[:most], rest[most:]], axis=1)], axis=0
        )

    def rest_of(packed, count):
        below = packed[count:]
        return jnp.concatenate([below[:, :HD], below[: count - below.shape[0], HD:]], axis=0)

    wop[t, d] = pack(wide_t(ow_ref[...], 256, 128)[:strip, :local]).astype(BF)
    own[0] = uw_ref[...].astype(BF)
    own[1] = dw_ref[...].astype(BF)
    ubs[t] = jnp.broadcast_to(ub_ref[...][None], ubs.shape[1:])

    ub_z = net.bank(1)
    wf_a = net.bank(4)

    class ChipGather:
        def __init__(self, i):
            self.i, self.bank = i, net.bank(8)

        def send_near(self):
            i = self.i
            net.start(own.at[i], wf.at[i, d], wf_a + 2 * i + c, (host, t), when=host != d)

            @pl.when(host == d)
            def _():
                wf[i, d] = own[i]

        def send_far(self):
            net.start(own.at[self.i], wf.at[self.i, d], wf_a + 2 * self.i + c, (host, zq))

        def copy(self, view, of, device, when=None):
            ref = wf.at[self.i, 2 * (of // 2) + view]
            net.start(ref, ref, self.bank + 2 * (of // 2) + view, (device, t), when=when, group="f")

        def wait(self, view, of):
            net.wait(wf.at[self.i, 2 * (of // 2) + view], self.bank + 2 * (of // 2) + view)

        def begin(self, at_home):
            i, when = self.i, home if at_home else jnp.logical_not(home)
            if not at_home:
                net.wait(wf.at[i, d], wf_a + 2 * i + c, when=when)
            net.wait(wf.at[i, sib], wf_a + 2 * i + 1 - c, when=when)
            for view, device in ((0, yn), (1, xn), (1, yn), (0, xn)):
                self.copy(view, d, device, when)

        def middle(self):
            self.wait(0, yn)
            self.copy(0, yn, xn)
            self.wait(1, xn)
            self.copy(1, xn, yn)

        def end(self):
            for view, of in ((1, yn), (0, xn), (0, dg), (1, dg)):
                self.wait(view, of)

    up, down = ChipGather(0), ChipGather(1)
    wo_z = net.bank(1)
    for k in (2, 1, 3):
        net.start(wop.at[t, d], wop.at[t, d], wo_z, (d, (t + k) % 4))
    up.send_near()
    down.send_near()
    for b in range(blocks):
        at = slice(BLOCK * b, BLOCK * (b + 1))
        segc[at, :] = jnp.broadcast_to(seg_ref[:, at].astype(F32), (BLOCK, BLOCK)).T
        wordc[at, :] = jnp.broadcast_to((typ_ref[:, at] == 0).astype(F32), (BLOCK, BLOCK)).T
    in_x.wait()
    xt[...] = x_ref[0].T
    for h in range(heads):
        at = slice(HD * h, HD * (h + 1))
        bias[:, 6 * HD * h : 6 * HD * (h + 1)] = jnp.concatenate(
            [qb_ref[i : i + 1, at] for i in range(4)] + [jnp.zeros((1, HD), F32), vb_ref[at][None]],
            axis=1,
        )

    gather_q.middle()
    up.send_far()
    net.start(ubs.at[t], ubs.at[t], ub_z, (d, zq))
    down.send_far()
    gather_q.middle2()
    net.wait(wop.at[0:3, d], wo_z)
    gather_o = PlaneGather("o", lambda b: wop.at[0:2, b], lambda b: wop.at[2:4, b])
    gather_o.begin()
    up.begin(True)
    gather_q.late()
    gather_q.end()
    low_half = lax.broadcasted_iota(jnp.int32, (rows, BLOCK), 1) < HD
    is_word = wordc[...] > 0.5
    for h in range(heads):
        base = 6 * HD * h
        at = slice(BLOCK * h, BLOCK * (h + 1))
        made = nn(x_ref[0], wq[:, :, base : base + 6 * HD].reshape(width, 6 * HD))
        made = made + bias[:, base : base + 6 * HD]
        qq[:, at] = jnp.where(is_word, made[:, :BLOCK], made[:, BLOCK : 2 * BLOCK]).astype(BF)
        both = made[:, 2 * BLOCK :]
        keys = jnp.where(low_half, both, pltpu.roll(both, HD, 1))
        keys = jnp.where(jnp.logical_xor(is_word, low_half), 0.0, keys)
        kv[:, at] = both.astype(BF)
        kk[:, at] = keys.astype(BF)
        kvt[h] = both.T[HD:].astype(BF)
        kkt[h] = keys.T.astype(BF)

    gather_o.middle()
    gather_o.middle2()
    ct_z = net.bank(1)

    def span(b):
        return BLOCK * max(0, b - 2), BLOCK * min(blocks, b + 3)

    kept = [0]
    for b in range(blocks):
        kept.append(kept[-1] + span(b)[1] - span(b)[0])
    for b in range(blocks):
        lo, hi = span(b)
        at_q = slice(BLOCK * b, BLOCK * (b + 1))
        same = segc[lo:hi, :] == seg_ref[:, at_q].astype(F32)
        found = []
        for h in range(heads):
            at = slice(BLOCK * h, BLOCK * (h + 1))
            scores = nt(kk[lo:hi, at], qq[at_q, at]) * SCALING
            scores = jnp.where(same, scores, NEGATIVE)
            weights = jnp.exp(scores - jnp.max(scores, axis=0, keepdims=True))
            weights = weights * (1.0 / jnp.sum(weights, axis=0, keepdims=True))
            probs[h, kept[b] : kept[b + 1]] = weights
            found.append(nn(kvt[h, :, lo:hi], weights.astype(BF)))
        found.append(jnp.zeros((HD, BLOCK), F32))
        ctx[at_q, :] = jnp.concatenate(found, axis=0).T[:, :local].astype(BF)
        if b == 2:
            up.begin(False)
        if b > 0:
            s = b - 1
            ctp[s] = pack(ctx[quarter * s : quarter * (s + 1), :])
            net.start(ctp.at[s], ct.at[t], ct_z, (d, s), when=t != s)
    ct[t] = ctp[t]

    down.begin(True)
    gather_o.late()
    down.begin(False)
    up.middle()
    gather_o.end()
    for s in range(4):
        wo[:, :, BLOCK * s : BLOCK * (s + 1)] = wop[s, :, :strip]
    most = strip // 2
    for s in (0, 2):
        at = slice(4 * BLOCK + HD * s, 4 * BLOCK + HD * (s + 2))
        one, other = wop[s, :, strip:], wop[s + 1, :, strip:]
        wo[:, :most, at] = jnp.concatenate([one[:, :, :HD], other[:, :, :HD]], axis=2)
        wo[:, most:, at] = jnp.concatenate([one[:, :, HD:], other[:, :, HD:]], axis=2)
    net.wait(ct.at[0:3], ct_z)
    for s in range(4):
        ctc[:, BLOCK * s : BLOCK * (s + 1)] = ct[s, :quarter]
    for s in (0, 2):
        ctc[:, 4 * BLOCK + HD * s : 4 * BLOCK + HD * (s + 2)] = jnp.concatenate(
            [rest_of(ct[s], quarter), rest_of(ct[s + 1], quarter)], axis=1
        )
    whole_wo = wo.reshape(width, width)
    attended = nt(ctc[...], whole_wo[...])
    normal, inverse = norm_rows(x_ref[0, own_rows, :].astype(F32) + attended + ob_ref[...][None])
    n1_s[...] = normal
    r1_s[...] = jnp.broadcast_to(inverse, r1_s.shape)
    normed = normal * ag_ref[...][None] + as_ref[...][None]
    a_s[...] = normed
    act[j] = normed.astype(BF)

    def rows_of(ref, first, count):
        return lambda owner: ref.at[
            0, pl.ds(pl.multiple_of(owner * quarter + first, 16), count)
        ]

    part = quarter // 2
    chunk = [slice(part * q, part * (q + 1)) for q in range(2)]

    class RowGather:
        def __init__(self, ref):
            self.ref, self.bank = ref, net.bank(8)

        def copy(self, q, rank, device):
            ref = self.ref.at[rank, chunk[q]]
            net.start(ref, ref, self.bank + 4 * q + rank, device)

        def wait(self, q, rank):
            net.wait(self.ref.at[rank, chunk[q]], self.bank + 4 * q + rank)

        def begin(self, q):
            self.copy(q, j, (d, zp))
            self.copy(q, j, (sib, t))

        def near(self, q):
            self.wait(q, 2 * pair + 1 - c)

        def middle(self, q):
            self.wait(q, 2 - 2 * pair + c)
            self.copy(q, 2 - 2 * pair + c, (sib, t))

        def far(self, q):
            self.wait(q, 3 - 2 * pair - c)

    class RowSum:
        def __init__(self, index):
            self.index, self.bank = index, net.bank(6)

        def hand(self, q, slot, partial_rows):
            where = 3 * self.index + slot
            rs_send[where, chunk[q]] = partial_rows.astype(BF)
            net.start(
                rs_send.at[where, chunk[q]], rs_recv.at[where, chunk[q]], self.bank + 3 * q + slot,
                (d, zp) if slot == 2 else (sib, t),
            )

        def take(self, q, slot):
            where = 3 * self.index + slot
            net.wait(rs_recv.at[where, chunk[q]], self.bank + 3 * q + slot)
            return rs_recv[where, chunk[q]].astype(F32)

        def near(self, q):
            self.hand(q, 0, part_m[1 - c, chunk[q]])

        def away(self, q):
            self.hand(q, 1, part_o[1 - c, chunk[q]])

        def across(self, q):
            self.hand(q, 2, part_o[c, chunk[q]] + self.take(q, 1))

        def total(self, q):
            return part_m[c, chunk[q]] + self.take(q, 0) + self.take(q, 2)

    rows_a = RowGather(act)
    rows_a.begin(0)
    rows_a.begin(1)
    down.middle()
    rows_a.middle(0)
    rows_a.middle(1)
    rows_a.near(0)
    rows_a.near(1)
    net.wait(ubs.at[zq], ub_z)
    up.end()
    near = pl.ds(2 * pair, 2)
    away = pl.ds(2 - 2 * pair, 2)

    def feed(half):
        hidden = nn(act[half].reshape(2 * quarter, width), wf[0].reshape(width, width))
        hidden = hidden + ubs[block][:1]
        bell = 0.5 * (1.0 + lax.erf(hidden * 0.7071067811865476))
        slope = bell + hidden * (0.3989422804014327 * jnp.exp(-0.5 * hidden * hidden))
        gelu_d[half] = slope.reshape(2, quarter, width)
        gl[half] = (hidden * bell).astype(BF).reshape(2, quarter, width)

    def feed_out(half, partial_ref):
        made = nt(gl[half].reshape(2 * quarter, width), wf[1].reshape(width, width))
        partial_ref[...] = made.reshape(2, quarter, width)

    feed(near)
    rows_a.far(0)
    rows_a.far(1)
    feed(away)
    down.end()
    sum_f = RowSum(0)
    feed_out(away, part_o)
    sum_f.away(0)
    sum_f.away(1)
    feed_out(near, part_m)
    sum_f.across(0)
    sum_f.across(1)
    sum_f.near(0)
    sum_f.near(1)
    in_cot.wait()
    rows_u = RowGather(dub)
    gain_sum, shift_sum, bias_sum = 0.0, 0.0, 0.0
    for q in range(2):
        ffn_out = sum_f.total(q) + db_ref[...][None]
        normal, inverse = norm_rows(a_s[chunk[q]] + ffn_out)
        rows_q = pl.ds(pl.multiple_of(t * quarter + part * q, 16), part)
        out_ref[0, rows_q, :] = (normal * fg_ref[...][None] + fs_ref[...][None]).astype(BF)
        upstream = cot_ref[0, rows_q, :].astype(F32)
        du = norm_rows_back(upstream, normal, inverse, fg_ref[...][None])
        dub[j, chunk[q]] = du.astype(BF)
        rows_u.begin(q)
        a_s[chunk[q]] = du
        gain_sum = gain_sum + jnp.sum(upstream * normal, axis=0, keepdims=True)
        shift_sum = shift_sum + jnp.sum(upstream, axis=0, keepdims=True)
        bias_sum = bias_sum + jnp.sum(du, axis=0, keepdims=True)
    line_out = [LineGather(rows_of(out_ref, part * q, part)) for q in range(2)]
    line_out[0].begin()
    sv[...] = jnp.zeros_like(sv)
    sv[0:1] = gain_sum
    sv[1:2] = shift_sum
    sv[2:3] = bias_sum

    def feed_back(half, rows_q, partial_ref):
        count = 2 * (rows_q.stop - rows_q.start)
        made = nn(dub[half, rows_q].reshape(count, width), wf[1].reshape(width, width))
        made = made * gelu_d[half, rows_q].reshape(count, width)
        low = made.astype(BF)
        dzb[half, rows_q] = low.reshape(2, count // 2, width)
        partial_ref[:, rows_q] = nt(low, wf[0].reshape(width, width)).reshape(2, count // 2, width)
        return jnp.sum(made, axis=0, keepdims=True)

    sum_b = RowSum(1)
    rows_u.near(0)
    rows_u.near(1)
    up_sum = feed_back(near, slice(0, quarter), part_m)
    sum_b.near(0)
    sum_b.near(1)
    rows_u.middle(0)
    rows_u.far(0)
    up_sum = up_sum + feed_back(away, chunk[0], part_o)
    sum_b.away(0)
    rows_u.middle(1)
    sum_b.across(0)
    rows_u.far(1)
    up_sum = up_sum + feed_back(away, chunk[1], part_o)
    sum_b.away(1)
    sv[6:7] = up_sum
    half = width // 2

    class StripSum:
        def __init__(self, i):
            self.i, self.bank = i, net.bank(9)
            self.by_chip = wf.at[i].reshape(2, 2, 2, strip, width)

        def make(self, left, right):
            made = tn(left[...].reshape(4 * quarter, width), right[...].reshape(4 * quarter, width))
            wf[self.i] = made.astype(BF).reshape(8, strip, width)

        def begin(self):
            net.start(
                self.by_chip.at[:, 1 - x, :, :, :half], st_a.at[self.i], self.bank, (xn, t)
            )
            net.start(
                self.by_chip.at[1 - y, :, :, :, half:], st_b.at[self.i], self.bank + 1, (yn, t)
            )

        def turn(self):
            i = self.i
            net.wait(st_a.at[i], self.bank)
            st_a[i] = (st_a[i].astype(F32) + self.by_chip[:, x, :, :, :half].astype(F32)).astype(BF)
            for core in range(2):
                net.start(
                    st_a.at[i, 1 - y, core], st_c.at[i, c], self.bank + 2 + c,
                    (2 * (yn // 2) + core, t),
                )
            net.start(st_a.at[i, y, 1 - c], st_g.at[i, 0], self.bank + 6, (sib, t))
            net.wait(st_b.at[i], self.bank + 1)
            st_b[i] = (st_b[i].astype(F32) + self.by_chip[y, :, :, :, half:].astype(F32)).astype(BF)
            for core in range(2):
                net.start(
                    st_b.at[i, 1 - x, core], st_d.at[i, c], self.bank + 4 + c,
                    (2 * (xn // 2) + core, t),
                )
            net.start(st_b.at[i, x, 1 - c], st_g.at[i, 1], self.bank + 7, (sib, t))

        def gather(self):
            i = self.i
            for core in range(2):
                net.wait(st_c.at[i, core], self.bank + 2 + core)
                net.wait(st_d.at[i, core], self.bank + 4 + core)
            net.wait(st_g.at[i, 0], self.bank + 6)
            net.wait(st_g.at[i, 1], self.bank + 7)
            for whose, first, second in (
                (c, st_a.at[i, y, c], st_b.at[i, x, c]), (1 - c, st_g.at[i, 0], st_g.at[i, 1])
            ):
                st_e[i, whose, :, :half] = (
                    first[...].astype(F32) + st_c[i, whose].astype(F32)
                ).astype(BF)
                st_e[i, whose, :, half:] = (
                    second[...].astype(F32) + st_d[i, whose].astype(F32)
                ).astype(BF)

        def deliver(self, when=None):
            i = self.i
            net.start(st_e.at[i, 1 - t // 2], st_f.at[i], self.bank + 8, (d, zq), when=when)

        def total(self):
            i = self.i
            net.wait(st_f.at[i], self.bank + 8)
            return st_e[i, t // 2].astype(F32) + st_f[i].astype(F32)

    class SmallSum:
        def __init__(self, index):
            self.index, self.bank = index, net.bank(2)

        def begin(self, values):
            i = self.index
            small_s[i, 0] = values
            for r in (xn, yn, dg):
                net.start(small_s.at[i, 0], small_r.at[i, chip], self.bank, (r, t))
            small_r[i, chip] = values

        def plane(self):
            i = self.index
            net.wait(small_r.at[i, 0:3], self.bank)
            total = small_r[i, 0]
            for k in range(1, 4):
                total = total + small_r[i, k]
            small_s[i, 1] = total
            net.start(small_s.at[i, 1], small_r.at[i, 4], self.bank + 1, (sib, t))

        def cores(self):
            net.wait(small_r.at[self.index, 4], self.bank + 1)
            return small_s[self.index, 1], small_r[self.index, 4]

    net.settle("f")
    down_sum, up_sums = StripSum(1), StripSum(0)
    down_sum.make(dub, gl)
    down_sum.begin()
    sum_b.across(1)
    line_out[1].begin()
    line_out[0].step(1)
    up_sums.make(act, dzb)
    up_sums.begin()
    dc_z = net.bank(1)
    gain_sum, shift_sum, bias_sum, dhb = 0.0, 0.0, 0.0, []
    for q in range(2):
        da = a_s[chunk[q]] + sum_b.total(q)
        normal = n1_s[chunk[q]]
        dh = norm_rows_back(da, normal, r1_s[chunk[q], :1], ag_ref[...][None])
        a_s[chunk[q]] = dh
        dhb.append(dh.astype(BF))
        made = nn(dhb[q], whole_wo[...])
        for s in range(4):
            rest = made[:, 4 * BLOCK + HD * s : 4 * BLOCK + HD * (s + 1)]
            rest = jnp.concatenate([rest, jnp.zeros((16, HD), F32)], axis=0)
            most = (part + 16) // 2
            dct[s, q] = jnp.concatenate(
                [
                    made[:, BLOCK * s : BLOCK * (s + 1)],
                    jnp.concatenate([rest[:most], rest[most:]], axis=1),
                ],
                axis=0,
            ).astype(BF)
        for k in (2, 1, 3):
            s = (t + k) % 4
            net.start(dct.at[s, q], dc.at[t, q], dc_z, (d, s))
        dc[t, q] = dct[t, q]
        gain_sum = gain_sum + jnp.sum(da * normal, axis=0, keepdims=True)
        shift_sum = shift_sum + jnp.sum(da, axis=0, keepdims=True)
        bias_sum = bias_sum + jnp.sum(dh, axis=0, keepdims=True)
    dhb = jnp.concatenate(dhb, axis=0)
    line_out[1].step(1)
    sv[3:4] = gain_sum
    sv[4:5] = shift_sum
    sv[5:6] = bias_sum
    small_a = SmallSum(0)
    small_a.begin(sv[...])
    down_sum.turn()
    wo[...] = tn(dhb, ctc[...]).astype(BF).reshape(8, strip, width)
    by_core = wo.reshape(4, 2, strip, width)
    go_b = net.bank(1)
    net.start(by_core.at[:, 1 - c], go_r, go_b, (sib, t))

    net.wait(dc.at[0:3], dc_z)
    up_sums.turn()
    net.wait(go_r, go_b)
    go_r[...] = (by_core[:, c].astype(F32) + go_r[...].astype(F32)).astype(BF)
    rp_b = net.bank(1)
    for r in (xn, yn, dg):
        net.start(go_r.at[r // 2], rp.at[chip], rp_b, (r, t))
    rp[chip] = go_r[chip]
    line_out[0].step(2)
    upper = lax.broadcasted_iota(jnp.int32, (part, BLOCK), 1) >= HD
    for s in range(4):
        for q in range(2):
            got = dc[s, q]
            at_q = slice(quarter * s + part * q, quarter * s + part * (q + 1))
            first = got[:part].astype(F32)
            blank = jnp.zeros((part, HD), BF)
            dco[at_q, :BLOCK] = jnp.concatenate([blank, got[:part, :HD]], axis=1)
            dco[at_q, BLOCK : 2 * BLOCK] = jnp.where(upper, first, 0.0).astype(BF)
            dco[at_q, 2 * BLOCK :] = jnp.concatenate([blank, rest_of(got, part)], axis=1)
    for h in range(heads):
        dkk[h][...] = jnp.zeros((rows, BLOCK), F32)
        dvv[h][...] = jnp.zeros((rows, BLOCK), F32)
    for b in range(blocks):
        lo, hi = span(b)
        at_q = slice(BLOCK * b, BLOCK * (b + 1))
        if b == 4:
            down_sum.gather()
            down_sum.deliver()
        for h in range(heads):
            at = slice(BLOCK * h, BLOCK * (h + 1))
            weights = probs[h, kept[b] : kept[b + 1]]
            dp = nt(kv[lo:hi, at], dco[at_q, at])
            ds = weights * (dp - jnp.sum(weights * dp, axis=0, keepdims=True))
            dsb = ds.astype(BF)
            dkk[h][lo:hi] += nn(dsb, qq[at_q, at])
            dvv[h][lo:hi] += nn(weights.astype(BF), dco[at_q, at])
            dqq[h][at_q] = nn(kkt[h, :, lo:hi], dsb).T * SCALING

    line_out[1].step(2)
    small_a.plane()
    for h in range(heads):
        base = 6 * HD * h
        first = jnp.where(is_word, dqq[h][...], 0.0)
        second = jnp.where(is_word, 0.0, dqq[h][...])
        keys = dkk[h][...]
        keys = jnp.where(is_word, keys, pltpu.roll(keys, HD, 1)) * SCALING
        third = jnp.where(low_half, keys, dvv[h][...])
        for i, piece in enumerate((first, second, third)):
            at = slice(base + BLOCK * i, base + BLOCK * (i + 1))
            dqkv[:, at] = piece.astype(BF)
            row, col = divmod(base + BLOCK * i, width)
            sv[row : row + 1, col : col + BLOCK] = jnp.sum(piece, axis=0, keepdims=True)

    first_rows = pl.ds(pl.multiple_of(jnp.where(low_z, rows // 2, 0), 16), rows // 2)
    other_rows = pl.ds(pl.multiple_of(jnp.where(low_z, 0, rows // 2), 16), rows // 2)
    first_two = pl.ds(jnp.where(low_z, 2, 0), 2)
    other_two = pl.ds(jnp.where(low_z, 0, 2), 2)

    def back_to_input(rows_b, quarters):
        made = nt(dqkv[rows_b, :], wq[...].reshape(width, 6 * local))
        dzb[quarters] = made.astype(BF).reshape(2, quarter, width)

    line_dx, line_in = [], []
    for q in range(2):
        cut = pl.ds(part * q, part)
        line_dx.append(
            LineReduce(
                lambda e, cut=cut: dzb.at[place(e), cut],
                dx_in.at[q], dx_cross.at[q], dx_back.at[q],
            )
        )
        line_in.append(LineGather(rows_of(ig_ref, part * q, part)))

    def arrive(q):
        total = line_dx[q].total() + a_s[part * q : part * (q + 1)]
        ig_ref[0, pl.ds(pl.multiple_of(t * quarter + part * q, 16), part)] = total.astype(BF)
        line_in[q].begin()

    back_to_input(first_rows, first_two)
    for q, e in ((0, 3), (0, 2), (1, 3), (1, 2)):
        line_dx[q].depart(e)
    up_sums.gather()
    up_sums.deliver(is_mid)
    plane_sum, other_sum = small_a.cores()
    first_core = c == 0
    own_units, other_units = plane_sum[6:7], other_sum[6:7]
    sent8[0:6] = plane_sum[0:6] + other_sum[0:6]
    sent8[6:7] = jnp.where(first_core, own_units, other_units)
    sent8[7:8] = jnp.where(first_core, other_units, own_units)
    vz_b = net.bank(2)
    for k in (2, 1, 3):
        net.start(sent8, vz.at[t], vz_b, (d, (t + k) % 4), when=first_core)
    vz[t] = sent8[...]
    back_to_input(other_rows, other_two)
    line_dx[0].depart(1)
    line_dx[1].depart(1)
    small_b = SmallSum(1)
    small_b.begin(sv[...])

    net.settle("q")
    wq[...] = nn(xt[...], dqkv[...]).astype(BF).reshape(8, strip, 6 * local)
    q_by_core = wq.reshape(4, 2, strip, 6 * local)
    gq_b = net.bank(1)
    net.start(q_by_core.at[:, 1 - c], gq_r, gq_b, (sib, t))
    line_dx[0].through(3)
    line_dx[0].through(2)
    net.wait(gq_r, gq_b)
    gq_r[...] = (q_by_core[:, c].astype(F32) + gq_r[...].astype(F32)).astype(BF)
    gp_b = net.bank(1)
    for r in (xn, yn, dg):
        net.start(gq_r.at[r // 2], gp.at[chip], gp_b, (r, t))
    gp[chip] = gq_r[chip]

    line_dx[0].pass_back()
    net.wait(rp.at[0:3], rp_b)
    total = rp[0].astype(F32)
    for k in range(1, 4):
        total = total + rp[k].astype(F32)
    for s in range(4):
        rest = total[:, 4 * BLOCK + HD * s : 4 * BLOCK + HD * (s + 1)]
        sp[s] = pack(
            jnp.concatenate([total[:, BLOCK * s : BLOCK * (s + 1)], rest], axis=1)
        ).astype(BF)
    rz_b = net.bank(1)
    rz[t] = sp[t]

    def send_rz(when):
        for k in range(1, 4):
            s = (t + k) % 4
            net.start(sp.at[s], rz.at[t], rz_b, (d, s), when=when)

    line_dx[1].through(3)
    line_dx[1].through(2)
    line_dx[1].pass_back()
    arrive(0)
    arrive(1)

    line_in[0].step(1)
    line_in[1].step(1)
    up_sums.deliver(is_end)
    send_rz(None)
    line_out[0].step(3)
    line_out[1].step(3)
    ends = [Local(out_ref, out_end)]
    line_in[0].step(2)
    line_in[1].step(2)
    small_b.plane()
    net.wait(vz.at[0:3], vz_b, when=first_core)

    @pl.when(first_core)
    def _():
        total = vz[0]
        for k in range(1, 4):
            total = total + vz[k]
        sw[0:6] = total[0:6]
        units = vz[t] + vz[zq]
        sw[6:7] = jnp.where(t < 2, units[6:7], units[7:8])
        sw[7:8] = units[7:8]

    net.start(sw, sw, vz_b + 1, (sib, t), when=first_core)
    net.wait(sw, vz_b + 1, when=c == 1)
    small_ref[0:8] = sw[...]
    plane_sum, other_sum = small_b.cores()
    small_ref[8:16] = plane_sum + other_sum
    dg_ref[...] = down_sum.total()
    ug_ref[...] = up_sums.total()
    ends += [Local(dg_ref, dg_end), Local(ug_ref, ug_end), Local(small_ref, small_end)]
    net.wait(rz.at[0:3], rz_b)
    total = rz[0].astype(F32)
    for s in range(1, 4):
        total = total + rz[s].astype(F32)
    total = jnp.concatenate([total[:strip], rest_of(total, strip)], axis=1)
    og_ref[...] = wide_t(total, BLOCK, 256)[:local, :strip]

    ends += [Local(og_ref, og_end)]
    net.wait(gp.at[0:3], gp_b)
    total = gp[0].astype(F32)
    for k in range(1, 4):
        total = total + gp[k].astype(F32)
    for h in range(heads):
        base = 6 * HD * h
        at = slice(HD * h, HD * (h + 1))
        for i in range(4):
            qg_ref[i, :, at] = total[:, base + HD * i : base + HD * (i + 1)]
        kg_ref[:, at] = total[:, base + 4 * HD : base + 5 * HD]
        vg_ref[:, at] = total[:, base + 5 * HD : base + 6 * HD]

    ends += [Local(qg_ref, qg_end), Local(kg_ref, kg_end), Local(vg_ref, vg_end)]
    for q in range(2):
        line_in[q].step(3)
    ends += [Local(ig_ref, ig_end)]
    net.settle()
    for copy in ends:
        copy.wait()
    assert net.banks == RECVS, net.banks


def end_kernel(*refs):
    sources, small = refs[:8], refs[8]
    targets, (qbg, vbg), vectors = refs[9:17], refs[17:19], refs[19:26]
    for source, target in zip(sources, targets):
        target[...] = source[...]
    fgg, fsg, dbg, agg, asg, obg, ubg = (small[i] for i in range(7))
    for ref, value in zip(vectors, (obg, ubg, dbg, agg, asg, fgg, fsg)):
        ref[...] = value
    width = small.shape[1]
    values = []
    for h in range(vbg.shape[0] // HD):
        row, col = divmod(6 * HD * h, width)
        piece = small[8 + row : 9 + row, col : col + 6 * HD]
        for i in range(4):
            qbg[i : i + 1, HD * h : HD * (h + 1)] = piece[:, HD * i : HD * (i + 1)]
        values.append(piece[:, 5 * HD :])
    vbg[...] = jnp.concatenate(values, axis=1)[0]


def fused(
    layer_input, segment_ids, token_types, query_weight, key_weight, value_weight, out_weight,
    up_weight, down_weight, query_bias, value_bias, out_bias, up_bias, down_bias, attn_gain,
    attn_shift, ffn_gain, ffn_shift, cotangent,
):
    rows, width = layer_input.shape[1:]
    strip, local = key_weight.shape
    quarter, heads, blocks = rows // 4, local // HD, rows // BLOCK
    kept = sum(BLOCK * (min(blocks, b + 3) - max(0, b - 2)) for b in range(blocks))
    args = [
        layer_input, segment_ids, token_types, query_weight, key_weight, value_weight, out_weight,
        up_weight, down_weight.T, query_bias, value_bias, out_bias, up_bias, down_bias, attn_gain,
        attn_shift, ffn_gain, ffn_shift, cotangent,
    ]

    def like(v, dtype=F32):
        return jax.ShapeDtypeStruct(v.shape, dtype)

    outs = [
        like(layer_input, BF), like(layer_input, BF), like(query_weight), like(key_weight),
        like(value_weight), like(out_weight), like(up_weight), jax.ShapeDtypeStruct((strip, width), F32),
        jax.ShapeDtypeStruct((16, width), F32),
    ]
    v = pltpu.VMEM
    scratch = [
        v(layer_input.shape, BF), v(query_weight.shape, F32), v(key_weight.shape, F32),
        v(value_weight.shape, F32), v(out_weight.shape, F32), v(up_weight.shape, F32),
        v((strip, width), F32), v(cotangent.shape, BF),
    ] + [v(o.shape, o.dtype) for o in outs] + [
        v((8, strip, 6 * local), BF), v((4, 8, 3 * strip // 2, BLOCK), BF), v((8, strip, width), BF),
        v((2, strip, width), BF),
        v((2, 8, strip, width), BF), v((4, 8, width), F32), v((rows, BLOCK), F32),
        v((rows, BLOCK), F32), v((width, rows), BF), v((1, 6 * local), F32),
        v((rows, heads * BLOCK), BF), v((rows, heads * BLOCK), BF), v((rows, heads * BLOCK), BF),
        v((heads, HD, rows), BF), v((heads, BLOCK, rows), BF),
        v((heads, kept, BLOCK), F32), v((rows, local), BF), v((4, 3 * quarter // 2, BLOCK), BF),
        v((4, 3 * quarter // 2, BLOCK), BF), v((quarter, width), BF),
        v((quarter, width), F32), v((quarter, width), F32), v((quarter, BLOCK), F32),
        v((4, quarter, width), BF), v((4, quarter, width), F32), v((4, quarter, width), BF),
        v((4, quarter, width), F32),
        v((6, quarter, width), BF), v((6, quarter, width), BF),
        v((4, quarter, width), BF), v((4, quarter, width), BF),
        v((2, 2, 2, strip, width // 2), BF), v((2, 2, 2, strip, width // 2), BF),
        v((2, 2, strip, width // 2), BF), v((2, 2, strip, width // 2), BF),
        v((2, 2, strip, width), BF), v((2, strip, width), BF),
        v((2, 2, strip, width // 2), BF),
        v((4, 2, BLOCK, BLOCK), BF), v((4, 2, BLOCK, BLOCK), BF),
        v((rows, heads * BLOCK), BF),
        v((4, strip, width), BF), v((4, strip, width), BF), v((4, 3 * strip // 2, BLOCK), BF),
        v((4, 3 * strip // 2, BLOCK), BF),
        v((rows, 6 * local), BF),
        v((2, 3, quarter // 2, width), BF), v((2, 2, quarter // 2, width), BF),
        v((2, quarter // 2, width), BF),
        v((4, strip, 6 * local), BF), v((4, strip, 6 * local), BF),
        v((8, width), F32), v((2, 2, 8, width), F32), v((2, 5, 8, width), F32),
        v((8, width), F32), v((8, width), F32), v((4, 8, width), F32),
        pltpu.SemaphoreType.DMA((SENDS,)), pltpu.SemaphoreType.DMA((RECVS,)),
        pltpu.SemaphoreType.DMA((17,)),
    ]
    spec = pl.BlockSpec(memory_space=pltpu.VMEM)
    anywhere = pl.BlockSpec(memory_space=pl.ANY)
    large_args = (0, 3, 4, 5, 6, 7, 8, 18)
    made = pl.pallas_call(
        layer_kernel,
        out_shape=outs,
        in_specs=[anywhere if n in large_args else spec for n in range(len(args))],
        out_specs=[anywhere] * len(outs),
        scratch_shapes=scratch,
        compiler_params=pltpu.CompilerParams(
            collective_id=0, has_side_effects=True, vmem_limit_bytes=58 << 20
        ),
        name="layer",
    )(*args)
    *large, small = made
    vector = jax.ShapeDtypeStruct((width,), F32)
    ended = pl.pallas_call(
        end_kernel,
        out_shape=[like(v, v.dtype) for v in large]
        + [like(query_bias), jax.ShapeDtypeStruct((local,), F32)]
        + [vector] * 7,
        in_specs=[spec] * len(made),
        out_specs=[spec] * 17,
        name="finish",
    )(*large, small)
    return (*ended[:7], ended[7].T, *ended[8:])


def solution(mesh):
    in_specs = (
        P("dp", None, None),
        P("dp", None),
        P("dp", None),
        P(None, "dp", "tensor"),
        P("dp", "tensor"),
        P("dp", "tensor"),
        P("tensor", "dp"),
        P("dp", "tensor"),
        P("tensor", "dp"),
        P(None, "tensor"),
        P("tensor"),
        P(),
        P("tensor"),
        P(),
        P(),
        P(),
        P(),
        P(),
        P("dp", None, None),
    )
    out_specs = (
        P("dp", None, None),
        P("dp", None, None),
        P(None, "dp", "tensor"),
        P("dp", "tensor"),
        P("dp", "tensor"),
        P("tensor", "dp"),
        P("dp", "tensor"),
        P("tensor", "dp"),
        P(None, "tensor"),
        P("tensor"),
        P(),
        P("tensor"),
        P(),
        P(),
        P(),
        P(),
        P(),
    )
    step = fused if fits(mesh) else shards
    return jax.shard_map(step, mesh=mesh, in_specs=in_specs, out_specs=out_specs, check_vma=False)
```

```python
from functools import partial

import jax
import jax.numpy as jnp
from jax import lax
from jax.experimental import pallas as pl
from jax.experimental.pallas import tpu as pltpu
from jax.sharding import PartitionSpec as P

HD = 64


EPSILON = 1e-05
SCALING = 0.125
NEGATIVE = -1000000000.0


def layer_norm_keep(values, norm_gain, norm_shift):
    centre = values - jnp.mean(values, axis=-1, keepdims=True)
    inverse = lax.rsqrt(jnp.mean(centre * centre, axis=-1, keepdims=True) + EPSILON)
    normal = centre * inverse
    return (normal * norm_gain + norm_shift, normal, inverse)


def layer_norm_back(upstream, normal, inverse, norm_gain):
    scaled = upstream * norm_gain
    gain_grad = jnp.sum(upstream * normal, axis=0)
    shift_grad = jnp.sum(upstream, axis=0)
    inner_term = (
        scaled
        - jnp.mean(scaled, axis=-1, keepdims=True)
        - normal * jnp.mean(scaled * normal, axis=-1, keepdims=True)
    )
    return (inverse * inner_term, gain_grad, shift_grad)


def heads_of(matrix):
    return matrix.reshape(matrix.shape[0], -1, HD)


def pick_queries(query_rows, type_row):
    word_tok = (type_row == 0)[:, None]
    return (
        jnp.where(word_tok, query_rows[0], query_rows[2]),
        jnp.where(word_tok, query_rows[1], query_rows[3]),
    )


def score_block(word_heads, entity_heads, key_heads, segment_row, type_row):
    to_words = jnp.einsum("qhd,khd->hqk", word_heads, key_heads, preferred_element_type=jnp.float32)
    to_entities = jnp.einsum(
        "qhd,khd->hqk", entity_heads, key_heads, preferred_element_type=jnp.float32
    )
    scores = jnp.where((type_row == 0)[None, None, :], to_words, to_entities) * SCALING
    allowed = (segment_row[:, None] == segment_row[None, :])[None]
    return jnp.where(allowed, scores, NEGATIVE)


def attend_forward(packed):
    query_rows, key_seq, value_seq, segment_row, type_row = packed
    word_query, entity_query = pick_queries(query_rows, type_row)
    scores = score_block(
        heads_of(word_query), heads_of(entity_query), heads_of(key_seq), segment_row, type_row
    )
    row_top = jnp.max(scores, axis=-1, keepdims=True)
    weights = jnp.exp(scores - row_top)
    totals = jnp.sum(weights, axis=-1, keepdims=True)
    attn_probs = (weights / totals).astype(jnp.bfloat16)
    context = jnp.einsum(
        "hqk,khd->qhd", attn_probs, heads_of(value_seq), preferred_element_type=jnp.float32
    )
    log_total = (row_top + jnp.log(totals))[..., 0]
    return (context.reshape(context.shape[0], -1).astype(jnp.bfloat16), log_total)


def attend_backward(packed):
    query_rows, key_seq, value_seq, segment_row, type_row, log_total, context_grad = packed
    word_query, entity_query = pick_queries(query_rows, type_row)
    word_heads = heads_of(word_query)
    entity_heads = heads_of(entity_query)
    key_heads = heads_of(key_seq)
    value_heads = heads_of(value_seq)
    grad_heads = heads_of(context_grad)
    scores = score_block(word_heads, entity_heads, key_heads, segment_row, type_row)
    attn_probs = jnp.exp(scores - log_total[..., None])
    prob_grad = jnp.einsum(
        "qhd,khd->hqk", grad_heads, value_heads, preferred_element_type=jnp.float32
    )
    score_grad = attn_probs * (prob_grad - jnp.sum(attn_probs * prob_grad, axis=-1, keepdims=True))
    score_low = score_grad.astype(jnp.bfloat16)
    word_key = (type_row == 0)[None, None, :]
    zeroes = jnp.zeros_like(score_low)
    word_part = jnp.where(word_key, score_low, zeroes)
    entity_part = jnp.where(word_key, zeroes, score_low)
    word_qgrad = (
        jnp.einsum("hqk,khd->qhd", word_part, key_heads, preferred_element_type=jnp.float32)
        * SCALING
    )
    entity_qgrad = (
        jnp.einsum("hqk,khd->qhd", entity_part, key_heads, preferred_element_type=jnp.float32)
        * SCALING
    )
    key_delta = (
        jnp.einsum("hqk,qhd->khd", word_part, word_heads, preferred_element_type=jnp.float32)
        + jnp.einsum("hqk,qhd->khd", entity_part, entity_heads, preferred_element_type=jnp.float32)
    ) * SCALING
    value_delta = jnp.einsum(
        "hqk,qhd->khd",
        attn_probs.astype(jnp.bfloat16),
        grad_heads,
        preferred_element_type=jnp.float32,
    )
    row_count = word_qgrad.shape[0]
    return (
        word_qgrad.reshape(row_count, -1),
        entity_qgrad.reshape(row_count, -1),
        key_delta.reshape(row_count, -1),
        value_delta.reshape(row_count, -1),
    )


def row_share(partial_rows):
    return lax.psum_scatter(partial_rows, "tensor", scatter_dimension=0, tiled=True)


def row_whole(rounded_rows):
    return lax.all_gather(rounded_rows, "tensor", axis=0, tiled=True)


def shards(
    layer_input,
    segment_ids,
    token_types,
    query_weight,
    key_weight,
    value_weight,
    out_weight,
    up_weight,
    down_weight,
    query_bias,
    value_bias,
    out_bias,
    up_bias,
    down_bias,
    attn_gain,
    attn_shift,
    ffn_gain,
    ffn_shift,
    cotangent,
):
    seq_count, seq_length, model_width = layer_input.shape
    tokens = layer_input.reshape(-1, model_width)
    row_count = tokens.shape[0]
    share = row_count // lax.axis_size("tensor")
    first_row = lax.axis_index("tensor") * share

    def own_rows(matrix):
        return lax.dynamic_slice_in_dim(matrix, first_row, share, 0)

    def combine_rows(partial_rows):
        return row_share(partial_rows)

    def whole_rows(rounded_rows):
        return row_whole(rounded_rows)

    query_complete, key_full, value_full, out_full = (
        lax.all_gather(query_weight.astype(jnp.bfloat16), "dp", axis=1, tiled=True),
        lax.all_gather(key_weight.astype(jnp.bfloat16), "dp", axis=0, tiled=True),
        lax.all_gather(value_weight.astype(jnp.bfloat16), "dp", axis=0, tiled=True),
        lax.all_gather(out_weight.astype(jnp.bfloat16), "dp", axis=1, tiled=True),
    )
    local_width = key_full.shape[1]
    query_rows = jnp.einsum(
        "gow,qwk->gqok", layer_input, query_complete, preferred_element_type=jnp.float32
    )
    query_rows = (query_rows + query_bias[None, :, None, :]).astype(jnp.bfloat16)
    keys_all = jnp.dot(layer_input, key_full, preferred_element_type=jnp.float32).astype(
        jnp.bfloat16
    )
    values_all = (
        jnp.dot(layer_input, value_full, preferred_element_type=jnp.float32) + value_bias
    ).astype(jnp.bfloat16)
    context, log_total = lax.map(
        attend_forward, (query_rows, keys_all, values_all, segment_ids, token_types)
    )
    context_rows = context.reshape(-1, local_width)
    attended = combine_rows(jnp.dot(context_rows, out_full, preferred_element_type=jnp.float32))
    residual = own_rows(tokens).astype(jnp.float32) + attended + out_bias
    normed, normal_one, inverse_one = layer_norm_keep(residual, attn_gain, attn_shift)
    normed_low = whole_rows(normed.astype(jnp.bfloat16))
    up_full, down_full = (
        lax.all_gather(up_weight.astype(jnp.bfloat16), "dp", axis=0, tiled=True),
        lax.all_gather(down_weight.astype(jnp.bfloat16), "dp", axis=1, tiled=True),
    )
    pre_act = jnp.dot(normed_low, up_full, preferred_element_type=jnp.float32) + up_bias
    activated, gelu_pull = jax.vjp(partial(jax.nn.gelu, approximate=False), pre_act)
    act_low = activated.astype(jnp.bfloat16)
    ffn_out = (
        combine_rows(jnp.dot(act_low, down_full, preferred_element_type=jnp.float32)) + down_bias
    )
    normed_out, normal_two, inverse_two = layer_norm_keep(normed + ffn_out, ffn_gain, ffn_shift)
    output = whole_rows(normed_out.astype(jnp.bfloat16)).reshape(layer_input.shape)
    upstream = own_rows(cotangent.reshape(-1, model_width)).astype(jnp.float32)
    sum_grad, ffngain_grad, ffnshift_grad = layer_norm_back(
        upstream, normal_two, inverse_two, ffn_gain
    )
    downbias_grad = jnp.sum(sum_grad, axis=0)
    sum_low = whole_rows(sum_grad.astype(jnp.bfloat16))
    up_back, down_back = (
        lax.all_gather(up_weight.astype(jnp.bfloat16), "dp", axis=0, tiled=True),
        lax.all_gather(down_weight.astype(jnp.bfloat16), "dp", axis=1, tiled=True),
    )
    down_local = jnp.dot(act_low.T, sum_low, preferred_element_type=jnp.float32)
    act_grad = jnp.dot(sum_low, down_back.T, preferred_element_type=jnp.float32)
    (pre_grad,) = gelu_pull(act_grad)
    upbias_grad = jnp.sum(pre_grad, axis=0)
    pre_low = pre_grad.astype(jnp.bfloat16)
    up_local = jnp.dot(normed_low.T, pre_low, preferred_element_type=jnp.float32)
    upproj_grad, downproj_grad = (
        lax.psum_scatter(up_local, "dp", scatter_dimension=0, tiled=True),
        lax.psum_scatter(down_local, "dp", scatter_dimension=1, tiled=True),
    )
    normed_grad = (
        combine_rows(jnp.dot(pre_low, up_back.T, preferred_element_type=jnp.float32)) + sum_grad
    )
    resid_grad, attngain_grad, attnshift_grad = layer_norm_back(
        normed_grad, normal_one, inverse_one, attn_gain
    )
    outbias_grad = jnp.sum(resid_grad, axis=0)
    resid_low = whole_rows(resid_grad.astype(jnp.bfloat16))
    query_pullback, key_pullback, value_pullback, out_back = (
        lax.all_gather(query_weight.astype(jnp.bfloat16), "dp", axis=1, tiled=True),
        lax.all_gather(key_weight.astype(jnp.bfloat16), "dp", axis=0, tiled=True),
        lax.all_gather(value_weight.astype(jnp.bfloat16), "dp", axis=0, tiled=True),
        lax.all_gather(out_weight.astype(jnp.bfloat16), "dp", axis=1, tiled=True),
    )
    outproj_local = jnp.dot(context_rows.T, resid_low, preferred_element_type=jnp.float32)
    context_grad = jnp.dot(resid_low, out_back.T, preferred_element_type=jnp.float32).astype(
        jnp.bfloat16
    )
    context_grad = context_grad.reshape(seq_count, seq_length, local_width)
    word_qgrad, entity_qgrad, key_delta, value_delta = lax.map(
        attend_backward,
        (query_rows, keys_all, values_all, segment_ids, token_types, log_total, context_grad),
    )
    is_word = (token_types == 0)[..., None]
    zero_rows = jnp.zeros_like(word_qgrad)
    query_delta = jnp.stack(
        [
            jnp.where(is_word, word_qgrad, zero_rows),
            jnp.where(is_word, entity_qgrad, zero_rows),
            jnp.where(is_word, zero_rows, word_qgrad),
            jnp.where(is_word, zero_rows, entity_qgrad),
        ],
        axis=1,
    )
    querybias_grad = jnp.sum(query_delta, axis=(0, 2))
    valuebias_grad = jnp.sum(value_delta, axis=(0, 1))
    query_reduced = query_delta.astype(jnp.bfloat16)
    key_reduced = key_delta.astype(jnp.bfloat16)
    value_reduced = value_delta.astype(jnp.bfloat16)
    query_local = jnp.einsum(
        "nvh,nkvw->khw", layer_input, query_reduced, preferred_element_type=jnp.float32
    )
    key_shard = jnp.einsum(
        "pui,pun->in", layer_input, key_reduced, preferred_element_type=jnp.float32
    )
    value_local = jnp.einsum(
        "pui,pun->in", layer_input, value_reduced, preferred_element_type=jnp.float32
    )
    input_part = (
        jnp.einsum(
            "kayo,azo->kyz", query_reduced, query_pullback, preferred_element_type=jnp.float32
        )
        + jnp.einsum("ohz,wz->ohw", key_reduced, key_pullback, preferred_element_type=jnp.float32)
        + jnp.einsum(
            "ohz,wz->ohw", value_reduced, value_pullback, preferred_element_type=jnp.float32
        )
    )
    input_total = combine_rows(input_part.reshape(-1, model_width))
    input_grad = whole_rows((input_total + resid_grad).astype(jnp.bfloat16)).reshape(
        layer_input.shape
    )
    query_grad, key_grad, value_grad, outproj_grad = (
        lax.psum_scatter(query_local, "dp", scatter_dimension=1, tiled=True),
        lax.psum_scatter(key_shard, "dp", scatter_dimension=0, tiled=True),
        lax.psum_scatter(value_local, "dp", scatter_dimension=0, tiled=True),
        lax.psum_scatter(outproj_local, "dp", scatter_dimension=1, tiled=True),
    )
    querybias_grad, valuebias_grad, upbias_grad = lax.psum(
        (querybias_grad, valuebias_grad, upbias_grad), "dp"
    )
    outbias_grad, downbias_grad, attngain_grad, attnshift_grad, ffngain_grad, ffnshift_grad = (
        lax.psum(
            (
                outbias_grad,
                downbias_grad,
                attngain_grad,
                attnshift_grad,
                ffngain_grad,
                ffnshift_grad,
            ),
            ("dp", "tensor"),
        )
    )
    return (
        output,
        input_grad,
        query_grad,
        key_grad,
        value_grad,
        outproj_grad,
        upproj_grad,
        downproj_grad,
        querybias_grad,
        valuebias_grad,
        outbias_grad,
        upbias_grad,
        downbias_grad,
        attngain_grad,
        attnshift_grad,
        ffngain_grad,
        ffnshift_grad,
    )


MESH = pl.DeviceIdType.MESH
BF = jnp.bfloat16
F32 = jnp.float32
BLOCK = 128


def fits(mesh):
    return mesh.shape["dp"] == 8 and mesh.shape["tensor"] == 4


def nn(a, b):
    return lax.dot_general(a, b, (((1,), (0,)), ((), ())), preferred_element_type=F32)


def nt(a, b):
    return lax.dot_general(a, b, (((1,), (1,)), ((), ())), preferred_element_type=F32)


def tn(a, b):
    return lax.dot_general(a, b, (((0,), (0,)), ((), ())), preferred_element_type=F32)


def norm_rows(values):
    centre = values - jnp.mean(values, axis=-1, keepdims=True)
    inverse = lax.rsqrt(jnp.mean(centre * centre, axis=-1, keepdims=True) + EPSILON)
    return centre * inverse, inverse


def norm_rows_back(upstream, normal, inverse, gain):
    scaled = upstream * gain
    return inverse * (
        scaled
        - jnp.mean(scaled, axis=-1, keepdims=True)
        - normal * jnp.mean(scaled * normal, axis=-1, keepdims=True)
    )


class Net:
    def __init__(self, send, recv, peer):
        self.send, self.recv, self.peer = send, recv, peer
        self.sends = 0
        self.locals = 0
        self.banks = 0
        self.pending = []

    def bank(self, count):
        base = self.banks
        self.banks += count
        return base

    def start(self, src, dst, sem, device, when=None, group=None):
        slot = self.sends % SENDS
        self.sends += 1
        self.finish([p for p in self.pending if p[3] == slot])

        def make():
            return pltpu.make_async_remote_copy(
                src_ref=src,
                dst_ref=dst,
                send_sem=self.send.at[slot],
                recv_sem=self.recv.at[sem],
                device_id=device,
                device_id_type=MESH,
            )

        if when is None:
            make().start()
        else:
            pl.when(when)(lambda: make().start())
        self.pending.append((make, when, group, slot))

    def finish(self, entries):
        for make, when, _, _ in entries:
            if when is None:
                make().wait_send()
            else:
                pl.when(when)(lambda make=make: make().wait_send())
        self.pending = [p for p in self.pending if p not in entries]

    def wait(self, dst, sem, when=None):
        def make():
            return pltpu.make_async_remote_copy(
                src_ref=dst,
                dst_ref=dst,
                send_sem=self.send.at[0],
                recv_sem=self.recv.at[sem],
                device_id=self.peer,
                device_id_type=MESH,
            )

        if when is None:
            make().wait_recv()
        else:
            pl.when(when)(lambda: make().wait_recv())

    def settle(self, *groups):
        self.finish([p for p in self.pending if not groups or p[2] in groups])


SENDS = 48
RECVS = 141


def layer_kernel(
    x_in, seg_ref, typ_ref, qw_in, kw_in, vw_in, ow_in, uw_in, dw_in, qb_ref, vb_ref,
    ob_ref, ub_ref, db_ref, ag_ref, as_ref, fg_ref, fs_ref, cot_in,
    out_end, ig_end, qg_end, kg_end, vg_end, og_end, ug_end, dg_end, small_end,
    x_ref, qw_ref, kw_ref, vw_ref, ow_ref, uw_ref, dw_ref, cot_ref,
    out_ref, ig_ref, qg_ref, kg_ref, vg_ref, og_ref, ug_ref, dg_ref, small_ref,
    wq, wop, wo, own, wf, ubs, segc, wordc, xt, bias, qq, kv, kk, kvt, kkt, probs, ctx, ctp, ct, ctc,
    a_s, n1_s, r1_s, act, gelu_d, gl, parts, rs_send, rs_recv, dub, dzb,
    st_a, st_b, st_c, st_d, st_e, st_f, st_g, dct, dc, dco, go_r, rp, sp, rz,
    dqkv, dx_in, dx_cross, dx_back, gq_r, gp, sv, small_s, small_r, sent8, sw, vz,
    send_sems, recv_sems, local_sems,
):
    d = lax.axis_index("dp")
    t = lax.axis_index("tensor")
    c = d % 2
    x = (d // 2) % 2
    y = d // 4
    pair = t % 2
    j = 2 * pair + c
    block = pair + 2 * c
    home = block == t
    zp = t + 1 - 2 * pair
    zq = (t + 2) % 4
    host = 2 * (d // 2) + t // 2
    chip = d // 2
    sib = d + 1 - 2 * c
    xn = d + 2 - 4 * x
    yn = d + 4 - 8 * y
    rows = x_ref.shape[1]
    quarter = rows // 4
    width = x_ref.shape[2]
    strip = qw_ref.shape[1]
    local = kw_ref.shape[1]
    heads = local // HD
    blocks = rows // BLOCK
    own_rows = pl.ds(pl.multiple_of(t * quarter, 16), quarter)
    net = Net(send_sems, recv_sems, (sib, t))

    def flip_x(device):
        return device + 2 - 4 * ((device // 2) % 2)

    def flip_y(device):
        return device + 4 - 8 * (device // 4)

    dg = flip_y(xn)
    part_m, part_o = parts.at[0:2], parts.at[2:4]
    sums_a, sums_b = parts.reshape(rows, width), gelu_d.reshape(rows, width)
    dqq = [sums_a.at[:, BLOCK * h : BLOCK * (h + 1)] for h in range(heads)]
    dkk = [sums_a.at[:, BLOCK * (heads + h) : BLOCK * (heads + h + 1)] for h in range(heads)]
    dvv = [sums_b.at[:, BLOCK * h : BLOCK * (h + 1)] for h in range(heads)]

    low_z = t < 2
    is_end = jnp.logical_or(t == 0, t == 3)
    is_mid = jnp.logical_not(is_end)
    z_out = jnp.where(low_z, t + 1, t - 1)
    z_back = jnp.where(low_z, 0, 3)

    def place(e):
        return jnp.where(low_z, e, 3 - e)

    def joint(one, other):
        return other if one is None else jnp.logical_and(one, other)

    class LineGather:
        def __init__(self, view, group=None):
            self.view, self.bank, self.group = view, net.bank(4), group

        def copy(self, owner, to, when):
            ref = self.view(owner)
            net.start(ref, ref, self.bank + owner, (d, to), when=when, group=self.group)

        def wait(self, owner, when=None):
            net.wait(self.view(owner), self.bank + owner, when=when)

        def begin(self):
            self.copy(t, z_out, None)
            self.copy(t, z_back, is_mid)

        def step(self, n):
            if n == 1:
                self.wait(place(0), is_mid)
                self.copy(place(0), z_out, is_mid)
                self.wait(place(2), is_mid)
                self.copy(place(2), z_back, is_mid)
            if n == 2:
                self.wait(place(3), is_mid)
                self.copy(place(3), z_back, is_mid)
            self.wait(place(n), is_end)

    class LineReduce:
        def __init__(self, own, came, cross, back):
            self.own, self.came, self.cross, self.back = own, came, cross, back
            self.in_b, self.cross_b, self.back_b = net.bank(3), net.bank(2), net.bank(1)

        def depart(self, e):
            net.start(self.own(e), self.came.at[e - 1], self.in_b + e - 1, (d, z_out), when=is_end)

        def add(self, e, ref):
            @pl.when(is_mid)
            def _():
                ref[...] = (self.own(e)[...].astype(F32) + ref[...].astype(F32)).astype(BF)

        def through(self, e):
            ref = self.came.at[e - 1]
            net.wait(ref, self.in_b + e - 1, when=is_mid)
            self.add(e, ref)
            net.start(ref, self.cross.at[3 - e], self.cross_b + 3 - e, (d, z_out), when=is_mid)

        def pass_back(self):
            net.wait(self.cross.at[0], self.cross_b, when=is_mid)
            self.add(0, self.cross.at[0])
            net.start(self.cross.at[0], self.back, self.back_b, (d, z_back), when=is_mid)

        def total(self):
            net.wait(self.came.at[0], self.in_b, when=is_mid)
            net.wait(self.cross.at[1], self.cross_b + 1, when=is_mid)
            net.wait(self.back, self.back_b, when=is_end)
            others = self.came[0].astype(F32) + self.cross[1].astype(F32)
            mine = self.own(jnp.where(is_mid, 1, 0))[...].astype(F32)
            return mine + jnp.where(is_mid, others, self.back[...].astype(F32))

    class Local:
        def __init__(self, source, target):
            self.copy = pltpu.make_async_copy(source, target, local_sems.at[net.locals])
            net.locals += 1
            self.copy.start()

        def wait(self):
            self.copy.wait()

    in_q, in_k, in_v = Local(qw_in, qw_ref), Local(kw_in, kw_ref), Local(vw_in, vw_ref)
    in_o, in_u, in_d = Local(ow_in, ow_ref), Local(uw_in, uw_ref), Local(dw_in, dw_ref)
    in_x, in_cot = Local(x_in, x_ref), Local(cot_in, cot_ref)

    barrier = pltpu.get_barrier_semaphore()
    for m in range(1, 8):
        pl.semaphore_signal(barrier, 1, device_id=((d + m) % 8, t), device_id_type=MESH)
    for k in range(1, 4):
        pl.semaphore_signal(barrier, 1, device_id=(d, (t + k) % 4), device_id_type=MESH)
    pl.semaphore_signal(barrier, 1, device_id=(sib, zq), device_id_type=MESH)

    for arrived in (in_q, in_k, in_v):
        arrived.wait()
    for h in range(heads):
        at = slice(HD * h, HD * (h + 1))
        piece = jnp.concatenate(
            [qw_ref[i, :, at] for i in range(4)] + [kw_ref[:, at], vw_ref[:, at]], axis=1
        )
        wq[d, :, 6 * HD * h : 6 * HD * (h + 1)] = piece.astype(BF)

    pl.semaphore_wait(barrier, 11)

    class PlaneGather:
        def __init__(self, group, *views):
            self.views, self.bank, self.group = views, net.bank(8 * len(views)), group

        def copy(self, view, block, device):
            ref = self.views[view](block)
            net.start(ref, ref, self.bank + 8 * view + block, (device, t), group=self.group)

        def wait(self, view, block):
            net.wait(self.views[view](block), self.bank + 8 * view + block)

        def begin(self):
            for view, device in ((0, yn), (1, xn), (1, yn), (0, xn), (0, sib), (1, sib)):
                self.copy(view, d, device)

        def middle(self):
            self.wait(0, yn)
            self.copy(0, yn, xn)
            self.wait(1, xn)
            self.copy(1, xn, yn)
            self.copy(0, yn, sib)
            self.copy(1, xn, sib)

        def middle2(self):
            for view, block in ((1, yn), (0, xn)):
                self.wait(view, block)
                self.copy(view, block, sib)

        def late(self):
            for view in range(2):
                self.wait(view, dg)
                self.copy(view, dg, sib)

        def end(self):
            for block in (sib, flip_x(sib), flip_y(sib), flip_x(flip_y(sib))):
                for view in range(len(self.views)):
                    self.wait(view, block)

    gather_q = PlaneGather("q", lambda b: wq.at[b, : strip // 2], lambda b: wq.at[b, strip // 2 :])
    gather_q.begin()

    def wide_t(value, high, wide):
        r, w = value.shape
        if w < wide:
            value = jnp.concatenate([value, jnp.zeros((r, wide - w), value.dtype)], axis=1)
        if r < high:
            value = jnp.concatenate([value, jnp.zeros((high - r, wide), value.dtype)], axis=0)
        return value.T

    for arrived in (in_o, in_u, in_d):
        arrived.wait()
    def pack(block):
        most = block.shape[0] // 2
        rest = block[:, BLOCK:]
        return jnp.concatenate(
            [block[:, :BLOCK], jnp.concatenate([rest[:most], rest[most:]], axis=1)], axis=0
        )

    def rest_of(packed, count):
        below = packed[count:]
        return jnp.concatenate([below[:, :HD], below[: count - below.shape[0], HD:]], axis=0)

    wop[t, d] = pack(wide_t(ow_ref[...], 256, 128)[:strip, :local]).astype(BF)
    own[0] = uw_ref[...].astype(BF)
    own[1] = dw_ref[...].astype(BF)
    ubs[t] = jnp.broadcast_to(ub_ref[...][None], ubs.shape[1:])

    ub_z = net.bank(1)
    wf_a = net.bank(4)

    class ChipGather:
        def __init__(self, i):
            self.i, self.bank = i, net.bank(8)

        def send_near(self):
            i = self.i
            net.start(own.at[i], wf.at[i, d], wf_a + 2 * i + c, (host, t), when=host != d)

            @pl.when(host == d)
            def _():
                wf[i, d] = own[i]

        def send_far(self):
            net.start(own.at[self.i], wf.at[self.i, d], wf_a + 2 * self.i + c, (host, zq))

        def copy(self, view, of, device, when=None):
            ref = wf.at[self.i, 2 * (of // 2) + view]
            net.start(ref, ref, self.bank + 2 * (of // 2) + view, (device, t), when=when, group="f")

        def wait(self, view, of):
            net.wait(wf.at[self.i, 2 * (of // 2) + view], self.bank + 2 * (of // 2) + view)

        def begin(self, at_home):
            i, when = self.i, home if at_home else jnp.logical_not(home)
            if not at_home:
                net.wait(wf.at[i, d], wf_a + 2 * i + c, when=when)
            net.wait(wf.at[i, sib], wf_a + 2 * i + 1 - c, when=when)
            for view, device in ((0, yn), (1, xn), (1, yn), (0, xn)):
                self.copy(view, d, device, when)

        def middle(self):
            self.wait(0, yn)
            self.copy(0, yn, xn)
            self.wait(1, xn)
            self.copy(1, xn, yn)

        def end(self):
            for view, of in ((1, yn), (0, xn), (0, dg), (1, dg)):
                self.wait(view, of)

    up, down = ChipGather(0), ChipGather(1)
    wo_z = net.bank(1)
    for k in (2, 1, 3):
        net.start(wop.at[t, d], wop.at[t, d], wo_z, (d, (t + k) % 4))
    up.send_near()
    down.send_near()
    for b in range(blocks):
        at = slice(BLOCK * b, BLOCK * (b + 1))
        segc[at, :] = jnp.broadcast_to(seg_ref[:, at].astype(F32), (BLOCK, BLOCK)).T
        wordc[at, :] = jnp.broadcast_to((typ_ref[:, at] == 0).astype(F32), (BLOCK, BLOCK)).T
    in_x.wait()
    xt[...] = x_ref[0].T
    for h in range(heads):
        at = slice(HD * h, HD * (h + 1))
        bias[:, 6 * HD * h : 6 * HD * (h + 1)] = jnp.concatenate(
            [qb_ref[i : i + 1, at] for i in range(4)] + [jnp.zeros((1, HD), F32), vb_ref[at][None]],
            axis=1,
        )

    gather_q.middle()
    up.send_far()
    net.start(ubs.at[t], ubs.at[t], ub_z, (d, zq))
    down.send_far()
    gather_q.middle2()
    net.wait(wop.at[0:3, d], wo_z)
    gather_o = PlaneGather("o", lambda b: wop.at[0:2, b], lambda b: wop.at[2:4, b])
    gather_o.begin()
    up.begin(True)
    gather_q.late()
    gather_q.end()
    low_half = lax.broadcasted_iota(jnp.int32, (rows, BLOCK), 1) < HD
    is_word = wordc[...] > 0.5
    for h in range(heads):
        base = 6 * HD * h
        at = slice(BLOCK * h, BLOCK * (h + 1))
        made = nn(x_ref[0], wq[:, :, base : base + 6 * HD].reshape(width, 6 * HD))
        made = made + bias[:, base : base + 6 * HD]
        qq[:, at] = jnp.where(is_word, made[:, :BLOCK], made[:, BLOCK : 2 * BLOCK]).astype(BF)
        both = made[:, 2 * BLOCK :]
        keys = jnp.where(low_half, both, pltpu.roll(both, HD, 1))
        keys = jnp.where(jnp.logical_xor(is_word, low_half), 0.0, keys)
        kv[:, at] = both.astype(BF)
        kk[:, at] = keys.astype(BF)
        kvt[h] = both.T[HD:].astype(BF)
        kkt[h] = keys.T.astype(BF)

    gather_o.middle()
    gather_o.middle2()
    ct_z = net.bank(1)

    def span(b):
        return BLOCK * max(0, b - 2), BLOCK * min(blocks, b + 3)

    kept = [0]
    for b in range(blocks):
        kept.append(kept[-1] + span(b)[1] - span(b)[0])
    for b in range(blocks):
        lo, hi = span(b)
        at_q = slice(BLOCK * b, BLOCK * (b + 1))
        same = segc[lo:hi, :] == seg_ref[:, at_q].astype(F32)
        found = []
        for h in range(heads):
            at = slice(BLOCK * h, BLOCK * (h + 1))
            scores = nt(kk[lo:hi, at], qq[at_q, at]) * SCALING
            scores = jnp.where(same, scores, NEGATIVE)
            weights = jnp.exp(scores - jnp.max(scores, axis=0, keepdims=True))
            weights = weights * (1.0 / jnp.sum(weights, axis=0, keepdims=True))
            probs[h, kept[b] : kept[b + 1]] = weights
            found.append(nn(kvt[h, :, lo:hi], weights.astype(BF)))
        found.append(jnp.zeros((HD, BLOCK), F32))
        ctx[at_q, :] = jnp.concatenate(found, axis=0).T[:, :local].astype(BF)
        if b == 2:
            up.begin(False)
        if b > 0:
            s = b - 1
            ctp[s] = pack(ctx[quarter * s : quarter * (s + 1), :])
            net.start(ctp.at[s], ct.at[t], ct_z, (d, s), when=t != s)
    ct[t] = ctp[t]

    down.begin(True)
    gather_o.late()
    down.begin(False)
    up.middle()
    gather_o.end()
    for s in range(4):
        wo[:, :, BLOCK * s : BLOCK * (s + 1)] = wop[s, :, :strip]
    most = strip // 2
    for s in (0, 2):
        at = slice(4 * BLOCK + HD * s, 4 * BLOCK + HD * (s + 2))
        one, other = wop[s, :, strip:], wop[s + 1, :, strip:]
        wo[:, :most, at] = jnp.concatenate([one[:, :, :HD], other[:, :, :HD]], axis=2)
        wo[:, most:, at] = jnp.concatenate([one[:, :, HD:], other[:, :, HD:]], axis=2)
    net.wait(ct.at[0:3], ct_z)
    for s in range(4):
        ctc[:, BLOCK * s : BLOCK * (s + 1)] = ct[s, :quarter]
    for s in (0, 2):
        ctc[:, 4 * BLOCK + HD * s : 4 * BLOCK + HD * (s + 2)] = jnp.concatenate(
            [rest_of(ct[s], quarter), rest_of(ct[s + 1], quarter)], axis=1
        )
    whole_wo = wo.reshape(width, width)
    attended = nt(ctc[...], whole_wo[...])
    normal, inverse = norm_rows(x_ref[0, own_rows, :].astype(F32) + attended + ob_ref[...][None])
    n1_s[...] = normal
    r1_s[...] = jnp.broadcast_to(inverse, r1_s.shape)
    normed = normal * ag_ref[...][None] + as_ref[...][None]
    a_s[...] = normed
    act[j] = normed.astype(BF)

    def rows_of(ref, first, count):
        return lambda owner: ref.at[
            0, pl.ds(pl.multiple_of(owner * quarter + first, 16), count)
        ]

    part = quarter // 2
    chunk = [slice(part * q, part * (q + 1)) for q in range(2)]

    class RowGather:
        def __init__(self, ref):
            self.ref, self.bank = ref, net.bank(8)

        def copy(self, q, rank, device):
            ref = self.ref.at[rank, chunk[q]]
            net.start(ref, ref, self.bank + 4 * q + rank, device)

        def wait(self, q, rank):
            net.wait(self.ref.at[rank, chunk[q]], self.bank + 4 * q + rank)

        def begin(self, q):
            self.copy(q, j, (d, zp))
            self.copy(q, j, (sib, t))

        def near(self, q):
            self.wait(q, 2 * pair + 1 - c)

        def middle(self, q):
            self.wait(q, 2 - 2 * pair + c)
            self.copy(q, 2 - 2 * pair + c, (sib, t))

        def far(self, q):
            self.wait(q, 3 - 2 * pair - c)

    class RowSum:
        def __init__(self, index):
            self.index, self.bank = index, net.bank(6)

        def hand(self, q, slot, partial_rows):
            where = 3 * self.index + slot
            rs_send[where, chunk[q]] = partial_rows.astype(BF)
            net.start(
                rs_send.at[where, chunk[q]], rs_recv.at[where, chunk[q]], self.bank + 3 * q + slot,
                (d, zp) if slot == 2 else (sib, t),
            )

        def take(self, q, slot):
            where = 3 * self.index + slot
            net.wait(rs_recv.at[where, chunk[q]], self.bank + 3 * q + slot)
            return rs_recv[where, chunk[q]].astype(F32)

        def near(self, q):
            self.hand(q, 0, part_m[1 - c, chunk[q]])

        def away(self, q):
            self.hand(q, 1, part_o[1 - c, chunk[q]])

        def across(self, q):
            self.hand(q, 2, part_o[c, chunk[q]] + self.take(q, 1))

        def total(self, q):
            return part_m[c, chunk[q]] + self.take(q, 0) + self.take(q, 2)

    rows_a = RowGather(act)
    rows_a.begin(0)
    rows_a.begin(1)
    down.middle()
    rows_a.middle(0)
    rows_a.middle(1)
    rows_a.near(0)
    rows_a.near(1)
    net.wait(ubs.at[zq], ub_z)
    up.end()
    near = pl.ds(2 * pair, 2)
    away = pl.ds(2 - 2 * pair, 2)

    def feed(half):
        hidden = nn(act[half].reshape(2 * quarter, width), wf[0].reshape(width, width))
        hidden = hidden + ubs[block][:1]
        bell = 0.5 * (1.0 + lax.erf(hidden * 0.7071067811865476))
        slope = bell + hidden * (0.3989422804014327 * jnp.exp(-0.5 * hidden * hidden))
        gelu_d[half] = slope.reshape(2, quarter, width)
        gl[half] = (hidden * bell).astype(BF).reshape(2, quarter, width)

    def feed_out(half, partial_ref):
        made = nt(gl[half].reshape(2 * quarter, width), wf[1].reshape(width, width))
        partial_ref[...] = made.reshape(2, quarter, width)

    feed(near)
    rows_a.far(0)
    rows_a.far(1)
    feed(away)
    down.end()
    sum_f = RowSum(0)
    feed_out(away, part_o)
    sum_f.away(0)
    sum_f.away(1)
    feed_out(near, part_m)
    sum_f.across(0)
    sum_f.across(1)
    sum_f.near(0)
    sum_f.near(1)
    in_cot.wait()
    rows_u = RowGather(dub)
    gain_sum, shift_sum, bias_sum = 0.0, 0.0, 0.0
    for q in range(2):
        ffn_out = sum_f.total(q) + db_ref[...][None]
        normal, inverse = norm_rows(a_s[chunk[q]] + ffn_out)
        rows_q = pl.ds(pl.multiple_of(t * quarter + part * q, 16), part)
        out_ref[0, rows_q, :] = (normal * fg_ref[...][None] + fs_ref[...][None]).astype(BF)
        upstream = cot_ref[0, rows_q, :].astype(F32)
        du = norm_rows_back(upstream, normal, inverse, fg_ref[...][None])
        dub[j, chunk[q]] = du.astype(BF)
        rows_u.begin(q)
        a_s[chunk[q]] = du
        gain_sum = gain_sum + jnp.sum(upstream * normal, axis=0, keepdims=True)
        shift_sum = shift_sum + jnp.sum(upstream, axis=0, keepdims=True)
        bias_sum = bias_sum + jnp.sum(du, axis=0, keepdims=True)
    line_out = [LineGather(rows_of(out_ref, part * q, part)) for q in range(2)]
    line_out[0].begin()
    sv[...] = jnp.zeros_like(sv)
    sv[0:1] = gain_sum
    sv[1:2] = shift_sum
    sv[2:3] = bias_sum

    def feed_back(half, rows_q, partial_ref):
        count = 2 * (rows_q.stop - rows_q.start)
        made = nn(dub[half, rows_q].reshape(count, width), wf[1].reshape(width, width))
        made = made * gelu_d[half, rows_q].reshape(count, width)
        low = made.astype(BF)
        dzb[half, rows_q] = low.reshape(2, count // 2, width)
        partial_ref[:, rows_q] = nt(low, wf[0].reshape(width, width)).reshape(2, count // 2, width)
        return jnp.sum(made, axis=0, keepdims=True)

    sum_b = RowSum(1)
    rows_u.near(0)
    rows_u.near(1)
    up_sum = feed_back(near, slice(0, quarter), part_m)
    sum_b.near(0)
    sum_b.near(1)
    rows_u.middle(0)
    rows_u.far(0)
    up_sum = up_sum + feed_back(away, chunk[0], part_o)
    sum_b.away(0)
    rows_u.middle(1)
    sum_b.across(0)
    rows_u.far(1)
    up_sum = up_sum + feed_back(away, chunk[1], part_o)
    sum_b.away(1)
    sv[6:7] = up_sum
    half = width // 2

    class StripSum:
        def __init__(self, i):
            self.i, self.bank = i, net.bank(9)
            self.by_chip = wf.at[i].reshape(2, 2, 2, strip, width)

        def make(self, left, right):
            made = tn(left[...].reshape(4 * quarter, width), right[...].reshape(4 * quarter, width))
            wf[self.i] = made.astype(BF).reshape(8, strip, width)

        def begin(self):
            net.start(
                self.by_chip.at[:, 1 - x, :, :, :half], st_a.at[self.i], self.bank, (xn, t)
            )
            net.start(
                self.by_chip.at[1 - y, :, :, :, half:], st_b.at[self.i], self.bank + 1, (yn, t)
            )

        def turn(self):
            i = self.i
            net.wait(st_a.at[i], self.bank)
            st_a[i] = (st_a[i].astype(F32) + self.by_chip[:, x, :, :, :half].astype(F32)).astype(BF)
            for core in range(2):
                net.start(
                    st_a.at[i, 1 - y, core], st_c.at[i, c], self.bank + 2 + c,
                    (2 * (yn // 2) + core, t),
                )
            net.start(st_a.at[i, y, 1 - c], st_g.at[i, 0], self.bank + 6, (sib, t))
            net.wait(st_b.at[i], self.bank + 1)
            st_b[i] = (st_b[i].astype(F32) + self.by_chip[y, :, :, :, half:].astype(F32)).astype(BF)
            for core in range(2):
                net.start(
                    st_b.at[i, 1 - x, core], st_d.at[i, c], self.bank + 4 + c,
                    (2 * (xn // 2) + core, t),
                )
            net.start(st_b.at[i, x, 1 - c], st_g.at[i, 1], self.bank + 7, (sib, t))

        def gather(self):
            i = self.i
            for core in range(2):
                net.wait(st_c.at[i, core], self.bank + 2 + core)
                net.wait(st_d.at[i, core], self.bank + 4 + core)
            net.wait(st_g.at[i, 0], self.bank + 6)
            net.wait(st_g.at[i, 1], self.bank + 7)
            for whose, first, second in (
                (c, st_a.at[i, y, c], st_b.at[i, x, c]), (1 - c, st_g.at[i, 0], st_g.at[i, 1])
            ):
                st_e[i, whose, :, :half] = (
                    first[...].astype(F32) + st_c[i, whose].astype(F32)
                ).astype(BF)
                st_e[i, whose, :, half:] = (
                    second[...].astype(F32) + st_d[i, whose].astype(F32)
                ).astype(BF)

        def deliver(self, when=None):
            i = self.i
            net.start(st_e.at[i, 1 - t // 2], st_f.at[i], self.bank + 8, (d, zq), when=when)

        def total(self):
            i = self.i
            net.wait(st_f.at[i], self.bank + 8)
            return st_e[i, t // 2].astype(F32) + st_f[i].astype(F32)

    class SmallSum:
        def __init__(self, index):
            self.index, self.bank = index, net.bank(2)

        def begin(self, values):
            i = self.index
            small_s[i, 0] = values
            for r in (xn, yn, dg):
                net.start(small_s.at[i, 0], small_r.at[i, chip], self.bank, (r, t))
            small_r[i, chip] = values

        def plane(self):
            i = self.index
            net.wait(small_r.at[i, 0:3], self.bank)
            total = small_r[i, 0]
            for k in range(1, 4):
                total = total + small_r[i, k]
            small_s[i, 1] = total
            net.start(small_s.at[i, 1], small_r.at[i, 4], self.bank + 1, (sib, t))

        def cores(self):
            net.wait(small_r.at[self.index, 4], self.bank + 1)
            return small_s[self.index, 1], small_r[self.index, 4]

    net.settle("f")
    down_sum, up_sums = StripSum(1), StripSum(0)
    down_sum.make(dub, gl)
    down_sum.begin()
    sum_b.across(1)
    up_sums.make(act, dzb)
    dc_z = net.bank(1)
    gain_sum, shift_sum, bias_sum, dhb = 0.0, 0.0, 0.0, []
    for q in range(2):
        da = a_s[chunk[q]] + sum_b.total(q)
        normal = n1_s[chunk[q]]
        dh = norm_rows_back(da, normal, r1_s[chunk[q], :1], ag_ref[...][None])
        a_s[chunk[q]] = dh
        dhb.append(dh.astype(BF))
        made = nn(dhb[q], whole_wo[...])
        for s in range(4):
            rest = made[:, 4 * BLOCK + HD * s : 4 * BLOCK + HD * (s + 1)]
            rest = jnp.concatenate([rest, jnp.zeros((16, HD), F32)], axis=0)
            most = (part + 16) // 2
            dct[s, q] = jnp.concatenate(
                [
                    made[:, BLOCK * s : BLOCK * (s + 1)],
                    jnp.concatenate([rest[:most], rest[most:]], axis=1),
                ],
                axis=0,
            ).astype(BF)
        for k in (2, 1, 3):
            s = (t + k) % 4
            net.start(dct.at[s, q], dc.at[t, q], dc_z, (d, s))
        dc[t, q] = dct[t, q]
        gain_sum = gain_sum + jnp.sum(da * normal, axis=0, keepdims=True)
        shift_sum = shift_sum + jnp.sum(da, axis=0, keepdims=True)
        bias_sum = bias_sum + jnp.sum(dh, axis=0, keepdims=True)
    dhb = jnp.concatenate(dhb, axis=0)
    line_out[1].begin()
    line_out[0].step(1)
    sv[3:4] = gain_sum
    sv[4:5] = shift_sum
    sv[5:6] = bias_sum
    small_a = SmallSum(0)
    small_a.begin(sv[...])
    down_sum.turn()
    up_sums.begin()
    wo[...] = tn(dhb, ctc[...]).astype(BF).reshape(8, strip, width)
    by_core = wo.reshape(4, 2, strip, width)
    go_b = net.bank(1)
    net.start(by_core.at[:, 1 - c], go_r, go_b, (sib, t))

    net.wait(dc.at[0:3], dc_z)
    upper = lax.broadcasted_iota(jnp.int32, (part, BLOCK), 1) >= HD
    for s in range(4):
        for q in range(2):
            got = dc[s, q]
            at_q = slice(quarter * s + part * q, quarter * s + part * (q + 1))
            first = got[:part].astype(F32)
            blank = jnp.zeros((part, HD), BF)
            dco[at_q, :BLOCK] = jnp.concatenate([blank, got[:part, :HD]], axis=1)
            dco[at_q, BLOCK : 2 * BLOCK] = jnp.where(upper, first, 0.0).astype(BF)
            dco[at_q, 2 * BLOCK :] = jnp.concatenate([blank, rest_of(got, part)], axis=1)
    for h in range(heads):
        dkk[h][...] = jnp.zeros((rows, BLOCK), F32)
        dvv[h][...] = jnp.zeros((rows, BLOCK), F32)
    for b in range(blocks):
        lo, hi = span(b)
        at_q = slice(BLOCK * b, BLOCK * (b + 1))
        if b == 3:
            line_out[1].step(1)
        if b == 4:
            line_out[0].step(2)
            down_sum.gather()
            down_sum.deliver()
        for h in range(heads):
            at = slice(BLOCK * h, BLOCK * (h + 1))
            weights = probs[h, kept[b] : kept[b + 1]]
            dp = nt(kv[lo:hi, at], dco[at_q, at])
            ds = weights * (dp - jnp.sum(weights * dp, axis=0, keepdims=True))
            dsb = ds.astype(BF)
            dkk[h][lo:hi] += nn(dsb, qq[at_q, at])
            dvv[h][lo:hi] += nn(weights.astype(BF), dco[at_q, at])
            dqq[h][at_q] = nn(kkt[h, :, lo:hi], dsb).T * SCALING

    small_a.plane()
    for h in range(heads):
        base = 6 * HD * h
        first = jnp.where(is_word, dqq[h][...], 0.0)
        second = jnp.where(is_word, 0.0, dqq[h][...])
        keys = dkk[h][...]
        keys = jnp.where(is_word, keys, pltpu.roll(keys, HD, 1)) * SCALING
        third = jnp.where(low_half, keys, dvv[h][...])
        for i, piece in enumerate((first, second, third)):
            at = slice(base + BLOCK * i, base + BLOCK * (i + 1))
            dqkv[:, at] = piece.astype(BF)
            row, col = divmod(base + BLOCK * i, width)
            sv[row : row + 1, col : col + BLOCK] = jnp.sum(piece, axis=0, keepdims=True)

    first_rows = pl.ds(pl.multiple_of(jnp.where(low_z, rows // 2, 0), 16), rows // 2)
    other_rows = pl.ds(pl.multiple_of(jnp.where(low_z, 0, rows // 2), 16), rows // 2)
    first_two = pl.ds(jnp.where(low_z, 2, 0), 2)
    other_two = pl.ds(jnp.where(low_z, 0, 2), 2)

    def back_to_input(rows_b, quarters):
        made = nt(dqkv[rows_b, :], wq[...].reshape(width, 6 * local))
        dzb[quarters] = made.astype(BF).reshape(2, quarter, width)

    line_dx, line_in = [], []
    for q in range(2):
        cut = pl.ds(part * q, part)
        line_dx.append(
            LineReduce(
                lambda e, cut=cut: dzb.at[place(e), cut],
                dx_in.at[q], dx_cross.at[q], dx_back.at[q],
            )
        )
        line_in.append(LineGather(rows_of(ig_ref, part * q, part)))

    def arrive(q):
        total = line_dx[q].total() + a_s[part * q : part * (q + 1)]
        ig_ref[0, pl.ds(pl.multiple_of(t * quarter + part * q, 16), part)] = total.astype(BF)
        line_in[q].begin()

    back_to_input(first_rows, first_two)
    for q, e in ((0, 3), (0, 2), (1, 3), (1, 2)):
        line_dx[q].depart(e)
    back_to_input(other_rows, other_two)
    line_dx[0].depart(1)
    line_dx[1].depart(1)
    line_out[1].step(2)
    small_b = SmallSum(1)
    small_b.begin(sv[...])

    net.settle("q")
    wq[...] = nn(xt[...], dqkv[...]).astype(BF).reshape(8, strip, 6 * local)
    q_by_core = wq.reshape(4, 2, strip, 6 * local)
    gq_b = net.bank(1)
    net.start(q_by_core.at[:, 1 - c], gq_r, gq_b, (sib, t))
    up_sums.turn()
    net.wait(go_r, go_b)
    go_r[...] = (by_core[:, c].astype(F32) + go_r[...].astype(F32)).astype(BF)
    rp_b = net.bank(1)
    for r in (xn, yn, dg):
        net.start(go_r.at[r // 2], rp.at[chip], rp_b, (r, t))
    rp[chip] = go_r[chip]
    plane_sum, other_sum = small_a.cores()
    first_core = c == 0
    own_units, other_units = plane_sum[6:7], other_sum[6:7]
    sent8[0:6] = plane_sum[0:6] + other_sum[0:6]
    sent8[6:7] = jnp.where(first_core, own_units, other_units)
    sent8[7:8] = jnp.where(first_core, other_units, own_units)
    vz_b = net.bank(2)
    for k in (2, 1, 3):
        net.start(sent8, vz.at[t], vz_b, (d, (t + k) % 4), when=first_core)
    vz[t] = sent8[...]
    line_dx[0].through(3)
    line_dx[0].through(2)
    net.wait(gq_r, gq_b)
    gq_r[...] = (q_by_core[:, c].astype(F32) + gq_r[...].astype(F32)).astype(BF)
    gp_b = net.bank(1)
    for r in (xn, yn, dg):
        net.start(gq_r.at[r // 2], gp.at[chip], gp_b, (r, t))
    gp[chip] = gq_r[chip]

    line_dx[0].pass_back()
    line_dx[1].through(3)
    line_dx[1].through(2)
    line_dx[1].pass_back()
    up_sums.gather()
    up_sums.deliver(is_mid)
    arrive(0)
    arrive(1)

    line_in[0].step(1)
    line_in[1].step(1)
    up_sums.deliver(is_end)
    net.wait(rp.at[0:3], rp_b)
    total = rp[0].astype(F32)
    for k in range(1, 4):
        total = total + rp[k].astype(F32)
    for s in range(4):
        rest = total[:, 4 * BLOCK + HD * s : 4 * BLOCK + HD * (s + 1)]
        sp[s] = pack(
            jnp.concatenate([total[:, BLOCK * s : BLOCK * (s + 1)], rest], axis=1)
        ).astype(BF)
    rz_b = net.bank(1)
    rz[t] = sp[t]

    def send_rz(when):
        for k in range(1, 4):
            s = (t + k) % 4
            net.start(sp.at[s], rz.at[t], rz_b, (d, s), when=when)

    send_rz(None)
    line_out[0].step(3)
    line_out[1].step(3)
    ends = [Local(out_ref, out_end)]
    line_in[0].step(2)
    line_in[1].step(2)
    small_b.plane()
    net.wait(vz.at[0:3], vz_b, when=first_core)

    @pl.when(first_core)
    def _():
        total = vz[0]
        for k in range(1, 4):
            total = total + vz[k]
        sw[0:6] = total[0:6]
        units = vz[t] + vz[zq]
        sw[6:7] = jnp.where(t < 2, units[6:7], units[7:8])
        sw[7:8] = units[7:8]

    net.start(sw, sw, vz_b + 1, (sib, t), when=first_core)
    net.wait(sw, vz_b + 1, when=c == 1)
    small_ref[0:8] = sw[...]
    plane_sum, other_sum = small_b.cores()
    small_ref[8:16] = plane_sum + other_sum
    dg_ref[...] = down_sum.total()
    ug_ref[...] = up_sums.total()
    ends += [Local(dg_ref, dg_end), Local(ug_ref, ug_end), Local(small_ref, small_end)]
    net.wait(rz.at[0:3], rz_b)
    total = rz[0].astype(F32)
    for s in range(1, 4):
        total = total + rz[s].astype(F32)
    total = jnp.concatenate([total[:strip], rest_of(total, strip)], axis=1)
    og_ref[...] = wide_t(total, BLOCK, 256)[:local, :strip]

    ends += [Local(og_ref, og_end)]
    net.wait(gp.at[0:3], gp_b)
    total = gp[0].astype(F32)
    for k in range(1, 4):
        total = total + gp[k].astype(F32)
    for h in range(heads):
        base = 6 * HD * h
        at = slice(HD * h, HD * (h + 1))
        for i in range(4):
            qg_ref[i, :, at] = total[:, base + HD * i : base + HD * (i + 1)]
        kg_ref[:, at] = total[:, base + 4 * HD : base + 5 * HD]
        vg_ref[:, at] = total[:, base + 5 * HD : base + 6 * HD]

    ends += [Local(qg_ref, qg_end), Local(kg_ref, kg_end), Local(vg_ref, vg_end)]
    for q in range(2):
        line_in[q].step(3)
    ends += [Local(ig_ref, ig_end)]
    net.settle()
    for copy in ends:
        copy.wait()
    assert net.banks == RECVS, net.banks


def end_kernel(*refs):
    sources, small = refs[:8], refs[8]
    targets, (qbg, vbg), vectors = refs[9:17], refs[17:19], refs[19:26]
    for source, target in zip(sources, targets):
        target[...] = source[...]
    fgg, fsg, dbg, agg, asg, obg, ubg = (small[i] for i in range(7))
    for ref, value in zip(vectors, (obg, ubg, dbg, agg, asg, fgg, fsg)):
        ref[...] = value
    width = small.shape[1]
    values = []
    for h in range(vbg.shape[0] // HD):
        row, col = divmod(6 * HD * h, width)
        piece = small[8 + row : 9 + row, col : col + 6 * HD]
        for i in range(4):
            qbg[i : i + 1, HD * h : HD * (h + 1)] = piece[:, HD * i : HD * (i + 1)]
        values.append(piece[:, 5 * HD :])
    vbg[...] = jnp.concatenate(values, axis=1)[0]


def fused(
    layer_input, segment_ids, token_types, query_weight, key_weight, value_weight, out_weight,
    up_weight, down_weight, query_bias, value_bias, out_bias, up_bias, down_bias, attn_gain,
    attn_shift, ffn_gain, ffn_shift, cotangent,
):
    rows, width = layer_input.shape[1:]
    strip, local = key_weight.shape
    quarter, heads, blocks = rows // 4, local // HD, rows // BLOCK
    kept = sum(BLOCK * (min(blocks, b + 3) - max(0, b - 2)) for b in range(blocks))
    args = [
        layer_input, segment_ids, token_types, query_weight, key_weight, value_weight, out_weight,
        up_weight, down_weight.T, query_bias, value_bias, out_bias, up_bias, down_bias, attn_gain,
        attn_shift, ffn_gain, ffn_shift, cotangent,
    ]

    def like(v, dtype=F32):
        return jax.ShapeDtypeStruct(v.shape, dtype)

    outs = [
        like(layer_input, BF), like(layer_input, BF), like(query_weight), like(key_weight),
        like(value_weight), like(out_weight), like(up_weight), jax.ShapeDtypeStruct((strip, width), F32),
        jax.ShapeDtypeStruct((16, width), F32),
    ]
    v = pltpu.VMEM
    scratch = [
        v(layer_input.shape, BF), v(query_weight.shape, F32), v(key_weight.shape, F32),
        v(value_weight.shape, F32), v(out_weight.shape, F32), v(up_weight.shape, F32),
        v((strip, width), F32), v(cotangent.shape, BF),
    ] + [v(o.shape, o.dtype) for o in outs] + [
        v((8, strip, 6 * local), BF), v((4, 8, 3 * strip // 2, BLOCK), BF), v((8, strip, width), BF),
        v((2, strip, width), BF),
        v((2, 8, strip, width), BF), v((4, 8, width), F32), v((rows, BLOCK), F32),
        v((rows, BLOCK), F32), v((width, rows), BF), v((1, 6 * local), F32),
        v((rows, heads * BLOCK), BF), v((rows, heads * BLOCK), BF), v((rows, heads * BLOCK), BF),
        v((heads, HD, rows), BF), v((heads, BLOCK, rows), BF),
        v((heads, kept, BLOCK), F32), v((rows, local), BF), v((4, 3 * quarter // 2, BLOCK), BF),
        v((4, 3 * quarter // 2, BLOCK), BF), v((quarter, width), BF),
        v((quarter, width), F32), v((quarter, width), F32), v((quarter, BLOCK), F32),
        v((4, quarter, width), BF), v((4, quarter, width), F32), v((4, quarter, width), BF),
        v((4, quarter, width), F32),
        v((6, quarter, width), BF), v((6, quarter, width), BF),
        v((4, quarter, width), BF), v((4, quarter, width), BF),
        v((2, 2, 2, strip, width // 2), BF), v((2, 2, 2, strip, width // 2), BF),
        v((2, 2, strip, width // 2), BF), v((2, 2, strip, width // 2), BF),
        v((2, 2, strip, width), BF), v((2, strip, width), BF),
        v((2, 2, strip, width // 2), BF),
        v((4, 2, BLOCK, BLOCK), BF), v((4, 2, BLOCK, BLOCK), BF),
        v((rows, heads * BLOCK), BF),
        v((4, strip, width), BF), v((4, strip, width), BF), v((4, 3 * strip // 2, BLOCK), BF),
        v((4, 3 * strip // 2, BLOCK), BF),
        v((rows, 6 * local), BF),
        v((2, 3, quarter // 2, width), BF), v((2, 2, quarter // 2, width), BF),
        v((2, quarter // 2, width), BF),
        v((4, strip, 6 * local), BF), v((4, strip, 6 * local), BF),
        v((8, width), F32), v((2, 2, 8, width), F32), v((2, 5, 8, width), F32),
        v((8, width), F32), v((8, width), F32), v((4, 8, width), F32),
        pltpu.SemaphoreType.DMA((SENDS,)), pltpu.SemaphoreType.DMA((RECVS,)),
        pltpu.SemaphoreType.DMA((17,)),
    ]
    spec = pl.BlockSpec(memory_space=pltpu.VMEM)
    anywhere = pl.BlockSpec(memory_space=pl.ANY)
    large_args = (0, 3, 4, 5, 6, 7, 8, 18)
    made = pl.pallas_call(
        layer_kernel,
        out_shape=outs,
        in_specs=[anywhere if n in large_args else spec for n in range(len(args))],
        out_specs=[anywhere] * len(outs),
        scratch_shapes=scratch,
        compiler_params=pltpu.CompilerParams(
            collective_id=0, has_side_effects=True, vmem_limit_bytes=58 << 20
        ),
        name="layer",
    )(*args)
    *large, small = made
    vector = jax.ShapeDtypeStruct((width,), F32)
    ended = pl.pallas_call(
        end_kernel,
        out_shape=[like(v, v.dtype) for v in large]
        + [like(query_bias), jax.ShapeDtypeStruct((local,), F32)]
        + [vector] * 7,
        in_specs=[spec] * len(made),
        out_specs=[spec] * 17,
        name="finish",
    )(*large, small)
    return (*ended[:7], ended[7].T, *ended[8:])


def solution(mesh):
    in_specs = (
        P("dp", None, None),
        P("dp", None),
        P("dp", None),
        P(None, "dp", "tensor"),
        P("dp", "tensor"),
        P("dp", "tensor"),
        P("tensor", "dp"),
        P("dp", "tensor"),
        P("tensor", "dp"),
        P(None, "tensor"),
        P("tensor"),
        P(),
        P("tensor"),
        P(),
        P(),
        P(),
        P(),
        P(),
        P("dp", None, None),
    )
    out_specs = (
        P("dp", None, None),
        P("dp", None, None),
        P(None, "dp", "tensor"),
        P("dp", "tensor"),
        P("dp", "tensor"),
        P("tensor", "dp"),
        P("dp", "tensor"),
        P("tensor", "dp"),
        P(None, "tensor"),
        P("tensor"),
        P(),
        P("tensor"),
        P(),
        P(),
        P(),
        P(),
        P(),
    )
    step = fused if fits(mesh) else shards
    return jax.shard_map(step, mesh=mesh, in_specs=in_specs, out_specs=out_specs, check_vma=False)
```

```python
from functools import partial

import jax
import jax.numpy as jnp
from jax import lax
from jax.experimental import pallas as pl
from jax.experimental.pallas import tpu as pltpu
from jax.sharding import PartitionSpec as P

HD = 64


EPSILON = 1e-05
SCALING = 0.125
NEGATIVE = -1000000000.0


def layer_norm_keep(values, norm_gain, norm_shift):
    centre = values - jnp.mean(values, axis=-1, keepdims=True)
    inverse = lax.rsqrt(jnp.mean(centre * centre, axis=-1, keepdims=True) + EPSILON)
    normal = centre * inverse
    return (normal * norm_gain + norm_shift, normal, inverse)


def layer_norm_back(upstream, normal, inverse, norm_gain):
    scaled = upstream * norm_gain
    gain_grad = jnp.sum(upstream * normal, axis=0)
    shift_grad = jnp.sum(upstream, axis=0)
    inner_term = (
        scaled
        - jnp.mean(scaled, axis=-1, keepdims=True)
        - normal * jnp.mean(scaled * normal, axis=-1, keepdims=True)
    )
    return (inverse * inner_term, gain_grad, shift_grad)


def heads_of(matrix):
    return matrix.reshape(matrix.shape[0], -1, HD)


def pick_queries(query_rows, type_row):
    word_tok = (type_row == 0)[:, None]
    return (
        jnp.where(word_tok, query_rows[0], query_rows[2]),
        jnp.where(word_tok, query_rows[1], query_rows[3]),
    )


def score_block(word_heads, entity_heads, key_heads, segment_row, type_row):
    to_words = jnp.einsum("qhd,khd->hqk", word_heads, key_heads, preferred_element_type=jnp.float32)
    to_entities = jnp.einsum(
        "qhd,khd->hqk", entity_heads, key_heads, preferred_element_type=jnp.float32
    )
    scores = jnp.where((type_row == 0)[None, None, :], to_words, to_entities) * SCALING
    allowed = (segment_row[:, None] == segment_row[None, :])[None]
    return jnp.where(allowed, scores, NEGATIVE)


def attend_forward(packed):
    query_rows, key_seq, value_seq, segment_row, type_row = packed
    word_query, entity_query = pick_queries(query_rows, type_row)
    scores = score_block(
        heads_of(word_query), heads_of(entity_query), heads_of(key_seq), segment_row, type_row
    )
    row_top = jnp.max(scores, axis=-1, keepdims=True)
    weights = jnp.exp(scores - row_top)
    totals = jnp.sum(weights, axis=-1, keepdims=True)
    attn_probs = (weights / totals).astype(jnp.bfloat16)
    context = jnp.einsum(
        "hqk,khd->qhd", attn_probs, heads_of(value_seq), preferred_element_type=jnp.float32
    )
    log_total = (row_top + jnp.log(totals))[..., 0]
    return (context.reshape(context.shape[0], -1).astype(jnp.bfloat16), log_total)


def attend_backward(packed):
    query_rows, key_seq, value_seq, segment_row, type_row, log_total, context_grad = packed
    word_query, entity_query = pick_queries(query_rows, type_row)
    word_heads = heads_of(word_query)
    entity_heads = heads_of(entity_query)
    key_heads = heads_of(key_seq)
    value_heads = heads_of(value_seq)
    grad_heads = heads_of(context_grad)
    scores = score_block(word_heads, entity_heads, key_heads, segment_row, type_row)
    attn_probs = jnp.exp(scores - log_total[..., None])
    prob_grad = jnp.einsum(
        "qhd,khd->hqk", grad_heads, value_heads, preferred_element_type=jnp.float32
    )
    score_grad = attn_probs * (prob_grad - jnp.sum(attn_probs * prob_grad, axis=-1, keepdims=True))
    score_low = score_grad.astype(jnp.bfloat16)
    word_key = (type_row == 0)[None, None, :]
    zeroes = jnp.zeros_like(score_low)
    word_part = jnp.where(word_key, score_low, zeroes)
    entity_part = jnp.where(word_key, zeroes, score_low)
    word_qgrad = (
        jnp.einsum("hqk,khd->qhd", word_part, key_heads, preferred_element_type=jnp.float32)
        * SCALING
    )
    entity_qgrad = (
        jnp.einsum("hqk,khd->qhd", entity_part, key_heads, preferred_element_type=jnp.float32)
        * SCALING
    )
    key_delta = (
        jnp.einsum("hqk,qhd->khd", word_part, word_heads, preferred_element_type=jnp.float32)
        + jnp.einsum("hqk,qhd->khd", entity_part, entity_heads, preferred_element_type=jnp.float32)
    ) * SCALING
    value_delta = jnp.einsum(
        "hqk,qhd->khd",
        attn_probs.astype(jnp.bfloat16),
        grad_heads,
        preferred_element_type=jnp.float32,
    )
    row_count = word_qgrad.shape[0]
    return (
        word_qgrad.reshape(row_count, -1),
        entity_qgrad.reshape(row_count, -1),
        key_delta.reshape(row_count, -1),
        value_delta.reshape(row_count, -1),
    )


def row_share(partial_rows):
    return lax.psum_scatter(partial_rows, "tensor", scatter_dimension=0, tiled=True)


def row_whole(rounded_rows):
    return lax.all_gather(rounded_rows, "tensor", axis=0, tiled=True)


def shards(
    layer_input,
    segment_ids,
    token_types,
    query_weight,
    key_weight,
    value_weight,
    out_weight,
    up_weight,
    down_weight,
    query_bias,
    value_bias,
    out_bias,
    up_bias,
    down_bias,
    attn_gain,
    attn_shift,
    ffn_gain,
    ffn_shift,
    cotangent,
):
    seq_count, seq_length, model_width = layer_input.shape
    tokens = layer_input.reshape(-1, model_width)
    row_count = tokens.shape[0]
    share = row_count // lax.axis_size("tensor")
    first_row = lax.axis_index("tensor") * share

    def own_rows(matrix):
        return lax.dynamic_slice_in_dim(matrix, first_row, share, 0)

    def combine_rows(partial_rows):
        return row_share(partial_rows)

    def whole_rows(rounded_rows):
        return row_whole(rounded_rows)

    query_complete, key_full, value_full, out_full = (
        lax.all_gather(query_weight.astype(jnp.bfloat16), "dp", axis=1, tiled=True),
        lax.all_gather(key_weight.astype(jnp.bfloat16), "dp", axis=0, tiled=True),
        lax.all_gather(value_weight.astype(jnp.bfloat16), "dp", axis=0, tiled=True),
        lax.all_gather(out_weight.astype(jnp.bfloat16), "dp", axis=1, tiled=True),
    )
    local_width = key_full.shape[1]
    query_rows = jnp.einsum(
        "gow,qwk->gqok", layer_input, query_complete, preferred_element_type=jnp.float32
    )
    query_rows = (query_rows + query_bias[None, :, None, :]).astype(jnp.bfloat16)
    keys_all = jnp.dot(layer_input, key_full, preferred_element_type=jnp.float32).astype(
        jnp.bfloat16
    )
    values_all = (
        jnp.dot(layer_input, value_full, preferred_element_type=jnp.float32) + value_bias
    ).astype(jnp.bfloat16)
    context, log_total = lax.map(
        attend_forward, (query_rows, keys_all, values_all, segment_ids, token_types)
    )
    context_rows = context.reshape(-1, local_width)
    attended = combine_rows(jnp.dot(context_rows, out_full, preferred_element_type=jnp.float32))
    residual = own_rows(tokens).astype(jnp.float32) + attended + out_bias
    normed, normal_one, inverse_one = layer_norm_keep(residual, attn_gain, attn_shift)
    normed_low = whole_rows(normed.astype(jnp.bfloat16))
    up_full, down_full = (
        lax.all_gather(up_weight.astype(jnp.bfloat16), "dp", axis=0, tiled=True),
        lax.all_gather(down_weight.astype(jnp.bfloat16), "dp", axis=1, tiled=True),
    )
    pre_act = jnp.dot(normed_low, up_full, preferred_element_type=jnp.float32) + up_bias
    activated, gelu_pull = jax.vjp(partial(jax.nn.gelu, approximate=False), pre_act)
    act_low = activated.astype(jnp.bfloat16)
    ffn_out = (
        combine_rows(jnp.dot(act_low, down_full, preferred_element_type=jnp.float32)) + down_bias
    )
    normed_out, normal_two, inverse_two = layer_norm_keep(normed + ffn_out, ffn_gain, ffn_shift)
    output = whole_rows(normed_out.astype(jnp.bfloat16)).reshape(layer_input.shape)
    upstream = own_rows(cotangent.reshape(-1, model_width)).astype(jnp.float32)
    sum_grad, ffngain_grad, ffnshift_grad = layer_norm_back(
        upstream, normal_two, inverse_two, ffn_gain
    )
    downbias_grad = jnp.sum(sum_grad, axis=0)
    sum_low = whole_rows(sum_grad.astype(jnp.bfloat16))
    up_back, down_back = (
        lax.all_gather(up_weight.astype(jnp.bfloat16), "dp", axis=0, tiled=True),
        lax.all_gather(down_weight.astype(jnp.bfloat16), "dp", axis=1, tiled=True),
    )
    down_local = jnp.dot(act_low.T, sum_low, preferred_element_type=jnp.float32)
    act_grad = jnp.dot(sum_low, down_back.T, preferred_element_type=jnp.float32)
    (pre_grad,) = gelu_pull(act_grad)
    upbias_grad = jnp.sum(pre_grad, axis=0)
    pre_low = pre_grad.astype(jnp.bfloat16)
    up_local = jnp.dot(normed_low.T, pre_low, preferred_element_type=jnp.float32)
    upproj_grad, downproj_grad = (
        lax.psum_scatter(up_local, "dp", scatter_dimension=0, tiled=True),
        lax.psum_scatter(down_local, "dp", scatter_dimension=1, tiled=True),
    )
    normed_grad = (
        combine_rows(jnp.dot(pre_low, up_back.T, preferred_element_type=jnp.float32)) + sum_grad
    )
    resid_grad, attngain_grad, attnshift_grad = layer_norm_back(
        normed_grad, normal_one, inverse_one, attn_gain
    )
    outbias_grad = jnp.sum(resid_grad, axis=0)
    resid_low = whole_rows(resid_grad.astype(jnp.bfloat16))
    query_pullback, key_pullback, value_pullback, out_back = (
        lax.all_gather(query_weight.astype(jnp.bfloat16), "dp", axis=1, tiled=True),
        lax.all_gather(key_weight.astype(jnp.bfloat16), "dp", axis=0, tiled=True),
        lax.all_gather(value_weight.astype(jnp.bfloat16), "dp", axis=0, tiled=True),
        lax.all_gather(out_weight.astype(jnp.bfloat16), "dp", axis=1, tiled=True),
    )
    outproj_local = jnp.dot(context_rows.T, resid_low, preferred_element_type=jnp.float32)
    context_grad = jnp.dot(resid_low, out_back.T, preferred_element_type=jnp.float32).astype(
        jnp.bfloat16
    )
    context_grad = context_grad.reshape(seq_count, seq_length, local_width)
    word_qgrad, entity_qgrad, key_delta, value_delta = lax.map(
        attend_backward,
        (query_rows, keys_all, values_all, segment_ids, token_types, log_total, context_grad),
    )
    is_word = (token_types == 0)[..., None]
    zero_rows = jnp.zeros_like(word_qgrad)
    query_delta = jnp.stack(
        [
            jnp.where(is_word, word_qgrad, zero_rows),
            jnp.where(is_word, entity_qgrad, zero_rows),
            jnp.where(is_word, zero_rows, word_qgrad),
            jnp.where(is_word, zero_rows, entity_qgrad),
        ],
        axis=1,
    )
    querybias_grad = jnp.sum(query_delta, axis=(0, 2))
    valuebias_grad = jnp.sum(value_delta, axis=(0, 1))
    query_reduced = query_delta.astype(jnp.bfloat16)
    key_reduced = key_delta.astype(jnp.bfloat16)
    value_reduced = value_delta.astype(jnp.bfloat16)
    query_local = jnp.einsum(
        "nvh,nkvw->khw", layer_input, query_reduced, preferred_element_type=jnp.float32
    )
    key_shard = jnp.einsum(
        "pui,pun->in", layer_input, key_reduced, preferred_element_type=jnp.float32
    )
    value_local = jnp.einsum(
        "pui,pun->in", layer_input, value_reduced, preferred_element_type=jnp.float32
    )
    input_part = (
        jnp.einsum(
            "kayo,azo->kyz", query_reduced, query_pullback, preferred_element_type=jnp.float32
        )
        + jnp.einsum("ohz,wz->ohw", key_reduced, key_pullback, preferred_element_type=jnp.float32)
        + jnp.einsum(
            "ohz,wz->ohw", value_reduced, value_pullback, preferred_element_type=jnp.float32
        )
    )
    input_total = combine_rows(input_part.reshape(-1, model_width))
    input_grad = whole_rows((input_total + resid_grad).astype(jnp.bfloat16)).reshape(
        layer_input.shape
    )
    query_grad, key_grad, value_grad, outproj_grad = (
        lax.psum_scatter(query_local, "dp", scatter_dimension=1, tiled=True),
        lax.psum_scatter(key_shard, "dp", scatter_dimension=0, tiled=True),
        lax.psum_scatter(value_local, "dp", scatter_dimension=0, tiled=True),
        lax.psum_scatter(outproj_local, "dp", scatter_dimension=1, tiled=True),
    )
    querybias_grad, valuebias_grad, upbias_grad = lax.psum(
        (querybias_grad, valuebias_grad, upbias_grad), "dp"
    )
    outbias_grad, downbias_grad, attngain_grad, attnshift_grad, ffngain_grad, ffnshift_grad = (
        lax.psum(
            (
                outbias_grad,
                downbias_grad,
                attngain_grad,
                attnshift_grad,
                ffngain_grad,
                ffnshift_grad,
            ),
            ("dp", "tensor"),
        )
    )
    return (
        output,
        input_grad,
        query_grad,
        key_grad,
        value_grad,
        outproj_grad,
        upproj_grad,
        downproj_grad,
        querybias_grad,
        valuebias_grad,
        outbias_grad,
        upbias_grad,
        downbias_grad,
        attngain_grad,
        attnshift_grad,
        ffngain_grad,
        ffnshift_grad,
    )


MESH = pl.DeviceIdType.MESH
BF = jnp.bfloat16
F32 = jnp.float32
BLOCK = 128


def fits(mesh):
    return mesh.shape["dp"] == 8 and mesh.shape["tensor"] == 4


def nn(a, b):
    return lax.dot_general(a, b, (((1,), (0,)), ((), ())), preferred_element_type=F32)


def nt(a, b):
    return lax.dot_general(a, b, (((1,), (1,)), ((), ())), preferred_element_type=F32)


def tn(a, b):
    return lax.dot_general(a, b, (((0,), (0,)), ((), ())), preferred_element_type=F32)


def norm_rows(values):
    centre = values - jnp.mean(values, axis=-1, keepdims=True)
    inverse = lax.rsqrt(jnp.mean(centre * centre, axis=-1, keepdims=True) + EPSILON)
    return centre * inverse, inverse


def norm_rows_back(upstream, normal, inverse, gain):
    scaled = upstream * gain
    return inverse * (
        scaled
        - jnp.mean(scaled, axis=-1, keepdims=True)
        - normal * jnp.mean(scaled * normal, axis=-1, keepdims=True)
    )


class Net:
    def __init__(self, send, recv, peer):
        self.send, self.recv, self.peer = send, recv, peer
        self.sends = 0
        self.locals = 0
        self.banks = 0
        self.pending = []

    def bank(self, count):
        base = self.banks
        self.banks += count
        return base

    def start(self, src, dst, sem, device, when=None, group=None):
        slot = self.sends % SENDS
        self.sends += 1
        self.finish([p for p in self.pending if p[3] == slot])

        def make():
            return pltpu.make_async_remote_copy(
                src_ref=src,
                dst_ref=dst,
                send_sem=self.send.at[slot],
                recv_sem=self.recv.at[sem],
                device_id=device,
                device_id_type=MESH,
            )

        if when is None:
            make().start()
        else:
            pl.when(when)(lambda: make().start())
        self.pending.append((make, when, group, slot))

    def finish(self, entries):
        for make, when, _, _ in entries:
            if when is None:
                make().wait_send()
            else:
                pl.when(when)(lambda make=make: make().wait_send())
        self.pending = [p for p in self.pending if p not in entries]

    def wait(self, dst, sem, when=None):
        def make():
            return pltpu.make_async_remote_copy(
                src_ref=dst,
                dst_ref=dst,
                send_sem=self.send.at[0],
                recv_sem=self.recv.at[sem],
                device_id=self.peer,
                device_id_type=MESH,
            )

        if when is None:
            make().wait_recv()
        else:
            pl.when(when)(lambda: make().wait_recv())

    def settle(self, *groups):
        self.finish([p for p in self.pending if not groups or p[2] in groups])


SENDS = 48
RECVS = 109


def layer_kernel(
    x_in, seg_ref, typ_ref, qw_in, kw_in, vw_in, ow_in, uw_in, dw_in, qb_ref, vb_ref,
    ob_ref, ub_ref, db_ref, ag_ref, as_ref, fg_ref, fs_ref, cot_in,
    out_end, ig_end, qg_end, kg_end, vg_end, og_end, ug_end, dg_end, small_end,
    x_ref, qw_ref, kw_ref, vw_ref, ow_ref, uw_ref, dw_ref, cot_ref,
    out_ref, ig_ref, qg_ref, kg_ref, vg_ref, og_ref, ug_ref, dg_ref, small_ref,
    wq, wop, wo, own, wf, ubs, segc, wordc, xt, bias, qq, kv, kk, kvt, kkt, probs, ctx, ctp, ct, ctc,
    a_s, n1_s, r1_s, act, gelu_d, gl, parts, rs_send, rs_recv, dub, dzb,
    st_a, st_b, st_c, st_d, st_e, st_f, st_g, dct, dc, dco, go_r, rp, sp, rz,
    dqkv, dx_in, dx_cross, dx_back, gq_r, gp, sv, small_s, small_r, sent8, sw, vz,
    send_sems, recv_sems, local_sems,
):
    d = lax.axis_index("dp")
    t = lax.axis_index("tensor")
    c = d % 2
    x = (d // 2) % 2
    y = d // 4
    pair = t % 2
    j = 2 * pair + c
    block = pair + 2 * c
    home = block == t
    zp = t + 1 - 2 * pair
    zq = (t + 2) % 4
    host = 2 * (d // 2) + t // 2
    chip = d // 2
    sib = d + 1 - 2 * c
    xn = d + 2 - 4 * x
    yn = d + 4 - 8 * y
    rows = x_ref.shape[1]
    quarter = rows // 4
    width = x_ref.shape[2]
    strip = qw_ref.shape[1]
    local = kw_ref.shape[1]
    heads = local // HD
    blocks = rows // BLOCK
    own_rows = pl.ds(pl.multiple_of(t * quarter, 16), quarter)
    net = Net(send_sems, recv_sems, (sib, t))

    def flip_x(device):
        return device + 2 - 4 * ((device // 2) % 2)

    def flip_y(device):
        return device + 4 - 8 * (device // 4)

    dg = flip_y(xn)
    part_m, part_o = parts.at[0:2], parts.at[2:4]
    sums_a, sums_b = parts.reshape(rows, width), gelu_d.reshape(rows, width)
    dqq = [sums_a.at[:, BLOCK * h : BLOCK * (h + 1)] for h in range(heads)]
    dkk = [sums_a.at[:, BLOCK * (heads + h) : BLOCK * (heads + h + 1)] for h in range(heads)]
    dvv = [sums_b.at[:, BLOCK * h : BLOCK * (h + 1)] for h in range(heads)]

    low_z = t < 2
    is_end = jnp.logical_or(t == 0, t == 3)
    is_mid = jnp.logical_not(is_end)
    z_out = jnp.where(low_z, t + 1, t - 1)
    z_back = jnp.where(low_z, 0, 3)

    def place(e):
        return jnp.where(low_z, e, 3 - e)

    def joint(one, other):
        return other if one is None else jnp.logical_and(one, other)

    class LineGather:
        def __init__(self, view, group=None):
            self.view, self.bank, self.group = view, net.bank(4), group

        def copy(self, owner, to, when):
            ref = self.view(owner)
            net.start(ref, ref, self.bank + owner, (d, to), when=when, group=self.group)

        def wait(self, owner, when=None):
            net.wait(self.view(owner), self.bank + owner, when=when)

        def begin(self):
            self.copy(t, z_out, None)
            self.copy(t, z_back, is_mid)

        def step(self, n):
            if n == 1:
                self.wait(place(0), is_mid)
                self.copy(place(0), z_out, is_mid)
                self.wait(place(2), is_mid)
                self.copy(place(2), z_back, is_mid)
            if n == 2:
                self.wait(place(3), is_mid)
                self.copy(place(3), z_back, is_mid)
            self.wait(place(n), is_end)

    class LineReduce:
        def __init__(self, own, came, cross, back):
            self.own, self.came, self.cross, self.back = own, came, cross, back
            self.in_b, self.cross_b, self.back_b = net.bank(3), net.bank(2), net.bank(1)

        def depart(self, e):
            net.start(self.own(e), self.came.at[e - 1], self.in_b + e - 1, (d, z_out), when=is_end)

        def add(self, e, ref):
            @pl.when(is_mid)
            def _():
                ref[...] = (self.own(e)[...].astype(F32) + ref[...].astype(F32)).astype(BF)

        def through(self, e):
            ref = self.came.at[e - 1]
            net.wait(ref, self.in_b + e - 1, when=is_mid)
            self.add(e, ref)
            net.start(ref, self.cross.at[3 - e], self.cross_b + 3 - e, (d, z_out), when=is_mid)

        def pass_back(self):
            net.wait(self.cross.at[0], self.cross_b, when=is_mid)
            self.add(0, self.cross.at[0])
            net.start(self.cross.at[0], self.back, self.back_b, (d, z_back), when=is_mid)

        def total(self):
            net.wait(self.came.at[0], self.in_b, when=is_mid)
            net.wait(self.cross.at[1], self.cross_b + 1, when=is_mid)
            net.wait(self.back, self.back_b, when=is_end)
            others = self.came[0].astype(F32) + self.cross[1].astype(F32)
            mine = self.own(jnp.where(is_mid, 1, 0))[...].astype(F32)
            return mine + jnp.where(is_mid, others, self.back[...].astype(F32))

    class Local:
        def __init__(self, source, target):
            self.copy = pltpu.make_async_copy(source, target, local_sems.at[net.locals])
            net.locals += 1
            self.copy.start()

        def wait(self):
            self.copy.wait()

    in_q, in_k, in_v = Local(qw_in, qw_ref), Local(kw_in, kw_ref), Local(vw_in, vw_ref)
    in_o, in_u, in_d = Local(ow_in, ow_ref), Local(uw_in, uw_ref), Local(dw_in, dw_ref)
    in_x, in_cot = Local(x_in, x_ref), Local(cot_in, cot_ref)

    barrier = pltpu.get_barrier_semaphore()
    for m in range(1, 8):
        pl.semaphore_signal(barrier, 1, device_id=((d + m) % 8, t), device_id_type=MESH)
    for k in range(1, 4):
        pl.semaphore_signal(barrier, 1, device_id=(d, (t + k) % 4), device_id_type=MESH)
    pl.semaphore_signal(barrier, 1, device_id=(sib, zq), device_id_type=MESH)

    for arrived in (in_q, in_k, in_v):
        arrived.wait()
    for h in range(heads):
        at = slice(HD * h, HD * (h + 1))
        piece = jnp.concatenate(
            [qw_ref[i, :, at] for i in range(4)] + [kw_ref[:, at], vw_ref[:, at]], axis=1
        )
        wq[d, :, 6 * HD * h : 6 * HD * (h + 1)] = piece.astype(BF)

    pl.semaphore_wait(barrier, 11)

    class PlaneGather:
        def __init__(self, group, view, whole):
            self.view, self.whole, self.group, self.bank = view, whole, group, net.bank(5)

        def copy(self, half, block, device, sem):
            ref = self.whole(block) if half is None else self.view(half, block)
            net.start(ref, ref, self.bank + sem, (device, t), group=self.group)

        def begin(self):
            self.copy(0, d, yn, 0)
            self.copy(1, d, xn, 1)
            self.copy(1, d, yn, 2)
            self.copy(0, d, xn, 2)
            self.copy(None, d, sib, 4)

        def middle(self):
            net.wait(self.view(0, yn), self.bank)
            self.copy(0, yn, xn, 3)
            net.wait(self.view(1, xn), self.bank + 1)
            self.copy(1, xn, yn, 3)

        def middle2(self):
            net.wait(self.whole(d), self.bank + 2)
            self.copy(None, yn, sib, 4)
            self.copy(None, xn, sib, 4)

        def late(self):
            net.wait(self.whole(dg), self.bank + 3)
            self.copy(None, dg, sib, 4)

        def end(self):
            net.wait(self.whole(slice(0, 4)), self.bank + 4)

    most = strip // 2

    gather_q = PlaneGather(
        "q", lambda half, b: wq.at[b, most * half : most * (half + 1)], lambda b: wq.at[b]
    )
    gather_q.begin()

    def wide_t(value, high, wide):
        r, w = value.shape
        if w < wide:
            value = jnp.concatenate([value, jnp.zeros((r, wide - w), value.dtype)], axis=1)
        if r < high:
            value = jnp.concatenate([value, jnp.zeros((high - r, wide), value.dtype)], axis=0)
        return value.T

    for arrived in (in_o, in_u, in_d):
        arrived.wait()
    def pack(block):
        most = block.shape[0] // 2
        rest = block[:, BLOCK:]
        return jnp.concatenate(
            [block[:, :BLOCK], jnp.concatenate([rest[:most], rest[most:]], axis=1)], axis=0
        )

    def rest_of(packed, count):
        below = packed[count:]
        return jnp.concatenate([below[:, :HD], below[: count - below.shape[0], HD:]], axis=0)

    wop[t, d] = pack(wide_t(ow_ref[...], 256, 128)[:strip, :local]).astype(BF)
    own[0] = uw_ref[...].astype(BF)
    own[1] = dw_ref[...].astype(BF)
    ubs[t] = jnp.broadcast_to(ub_ref[...][None], ubs.shape[1:])

    ub_z = net.bank(1)
    wf_a = net.bank(4)

    class ChipGather:
        def __init__(self, i):
            self.i, self.bank = i, net.bank(3)

        def send_near(self):
            i = self.i
            net.start(own.at[i], wf.at[i, d], wf_a + 2 * i + c, (host, t), when=host != d)

            @pl.when(host == d)
            def _():
                wf[i, d] = own[i]

        def send_far(self):
            net.start(own.at[self.i], wf.at[self.i, d], wf_a + 2 * self.i + c, (host, zq))

        def copy(self, view, of, device, sem, when=None):
            ref = wf.at[self.i, 2 * (of // 2) + view]
            net.start(ref, ref, self.bank + sem, (device, t), when=when, group="f")

        def wait(self, view, of, sem):
            net.wait(wf.at[self.i, 2 * (of // 2) + view], self.bank + sem)

        def begin(self, at_home):
            i, when = self.i, home if at_home else jnp.logical_not(home)
            if not at_home:
                net.wait(wf.at[i, d], wf_a + 2 * i + c, when=when)
            net.wait(wf.at[i, sib], wf_a + 2 * i + 1 - c, when=when)
            for view, device, sem in ((0, yn, 0), (1, xn, 1), (1, yn, 2), (0, xn, 2)):
                self.copy(view, d, device, sem, when)

        def middle(self):
            self.wait(0, yn, 0)
            self.copy(0, yn, xn, 2)
            self.wait(1, xn, 1)
            self.copy(1, xn, yn, 2)

        def end(self):
            net.wait(wf.at[self.i, 0:4], self.bank + 2)

    up, down = ChipGather(0), ChipGather(1)
    wo_z = net.bank(1)
    for k in (2, 1, 3):
        net.start(wop.at[t, d], wop.at[t, d], wo_z, (d, (t + k) % 4))
    up.send_near()
    down.send_near()
    for b in range(blocks):
        at = slice(BLOCK * b, BLOCK * (b + 1))
        segc[at, :] = jnp.broadcast_to(seg_ref[:, at].astype(F32), (BLOCK, BLOCK)).T
        wordc[at, :] = jnp.broadcast_to((typ_ref[:, at] == 0).astype(F32), (BLOCK, BLOCK)).T
    in_x.wait()
    xt[...] = x_ref[0].T
    for h in range(heads):
        at = slice(HD * h, HD * (h + 1))
        bias[:, 6 * HD * h : 6 * HD * (h + 1)] = jnp.concatenate(
            [qb_ref[i : i + 1, at] for i in range(4)] + [jnp.zeros((1, HD), F32), vb_ref[at][None]],
            axis=1,
        )

    gather_q.middle()
    up.send_far()
    gather_q.middle2()
    net.wait(wop.at[0:3, d], wo_z)
    gather_o = PlaneGather(
        "o", lambda half, b: wop.at[2 * half : 2 * half + 2, b], lambda b: wop.at[:, b]
    )
    gather_o.begin()
    down.send_far()
    net.start(ubs.at[t], ubs.at[t], ub_z, (d, zq))
    up.begin(True)
    gather_q.late()
    gather_q.end()
    low_half = lax.broadcasted_iota(jnp.int32, (rows, BLOCK), 1) < HD
    is_word = wordc[...] > 0.5
    for h in range(heads):
        base = 6 * HD * h
        at = slice(BLOCK * h, BLOCK * (h + 1))
        made = nn(x_ref[0], wq[:, :, base : base + 6 * HD].reshape(width, 6 * HD))
        made = made + bias[:, base : base + 6 * HD]
        qq[:, at] = jnp.where(is_word, made[:, :BLOCK], made[:, BLOCK : 2 * BLOCK]).astype(BF)
        both = made[:, 2 * BLOCK :]
        keys = jnp.where(low_half, both, pltpu.roll(both, HD, 1))
        keys = jnp.where(jnp.logical_xor(is_word, low_half), 0.0, keys)
        kv[:, at] = both.astype(BF)
        kk[:, at] = keys.astype(BF)
        kvt[h] = both.T[HD:].astype(BF)
        kkt[h] = keys.T.astype(BF)

    gather_o.middle()
    gather_o.middle2()
    ct_z = net.bank(1)

    def span(b):
        return BLOCK * max(0, b - 2), BLOCK * min(blocks, b + 3)

    kept = [0]
    for b in range(blocks):
        kept.append(kept[-1] + span(b)[1] - span(b)[0])
    for b in range(blocks):
        lo, hi = span(b)
        at_q = slice(BLOCK * b, BLOCK * (b + 1))
        same = segc[lo:hi, :] == seg_ref[:, at_q].astype(F32)
        found = []
        for h in range(heads):
            at = slice(BLOCK * h, BLOCK * (h + 1))
            scores = nt(kk[lo:hi, at], qq[at_q, at]) * SCALING
            scores = jnp.where(same, scores, NEGATIVE)
            weights = jnp.exp(scores - jnp.max(scores, axis=0, keepdims=True))
            weights = weights * (1.0 / jnp.sum(weights, axis=0, keepdims=True))
            probs[h, kept[b] : kept[b + 1]] = weights
            found.append(nn(kvt[h, :, lo:hi], weights.astype(BF)))
        found.append(jnp.zeros((HD, BLOCK), F32))
        ctx[at_q, :] = jnp.concatenate(found, axis=0).T[:, :local].astype(BF)
        if b == 2:
            up.begin(False)
        if b > 0:
            s = b - 1
            ctp[s] = pack(ctx[quarter * s : quarter * (s + 1), :])
            net.start(ctp.at[s], ct.at[t], ct_z, (d, s), when=t != s)
    ct[t] = ctp[t]

    down.begin(True)
    gather_o.late()
    down.begin(False)
    up.middle()
    gather_o.end()
    for s in range(4):
        wo[:, :, BLOCK * s : BLOCK * (s + 1)] = wop[s, :, :strip]
    for s in (0, 2):
        at = slice(4 * BLOCK + HD * s, 4 * BLOCK + HD * (s + 2))
        one, other = wop[s, :, strip:], wop[s + 1, :, strip:]
        wo[:, :most, at] = jnp.concatenate([one[:, :, :HD], other[:, :, :HD]], axis=2)
        wo[:, most:, at] = jnp.concatenate([one[:, :, HD:], other[:, :, HD:]], axis=2)
    net.wait(ct.at[0:3], ct_z)
    for s in range(4):
        ctc[:, BLOCK * s : BLOCK * (s + 1)] = ct[s, :quarter]
    for s in (0, 2):
        ctc[:, 4 * BLOCK + HD * s : 4 * BLOCK + HD * (s + 2)] = jnp.concatenate(
            [rest_of(ct[s], quarter), rest_of(ct[s + 1], quarter)], axis=1
        )
    whole_wo = wo.reshape(width, width)
    attended = nt(ctc[...], whole_wo[...])
    normal, inverse = norm_rows(x_ref[0, own_rows, :].astype(F32) + attended + ob_ref[...][None])
    n1_s[...] = normal
    r1_s[...] = jnp.broadcast_to(inverse, r1_s.shape)
    normed = normal * ag_ref[...][None] + as_ref[...][None]
    a_s[...] = normed
    act[j] = normed.astype(BF)

    def rows_of(ref, first, count):
        return lambda owner: ref.at[
            0, pl.ds(pl.multiple_of(owner * quarter + first, 16), count)
        ]

    part = quarter // 2
    chunk = [slice(part * q, part * (q + 1)) for q in range(2)]

    class RowGather:
        def __init__(self, ref):
            self.ref, self.bank = ref, net.bank(8)

        def copy(self, q, rank, device):
            ref = self.ref.at[rank, chunk[q]]
            net.start(ref, ref, self.bank + 4 * q + rank, device)

        def wait(self, q, rank):
            net.wait(self.ref.at[rank, chunk[q]], self.bank + 4 * q + rank)

        def begin(self, q):
            self.copy(q, j, (d, zp))
            self.copy(q, j, (sib, t))

        def near(self, q):
            self.wait(q, 2 * pair + 1 - c)

        def middle(self, q):
            self.wait(q, 2 - 2 * pair + c)
            self.copy(q, 2 - 2 * pair + c, (sib, t))

        def far(self, q):
            self.wait(q, 3 - 2 * pair - c)

    class RowSum:
        def __init__(self, index):
            self.index, self.bank = index, net.bank(6)

        def hand(self, q, slot, partial_rows):
            where = 3 * self.index + slot
            rs_send[where, chunk[q]] = partial_rows.astype(BF)
            net.start(
                rs_send.at[where, chunk[q]], rs_recv.at[where, chunk[q]], self.bank + 3 * q + slot,
                (d, zp) if slot == 2 else (sib, t),
            )

        def take(self, q, slot):
            where = 3 * self.index + slot
            net.wait(rs_recv.at[where, chunk[q]], self.bank + 3 * q + slot)
            return rs_recv[where, chunk[q]].astype(F32)

        def near(self, q):
            self.hand(q, 0, part_m[1 - c, chunk[q]])

        def away(self, q):
            self.hand(q, 1, part_o[1 - c, chunk[q]])

        def across(self, q):
            self.hand(q, 2, part_o[c, chunk[q]] + self.take(q, 1))

        def total(self, q):
            return part_m[c, chunk[q]] + self.take(q, 0) + self.take(q, 2)

    rows_a = RowGather(act)
    rows_a.begin(0)
    rows_a.begin(1)
    down.middle()
    rows_a.middle(0)
    rows_a.middle(1)
    rows_a.near(0)
    rows_a.near(1)
    net.wait(ubs.at[zq], ub_z)
    up.end()
    near = pl.ds(2 * pair, 2)
    away = pl.ds(2 - 2 * pair, 2)

    def feed(half):
        hidden = nn(act[half].reshape(2 * quarter, width), wf[0].reshape(width, width))
        hidden = hidden + ubs[block][:1]
        bell = 0.5 * (1.0 + lax.erf(hidden * 0.7071067811865476))
        slope = bell + hidden * (0.3989422804014327 * jnp.exp(-0.5 * hidden * hidden))
        gelu_d[half] = slope.reshape(2, quarter, width)
        gl[half] = (hidden * bell).astype(BF).reshape(2, quarter, width)

    def feed_out(half, partial_ref):
        made = nt(gl[half].reshape(2 * quarter, width), wf[1].reshape(width, width))
        partial_ref[...] = made.reshape(2, quarter, width)

    feed(near)
    rows_a.far(0)
    rows_a.far(1)
    feed(away)
    down.end()
    sum_f = RowSum(0)
    feed_out(away, part_o)
    sum_f.away(0)
    sum_f.away(1)
    feed_out(near, part_m)
    sum_f.across(0)
    sum_f.across(1)
    sum_f.near(0)
    sum_f.near(1)
    in_cot.wait()
    rows_u = RowGather(dub)
    gain_sum, shift_sum, bias_sum = 0.0, 0.0, 0.0
    for q in range(2):
        ffn_out = sum_f.total(q) + db_ref[...][None]
        normal, inverse = norm_rows(a_s[chunk[q]] + ffn_out)
        rows_q = pl.ds(pl.multiple_of(t * quarter + part * q, 16), part)
        out_ref[0, rows_q, :] = (normal * fg_ref[...][None] + fs_ref[...][None]).astype(BF)
        upstream = cot_ref[0, rows_q, :].astype(F32)
        du = norm_rows_back(upstream, normal, inverse, fg_ref[...][None])
        dub[j, chunk[q]] = du.astype(BF)
        rows_u.begin(q)
        a_s[chunk[q]] = du
        gain_sum = gain_sum + jnp.sum(upstream * normal, axis=0, keepdims=True)
        shift_sum = shift_sum + jnp.sum(upstream, axis=0, keepdims=True)
        bias_sum = bias_sum + jnp.sum(du, axis=0, keepdims=True)
    line_out = [LineGather(rows_of(out_ref, part * q, part)) for q in range(2)]
    line_out[0].begin()
    sv[...] = jnp.zeros_like(sv)
    sv[0:1] = gain_sum
    sv[1:2] = shift_sum
    sv[2:3] = bias_sum

    def feed_back(half, rows_q, partial_ref):
        count = 2 * (rows_q.stop - rows_q.start)
        made = nn(dub[half, rows_q].reshape(count, width), wf[1].reshape(width, width))
        made = made * gelu_d[half, rows_q].reshape(count, width)
        low = made.astype(BF)
        dzb[half, rows_q] = low.reshape(2, count // 2, width)
        partial_ref[:, rows_q] = nt(low, wf[0].reshape(width, width)).reshape(2, count // 2, width)
        return jnp.sum(made, axis=0, keepdims=True)

    sum_b = RowSum(1)
    rows_u.near(0)
    rows_u.near(1)
    up_sum = feed_back(near, slice(0, quarter), part_m)
    sum_b.near(0)
    sum_b.near(1)
    rows_u.middle(0)
    rows_u.far(0)
    up_sum = up_sum + feed_back(away, chunk[0], part_o)
    sum_b.away(0)
    rows_u.middle(1)
    sum_b.across(0)
    rows_u.far(1)
    up_sum = up_sum + feed_back(away, chunk[1], part_o)
    sum_b.away(1)
    sv[6:7] = up_sum
    half = width // 2

    class StripSum:
        def __init__(self, i):
            self.i, self.bank = i, net.bank(9)
            self.by_chip = wf.at[i].reshape(2, 2, 2, strip, width)

        def make(self, left, right):
            made = tn(left[...].reshape(4 * quarter, width), right[...].reshape(4 * quarter, width))
            wf[self.i] = made.astype(BF).reshape(8, strip, width)

        def begin(self):
            net.start(
                self.by_chip.at[:, 1 - x, :, :, :half], st_a.at[self.i], self.bank, (xn, t)
            )
            net.start(
                self.by_chip.at[1 - y, :, :, :, half:], st_b.at[self.i], self.bank + 1, (yn, t)
            )

        def turn(self):
            i = self.i
            net.wait(st_a.at[i], self.bank)
            st_a[i] = (st_a[i].astype(F32) + self.by_chip[:, x, :, :, :half].astype(F32)).astype(BF)
            for core in range(2):
                net.start(
                    st_a.at[i, 1 - y, core], st_c.at[i, c], self.bank + 2 + c,
                    (2 * (yn // 2) + core, t),
                )
            net.start(st_a.at[i, y, 1 - c], st_g.at[i, 0], self.bank + 6, (sib, t))
            net.wait(st_b.at[i], self.bank + 1)
            st_b[i] = (st_b[i].astype(F32) + self.by_chip[y, :, :, :, half:].astype(F32)).astype(BF)
            for core in range(2):
                net.start(
                    st_b.at[i, 1 - x, core], st_d.at[i, c], self.bank + 4 + c,
                    (2 * (xn // 2) + core, t),
                )
            net.start(st_b.at[i, x, 1 - c], st_g.at[i, 1], self.bank + 7, (sib, t))

        def gather(self):
            i = self.i
            for core in range(2):
                net.wait(st_c.at[i, core], self.bank + 2 + core)
                net.wait(st_d.at[i, core], self.bank + 4 + core)
            net.wait(st_g.at[i, 0], self.bank + 6)
            net.wait(st_g.at[i, 1], self.bank + 7)
            for whose, first, second in (
                (c, st_a.at[i, y, c], st_b.at[i, x, c]), (1 - c, st_g.at[i, 0], st_g.at[i, 1])
            ):
                st_e[i, whose, :, :half] = (
                    first[...].astype(F32) + st_c[i, whose].astype(F32)
                ).astype(BF)
                st_e[i, whose, :, half:] = (
                    second[...].astype(F32) + st_d[i, whose].astype(F32)
                ).astype(BF)

        def deliver(self, when=None):
            i = self.i
            net.start(st_e.at[i, 1 - t // 2], st_f.at[i], self.bank + 8, (d, zq), when=when)

        def total(self):
            i = self.i
            net.wait(st_f.at[i], self.bank + 8)
            return st_e[i, t // 2].astype(F32) + st_f[i].astype(F32)

    class SmallSum:
        def __init__(self, index):
            self.index, self.bank = index, net.bank(2)

        def begin(self, values):
            i = self.index
            small_s[i, 0] = values
            for r in (xn, yn, dg):
                net.start(small_s.at[i, 0], small_r.at[i, chip], self.bank, (r, t))
            small_r[i, chip] = values

        def plane(self):
            i = self.index
            net.wait(small_r.at[i, 0:3], self.bank)
            total = small_r[i, 0]
            for k in range(1, 4):
                total = total + small_r[i, k]
            small_s[i, 1] = total
            net.start(small_s.at[i, 1], small_r.at[i, 4], self.bank + 1, (sib, t))

        def cores(self):
            net.wait(small_r.at[self.index, 4], self.bank + 1)
            return small_s[self.index, 1], small_r[self.index, 4]

    net.settle("f")
    down_sum, up_sums = StripSum(1), StripSum(0)
    down_sum.make(dub, gl)
    down_sum.begin()
    sum_b.across(1)
    up_sums.make(act, dzb)
    dc_z = net.bank(1)
    gain_sum, shift_sum, bias_sum, dhb = 0.0, 0.0, 0.0, []
    for q in range(2):
        da = a_s[chunk[q]] + sum_b.total(q)
        normal = n1_s[chunk[q]]
        dh = norm_rows_back(da, normal, r1_s[chunk[q], :1], ag_ref[...][None])
        a_s[chunk[q]] = dh
        dhb.append(dh.astype(BF))
        made = nn(dhb[q], whole_wo[...])
        for s in range(4):
            rest = made[:, 4 * BLOCK + HD * s : 4 * BLOCK + HD * (s + 1)]
            rest = jnp.concatenate([rest, jnp.zeros((16, HD), F32)], axis=0)
            most = (part + 16) // 2
            dct[s, q] = jnp.concatenate(
                [
                    made[:, BLOCK * s : BLOCK * (s + 1)],
                    jnp.concatenate([rest[:most], rest[most:]], axis=1),
                ],
                axis=0,
            ).astype(BF)
        for k in (2, 1, 3):
            s = (t + k) % 4
            net.start(dct.at[s, q], dc.at[t, q], dc_z, (d, s))
        dc[t, q] = dct[t, q]
        gain_sum = gain_sum + jnp.sum(da * normal, axis=0, keepdims=True)
        shift_sum = shift_sum + jnp.sum(da, axis=0, keepdims=True)
        bias_sum = bias_sum + jnp.sum(dh, axis=0, keepdims=True)
    dhb = jnp.concatenate(dhb, axis=0)
    line_out[1].begin()
    line_out[0].step(1)
    sv[3:4] = gain_sum
    sv[4:5] = shift_sum
    sv[5:6] = bias_sum
    small_a = SmallSum(0)
    small_a.begin(sv[...])
    down_sum.turn()
    up_sums.begin()
    wo[...] = tn(dhb, ctc[...]).astype(BF).reshape(8, strip, width)
    by_core = wo.reshape(4, 2, strip, width)
    go_b = net.bank(1)
    net.start(by_core.at[:, 1 - c], go_r, go_b, (sib, t))

    net.wait(dc.at[0:3], dc_z)
    upper = lax.broadcasted_iota(jnp.int32, (part, BLOCK), 1) >= HD
    for s in range(4):
        for q in range(2):
            got = dc[s, q]
            at_q = slice(quarter * s + part * q, quarter * s + part * (q + 1))
            first = got[:part].astype(F32)
            blank = jnp.zeros((part, HD), BF)
            dco[at_q, :BLOCK] = jnp.concatenate([blank, got[:part, :HD]], axis=1)
            dco[at_q, BLOCK : 2 * BLOCK] = jnp.where(upper, first, 0.0).astype(BF)
            dco[at_q, 2 * BLOCK :] = jnp.concatenate([blank, rest_of(got, part)], axis=1)
    for h in range(heads):
        dkk[h][...] = jnp.zeros((rows, BLOCK), F32)
        dvv[h][...] = jnp.zeros((rows, BLOCK), F32)
    for b in range(blocks):
        lo, hi = span(b)
        at_q = slice(BLOCK * b, BLOCK * (b + 1))
        if b == 3:
            line_out[1].step(1)
        if b == 4:
            line_out[0].step(2)
            down_sum.gather()
            down_sum.deliver()
        for h in range(heads):
            at = slice(BLOCK * h, BLOCK * (h + 1))
            weights = probs[h, kept[b] : kept[b + 1]]
            dp = nt(kv[lo:hi, at], dco[at_q, at])
            ds = weights * (dp - jnp.sum(weights * dp, axis=0, keepdims=True))
            dsb = ds.astype(BF)
            dkk[h][lo:hi] += nn(dsb, qq[at_q, at])
            dvv[h][lo:hi] += nn(weights.astype(BF), dco[at_q, at])
            dqq[h][at_q] = nn(kkt[h, :, lo:hi], dsb).T * SCALING

    small_a.plane()
    for h in range(heads):
        base = 6 * HD * h
        first = jnp.where(is_word, dqq[h][...], 0.0)
        second = jnp.where(is_word, 0.0, dqq[h][...])
        keys = dkk[h][...]
        keys = jnp.where(is_word, keys, pltpu.roll(keys, HD, 1)) * SCALING
        third = jnp.where(low_half, keys, dvv[h][...])
        for i, piece in enumerate((first, second, third)):
            at = slice(base + BLOCK * i, base + BLOCK * (i + 1))
            dqkv[:, at] = piece.astype(BF)
            row, col = divmod(base + BLOCK * i, width)
            sv[row : row + 1, col : col + BLOCK] = jnp.sum(piece, axis=0, keepdims=True)

    first_rows = pl.ds(pl.multiple_of(jnp.where(low_z, rows // 2, 0), 16), rows // 2)
    other_rows = pl.ds(pl.multiple_of(jnp.where(low_z, 0, rows // 2), 16), rows // 2)
    first_two = pl.ds(jnp.where(low_z, 2, 0), 2)
    other_two = pl.ds(jnp.where(low_z, 0, 2), 2)

    def back_to_input(rows_b, quarters):
        made = nt(dqkv[rows_b, :], wq[...].reshape(width, 6 * local))
        dzb[quarters] = made.astype(BF).reshape(2, quarter, width)

    line_dx, line_in = [], []
    for q in range(2):
        cut = pl.ds(part * q, part)
        line_dx.append(
            LineReduce(
                lambda e, cut=cut: dzb.at[place(e), cut],
                dx_in.at[q], dx_cross.at[q], dx_back.at[q],
            )
        )
        line_in.append(LineGather(rows_of(ig_ref, part * q, part)))

    def arrive(q):
        total = line_dx[q].total() + a_s[part * q : part * (q + 1)]
        ig_ref[0, pl.ds(pl.multiple_of(t * quarter + part * q, 16), part)] = total.astype(BF)
        line_in[q].begin()

    back_to_input(first_rows, first_two)
    for q, e in ((0, 3), (0, 2), (1, 3), (1, 2)):
        line_dx[q].depart(e)
    back_to_input(other_rows, other_two)
    line_dx[0].depart(1)
    line_dx[1].depart(1)
    line_out[1].step(2)
    small_b = SmallSum(1)
    small_b.begin(sv[...])

    net.settle("q")
    wq[...] = nn(xt[...], dqkv[...]).astype(BF).reshape(8, strip, 6 * local)
    q_by_core = wq.reshape(4, 2, strip, 6 * local)
    gq_b = net.bank(1)
    net.start(q_by_core.at[:, 1 - c], gq_r, gq_b, (sib, t))
    up_sums.turn()
    net.wait(go_r, go_b)
    go_r[...] = (by_core[:, c].astype(F32) + go_r[...].astype(F32)).astype(BF)
    rp_b = net.bank(1)
    for r in (xn, yn, dg):
        net.start(go_r.at[r // 2], rp.at[chip], rp_b, (r, t))
    rp[chip] = go_r[chip]
    plane_sum, other_sum = small_a.cores()
    first_core = c == 0
    own_units, other_units = plane_sum[6:7], other_sum[6:7]
    sent8[0:6] = plane_sum[0:6] + other_sum[0:6]
    sent8[6:7] = jnp.where(first_core, own_units, other_units)
    sent8[7:8] = jnp.where(first_core, other_units, own_units)
    line_dx[0].through(3)
    line_dx[0].through(2)
    net.wait(gq_r, gq_b)
    gq_r[...] = (q_by_core[:, c].astype(F32) + gq_r[...].astype(F32)).astype(BF)
    gp_b = net.bank(1)
    for r in (xn, yn, dg):
        net.start(gq_r.at[r // 2], gp.at[chip], gp_b, (r, t))
    gp[chip] = gq_r[chip]

    line_dx[0].pass_back()
    line_dx[1].through(3)
    line_dx[1].through(2)
    line_dx[1].pass_back()
    up_sums.gather()
    up_sums.deliver(is_mid)
    arrive(0)
    arrive(1)

    line_in[0].step(1)
    line_in[1].step(1)
    up_sums.deliver(is_end)
    net.wait(rp.at[0:3], rp_b)
    total = rp[0].astype(F32)
    for k in range(1, 4):
        total = total + rp[k].astype(F32)
    for s in range(4):
        rest = total[:, 4 * BLOCK + HD * s : 4 * BLOCK + HD * (s + 1)]
        sp[s] = pack(
            jnp.concatenate([total[:, BLOCK * s : BLOCK * (s + 1)], rest], axis=1)
        ).astype(BF)
    rz_b = net.bank(1)
    rz[t] = sp[t]

    def send_rz(when):
        for k in range(1, 4):
            s = (t + k) % 4
            net.start(sp.at[s], rz.at[t], rz_b, (d, s), when=when)

    send_rz(None)
    vz_b = net.bank(2)
    for k in (2, 1, 3):
        net.start(sent8, vz.at[t], vz_b, (d, (t + k) % 4), when=first_core)
    vz[t] = sent8[...]
    line_out[0].step(3)
    line_out[1].step(3)
    ends = [Local(out_ref, out_end)]
    line_in[0].step(2)
    line_in[1].step(2)
    small_b.plane()
    net.wait(vz.at[0:3], vz_b, when=first_core)

    @pl.when(first_core)
    def _():
        total = vz[0]
        for k in range(1, 4):
            total = total + vz[k]
        sw[0:6] = total[0:6]
        units = vz[t] + vz[zq]
        sw[6:7] = jnp.where(t < 2, units[6:7], units[7:8])
        sw[7:8] = units[7:8]

    net.start(sw, sw, vz_b + 1, (sib, t), when=first_core)
    net.wait(sw, vz_b + 1, when=c == 1)
    small_ref[0:8] = sw[...]
    plane_sum, other_sum = small_b.cores()
    small_ref[8:16] = plane_sum + other_sum
    dg_ref[...] = down_sum.total()
    ug_ref[...] = up_sums.total()
    ends += [Local(dg_ref, dg_end), Local(ug_ref, ug_end), Local(small_ref, small_end)]
    net.wait(rz.at[0:3], rz_b)
    total = rz[0].astype(F32)
    for s in range(1, 4):
        total = total + rz[s].astype(F32)
    total = jnp.concatenate([total[:strip], rest_of(total, strip)], axis=1)
    og_ref[...] = wide_t(total, BLOCK, 256)[:local, :strip]

    ends += [Local(og_ref, og_end)]
    net.wait(gp.at[0:3], gp_b)
    total = gp[0].astype(F32)
    for k in range(1, 4):
        total = total + gp[k].astype(F32)
    for h in range(heads):
        base = 6 * HD * h
        at = slice(HD * h, HD * (h + 1))
        for i in range(4):
            qg_ref[i, :, at] = total[:, base + HD * i : base + HD * (i + 1)]
        kg_ref[:, at] = total[:, base + 4 * HD : base + 5 * HD]
        vg_ref[:, at] = total[:, base + 5 * HD : base + 6 * HD]

    ends += [Local(qg_ref, qg_end), Local(kg_ref, kg_end), Local(vg_ref, vg_end)]
    for q in range(2):
        line_in[q].step(3)
    ends += [Local(ig_ref, ig_end)]
    net.settle()
    for copy in ends:
        copy.wait()
    assert net.banks == RECVS, net.banks


def end_kernel(*refs):
    sources, small = refs[:8], refs[8]
    targets, (qbg, vbg), vectors = refs[9:17], refs[17:19], refs[19:26]
    for source, target in zip(sources, targets):
        target[...] = source[...]
    fgg, fsg, dbg, agg, asg, obg, ubg = (small[i] for i in range(7))
    for ref, value in zip(vectors, (obg, ubg, dbg, agg, asg, fgg, fsg)):
        ref[...] = value
    width = small.shape[1]
    values = []
    for h in range(vbg.shape[0] // HD):
        row, col = divmod(6 * HD * h, width)
        piece = small[8 + row : 9 + row, col : col + 6 * HD]
        for i in range(4):
            qbg[i : i + 1, HD * h : HD * (h + 1)] = piece[:, HD * i : HD * (i + 1)]
        values.append(piece[:, 5 * HD :])
    vbg[...] = jnp.concatenate(values, axis=1)[0]


def fused(
    layer_input, segment_ids, token_types, query_weight, key_weight, value_weight, out_weight,
    up_weight, down_weight, query_bias, value_bias, out_bias, up_bias, down_bias, attn_gain,
    attn_shift, ffn_gain, ffn_shift, cotangent,
):
    rows, width = layer_input.shape[1:]
    strip, local = key_weight.shape
    quarter, heads, blocks = rows // 4, local // HD, rows // BLOCK
    kept = sum(BLOCK * (min(blocks, b + 3) - max(0, b - 2)) for b in range(blocks))
    args = [
        layer_input, segment_ids, token_types, query_weight, key_weight, value_weight, out_weight,
        up_weight, down_weight.T, query_bias, value_bias, out_bias, up_bias, down_bias, attn_gain,
        attn_shift, ffn_gain, ffn_shift, cotangent,
    ]

    def like(v, dtype=F32):
        return jax.ShapeDtypeStruct(v.shape, dtype)

    outs = [
        like(layer_input, BF), like(layer_input, BF), like(query_weight), like(key_weight),
        like(value_weight), like(out_weight), like(up_weight), jax.ShapeDtypeStruct((strip, width), F32),
        jax.ShapeDtypeStruct((16, width), F32),
    ]
    v = pltpu.VMEM
    scratch = [
        v(layer_input.shape, BF), v(query_weight.shape, F32), v(key_weight.shape, F32),
        v(value_weight.shape, F32), v(out_weight.shape, F32), v(up_weight.shape, F32),
        v((strip, width), F32), v(cotangent.shape, BF),
    ] + [v(o.shape, o.dtype) for o in outs] + [
        v((8, strip, 6 * local), BF), v((4, 8, 3 * strip // 2, BLOCK), BF), v((8, strip, width), BF),
        v((2, strip, width), BF),
        v((2, 8, strip, width), BF), v((4, 8, width), F32), v((rows, BLOCK), F32),
        v((rows, BLOCK), F32), v((width, rows), BF), v((1, 6 * local), F32),
        v((rows, heads * BLOCK), BF), v((rows, heads * BLOCK), BF), v((rows, heads * BLOCK), BF),
        v((heads, HD, rows), BF), v((heads, BLOCK, rows), BF),
        v((heads, kept, BLOCK), F32), v((rows, local), BF), v((4, 3 * quarter // 2, BLOCK), BF),
        v((4, 3 * quarter // 2, BLOCK), BF), v((quarter, width), BF),
        v((quarter, width), F32), v((quarter, width), F32), v((quarter, BLOCK), F32),
        v((4, quarter, width), BF), v((4, quarter, width), F32), v((4, quarter, width), BF),
        v((4, quarter, width), F32),
        v((6, quarter, width), BF), v((6, quarter, width), BF),
        v((4, quarter, width), BF), v((4, quarter, width), BF),
        v((2, 2, 2, strip, width // 2), BF), v((2, 2, 2, strip, width // 2), BF),
        v((2, 2, strip, width // 2), BF), v((2, 2, strip, width // 2), BF),
        v((2, 2, strip, width), BF), v((2, strip, width), BF),
        v((2, 2, strip, width // 2), BF),
        v((4, 2, BLOCK, BLOCK), BF), v((4, 2, BLOCK, BLOCK), BF),
        v((rows, heads * BLOCK), BF),
        v((4, strip, width), BF), v((4, strip, width), BF), v((4, 3 * strip // 2, BLOCK), BF),
        v((4, 3 * strip // 2, BLOCK), BF),
        v((rows, 6 * local), BF),
        v((2, 3, quarter // 2, width), BF), v((2, 2, quarter // 2, width), BF),
        v((2, quarter // 2, width), BF),
        v((4, strip, 6 * local), BF), v((4, strip, 6 * local), BF),
        v((8, width), F32), v((2, 2, 8, width), F32), v((2, 5, 8, width), F32),
        v((8, width), F32), v((8, width), F32), v((4, 8, width), F32),
        pltpu.SemaphoreType.DMA((SENDS,)), pltpu.SemaphoreType.DMA((RECVS,)),
        pltpu.SemaphoreType.DMA((17,)),
    ]
    spec = pl.BlockSpec(memory_space=pltpu.VMEM)
    anywhere = pl.BlockSpec(memory_space=pl.ANY)
    large_args = (0, 3, 4, 5, 6, 7, 8, 18)
    made = pl.pallas_call(
        layer_kernel,
        out_shape=outs,
        in_specs=[anywhere if n in large_args else spec for n in range(len(args))],
        out_specs=[anywhere] * len(outs),
        scratch_shapes=scratch,
        compiler_params=pltpu.CompilerParams(
            collective_id=0, has_side_effects=True, vmem_limit_bytes=58 << 20
        ),
        name="layer",
    )(*args)
    *large, small = made
    vector = jax.ShapeDtypeStruct((width,), F32)
    ended = pl.pallas_call(
        end_kernel,
        out_shape=[like(v, v.dtype) for v in large]
        + [like(query_bias), jax.ShapeDtypeStruct((local,), F32)]
        + [vector] * 7,
        in_specs=[spec] * len(made),
        out_specs=[spec] * 17,
        name="finish",
    )(*large, small)
    return (*ended[:7], ended[7].T, *ended[8:])


def solution(mesh):
    in_specs = (
        P("dp", None, None),
        P("dp", None),
        P("dp", None),
        P(None, "dp", "tensor"),
        P("dp", "tensor"),
        P("dp", "tensor"),
        P("tensor", "dp"),
        P("dp", "tensor"),
        P("tensor", "dp"),
        P(None, "tensor"),
        P("tensor"),
        P(),
        P("tensor"),
        P(),
        P(),
        P(),
        P(),
        P(),
        P("dp", None, None),
    )
    out_specs = (
        P("dp", None, None),
        P("dp", None, None),
        P(None, "dp", "tensor"),
        P("dp", "tensor"),
        P("dp", "tensor"),
        P("tensor", "dp"),
        P("dp", "tensor"),
        P("tensor", "dp"),
        P(None, "tensor"),
        P("tensor"),
        P(),
        P("tensor"),
        P(),
        P(),
        P(),
        P(),
        P(),
    )
    step = fused if fits(mesh) else shards
    return jax.shard_map(step, mesh=mesh, in_specs=in_specs, out_specs=out_specs, check_vma=False)
```

```python
from functools import partial

import jax
import jax.numpy as jnp
from jax import lax
from jax.experimental import pallas as pl
from jax.experimental.pallas import tpu as pltpu
from jax.sharding import PartitionSpec as P

HD = 64


EPSILON = 1e-05
SCALING = 0.125
NEGATIVE = -1000000000.0


def layer_norm_keep(values, norm_gain, norm_shift):
    centre = values - jnp.mean(values, axis=-1, keepdims=True)
    inverse = lax.rsqrt(jnp.mean(centre * centre, axis=-1, keepdims=True) + EPSILON)
    normal = centre * inverse
    return (normal * norm_gain + norm_shift, normal, inverse)


def layer_norm_back(upstream, normal, inverse, norm_gain):
    scaled = upstream * norm_gain
    gain_grad = jnp.sum(upstream * normal, axis=0)
    shift_grad = jnp.sum(upstream, axis=0)
    inner_term = (
        scaled
        - jnp.mean(scaled, axis=-1, keepdims=True)
        - normal * jnp.mean(scaled * normal, axis=-1, keepdims=True)
    )
    return (inverse * inner_term, gain_grad, shift_grad)


def heads_of(matrix):
    return matrix.reshape(matrix.shape[0], -1, HD)


def pick_queries(query_rows, type_row):
    word_tok = (type_row == 0)[:, None]
    return (
        jnp.where(word_tok, query_rows[0], query_rows[2]),
        jnp.where(word_tok, query_rows[1], query_rows[3]),
    )


def score_block(word_heads, entity_heads, key_heads, segment_row, type_row):
    to_words = jnp.einsum("qhd,khd->hqk", word_heads, key_heads, preferred_element_type=jnp.float32)
    to_entities = jnp.einsum(
        "qhd,khd->hqk", entity_heads, key_heads, preferred_element_type=jnp.float32
    )
    scores = jnp.where((type_row == 0)[None, None, :], to_words, to_entities) * SCALING
    allowed = (segment_row[:, None] == segment_row[None, :])[None]
    return jnp.where(allowed, scores, NEGATIVE)


def attend_forward(packed):
    query_rows, key_seq, value_seq, segment_row, type_row = packed
    word_query, entity_query = pick_queries(query_rows, type_row)
    scores = score_block(
        heads_of(word_query), heads_of(entity_query), heads_of(key_seq), segment_row, type_row
    )
    row_top = jnp.max(scores, axis=-1, keepdims=True)
    weights = jnp.exp(scores - row_top)
    totals = jnp.sum(weights, axis=-1, keepdims=True)
    attn_probs = (weights / totals).astype(jnp.bfloat16)
    context = jnp.einsum(
        "hqk,khd->qhd", attn_probs, heads_of(value_seq), preferred_element_type=jnp.float32
    )
    log_total = (row_top + jnp.log(totals))[..., 0]
    return (context.reshape(context.shape[0], -1).astype(jnp.bfloat16), log_total)


def attend_backward(packed):
    query_rows, key_seq, value_seq, segment_row, type_row, log_total, context_grad = packed
    word_query, entity_query = pick_queries(query_rows, type_row)
    word_heads = heads_of(word_query)
    entity_heads = heads_of(entity_query)
    key_heads = heads_of(key_seq)
    value_heads = heads_of(value_seq)
    grad_heads = heads_of(context_grad)
    scores = score_block(word_heads, entity_heads, key_heads, segment_row, type_row)
    attn_probs = jnp.exp(scores - log_total[..., None])
    prob_grad = jnp.einsum(
        "qhd,khd->hqk", grad_heads, value_heads, preferred_element_type=jnp.float32
    )
    score_grad = attn_probs * (prob_grad - jnp.sum(attn_probs * prob_grad, axis=-1, keepdims=True))
    score_low = score_grad.astype(jnp.bfloat16)
    word_key = (type_row == 0)[None, None, :]
    zeroes = jnp.zeros_like(score_low)
    word_part = jnp.where(word_key, score_low, zeroes)
    entity_part = jnp.where(word_key, zeroes, score_low)
    word_qgrad = (
        jnp.einsum("hqk,khd->qhd", word_part, key_heads, preferred_element_type=jnp.float32)
        * SCALING
    )
    entity_qgrad = (
        jnp.einsum("hqk,khd->qhd", entity_part, key_heads, preferred_element_type=jnp.float32)
        * SCALING
    )
    key_delta = (
        jnp.einsum("hqk,qhd->khd", word_part, word_heads, preferred_element_type=jnp.float32)
        + jnp.einsum("hqk,qhd->khd", entity_part, entity_heads, preferred_element_type=jnp.float32)
    ) * SCALING
    value_delta = jnp.einsum(
        "hqk,qhd->khd",
        attn_probs.astype(jnp.bfloat16),
        grad_heads,
        preferred_element_type=jnp.float32,
    )
    row_count = word_qgrad.shape[0]
    return (
        word_qgrad.reshape(row_count, -1),
        entity_qgrad.reshape(row_count, -1),
        key_delta.reshape(row_count, -1),
        value_delta.reshape(row_count, -1),
    )


def row_share(partial_rows):
    return lax.psum_scatter(partial_rows, "tensor", scatter_dimension=0, tiled=True)


def row_whole(rounded_rows):
    return lax.all_gather(rounded_rows, "tensor", axis=0, tiled=True)


def shards(
    layer_input,
    segment_ids,
    token_types,
    query_weight,
    key_weight,
    value_weight,
    out_weight,
    up_weight,
    down_weight,
    query_bias,
    value_bias,
    out_bias,
    up_bias,
    down_bias,
    attn_gain,
    attn_shift,
    ffn_gain,
    ffn_shift,
    cotangent,
):
    seq_count, seq_length, model_width = layer_input.shape
    tokens = layer_input.reshape(-1, model_width)
    row_count = tokens.shape[0]
    share = row_count // lax.axis_size("tensor")
    first_row = lax.axis_index("tensor") * share

    def own_rows(matrix):
        return lax.dynamic_slice_in_dim(matrix, first_row, share, 0)

    def combine_rows(partial_rows):
        return row_share(partial_rows)

    def whole_rows(rounded_rows):
        return row_whole(rounded_rows)

    query_complete, key_full, value_full, out_full = (
        lax.all_gather(query_weight.astype(jnp.bfloat16), "dp", axis=1, tiled=True),
        lax.all_gather(key_weight.astype(jnp.bfloat16), "dp", axis=0, tiled=True),
        lax.all_gather(value_weight.astype(jnp.bfloat16), "dp", axis=0, tiled=True),
        lax.all_gather(out_weight.astype(jnp.bfloat16), "dp", axis=1, tiled=True),
    )
    local_width = key_full.shape[1]
    query_rows = jnp.einsum(
        "gow,qwk->gqok", layer_input, query_complete, preferred_element_type=jnp.float32
    )
    query_rows = (query_rows + query_bias[None, :, None, :]).astype(jnp.bfloat16)
    keys_all = jnp.dot(layer_input, key_full, preferred_element_type=jnp.float32).astype(
        jnp.bfloat16
    )
    values_all = (
        jnp.dot(layer_input, value_full, preferred_element_type=jnp.float32) + value_bias
    ).astype(jnp.bfloat16)
    context, log_total = lax.map(
        attend_forward, (query_rows, keys_all, values_all, segment_ids, token_types)
    )
    context_rows = context.reshape(-1, local_width)
    attended = combine_rows(jnp.dot(context_rows, out_full, preferred_element_type=jnp.float32))
    residual = own_rows(tokens).astype(jnp.float32) + attended + out_bias
    normed, normal_one, inverse_one = layer_norm_keep(residual, attn_gain, attn_shift)
    normed_low = whole_rows(normed.astype(jnp.bfloat16))
    up_full, down_full = (
        lax.all_gather(up_weight.astype(jnp.bfloat16), "dp", axis=0, tiled=True),
        lax.all_gather(down_weight.astype(jnp.bfloat16), "dp", axis=1, tiled=True),
    )
    pre_act = jnp.dot(normed_low, up_full, preferred_element_type=jnp.float32) + up_bias
    activated, gelu_pull = jax.vjp(partial(jax.nn.gelu, approximate=False), pre_act)
    act_low = activated.astype(jnp.bfloat16)
    ffn_out = (
        combine_rows(jnp.dot(act_low, down_full, preferred_element_type=jnp.float32)) + down_bias
    )
    normed_out, normal_two, inverse_two = layer_norm_keep(normed + ffn_out, ffn_gain, ffn_shift)
    output = whole_rows(normed_out.astype(jnp.bfloat16)).reshape(layer_input.shape)
    upstream = own_rows(cotangent.reshape(-1, model_width)).astype(jnp.float32)
    sum_grad, ffngain_grad, ffnshift_grad = layer_norm_back(
        upstream, normal_two, inverse_two, ffn_gain
    )
    downbias_grad = jnp.sum(sum_grad, axis=0)
    sum_low = whole_rows(sum_grad.astype(jnp.bfloat16))
    up_back, down_back = (
        lax.all_gather(up_weight.astype(jnp.bfloat16), "dp", axis=0, tiled=True),
        lax.all_gather(down_weight.astype(jnp.bfloat16), "dp", axis=1, tiled=True),
    )
    down_local = jnp.dot(act_low.T, sum_low, preferred_element_type=jnp.float32)
    act_grad = jnp.dot(sum_low, down_back.T, preferred_element_type=jnp.float32)
    (pre_grad,) = gelu_pull(act_grad)
    upbias_grad = jnp.sum(pre_grad, axis=0)
    pre_low = pre_grad.astype(jnp.bfloat16)
    up_local = jnp.dot(normed_low.T, pre_low, preferred_element_type=jnp.float32)
    upproj_grad, downproj_grad = (
        lax.psum_scatter(up_local, "dp", scatter_dimension=0, tiled=True),
        lax.psum_scatter(down_local, "dp", scatter_dimension=1, tiled=True),
    )
    normed_grad = (
        combine_rows(jnp.dot(pre_low, up_back.T, preferred_element_type=jnp.float32)) + sum_grad
    )
    resid_grad, attngain_grad, attnshift_grad = layer_norm_back(
        normed_grad, normal_one, inverse_one, attn_gain
    )
    outbias_grad = jnp.sum(resid_grad, axis=0)
    resid_low = whole_rows(resid_grad.astype(jnp.bfloat16))
    query_pullback, key_pullback, value_pullback, out_back = (
        lax.all_gather(query_weight.astype(jnp.bfloat16), "dp", axis=1, tiled=True),
        lax.all_gather(key_weight.astype(jnp.bfloat16), "dp", axis=0, tiled=True),
        lax.all_gather(value_weight.astype(jnp.bfloat16), "dp", axis=0, tiled=True),
        lax.all_gather(out_weight.astype(jnp.bfloat16), "dp", axis=1, tiled=True),
    )
    outproj_local = jnp.dot(context_rows.T, resid_low, preferred_element_type=jnp.float32)
    context_grad = jnp.dot(resid_low, out_back.T, preferred_element_type=jnp.float32).astype(
        jnp.bfloat16
    )
    context_grad = context_grad.reshape(seq_count, seq_length, local_width)
    word_qgrad, entity_qgrad, key_delta, value_delta = lax.map(
        attend_backward,
        (query_rows, keys_all, values_all, segment_ids, token_types, log_total, context_grad),
    )
    is_word = (token_types == 0)[..., None]
    zero_rows = jnp.zeros_like(word_qgrad)
    query_delta = jnp.stack(
        [
            jnp.where(is_word, word_qgrad, zero_rows),
            jnp.where(is_word, entity_qgrad, zero_rows),
            jnp.where(is_word, zero_rows, word_qgrad),
            jnp.where(is_word, zero_rows, entity_qgrad),
        ],
        axis=1,
    )
    querybias_grad = jnp.sum(query_delta, axis=(0, 2))
    valuebias_grad = jnp.sum(value_delta, axis=(0, 1))
    query_reduced = query_delta.astype(jnp.bfloat16)
    key_reduced = key_delta.astype(jnp.bfloat16)
    value_reduced = value_delta.astype(jnp.bfloat16)
    query_local = jnp.einsum(
        "nvh,nkvw->khw", layer_input, query_reduced, preferred_element_type=jnp.float32
    )
    key_shard = jnp.einsum(
        "pui,pun->in", layer_input, key_reduced, preferred_element_type=jnp.float32
    )
    value_local = jnp.einsum(
        "pui,pun->in", layer_input, value_reduced, preferred_element_type=jnp.float32
    )
    input_part = (
        jnp.einsum(
            "kayo,azo->kyz", query_reduced, query_pullback, preferred_element_type=jnp.float32
        )
        + jnp.einsum("ohz,wz->ohw", key_reduced, key_pullback, preferred_element_type=jnp.float32)
        + jnp.einsum(
            "ohz,wz->ohw", value_reduced, value_pullback, preferred_element_type=jnp.float32
        )
    )
    input_total = combine_rows(input_part.reshape(-1, model_width))
    input_grad = whole_rows((input_total + resid_grad).astype(jnp.bfloat16)).reshape(
        layer_input.shape
    )
    query_grad, key_grad, value_grad, outproj_grad = (
        lax.psum_scatter(query_local, "dp", scatter_dimension=1, tiled=True),
        lax.psum_scatter(key_shard, "dp", scatter_dimension=0, tiled=True),
        lax.psum_scatter(value_local, "dp", scatter_dimension=0, tiled=True),
        lax.psum_scatter(outproj_local, "dp", scatter_dimension=1, tiled=True),
    )
    querybias_grad, valuebias_grad, upbias_grad = lax.psum(
        (querybias_grad, valuebias_grad, upbias_grad), "dp"
    )
    outbias_grad, downbias_grad, attngain_grad, attnshift_grad, ffngain_grad, ffnshift_grad = (
        lax.psum(
            (
                outbias_grad,
                downbias_grad,
                attngain_grad,
                attnshift_grad,
                ffngain_grad,
                ffnshift_grad,
            ),
            ("dp", "tensor"),
        )
    )
    return (
        output,
        input_grad,
        query_grad,
        key_grad,
        value_grad,
        outproj_grad,
        upproj_grad,
        downproj_grad,
        querybias_grad,
        valuebias_grad,
        outbias_grad,
        upbias_grad,
        downbias_grad,
        attngain_grad,
        attnshift_grad,
        ffngain_grad,
        ffnshift_grad,
    )


MESH = pl.DeviceIdType.MESH
BF = jnp.bfloat16
F32 = jnp.float32
BLOCK = 128


def fits(mesh):
    return mesh.shape["dp"] == 8 and mesh.shape["tensor"] == 4


def nn(a, b):
    return lax.dot_general(a, b, (((1,), (0,)), ((), ())), preferred_element_type=F32)


def nt(a, b):
    return lax.dot_general(a, b, (((1,), (1,)), ((), ())), preferred_element_type=F32)


def tn(a, b):
    return lax.dot_general(a, b, (((0,), (0,)), ((), ())), preferred_element_type=F32)


def norm_rows(values):
    centre = values - jnp.mean(values, axis=-1, keepdims=True)
    inverse = lax.rsqrt(jnp.mean(centre * centre, axis=-1, keepdims=True) + EPSILON)
    return centre * inverse, inverse


def norm_rows_back(upstream, normal, inverse, gain):
    scaled = upstream * gain
    return inverse * (
        scaled
        - jnp.mean(scaled, axis=-1, keepdims=True)
        - normal * jnp.mean(scaled * normal, axis=-1, keepdims=True)
    )


class Net:
    def __init__(self, send, recv, peer):
        self.send, self.recv, self.peer = send, recv, peer
        self.sends = 0
        self.locals = 0
        self.banks = 0
        self.pending = []

    def bank(self, count):
        base = self.banks
        self.banks += count
        return base

    def start(self, src, dst, sem, device, when=None, group=None):
        slot = self.sends % SENDS
        self.sends += 1
        self.finish([p for p in self.pending if p[3] == slot])

        def make():
            return pltpu.make_async_remote_copy(
                src_ref=src,
                dst_ref=dst,
                send_sem=self.send.at[slot],
                recv_sem=self.recv.at[sem],
                device_id=device,
                device_id_type=MESH,
            )

        if when is None:
            make().start()
        else:
            pl.when(when)(lambda: make().start())
        self.pending.append((make, when, group, slot))

    def finish(self, entries):
        for make, when, _, _ in entries:
            if when is None:
                make().wait_send()
            else:
                pl.when(when)(lambda make=make: make().wait_send())
        self.pending = [p for p in self.pending if p not in entries]

    def wait(self, dst, sem, when=None):
        def make():
            return pltpu.make_async_remote_copy(
                src_ref=dst,
                dst_ref=dst,
                send_sem=self.send.at[0],
                recv_sem=self.recv.at[sem],
                device_id=self.peer,
                device_id_type=MESH,
            )

        if when is None:
            make().wait_recv()
        else:
            pl.when(when)(lambda: make().wait_recv())

    def settle(self, *groups):
        self.finish([p for p in self.pending if not groups or p[2] in groups])


SENDS = 48
RECVS = 119


def layer_kernel(
    x_in, seg_ref, typ_ref, qw_in, kw_in, vw_in, ow_in, uw_in, dw_in, qb_ref, vb_ref,
    ob_ref, ub_ref, db_ref, ag_ref, as_ref, fg_ref, fs_ref, cot_in,
    out_end, ig_end, qg_end, kg_end, vg_end, og_end, ug_end, dg_end, small_end,
    x_ref, qw_ref, kw_ref, vw_ref, ow_ref, uw_ref, dw_ref, cot_ref,
    out_ref, ig_ref, qg_ref, kg_ref, vg_ref, og_ref, ug_ref, dg_ref, small_ref,
    wq, wop, wo, own, wf, ubs, segc, wordc, xt, bias, qq, kv, kk, kvt, kkt, probs, ctx, ctp, ct, ctc,
    a_s, n1_s, r1_s, act, gelu_d, gl, parts, rs_send, rs_recv, dub, dzb,
    st_a, st_b, st_c, st_d, st_e, st_f, st_g, dct, dc, dco, go_r, rp, sp, rz,
    dqkv, dx_in, dx_cross, dx_back, gq_r, gp, sv, small_s, small_r, sent8, sw, vz,
    send_sems, recv_sems, local_sems,
):
    d = lax.axis_index("dp")
    t = lax.axis_index("tensor")
    c = d % 2
    x = (d // 2) % 2
    y = d // 4
    pair = t % 2
    j = 2 * pair + c
    block = pair + 2 * c
    home = block == t
    zp = t + 1 - 2 * pair
    zq = (t + 2) % 4
    host = 2 * (d // 2) + t // 2
    chip = d // 2
    sib = d + 1 - 2 * c
    xn = d + 2 - 4 * x
    yn = d + 4 - 8 * y
    rows = x_ref.shape[1]
    quarter = rows // 4
    width = x_ref.shape[2]
    strip = qw_ref.shape[1]
    local = kw_ref.shape[1]
    heads = local // HD
    blocks = rows // BLOCK
    own_rows = pl.ds(pl.multiple_of(t * quarter, 16), quarter)
    net = Net(send_sems, recv_sems, (sib, t))

    def flip_x(device):
        return device + 2 - 4 * ((device // 2) % 2)

    def flip_y(device):
        return device + 4 - 8 * (device // 4)

    dg = flip_y(xn)
    part_m, part_o = parts.at[0:2], parts.at[2:4]
    sums_a, sums_b = parts.reshape(rows, width), gelu_d.reshape(rows, width)
    dqq = [sums_a.at[:, BLOCK * h : BLOCK * (h + 1)] for h in range(heads)]
    dkk = [sums_a.at[:, BLOCK * (heads + h) : BLOCK * (heads + h + 1)] for h in range(heads)]
    dvv = [sums_b.at[:, BLOCK * h : BLOCK * (h + 1)] for h in range(heads)]

    low_z = t < 2
    is_end = jnp.logical_or(t == 0, t == 3)
    is_mid = jnp.logical_not(is_end)
    z_out = jnp.where(low_z, t + 1, t - 1)
    z_back = jnp.where(low_z, 0, 3)

    def place(e):
        return jnp.where(low_z, e, 3 - e)

    def joint(one, other):
        return other if one is None else jnp.logical_and(one, other)

    class LineGather:
        def __init__(self, view, group=None):
            self.view, self.bank, self.group = view, net.bank(4), group

        def copy(self, owner, to, when):
            ref = self.view(owner)
            net.start(ref, ref, self.bank + owner, (d, to), when=when, group=self.group)

        def wait(self, owner, when=None):
            net.wait(self.view(owner), self.bank + owner, when=when)

        def begin(self):
            self.copy(t, z_out, None)
            self.copy(t, z_back, is_mid)

        def step(self, n):
            if n == 1:
                self.wait(place(0), is_mid)
                self.copy(place(0), z_out, is_mid)
                self.wait(place(2), is_mid)
                self.copy(place(2), z_back, is_mid)
            if n == 2:
                self.wait(place(3), is_mid)
                self.copy(place(3), z_back, is_mid)
            self.wait(place(n), is_end)

    class LineReduce:
        def __init__(self, own, came, cross, back):
            self.own, self.came, self.cross, self.back = own, came, cross, back
            self.in_b, self.cross_b, self.back_b = net.bank(3), net.bank(2), net.bank(1)

        def depart(self, e):
            net.start(self.own(e), self.came.at[e - 1], self.in_b + e - 1, (d, z_out), when=is_end)

        def add(self, e, ref):
            @pl.when(is_mid)
            def _():
                ref[...] = (self.own(e)[...].astype(F32) + ref[...].astype(F32)).astype(BF)

        def through(self, e):
            ref = self.came.at[e - 1]
            net.wait(ref, self.in_b + e - 1, when=is_mid)
            self.add(e, ref)
            net.start(ref, self.cross.at[3 - e], self.cross_b + 3 - e, (d, z_out), when=is_mid)

        def pass_back(self):
            net.wait(self.cross.at[0], self.cross_b, when=is_mid)
            self.add(0, self.cross.at[0])
            net.start(self.cross.at[0], self.back, self.back_b, (d, z_back), when=is_mid)

        def total(self):
            net.wait(self.came.at[0], self.in_b, when=is_mid)
            net.wait(self.cross.at[1], self.cross_b + 1, when=is_mid)
            net.wait(self.back, self.back_b, when=is_end)
            others = self.came[0].astype(F32) + self.cross[1].astype(F32)
            mine = self.own(jnp.where(is_mid, 1, 0))[...].astype(F32)
            return mine + jnp.where(is_mid, others, self.back[...].astype(F32))

    class Local:
        def __init__(self, source, target):
            self.copy = pltpu.make_async_copy(source, target, local_sems.at[net.locals])
            net.locals += 1
            self.copy.start()

        def wait(self):
            self.copy.wait()

    in_q, in_k, in_v = Local(qw_in, qw_ref), Local(kw_in, kw_ref), Local(vw_in, vw_ref)
    in_o, in_u, in_d = Local(ow_in, ow_ref), Local(uw_in, uw_ref), Local(dw_in, dw_ref)
    in_x, in_cot = Local(x_in, x_ref), Local(cot_in, cot_ref)

    barrier = pltpu.get_barrier_semaphore()
    for m in range(1, 8):
        pl.semaphore_signal(barrier, 1, device_id=((d + m) % 8, t), device_id_type=MESH)
    for k in range(1, 4):
        pl.semaphore_signal(barrier, 1, device_id=(d, (t + k) % 4), device_id_type=MESH)
    pl.semaphore_signal(barrier, 1, device_id=(sib, zq), device_id_type=MESH)

    for arrived in (in_q, in_k, in_v):
        arrived.wait()
    for h in range(heads):
        at = slice(HD * h, HD * (h + 1))
        piece = jnp.concatenate(
            [qw_ref[i, :, at] for i in range(4)] + [kw_ref[:, at], vw_ref[:, at]], axis=1
        )
        wq[d, :, 6 * HD * h : 6 * HD * (h + 1)] = piece.astype(BF)

    pl.semaphore_wait(barrier, 11)

    class PlaneGather:
        def __init__(self, group, view, whole):
            self.view, self.whole, self.group, self.bank = view, whole, group, net.bank(5)

        def copy(self, half, block, device, sem):
            ref = self.whole(block) if half is None else self.view(half, block)
            net.start(ref, ref, self.bank + sem, (device, t), group=self.group)

        def begin(self):
            self.copy(0, d, yn, 0)
            self.copy(1, d, xn, 1)
            self.copy(1, d, yn, 2)
            self.copy(0, d, xn, 2)
            self.copy(None, d, sib, 4)

        def middle(self):
            net.wait(self.view(0, yn), self.bank)
            self.copy(0, yn, xn, 3)
            net.wait(self.view(1, xn), self.bank + 1)
            self.copy(1, xn, yn, 3)

        def middle2(self):
            net.wait(self.whole(d), self.bank + 2)
            self.copy(None, yn, sib, 4)
            self.copy(None, xn, sib, 4)

        def late(self):
            net.wait(self.whole(dg), self.bank + 3)
            self.copy(None, dg, sib, 4)

        def end(self):
            net.wait(self.whole(slice(0, 4)), self.bank + 4)

    most = strip // 2

    gather_q = PlaneGather(
        "q", lambda half, b: wq.at[b, most * half : most * (half + 1)], lambda b: wq.at[b]
    )
    gather_q.begin()

    def wide_t(value, high, wide):
        r, w = value.shape
        if w < wide:
            value = jnp.concatenate([value, jnp.zeros((r, wide - w), value.dtype)], axis=1)
        if r < high:
            value = jnp.concatenate([value, jnp.zeros((high - r, wide), value.dtype)], axis=0)
        return value.T

    for arrived in (in_o, in_u, in_d):
        arrived.wait()
    def pack(block):
        most = block.shape[0] // 2
        rest = block[:, BLOCK:]
        return jnp.concatenate(
            [block[:, :BLOCK], jnp.concatenate([rest[:most], rest[most:]], axis=1)], axis=0
        )

    def rest_of(packed, count):
        below = packed[count:]
        return jnp.concatenate([below[:, :HD], below[: count - below.shape[0], HD:]], axis=0)

    wop[t, d] = pack(wide_t(ow_ref[...], 256, 128)[:strip, :local]).astype(BF)
    own[0] = uw_ref[...].astype(BF)
    own[1] = dw_ref[...].astype(BF)
    ubs[t] = jnp.broadcast_to(ub_ref[...][None], ubs.shape[1:])

    ub_z = net.bank(1)
    wf_a = net.bank(4)

    class ChipGather:
        def __init__(self, i):
            self.i, self.bank = i, net.bank(3)

        def send_near(self):
            i = self.i
            net.start(own.at[i], wf.at[i, d], wf_a + 2 * i + c, (host, t), when=host != d)

            @pl.when(host == d)
            def _():
                wf[i, d] = own[i]

        def send_far(self):
            net.start(own.at[self.i], wf.at[self.i, d], wf_a + 2 * self.i + c, (host, zq))

        def copy(self, view, of, device, sem, when=None):
            ref = wf.at[self.i, 2 * (of // 2) + view]
            net.start(ref, ref, self.bank + sem, (device, t), when=when, group="f")

        def wait(self, view, of, sem):
            net.wait(wf.at[self.i, 2 * (of // 2) + view], self.bank + sem)

        def begin(self, at_home):
            i, when = self.i, home if at_home else jnp.logical_not(home)
            if not at_home:
                net.wait(wf.at[i, d], wf_a + 2 * i + c, when=when)
            net.wait(wf.at[i, sib], wf_a + 2 * i + 1 - c, when=when)
            for view, device, sem in ((0, yn, 0), (1, xn, 1), (1, yn, 2), (0, xn, 2)):
                self.copy(view, d, device, sem, when)

        def middle(self):
            self.wait(0, yn, 0)
            self.copy(0, yn, xn, 2)
            self.wait(1, xn, 1)
            self.copy(1, xn, yn, 2)

        def end(self):
            net.wait(wf.at[self.i, 0:4], self.bank + 2)

    up, down = ChipGather(0), ChipGather(1)
    wo_z = net.bank(1)
    for k in (2, 1, 3):
        net.start(wop.at[t, d], wop.at[t, d], wo_z, (d, (t + k) % 4))
    up.send_near()
    down.send_near()
    for b in range(blocks):
        at = slice(BLOCK * b, BLOCK * (b + 1))
        segc[at, :] = jnp.broadcast_to(seg_ref[:, at].astype(F32), (BLOCK, BLOCK)).T
        wordc[at, :] = jnp.broadcast_to((typ_ref[:, at] == 0).astype(F32), (BLOCK, BLOCK)).T
    in_x.wait()
    xt[...] = x_ref[0].T
    for h in range(heads):
        at = slice(HD * h, HD * (h + 1))
        bias[:, 6 * HD * h : 6 * HD * (h + 1)] = jnp.concatenate(
            [qb_ref[i : i + 1, at] for i in range(4)] + [jnp.zeros((1, HD), F32), vb_ref[at][None]],
            axis=1,
        )

    gather_q.middle()
    up.send_far()
    gather_q.middle2()
    net.wait(wop.at[0:3, d], wo_z)
    gather_o = PlaneGather(
        "o", lambda half, b: wop.at[2 * half : 2 * half + 2, b], lambda b: wop.at[:, b]
    )
    gather_o.begin()
    down.send_far()
    net.start(ubs.at[t], ubs.at[t], ub_z, (d, zq))
    up.begin(True)
    gather_q.late()
    gather_q.end()
    low_half = lax.broadcasted_iota(jnp.int32, (rows, BLOCK), 1) < HD
    is_word = wordc[...] > 0.5
    for h in range(heads):
        base = 6 * HD * h
        at = slice(BLOCK * h, BLOCK * (h + 1))
        made = nn(x_ref[0], wq[:, :, base : base + 6 * HD].reshape(width, 6 * HD))
        made = made + bias[:, base : base + 6 * HD]
        qq[:, at] = jnp.where(is_word, made[:, :BLOCK], made[:, BLOCK : 2 * BLOCK]).astype(BF)
        both = made[:, 2 * BLOCK :]
        keys = jnp.where(low_half, both, pltpu.roll(both, HD, 1))
        keys = jnp.where(jnp.logical_xor(is_word, low_half), 0.0, keys)
        kv[:, at] = both.astype(BF)
        kk[:, at] = keys.astype(BF)
        kvt[h] = both.T[HD:].astype(BF)
        kkt[h] = keys.T.astype(BF)

    gather_o.middle()
    gather_o.middle2()
    ct_z = net.bank(1)

    def span(b):
        return BLOCK * max(0, b - 2), BLOCK * min(blocks, b + 3)

    kept = [0]
    for b in range(blocks):
        kept.append(kept[-1] + span(b)[1] - span(b)[0])
    for b in range(blocks):
        lo, hi = span(b)
        at_q = slice(BLOCK * b, BLOCK * (b + 1))
        same = segc[lo:hi, :] == seg_ref[:, at_q].astype(F32)
        found, raw = [], []
        for h in range(heads):
            at = slice(BLOCK * h, BLOCK * (h + 1))
            raw.append(nt(kk[lo:hi, at], qq[at_q, at]))
        for h in range(heads):
            scores = jnp.where(same, raw[h] * SCALING, NEGATIVE)
            weights = jnp.exp(scores - jnp.max(scores, axis=0, keepdims=True))
            weights = weights * (1.0 / jnp.sum(weights, axis=0, keepdims=True))
            probs[h, kept[b] : kept[b + 1]] = weights
            raw[h] = weights.astype(BF)
        for h in range(heads):
            found.append(nn(kvt[h, :, lo:hi], raw[h]))
        found.append(jnp.zeros((HD, BLOCK), F32))
        ctx[at_q, :] = jnp.concatenate(found, axis=0).T[:, :local].astype(BF)
        if b == 2:
            up.begin(False)
        if b > 0:
            s = b - 1
            ctp[s] = pack(ctx[quarter * s : quarter * (s + 1), :])
            net.start(ctp.at[s], ct.at[t], ct_z, (d, s), when=t != s)
    ct[t] = ctp[t]

    down.begin(True)
    gather_o.late()
    down.begin(False)
    up.middle()
    gather_o.end()
    for s in range(4):
        wo[:, :, BLOCK * s : BLOCK * (s + 1)] = wop[s, :, :strip]
    for s in (0, 2):
        at = slice(4 * BLOCK + HD * s, 4 * BLOCK + HD * (s + 2))
        one, other = wop[s, :, strip:], wop[s + 1, :, strip:]
        wo[:, :most, at] = jnp.concatenate([one[:, :, :HD], other[:, :, :HD]], axis=2)
        wo[:, most:, at] = jnp.concatenate([one[:, :, HD:], other[:, :, HD:]], axis=2)
    net.wait(ct.at[0:3], ct_z)
    for s in range(4):
        ctc[:, BLOCK * s : BLOCK * (s + 1)] = ct[s, :quarter]
    for s in (0, 2):
        ctc[:, 4 * BLOCK + HD * s : 4 * BLOCK + HD * (s + 2)] = jnp.concatenate(
            [rest_of(ct[s], quarter), rest_of(ct[s + 1], quarter)], axis=1
        )
    whole_wo = wo.reshape(width, width)
    attended = nt(ctc[...], whole_wo[...])
    normal, inverse = norm_rows(x_ref[0, own_rows, :].astype(F32) + attended + ob_ref[...][None])
    n1_s[...] = normal
    r1_s[...] = jnp.broadcast_to(inverse, r1_s.shape)
    normed = normal * ag_ref[...][None] + as_ref[...][None]
    a_s[...] = normed
    act[j] = normed.astype(BF)

    def rows_of(ref, first, count):
        return lambda owner: ref.at[
            0, pl.ds(pl.multiple_of(owner * quarter + first, 16), count)
        ]

    part = quarter // 2
    chunk = [slice(part * q, part * (q + 1)) for q in range(2)]

    class RowGather:
        def __init__(self, ref):
            self.ref, self.bank = ref, net.bank(8)

        def copy(self, q, rank, device):
            ref = self.ref.at[rank, chunk[q]]
            net.start(ref, ref, self.bank + 4 * q + rank, device)

        def wait(self, q, rank):
            net.wait(self.ref.at[rank, chunk[q]], self.bank + 4 * q + rank)

        def begin(self, q):
            self.copy(q, j, (d, zp))
            self.copy(q, j, (sib, t))

        def near(self, q):
            self.wait(q, 2 * pair + 1 - c)

        def middle(self, q):
            self.wait(q, 2 - 2 * pair + c)
            self.copy(q, 2 - 2 * pair + c, (sib, t))

        def far(self, q):
            self.wait(q, 3 - 2 * pair - c)

    class RowSum:
        def __init__(self, index):
            self.index, self.bank = index, net.bank(6)

        def hand(self, q, slot, partial_rows):
            where = 3 * self.index + slot
            rs_send[where, chunk[q]] = partial_rows.astype(BF)
            net.start(
                rs_send.at[where, chunk[q]], rs_recv.at[where, chunk[q]], self.bank + 3 * q + slot,
                (d, zp) if slot == 2 else (sib, t),
            )

        def take(self, q, slot):
            where = 3 * self.index + slot
            net.wait(rs_recv.at[where, chunk[q]], self.bank + 3 * q + slot)
            return rs_recv[where, chunk[q]].astype(F32)

        def near(self, q):
            self.hand(q, 0, part_m[1 - c, chunk[q]])

        def away(self, q):
            self.hand(q, 1, part_o[1 - c, chunk[q]])

        def across(self, q):
            self.hand(q, 2, part_o[c, chunk[q]] + self.take(q, 1))

        def total(self, q):
            return part_m[c, chunk[q]] + self.take(q, 0) + self.take(q, 2)

    rows_a = RowGather(act)
    rows_a.begin(0)
    rows_a.begin(1)
    down.middle()
    rows_a.middle(0)
    rows_a.middle(1)
    rows_a.near(0)
    rows_a.near(1)
    net.wait(ubs.at[zq], ub_z)
    up.end()
    near = pl.ds(2 * pair, 2)
    away = pl.ds(2 - 2 * pair, 2)

    def feed(half):
        hidden = nn(act[half].reshape(2 * quarter, width), wf[0].reshape(width, width))
        hidden = hidden + ubs[block][:1]
        bell = 0.5 * (1.0 + lax.erf(hidden * 0.7071067811865476))
        slope = bell + hidden * (0.3989422804014327 * jnp.exp(-0.5 * hidden * hidden))
        gelu_d[half] = slope.reshape(2, quarter, width)
        gl[half] = (hidden * bell).astype(BF).reshape(2, quarter, width)

    def feed_out(half, partial_ref):
        made = nt(gl[half].reshape(2 * quarter, width), wf[1].reshape(width, width))
        partial_ref[...] = made.reshape(2, quarter, width)

    feed(near)
    rows_a.far(0)
    rows_a.far(1)
    feed(away)
    down.end()
    sum_f = RowSum(0)
    feed_out(away, part_o)
    sum_f.away(0)
    sum_f.away(1)
    feed_out(near, part_m)
    sum_f.across(0)
    sum_f.across(1)
    sum_f.near(0)
    sum_f.near(1)
    in_cot.wait()
    rows_u = RowGather(dub)
    gain_sum, shift_sum, bias_sum = 0.0, 0.0, 0.0
    for q in range(2):
        ffn_out = sum_f.total(q) + db_ref[...][None]
        normal, inverse = norm_rows(a_s[chunk[q]] + ffn_out)
        rows_q = pl.ds(pl.multiple_of(t * quarter + part * q, 16), part)
        out_ref[0, rows_q, :] = (normal * fg_ref[...][None] + fs_ref[...][None]).astype(BF)
        upstream = cot_ref[0, rows_q, :].astype(F32)
        du = norm_rows_back(upstream, normal, inverse, fg_ref[...][None])
        dub[j, chunk[q]] = du.astype(BF)
        rows_u.begin(q)
        a_s[chunk[q]] = du
        gain_sum = gain_sum + jnp.sum(upstream * normal, axis=0, keepdims=True)
        shift_sum = shift_sum + jnp.sum(upstream, axis=0, keepdims=True)
        bias_sum = bias_sum + jnp.sum(du, axis=0, keepdims=True)
    line_out = [LineGather(rows_of(out_ref, part * q, part)) for q in range(2)]
    line_out[0].begin()
    sv[...] = jnp.zeros_like(sv)
    sv[0:1] = gain_sum
    sv[1:2] = shift_sum
    sv[2:3] = bias_sum

    def feed_back(half, rows_q, partial_ref):
        count = 2 * (rows_q.stop - rows_q.start)
        made = nn(dub[half, rows_q].reshape(count, width), wf[1].reshape(width, width))
        made = made * gelu_d[half, rows_q].reshape(count, width)
        low = made.astype(BF)
        dzb[half, rows_q] = low.reshape(2, count // 2, width)
        partial_ref[:, rows_q] = nt(low, wf[0].reshape(width, width)).reshape(2, count // 2, width)
        return jnp.sum(made, axis=0, keepdims=True)

    sum_b = RowSum(1)
    rows_u.near(0)
    rows_u.near(1)
    up_sum = feed_back(near, slice(0, quarter), part_m)
    sum_b.near(0)
    sum_b.near(1)
    rows_u.middle(0)
    rows_u.far(0)
    up_sum = up_sum + feed_back(away, chunk[0], part_o)
    sum_b.away(0)
    rows_u.middle(1)
    sum_b.across(0)
    rows_u.far(1)
    up_sum = up_sum + feed_back(away, chunk[1], part_o)
    sum_b.away(1)
    sv[6:7] = up_sum
    half = width // 2

    class StripSum:
        def __init__(self, i):
            self.i, self.bank = i, net.bank(9)
            self.by_chip = wf.at[i].reshape(2, 2, 2, strip, width)

        def make(self, left, right):
            made = tn(left[...].reshape(4 * quarter, width), right[...].reshape(4 * quarter, width))
            wf[self.i] = made.astype(BF).reshape(8, strip, width)

        def begin(self):
            net.start(
                self.by_chip.at[:, 1 - x, :, :, :half], st_a.at[self.i], self.bank, (xn, t)
            )
            net.start(
                self.by_chip.at[1 - y, :, :, :, half:], st_b.at[self.i], self.bank + 1, (yn, t)
            )

        def turn(self):
            i = self.i
            net.wait(st_a.at[i], self.bank)
            st_a[i] = (st_a[i].astype(F32) + self.by_chip[:, x, :, :, :half].astype(F32)).astype(BF)
            for core in range(2):
                net.start(
                    st_a.at[i, 1 - y, core], st_c.at[i, c], self.bank + 2 + c,
                    (2 * (yn // 2) + core, t),
                )
            net.start(st_a.at[i, y, 1 - c], st_g.at[i, 0], self.bank + 6, (sib, t))
            net.wait(st_b.at[i], self.bank + 1)
            st_b[i] = (st_b[i].astype(F32) + self.by_chip[y, :, :, :, half:].astype(F32)).astype(BF)
            for core in range(2):
                net.start(
                    st_b.at[i, 1 - x, core], st_d.at[i, c], self.bank + 4 + c,
                    (2 * (xn // 2) + core, t),
                )
            net.start(st_b.at[i, x, 1 - c], st_g.at[i, 1], self.bank + 7, (sib, t))

        def gather(self):
            i = self.i
            for core in range(2):
                net.wait(st_c.at[i, core], self.bank + 2 + core)
                net.wait(st_d.at[i, core], self.bank + 4 + core)
            net.wait(st_g.at[i, 0], self.bank + 6)
            net.wait(st_g.at[i, 1], self.bank + 7)
            for whose, first, second in (
                (c, st_a.at[i, y, c], st_b.at[i, x, c]), (1 - c, st_g.at[i, 0], st_g.at[i, 1])
            ):
                st_e[i, whose, :, :half] = (
                    first[...].astype(F32) + st_c[i, whose].astype(F32)
                ).astype(BF)
                st_e[i, whose, :, half:] = (
                    second[...].astype(F32) + st_d[i, whose].astype(F32)
                ).astype(BF)

        def deliver(self, when=None):
            i = self.i
            net.start(st_e.at[i, 1 - t // 2], st_f.at[i], self.bank + 8, (d, zq), when=when)

        def total(self):
            i = self.i
            net.wait(st_f.at[i], self.bank + 8)
            return st_e[i, t // 2].astype(F32) + st_f[i].astype(F32)

    class SmallSum:
        def __init__(self, index):
            self.index, self.bank = index, net.bank(2)

        def begin(self, values):
            i = self.index
            small_s[i, 0] = values
            for r in (xn, yn, dg):
                net.start(small_s.at[i, 0], small_r.at[i, chip], self.bank, (r, t))
            small_r[i, chip] = values

        def plane(self):
            i = self.index
            net.wait(small_r.at[i, 0:3], self.bank)
            total = small_r[i, 0]
            for k in range(1, 4):
                total = total + small_r[i, k]
            small_s[i, 1] = total
            net.start(small_s.at[i, 1], small_r.at[i, 4], self.bank + 1, (sib, t))

        def cores(self):
            net.wait(small_r.at[self.index, 4], self.bank + 1)
            return small_s[self.index, 1], small_r[self.index, 4]

    net.settle("f")
    down_sum, up_sums = StripSum(1), StripSum(0)
    down_sum.make(dub, gl)
    down_sum.begin()
    sum_b.across(1)
    up_sums.make(act, dzb)
    dc_z = net.bank(1)
    gain_sum, shift_sum, bias_sum, dhb = 0.0, 0.0, 0.0, []
    for q in range(2):
        da = a_s[chunk[q]] + sum_b.total(q)
        normal = n1_s[chunk[q]]
        dh = norm_rows_back(da, normal, r1_s[chunk[q], :1], ag_ref[...][None])
        a_s[chunk[q]] = dh
        dhb.append(dh.astype(BF))
        made = nn(dhb[q], whole_wo[...])
        for s in range(4):
            rest = made[:, 4 * BLOCK + HD * s : 4 * BLOCK + HD * (s + 1)]
            rest = jnp.concatenate([rest, jnp.zeros((16, HD), F32)], axis=0)
            most = (part + 16) // 2
            dct[s, q] = jnp.concatenate(
                [
                    made[:, BLOCK * s : BLOCK * (s + 1)],
                    jnp.concatenate([rest[:most], rest[most:]], axis=1),
                ],
                axis=0,
            ).astype(BF)
        for k in (2, 1, 3):
            s = (t + k) % 4
            net.start(dct.at[s, q], dc.at[t, q], dc_z, (d, s))
        dc[t, q] = dct[t, q]
        gain_sum = gain_sum + jnp.sum(da * normal, axis=0, keepdims=True)
        shift_sum = shift_sum + jnp.sum(da, axis=0, keepdims=True)
        bias_sum = bias_sum + jnp.sum(dh, axis=0, keepdims=True)
    dhb = jnp.concatenate(dhb, axis=0)
    line_out[1].begin()
    line_out[0].step(1)
    sv[3:4] = gain_sum
    sv[4:5] = shift_sum
    sv[5:6] = bias_sum
    small_a = SmallSum(0)
    small_a.begin(sv[...])
    down_sum.turn()
    up_sums.begin()
    wo[...] = tn(dhb, ctc[...]).astype(BF).reshape(8, strip, width)
    by_core = wo.reshape(4, 2, strip, width)
    go_b = net.bank(1)
    net.start(by_core.at[:, 1 - c], go_r, go_b, (sib, t))

    net.wait(dc.at[0:3], dc_z)
    upper = lax.broadcasted_iota(jnp.int32, (part, BLOCK), 1) >= HD
    for s in range(4):
        for q in range(2):
            got = dc[s, q]
            at_q = slice(quarter * s + part * q, quarter * s + part * (q + 1))
            first = got[:part].astype(F32)
            blank = jnp.zeros((part, HD), BF)
            dco[at_q, :BLOCK] = jnp.concatenate([blank, got[:part, :HD]], axis=1)
            dco[at_q, BLOCK : 2 * BLOCK] = jnp.where(upper, first, 0.0).astype(BF)
            dco[at_q, 2 * BLOCK :] = jnp.concatenate([blank, rest_of(got, part)], axis=1)
    for h in range(heads):
        dkk[h][...] = jnp.zeros((rows, BLOCK), F32)
        dvv[h][...] = jnp.zeros((rows, BLOCK), F32)
    for b in range(blocks):
        lo, hi = span(b)
        at_q = slice(BLOCK * b, BLOCK * (b + 1))
        if b == 3:
            line_out[1].step(1)
        if b == 4:
            line_out[0].step(2)
            down_sum.gather()
            down_sum.deliver()
        columns = [slice(BLOCK * h, BLOCK * (h + 1)) for h in range(heads)]
        lows = []
        for h, at in enumerate(columns):
            dp = nt(kv[lo:hi, at], dco[at_q, at])
            weights = probs[h, kept[b] : kept[b + 1]]
            ds = weights * (dp - jnp.sum(weights * dp, axis=0, keepdims=True))
            lows.append((ds.astype(BF), weights.astype(BF)))
        for h, at in enumerate(columns):
            low, weights = lows[h]
            blank = jnp.zeros((BLOCK, BLOCK), BF)
            beside = jnp.concatenate(
                [
                    jnp.concatenate([qq[at_q, at], blank], axis=1),
                    jnp.concatenate([blank, dco[at_q, at]], axis=1),
                ],
                axis=0,
            )
            made = nn(jnp.concatenate([low, weights], axis=1), beside)
            dkk[h][lo:hi] += made[:, :BLOCK]
            dvv[h][lo:hi] += made[:, BLOCK:]
            dqq[h][at_q] = nn(kkt[h, :, lo:hi], low).T * SCALING

    small_a.plane()
    for h in range(heads):
        base = 6 * HD * h
        first = jnp.where(is_word, dqq[h][...], 0.0)
        second = jnp.where(is_word, 0.0, dqq[h][...])
        keys = dkk[h][...]
        keys = jnp.where(is_word, keys, pltpu.roll(keys, HD, 1)) * SCALING
        third = jnp.where(low_half, keys, dvv[h][...])
        for i, piece in enumerate((first, second, third)):
            at = slice(base + BLOCK * i, base + BLOCK * (i + 1))
            dqkv[:, at] = piece.astype(BF)
            row, col = divmod(base + BLOCK * i, width)
            sv[row : row + 1, col : col + BLOCK] = jnp.sum(piece, axis=0, keepdims=True)

    first_rows = pl.ds(pl.multiple_of(jnp.where(low_z, rows // 2, 0), 16), rows // 2)
    other_rows = pl.ds(pl.multiple_of(jnp.where(low_z, 0, rows // 2), 16), rows // 2)
    first_two = pl.ds(jnp.where(low_z, 2, 0), 2)
    other_two = pl.ds(jnp.where(low_z, 0, 2), 2)

    def back_to_input(rows_b, quarters):
        made = nt(dqkv[rows_b, :], wq[...].reshape(width, 6 * local))
        dzb[quarters] = made.astype(BF).reshape(2, quarter, width)

    third = [slice(width // 3 * q, width // 3 * (q + 1)) for q in range(3)]
    line_dx, line_in = [], []
    for q, cut in enumerate(third):
        line_dx.append(
            LineReduce(
                lambda e, cut=cut: dzb.at[place(e), :, cut],
                dx_in.at[q], dx_cross.at[q], dx_back.at[q],
            )
        )
        line_in.append(
            LineGather(
                lambda owner, cut=cut: ig_ref.at[
                    0, pl.ds(pl.multiple_of(owner * quarter, 16), quarter), cut
                ]
            )
        )

    def arrive(q):
        total = line_dx[q].total() + a_s[:, third[q]]
        ig_ref[0, own_rows, third[q]] = total.astype(BF)
        line_in[q].begin()

    back_to_input(first_rows, first_two)
    for q in range(3):
        line_dx[q].depart(3)
        line_dx[q].depart(2)
    back_to_input(other_rows, other_two)
    for q in range(3):
        line_dx[q].depart(1)
    line_out[1].step(2)
    small_b = SmallSum(1)
    small_b.begin(sv[...])

    net.settle("q")
    wq[...] = nn(xt[...], dqkv[...]).astype(BF).reshape(8, strip, 6 * local)
    q_by_core = wq.reshape(4, 2, strip, 6 * local)
    gq_b = net.bank(1)
    net.start(q_by_core.at[:, 1 - c], gq_r, gq_b, (sib, t))
    up_sums.turn()
    net.wait(go_r, go_b)
    go_r[...] = (by_core[:, c].astype(F32) + go_r[...].astype(F32)).astype(BF)
    rp_b = net.bank(1)
    for r in (xn, yn, dg):
        net.start(go_r.at[r // 2], rp.at[chip], rp_b, (r, t))
    rp[chip] = go_r[chip]
    plane_sum, other_sum = small_a.cores()
    first_core = c == 0
    own_units, other_units = plane_sum[6:7], other_sum[6:7]
    sent8[0:6] = plane_sum[0:6] + other_sum[0:6]
    sent8[6:7] = jnp.where(first_core, own_units, other_units)
    sent8[7:8] = jnp.where(first_core, other_units, own_units)
    line_dx[0].through(3)
    line_dx[0].through(2)
    net.wait(gq_r, gq_b)
    gq_r[...] = (q_by_core[:, c].astype(F32) + gq_r[...].astype(F32)).astype(BF)
    gp_b = net.bank(1)
    for r in (xn, yn, dg):
        net.start(gq_r.at[r // 2], gp.at[chip], gp_b, (r, t))
    gp[chip] = gq_r[chip]

    line_dx[0].pass_back()
    line_dx[1].through(3)
    line_dx[1].through(2)
    line_dx[1].pass_back()
    line_dx[2].through(3)
    line_dx[2].through(2)
    line_dx[2].pass_back()
    arrive(0)
    arrive(1)
    arrive(2)

    for q in range(3):
        line_in[q].step(1)
    up_sums.gather()
    up_sums.deliver()
    net.wait(rp.at[0:3], rp_b)
    total = rp[0].astype(F32)
    for k in range(1, 4):
        total = total + rp[k].astype(F32)
    for s in range(4):
        rest = total[:, 4 * BLOCK + HD * s : 4 * BLOCK + HD * (s + 1)]
        sp[s] = pack(
            jnp.concatenate([total[:, BLOCK * s : BLOCK * (s + 1)], rest], axis=1)
        ).astype(BF)
    rz_b = net.bank(1)
    rz[t] = sp[t]

    def send_rz(when):
        for k in range(1, 4):
            s = (t + k) % 4
            net.start(sp.at[s], rz.at[t], rz_b, (d, s), when=when)

    send_rz(None)
    vz_b = net.bank(2)
    for k in (2, 1, 3):
        net.start(sent8, vz.at[t], vz_b, (d, (t + k) % 4), when=first_core)
    vz[t] = sent8[...]
    line_out[0].step(3)
    line_out[1].step(3)
    ends = [Local(out_ref, out_end)]
    for q in range(3):
        line_in[q].step(2)
    small_b.plane()
    net.wait(vz.at[0:3], vz_b, when=first_core)

    @pl.when(first_core)
    def _():
        total = vz[0]
        for k in range(1, 4):
            total = total + vz[k]
        sw[0:6] = total[0:6]
        units = vz[t] + vz[zq]
        sw[6:7] = jnp.where(t < 2, units[6:7], units[7:8])
        sw[7:8] = units[7:8]

    net.start(sw, sw, vz_b + 1, (sib, t), when=first_core)
    net.wait(sw, vz_b + 1, when=c == 1)
    small_ref[0:8] = sw[...]
    plane_sum, other_sum = small_b.cores()
    small_ref[8:16] = plane_sum + other_sum
    dg_ref[...] = down_sum.total()
    ug_ref[...] = up_sums.total()
    ends += [Local(dg_ref, dg_end), Local(ug_ref, ug_end), Local(small_ref, small_end)]
    net.wait(rz.at[0:3], rz_b)
    total = rz[0].astype(F32)
    for s in range(1, 4):
        total = total + rz[s].astype(F32)
    total = jnp.concatenate([total[:strip], rest_of(total, strip)], axis=1)
    og_ref[...] = wide_t(total, BLOCK, 256)[:local, :strip]

    ends += [Local(og_ref, og_end)]
    net.wait(gp.at[0:3], gp_b)
    total = gp[0].astype(F32)
    for k in range(1, 4):
        total = total + gp[k].astype(F32)
    for h in range(heads):
        base = 6 * HD * h
        at = slice(HD * h, HD * (h + 1))
        for i in range(4):
            qg_ref[i, :, at] = total[:, base + HD * i : base + HD * (i + 1)]
        kg_ref[:, at] = total[:, base + 4 * HD : base + 5 * HD]
        vg_ref[:, at] = total[:, base + 5 * HD : base + 6 * HD]

    ends += [Local(qg_ref, qg_end), Local(kg_ref, kg_end), Local(vg_ref, vg_end)]
    for q in range(3):
        line_in[q].step(3)
    ends += [Local(ig_ref, ig_end)]
    net.settle()
    for copy in ends:
        copy.wait()
    assert net.banks == RECVS, net.banks


def end_kernel(*refs):
    sources, small = refs[:8], refs[8]
    targets, (qbg, vbg), vectors = refs[9:17], refs[17:19], refs[19:26]
    for source, target in zip(sources, targets):
        target[...] = source[...]
    fgg, fsg, dbg, agg, asg, obg, ubg = (small[i] for i in range(7))
    for ref, value in zip(vectors, (obg, ubg, dbg, agg, asg, fgg, fsg)):
        ref[...] = value
    width = small.shape[1]
    values = []
    for h in range(vbg.shape[0] // HD):
        row, col = divmod(6 * HD * h, width)
        piece = small[8 + row : 9 + row, col : col + 6 * HD]
        for i in range(4):
            qbg[i : i + 1, HD * h : HD * (h + 1)] = piece[:, HD * i : HD * (i + 1)]
        values.append(piece[:, 5 * HD :])
    vbg[...] = jnp.concatenate(values, axis=1)[0]


def fused(
    layer_input, segment_ids, token_types, query_weight, key_weight, value_weight, out_weight,
    up_weight, down_weight, query_bias, value_bias, out_bias, up_bias, down_bias, attn_gain,
    attn_shift, ffn_gain, ffn_shift, cotangent,
):
    rows, width = layer_input.shape[1:]
    strip, local = key_weight.shape
    quarter, heads, blocks = rows // 4, local // HD, rows // BLOCK
    kept = sum(BLOCK * (min(blocks, b + 3) - max(0, b - 2)) for b in range(blocks))
    args = [
        layer_input, segment_ids, token_types, query_weight, key_weight, value_weight, out_weight,
        up_weight, down_weight.T, query_bias, value_bias, out_bias, up_bias, down_bias, attn_gain,
        attn_shift, ffn_gain, ffn_shift, cotangent,
    ]

    def like(v, dtype=F32):
        return jax.ShapeDtypeStruct(v.shape, dtype)

    outs = [
        like(layer_input, BF), like(layer_input, BF), like(query_weight), like(key_weight),
        like(value_weight), like(out_weight), like(up_weight), jax.ShapeDtypeStruct((strip, width), F32),
        jax.ShapeDtypeStruct((16, width), F32),
    ]
    v = pltpu.VMEM
    scratch = [
        v(layer_input.shape, BF), v(query_weight.shape, F32), v(key_weight.shape, F32),
        v(value_weight.shape, F32), v(out_weight.shape, F32), v(up_weight.shape, F32),
        v((strip, width), F32), v(cotangent.shape, BF),
    ] + [v(o.shape, o.dtype) for o in outs] + [
        v((8, strip, 6 * local), BF), v((4, 8, 3 * strip // 2, BLOCK), BF), v((8, strip, width), BF),
        v((2, strip, width), BF),
        v((2, 8, strip, width), BF), v((4, 8, width), F32), v((rows, BLOCK), F32),
        v((rows, BLOCK), F32), v((width, rows), BF), v((1, 6 * local), F32),
        v((rows, heads * BLOCK), BF), v((rows, heads * BLOCK), BF), v((rows, heads * BLOCK), BF),
        v((heads, HD, rows), BF), v((heads, BLOCK, rows), BF),
        v((heads, kept, BLOCK), F32), v((rows, local), BF), v((4, 3 * quarter // 2, BLOCK), BF),
        v((4, 3 * quarter // 2, BLOCK), BF), v((quarter, width), BF),
        v((quarter, width), F32), v((quarter, width), F32), v((quarter, BLOCK), F32),
        v((4, quarter, width), BF), v((4, quarter, width), F32), v((4, quarter, width), BF),
        v((4, quarter, width), F32),
        v((6, quarter, width), BF), v((6, quarter, width), BF),
        v((4, quarter, width), BF), v((4, quarter, width), BF),
        v((2, 2, 2, strip, width // 2), BF), v((2, 2, 2, strip, width // 2), BF),
        v((2, 2, strip, width // 2), BF), v((2, 2, strip, width // 2), BF),
        v((2, 2, strip, width), BF), v((2, strip, width), BF),
        v((2, 2, strip, width // 2), BF),
        v((4, 2, BLOCK, BLOCK), BF), v((4, 2, BLOCK, BLOCK), BF),
        v((rows, heads * BLOCK), BF),
        v((4, strip, width), BF), v((4, strip, width), BF), v((4, 3 * strip // 2, BLOCK), BF),
        v((4, 3 * strip // 2, BLOCK), BF),
        v((rows, 6 * local), BF),
        v((3, 3, quarter, width // 3), BF), v((3, 2, quarter, width // 3), BF),
        v((3, quarter, width // 3), BF),
        v((4, strip, 6 * local), BF), v((4, strip, 6 * local), BF),
        v((8, width), F32), v((2, 2, 8, width), F32), v((2, 5, 8, width), F32),
        v((8, width), F32), v((8, width), F32), v((4, 8, width), F32),
        pltpu.SemaphoreType.DMA((SENDS,)), pltpu.SemaphoreType.DMA((RECVS,)),
        pltpu.SemaphoreType.DMA((17,)),
    ]
    spec = pl.BlockSpec(memory_space=pltpu.VMEM)
    anywhere = pl.BlockSpec(memory_space=pl.ANY)
    large_args = (0, 3, 4, 5, 6, 7, 8, 18)
    made = pl.pallas_call(
        layer_kernel,
        out_shape=outs,
        in_specs=[anywhere if n in large_args else spec for n in range(len(args))],
        out_specs=[anywhere] * len(outs),
        scratch_shapes=scratch,
        compiler_params=pltpu.CompilerParams(
            collective_id=0, has_side_effects=True, vmem_limit_bytes=58 << 20
        ),
        name="layer",
    )(*args)
    *large, small = made
    vector = jax.ShapeDtypeStruct((width,), F32)
    ended = pl.pallas_call(
        end_kernel,
        out_shape=[like(v, v.dtype) for v in large]
        + [like(query_bias), jax.ShapeDtypeStruct((local,), F32)]
        + [vector] * 7,
        in_specs=[spec] * len(made),
        out_specs=[spec] * 17,
        name="finish",
    )(*large, small)
    return (*ended[:7], ended[7].T, *ended[8:])


def solution(mesh):
    in_specs = (
        P("dp", None, None),
        P("dp", None),
        P("dp", None),
        P(None, "dp", "tensor"),
        P("dp", "tensor"),
        P("dp", "tensor"),
        P("tensor", "dp"),
        P("dp", "tensor"),
        P("tensor", "dp"),
        P(None, "tensor"),
        P("tensor"),
        P(),
        P("tensor"),
        P(),
        P(),
        P(),
        P(),
        P(),
        P("dp", None, None),
    )
    out_specs = (
        P("dp", None, None),
        P("dp", None, None),
        P(None, "dp", "tensor"),
        P("dp", "tensor"),
        P("dp", "tensor"),
        P("tensor", "dp"),
        P("dp", "tensor"),
        P("tensor", "dp"),
        P(None, "tensor"),
        P("tensor"),
        P(),
        P("tensor"),
        P(),
        P(),
        P(),
        P(),
        P(),
    )
    step = fused if fits(mesh) else shards
    return jax.shard_map(step, mesh=mesh, in_specs=in_specs, out_specs=out_specs, check_vma=False)
```
